32 devices in a mesh: blk: 8 (over y, x, core), ch: 4 (over z).
Axes of the slice: x: 2, y: 2, z: 4, core: 2. Of those that a mesh axis runs over, the one named last changes fastest.
Arguments:
- features_in: bfloat16 [32, 128, 2048], P('blk', None, 'ch'), may hold values from -6 to 6
- w_reduce: bfloat16 [2, 512, 2048], P(None, 'ch'), may hold values from -0.125 to 0.125
- w_dilated: bfloat16 [2, 512, 9, 512], P(None, 'ch'), may hold values from -0.09375 to 0.09375
- w_expand: bfloat16 [2, 512, 2048], P(None, None, 'ch'), may hold values from -0.25 to 0.25
- w_heads: bfloat16 [2, 4, 512, 9, 2048], P(None, None, 'ch'), may hold values from -0.046875 to 0.046875
- w_messages: bfloat16 [2, 6, 512, 9, 512], P(None, None, 'ch'), may hold values from -0.09375 to 0.09375
- norm_gain: float32 [2, 2, 512], P(None, None, 'ch'), may hold values from 0.5 to 1.5
- norm_bias: float32 [2, 2, 512], P(None, None, 'ch'), may hold values from -3 to 3
- wide_gain: float32 [2, 2048], P(None, 'ch'), may hold values from 0.5 to 1.5
- wide_bias: float32 [2, 2048], P(None, 'ch'), may hold values from -3 to 3
- gate_gain: float32 [2, 6, 512], P(None, None, 'ch'), may hold values from -4 to 4
- gate_bias: float32 [2, 6, 512], P(None, None, 'ch'), may hold values from -4 to 4
- canvas_ids: int32 [32, 128], replicated, may hold values from 0 to 8, as said below
- output_cotangent: bfloat16 [32, 128, 2048], P('blk', None, 'ch'), may hold values from -6 to 6
- task_cotangents: bfloat16 [2, 2, 32, 128, 512], P(None, None, 'blk', None, 'ch'), may hold values from -6 to 6
Outputs:
- output: bfloat16 [32, 128, 2048], P('blk', None, 'ch')
- task_maps: bfloat16 [2, 2, 32, 128, 512], P(None, None, 'blk', None, 'ch')
- input_grad: float32 [32, 128, 2048], P('blk', None, 'ch')
- w_reduce_grad: float32 [2, 2048, 512], P(None, 'blk', 'ch')
- w_dilated_grad: float32 [2, 9, 512, 512], P(None, None, 'blk', 'ch')
- w_expand_grad: float32 [2, 512, 2048], P(None, 'blk', 'ch')
- w_heads_grad: float32 [2, 4, 9, 2048, 512], P(None, None, None, 'blk', 'ch')
- w_messages_grad: float32 [2, 6, 9, 512, 512], P(None, None, None, 'blk', 'ch')
- norm_gain_grad: float32 [2, 2, 512], P(None, None, 'ch')
- norm_bias_grad: float32 [2, 2, 512], P(None, None, 'ch')
- wide_gain_grad: float32 [2, 2048], P(None, 'ch')
- wide_bias_grad: float32 [2, 2048], P(None, 'ch')
- gate_gain_grad: float32 [2, 6, 512], P(None, None, 'ch')
- gate_bias_grad: float32 [2, 6, 512], P(None, None, 'ch')
The draws below stay inside these ranges and needn't reach their ends.
Inputs may be any that keep to these rules, and one draw needn't show every extreme that they name: `canvas_ids`: each image id marks one rectangle of the canvas; images lie in four vertical strips, and one image covers every canvas row.
All inputs are finite; a program needn't handle non-finite values.
Results may differ from the reference program's by a relative error of at most 0.03.
Values may be sent and summed in bfloat16 or wider, within the bound.
A program may use at most 384 MiB of HBM per device.

```python
import jax
import jax.numpy as jnp
from jax import lax

FEAT = 2048
MID = 512
CANVAS_COLS = 128
LAYERS = 2
CANVAS_ROWS = 32


def draw_canvas_ids(key, part):
    key = jax.random.fold_in(key, 11)
    keys = jax.random.split(key, 3)
    shuffled = jax.random.permutation(keys[0], CANVAS_COLS - 1)
    borders = jnp.sort(shuffled[:3] + 1)
    column = jnp.arange(CANVAS_COLS, dtype=jnp.int32)
    strip = jnp.sum((column[:, None] >= borders[None, :]).astype(jnp.int32), axis=1)
    row_cut = jax.random.randint(keys[1], (4,), 1, CANVAS_ROWS)
    spanning = jax.random.randint(keys[2], (), 0, 4)
    row_index = jnp.arange(CANVAS_ROWS, dtype=jnp.int32)
    below = (row_index[:, None] >= row_cut[strip][None, :]).astype(jnp.int32)
    image_ids = jnp.where((strip == spanning)[None, :], 8, strip[None, :] * 2 + below)
    return image_ids.astype(jnp.int32)


def steps_of(key, dims, pieces, smallest, high):
    level, own = 1.0, jax.random.fold_in(key, 6)
    for dim, shards_of in pieces:
        draws = jnp.exp(jax.random.uniform(jax.random.fold_in(own, dim), (shards_of,), jnp.float32, smallest / len(pieces), high / len(pieces)))
        level = level * jnp.repeat(draws, dims[dim] // shards_of).reshape([-1 if axis == dim else 1 for axis in range(len(dims))])
    return level


def centred(rng, dims, scale, limit, cuts=(), held_as=jnp.bfloat16):
    entries = scale * jax.random.normal(rng, dims, jnp.float32)
    if cuts:
        entries = entries * steps_of(rng, dims, cuts, -0.22, 0.18)
    return jnp.clip(entries, -limit, limit).astype(held_as)


def setup_inputs(seed: int = 0) -> dict:
    key_of = jax.random.split(jax.random.key(seed), 16)
    features_in = centred(key_of[0], (CANVAS_ROWS, CANVAS_COLS, FEAT), 1.0, 6.0, ((0, 8), (2, 4)))
    w_reduce = centred(key_of[1], (LAYERS, MID, FEAT), FEAT ** -0.5, 0.125, ((1, 4),))
    w_dilated = centred(key_of[2], (LAYERS, MID, 9, MID), (9 * MID) ** -0.5, 0.09375, ((1, 4),))
    w_expand = centred(key_of[3], (LAYERS, MID, FEAT), MID ** -0.5, 0.25, ((2, 4),))
    w_heads = centred(key_of[4], (LAYERS, 4, MID, 9, FEAT), (9 * FEAT) ** -0.5, 0.046875, ((2, 4),))
    w_messages = centred(key_of[5], (LAYERS, 6, MID, 9, MID), (9 * MID) ** -0.5, 0.09375, ((2, 4),))
    norm_gain = jnp.clip(1.0 + 0.1 * jax.random.normal(key_of[6], (LAYERS, 2, MID), jnp.float32), 0.5, 1.5)
    norm_bias = centred(key_of[7], (LAYERS, 2, MID), 0.5, 3.0, ((2, 4),), jnp.float32)
    wide_gain = jnp.clip(1.0 + 0.1 * jax.random.normal(key_of[8], (LAYERS, FEAT), jnp.float32), 0.5, 1.5)
    wide_bias = centred(key_of[9], (LAYERS, FEAT), 0.5, 3.0, ((1, 4),), jnp.float32)
    gate_gain = centred(key_of[10], (LAYERS, 6, MID), 1.0, 4.0, ((2, 4),), jnp.float32)
    gate_bias = centred(key_of[11], (LAYERS, 6, MID), 1.0, 4.0, ((2, 4),), jnp.float32)
    canvas_ids = draw_canvas_ids(jax.random.fold_in(key_of[15], 71), 0)
    output_cotangent = centred(key_of[13], (CANVAS_ROWS, CANVAS_COLS, FEAT), 1.0, 6.0, ((0, 8), (2, 4)))
    task_cotangents = centred(key_of[14], (LAYERS, 2, CANVAS_ROWS, CANVAS_COLS, MID), 1.0, 6.0, ((2, 8), (4, 4)))
    return {"features_in": features_in, "w_reduce": w_reduce, "w_dilated": w_dilated, "w_expand": w_expand, "w_heads": w_heads, "w_messages": w_messages, "norm_gain": norm_gain, "norm_bias": norm_bias, "wide_gain": wide_gain, "wide_bias": wide_bias, "gate_gain": gate_gain, "gate_bias": gate_bias, "canvas_ids": canvas_ids, "output_cotangent": output_cotangent, "task_cotangents": task_cotangents}


epsilon = 1e-05
tap_offsets = tuple(((row_step, col_step) for row_step in (-1, 0, 1) for col_step in (-1, 0, 1)))
message_pairs = ((1, 0), (2, 0), (3, 0), (0, 3), (1, 3), (2, 3))

@jax.custom_vjp
def low(v):
    return lax.optimization_barrier(v.astype(jnp.bfloat16)).astype(jnp.float32)

@jax.custom_vjp
def low_back(v):
    return v

def low_keep(v):
    return (low(v), None)

def low_pass(kept, grad):
    return (grad,)

def back_keep(v):
    return (v, None)

def back_low(kept, grad):
    return (low(grad),)
low.defvjp(low_keep, low_pass)
low_back.defvjp(back_keep, back_low)

def neighbour_masks(canvas_ids, dilation):
    row_count = canvas_ids.shape[0]
    col_count = canvas_ids.shape[1]
    padded = jnp.pad(canvas_ids, 2, constant_values=-1)
    result = []
    for row_step, col_step in tap_offsets:
        top = 2 + row_step * dilation
        left = 2 + col_step * dilation
        beside = padded[top:top + row_count, left:left + col_count]
        result.append((beside == canvas_ids).astype(jnp.float32))
    return jnp.stack(result)

def convolve(values, weights, tap_masks, dilation):
    row_count = values.shape[0]
    col_count = values.shape[1]
    padded = jnp.pad(values, ((2, 2), (2, 2), (0, 0)))
    running = jnp.zeros((row_count, col_count, weights.shape[0], weights.shape[3]), jnp.float32)
    for tap_index, (row_step, col_step) in enumerate(tap_offsets):
        top = 2 + row_step * dilation
        left = 2 + col_step * dilation
        window = padded[top:top + row_count, left:left + col_count]
        product = jnp.einsum('rwc,kco->rwko', window, weights[:, tap_index], precision=lax.Precision.HIGHEST)
        running = running + tap_masks[tap_index][:, :, None, None] * product
    return running

def batch_norm(hidden, gain, bias):
    mean_value = lax.optimization_barrier(jnp.mean(hidden, axis=(0, 1)))
    variance = lax.optimization_barrier(jnp.mean(hidden * hidden, axis=(0, 1))) - mean_value * mean_value
    return gain * ((hidden - mean_value) * lax.rsqrt(variance + epsilon)) + bias

def pad_layer(inputs, reduce_w, dilated_w, expand_w, heads_w, messages_w, narrow_gain, narrow_bias, wide_g, wide_b, gate_g, gate_b, masks_one, masks_two):
    first_pre = low_back(jnp.dot(inputs, reduce_w, precision=lax.Precision.HIGHEST))
    first_act = low(jax.nn.silu(batch_norm(first_pre, narrow_gain[0], narrow_bias[0])))
    second_pre = low_back(convolve(first_act, dilated_w[None], masks_two, 2)[:, :, 0])
    second_act = low(jax.nn.silu(batch_norm(second_pre, narrow_gain[1], narrow_bias[1])))
    third_pre = low_back(jnp.dot(second_act, expand_w, precision=lax.Precision.HIGHEST))
    output = low(jax.nn.silu(batch_norm(third_pre, wide_g, wide_b) + inputs))
    heads_pre = low_back(convolve(output, heads_w, masks_one, 1))
    features = low(jax.nn.silu(heads_pre))
    depth_map = features[:, :, 0]
    segment_map = features[:, :, 3]
    for pair_index, (source, target) in enumerate(message_pairs):
        message = low_back(convolve(features[:, :, source], messages_w[pair_index][None], masks_one, 1)[:, :, 0])
        gate_value = jax.nn.sigmoid(gate_g[pair_index] * features[:, :, target] + gate_b[pair_index])
        if target == 0:
            depth_map = depth_map + gate_value * message
        else:
            segment_map = segment_map + gate_value * message
    return (output, jnp.stack([depth_map, segment_map]))

def reference(features_in, w_reduce, w_dilated, w_expand, w_heads, w_messages, norm_gain, norm_bias, wide_gain, wide_bias, gate_gain, gate_bias, canvas_ids, output_cotangent, task_cotangents):
    masks_one = neighbour_masks(canvas_ids, 1)
    masks_two = neighbour_masks(canvas_ids, 2)

    def forward(inputs, reduce_w, dilated_w, expand_w, heads_w, messages_w, narrow_gain, narrow_bias, wide_g, wide_b, gate_g, gate_b):
        current = inputs
        task_list = []
        for layer_index in range(LAYERS):
            current, maps = pad_layer(current, reduce_w[layer_index], dilated_w[layer_index], expand_w[layer_index], heads_w[layer_index], messages_w[layer_index], narrow_gain[layer_index], narrow_bias[layer_index], wide_g[layer_index], wide_b[layer_index], gate_g[layer_index], gate_b[layer_index], masks_one, masks_two)
            task_list.append(maps)
        return (current, jnp.stack(task_list))
    reduce_old = jnp.transpose(w_reduce.astype(jnp.float32), (0, 2, 1))
    dilated_old = jnp.transpose(w_dilated.astype(jnp.float32), (0, 2, 3, 1))
    heads_old = jnp.transpose(w_heads.astype(jnp.float32), (0, 1, 3, 4, 2))
    messages_old = jnp.transpose(w_messages.astype(jnp.float32), (0, 1, 3, 4, 2))
    floats = (features_in.astype(jnp.float32), reduce_old, dilated_old, w_expand.astype(jnp.float32), heads_old, messages_old, norm_gain.astype(jnp.float32), norm_bias.astype(jnp.float32), wide_gain.astype(jnp.float32), wide_bias.astype(jnp.float32), gate_gain.astype(jnp.float32), gate_bias.astype(jnp.float32))
    outputs, pullback = jax.vjp(forward, *floats)
    grads = pullback((output_cotangent.astype(jnp.float32), task_cotangents.astype(jnp.float32)))
    return (outputs[0].astype(jnp.bfloat16), outputs[1].astype(jnp.bfloat16), grads[0], grads[1], grads[2], grads[3], grads[4], grads[5], grads[6], grads[7], grads[8], grads[9], grads[10], grads[11])
```

```python
import functools
import types

import jax
import jax.numpy as jnp
from jax import lax
from jax.experimental import pallas as pl
from jax.experimental.pallas import tpu as pltpu
from jax.sharding import PartitionSpec as P

epsilon = 1e-05
BLK = "blk"
CH = "ch"
tap_offsets = tuple(((row_step, col_step) for row_step in (-1, 0, 1) for col_step in (-1, 0, 1)))
message_pairs = ((1, 0), (2, 0), (3, 0), (0, 3), (1, 3), (2, 3))


def extended_2(block, sides, width):
    for axis, dim in sides:
        count = lax.axis_size(axis)
        forward = [(i, i + 1) for i in range(count - 1)]
        backward = [(target, source) for source, target in forward]
        low = lax.ppermute(
            lax.slice_in_dim(block, block.shape[dim] - width, None, axis=dim), axis, forward
        )
        high = lax.ppermute(lax.slice_in_dim(block, 0, width, axis=dim), axis, backward)
        block = jnp.concatenate([low, block, high], axis=dim)
    return block


def silu_slope(values):
    sigmoid_value = jax.nn.sigmoid(values)
    return sigmoid_value * (1.0 + values * (1.0 - sigmoid_value))


def gather_channels(values):
    return lax.all_gather(values, CH, axis=3, tiled=True)


def reduce_channels(values):
    return lax.psum_scatter(
        values.astype(jnp.bfloat16), CH, scatter_dimension=3, tiled=True
    ).astype(jnp.float32)


def extend_rows(values, halo_width):
    return extended_2(values, ((BLK, 0),), halo_width)


def pixel_totals(first_sum, second_sum):
    return lax.psum((first_sum, second_sum), BLK)


def weight_totals(reduce_grad, dilated_grad, expand_grad, heads_grad, messages_grad):
    return (
        lax.psum_scatter(
            reduce_grad.astype(jnp.bfloat16), BLK, scatter_dimension=1, tiled=True
        ).astype(jnp.float32),
        lax.psum_scatter(
            dilated_grad.astype(jnp.bfloat16), BLK, scatter_dimension=2, tiled=True
        ).astype(jnp.float32),
        lax.psum_scatter(
            expand_grad.astype(jnp.bfloat16), BLK, scatter_dimension=1, tiled=True
        ).astype(jnp.float32),
        lax.psum_scatter(
            heads_grad.astype(jnp.bfloat16), BLK, scatter_dimension=3, tiled=True
        ).astype(jnp.float32),
        lax.psum_scatter(
            messages_grad.astype(jnp.bfloat16), BLK, scatter_dimension=3, tiled=True
        ).astype(jnp.float32),
    )


def widen(values, halo_width):
    return extend_rows(gather_channels(values), halo_width)


def local_masks(canvas_ids, row_count, dilation):
    col_count = canvas_ids.shape[1]
    padded = jnp.pad(canvas_ids, 2, constant_values=-1)
    start = lax.axis_index(BLK) * row_count
    window = lax.dynamic_slice(padded, (start, jnp.int32(0)), (row_count + 4, col_count + 4))
    centre = window[2 : 2 + row_count, 2 : 2 + col_count]
    result = []
    for row_step, col_step in tap_offsets:
        top = 2 + row_step * dilation
        left = 2 + col_step * dilation
        result.append(window[top : top + row_count, left : left + col_count] == centre)
    return jnp.stack(result)


def shifted(padded, halo_width, dilation, row_step, col_step, row_count, col_count):
    top = halo_width + row_step * dilation
    left = dilation + col_step * dilation
    return padded[top : top + row_count, left : left + col_count]


def conv_forward(extended, halo_width, dilation, weights, tap_masks):
    row_count = extended.shape[0] - 2 * halo_width
    col_count = extended.shape[1]
    padded = jnp.pad(extended, ((0, 0), (dilation, dilation), (0, 0)))
    running = jnp.zeros((row_count, col_count, weights.shape[0], weights.shape[1]), jnp.float32)
    for tap_index, (row_step, col_step) in enumerate(tap_offsets):
        window = shifted(padded, halo_width, dilation, row_step, col_step, row_count, col_count)
        product = jnp.einsum(
            "rwc,koc->rwko", window, weights[:, :, tap_index], preferred_element_type=jnp.float32
        )
        running = running + jnp.where(tap_masks[tap_index][:, :, None, None], product, 0.0)
    return running


def conv_weight_grad(extended, halo_width, dilation, gradient, tap_masks):
    row_count = extended.shape[0] - 2 * halo_width
    col_count = extended.shape[1]
    padded = jnp.pad(extended, ((0, 0), (dilation, dilation), (0, 0)))
    result = []
    for tap_index, (row_step, col_step) in enumerate(tap_offsets):
        window = shifted(padded, halo_width, dilation, row_step, col_step, row_count, col_count)
        masked = jnp.where(
            tap_masks[tap_index][:, :, None, None], gradient, jnp.zeros((), gradient.dtype)
        )
        result.append(
            jnp.einsum("rwc,rwko->kco", window, masked, preferred_element_type=jnp.float32)
        )
    return jnp.stack(result, axis=1)


def conv_input_grad(grad_extended, halo_width, dilation, weights, tap_masks):
    row_count = grad_extended.shape[0] - 2 * halo_width
    col_count = grad_extended.shape[1]
    padded = jnp.pad(grad_extended, ((0, 0), (dilation, dilation), (0, 0), (0, 0)))
    running = jnp.zeros((row_count, col_count, weights.shape[3]), jnp.float32)
    for tap_index, (row_step, col_step) in enumerate(tap_offsets):
        window = shifted(padded, halo_width, dilation, -row_step, -col_step, row_count, col_count)
        product = jnp.einsum(
            "rwko,koc->rwc", window, weights[:, :, tap_index], preferred_element_type=jnp.float32
        )
        running = running + jnp.where(tap_masks[8 - tap_index][:, :, None], product, 0.0)
    return running


def norm_forward(hidden, gain, bias, pixel_count):
    total_sum, square_sum = pixel_totals(
        jnp.sum(hidden, axis=(0, 1)), jnp.sum(hidden * hidden, axis=(0, 1))
    )
    mean_value = total_sum / pixel_count
    variance = square_sum / pixel_count - mean_value * mean_value
    inverse = lax.rsqrt(variance + epsilon)
    normed = (hidden - mean_value) * inverse
    return (gain * normed + bias, normed, inverse)


def norm_backward(upstream, normed, inverse, gain, pixel_count):
    bias_grad, gain_grad = pixel_totals(
        jnp.sum(upstream, axis=(0, 1)), jnp.sum(upstream * normed, axis=(0, 1))
    )
    hidden_grad = (
        gain * inverse * (upstream - bias_grad / pixel_count - normed * gain_grad / pixel_count)
    )
    return (hidden_grad, gain_grad, bias_grad)


def layer_forward(inputs, params, masks_one, masks_two, pixel_count):
    (
        reduce_w,
        dilated_w,
        expand_w,
        heads_w,
        messages_w,
        narrow_gain,
        narrow_bias,
        wide_g,
        wide_b,
        gate_g,
        gate_b,
    ) = params
    stored = types.SimpleNamespace()
    inputs_full = gather_channels(inputs[:, :, None, :])[:, :, 0, :]
    first_pre = jnp.einsum("rwc,oc->rwo", inputs_full, reduce_w, preferred_element_type=jnp.float32)
    first_norm, first_normed, first_inverse = norm_forward(
        first_pre, narrow_gain[0], narrow_bias[0], pixel_count
    )
    first_act = jax.nn.silu(first_norm).astype(jnp.bfloat16)
    first_ext = widen(first_act[:, :, None, :], 2)[:, :, 0, :]
    second_pre = conv_forward(first_ext, 2, 2, dilated_w[None], masks_two)[:, :, 0, :]
    second_norm, second_normed, second_inverse = norm_forward(
        second_pre, narrow_gain[1], narrow_bias[1], pixel_count
    )
    second_act = jax.nn.silu(second_norm).astype(jnp.bfloat16)
    second_full = gather_channels(second_act[:, :, None, :])[:, :, 0, :]
    third_pre = jnp.einsum("rwc,co->rwo", second_full, expand_w, preferred_element_type=jnp.float32)
    third_norm, third_normed, third_inverse = norm_forward(third_pre, wide_g, wide_b, pixel_count)
    summed = third_norm + inputs.astype(jnp.float32)
    output = jax.nn.silu(summed).astype(jnp.bfloat16)
    output_ext = widen(output[:, :, None, :], 1)[:, :, 0, :]
    heads_pre = conv_forward(output_ext, 1, 1, heads_w, masks_one)
    features = jax.nn.silu(heads_pre).astype(jnp.bfloat16)
    features_ext = widen(features, 1)
    feature_values = features.astype(jnp.float32)
    depth_map = feature_values[:, :, 0]
    segment_map = feature_values[:, :, 3]
    message_list = []
    for pair_index, (source, target) in enumerate(message_pairs):
        message = conv_forward(
            features_ext[:, :, source], 1, 1, messages_w[pair_index][None], masks_one
        )[:, :, 0]
        gate_value = jax.nn.sigmoid(
            gate_g[pair_index] * feature_values[:, :, target] + gate_b[pair_index]
        )
        message_list.append(message)
        if target == 0:
            depth_map = depth_map + gate_value * message
        else:
            segment_map = segment_map + gate_value * message
    stored.inputs_full = inputs_full
    stored.first_norm = first_norm
    stored.first_normed = first_normed
    stored.first_inverse = first_inverse
    stored.first_ext = first_ext
    stored.second_norm = second_norm
    stored.second_normed = second_normed
    stored.second_inverse = second_inverse
    stored.second_full = second_full
    stored.third_normed = third_normed
    stored.third_inverse = third_inverse
    stored.summed = summed
    stored.output_ext = output_ext
    stored.heads_pre = heads_pre
    stored.features = feature_values
    stored.features_ext = features_ext
    stored.messages = message_list
    return (output, depth_map, segment_map, stored)


def layer_backward(
    stored, upstream, depth_grad, segment_grad, params, masks_one, masks_two, pixel_count
):
    (
        reduce_w,
        dilated_w,
        expand_w,
        heads_w,
        messages_w,
        narrow_gain,
        narrow_bias,
        wide_g,
        wide_b,
        gate_g,
        gate_b,
    ) = params
    feature_values = stored.features
    zero_map = jnp.zeros_like(depth_grad)
    feature_grads = [depth_grad, zero_map, zero_map, segment_grad]
    message_grads = []
    gain_terms = []
    bias_terms = []
    for pair_index, (source, target) in enumerate(message_pairs):
        target_grad = depth_grad if target == 0 else segment_grad
        gate_value = jax.nn.sigmoid(
            gate_g[pair_index] * feature_values[:, :, target] + gate_b[pair_index]
        )
        message_grads.append(target_grad * gate_value)
        slope = target_grad * stored.messages[pair_index] * gate_value * (1.0 - gate_value)
        gain_terms.append(jnp.sum(slope * feature_values[:, :, target], axis=(0, 1)))
        bias_terms.append(jnp.sum(slope, axis=(0, 1)))
        feature_grads[target] = feature_grads[target] + slope * gate_g[pair_index]
    gate_gain_grad, gate_bias_grad = pixel_totals(jnp.stack(gain_terms), jnp.stack(bias_terms))
    message_stack = jnp.stack(message_grads, axis=2).astype(jnp.bfloat16)
    message_ext = extend_rows(message_stack, 1)
    weight_parts = []
    source_partials = [None, None, None, None]
    for pair_index, (source, target) in enumerate(message_pairs):
        weight_parts.append(
            conv_weight_grad(
                stored.features_ext[:, :, source],
                1,
                1,
                message_stack[:, :, pair_index : pair_index + 1],
                masks_one,
            )
        )
        partial_grad = conv_input_grad(
            message_ext[:, :, pair_index : pair_index + 1],
            1,
            1,
            messages_w[pair_index][None],
            masks_one,
        )
        if source_partials[source] is None:
            source_partials[source] = partial_grad
        else:
            source_partials[source] = source_partials[source] + partial_grad
    messages_w_grad = jnp.concatenate(weight_parts, axis=0)
    source_sums = reduce_channels(jnp.stack(source_partials, axis=2))
    features_total = jnp.stack(feature_grads, axis=2) + source_sums
    heads_grad = (features_total * silu_slope(stored.heads_pre)).astype(jnp.bfloat16)
    heads_w_grad = conv_weight_grad(stored.output_ext, 1, 1, heads_grad, masks_one)
    heads_ext = extend_rows(heads_grad, 1)
    output_partial = conv_input_grad(heads_ext, 1, 1, heads_w, masks_one)
    output_total = upstream + reduce_channels(output_partial[:, :, None, :])[:, :, 0, :]
    summed_grad = output_total * silu_slope(stored.summed)
    third_grad, wide_gain_grad, wide_bias_grad = norm_backward(
        summed_grad, stored.third_normed, stored.third_inverse, wide_g, pixel_count
    )
    third_low = third_grad.astype(jnp.bfloat16)
    expand_w_grad = jnp.einsum(
        "rwc,rwo->co", stored.second_full, third_low, preferred_element_type=jnp.float32
    )
    second_partial = jnp.einsum(
        "rwo,co->rwc", third_low, expand_w, preferred_element_type=jnp.float32
    )
    second_act_grad = reduce_channels(second_partial[:, :, None, :])[:, :, 0, :]
    second_grad, second_gain_grad, second_bias_grad = norm_backward(
        second_act_grad * silu_slope(stored.second_norm),
        stored.second_normed,
        stored.second_inverse,
        narrow_gain[1],
        pixel_count,
    )
    second_low = second_grad.astype(jnp.bfloat16)[:, :, None, :]
    dilated_w_grad = conv_weight_grad(stored.first_ext, 2, 2, second_low, masks_two)[0]
    second_ext = extend_rows(second_low, 2)
    first_partial = conv_input_grad(second_ext, 2, 2, dilated_w[None], masks_two)
    first_act_grad = reduce_channels(first_partial[:, :, None, :])[:, :, 0, :]
    first_grad, first_gain_grad, first_bias_grad = norm_backward(
        first_act_grad * silu_slope(stored.first_norm),
        stored.first_normed,
        stored.first_inverse,
        narrow_gain[0],
        pixel_count,
    )
    first_low = first_grad.astype(jnp.bfloat16)
    reduce_w_grad = jnp.einsum(
        "rwc,rwo->co", stored.inputs_full, first_low, preferred_element_type=jnp.float32
    )
    inputs_partial = jnp.einsum(
        "rwo,oc->rwc", first_low, reduce_w, preferred_element_type=jnp.float32
    )
    inputs_grad = reduce_channels(inputs_partial[:, :, None, :])[:, :, 0, :] + summed_grad
    weight_grads = (reduce_w_grad, dilated_w_grad, expand_w_grad, heads_w_grad, messages_w_grad)
    small_grads = (
        jnp.stack([first_gain_grad, second_gain_grad]),
        jnp.stack([first_bias_grad, second_bias_grad]),
        wide_gain_grad,
        wide_bias_grad,
        gate_gain_grad,
        gate_bias_grad,
    )
    return (inputs_grad, weight_grads, small_grads)


def plain_shards(
    features_in,
    w_reduce,
    w_dilated,
    w_expand,
    w_heads,
    w_messages,
    norm_gain,
    norm_bias,
    wide_gain,
    wide_bias,
    gate_gain,
    gate_bias,
    canvas_ids,
    output_cotangent,
    task_cotangents,
):
    row_count = features_in.shape[0]
    col_count = features_in.shape[1]
    pixel_count = float(row_count * col_count * lax.axis_size(BLK))
    masks_one = local_masks(canvas_ids, row_count, 1)
    masks_two = local_masks(canvas_ids, row_count, 2)
    layer_count = w_reduce.shape[0]
    layer_params = []
    for layer_index in range(layer_count):
        layer_params.append(
            (
                w_reduce[layer_index],
                w_dilated[layer_index],
                w_expand[layer_index],
                w_heads[layer_index],
                w_messages[layer_index],
                norm_gain[layer_index],
                norm_bias[layer_index],
                wide_gain[layer_index],
                wide_bias[layer_index],
                gate_gain[layer_index],
                gate_bias[layer_index],
            )
        )
    current = features_in
    stored_list = []
    task_list = []
    for layer_index in range(layer_count):
        current, depth_map, segment_map, stored = layer_forward(
            current, layer_params[layer_index], masks_one, masks_two, pixel_count
        )
        stored_list.append(stored)
        task_list.append(jnp.stack([depth_map, segment_map]).astype(jnp.bfloat16))
    upstream = output_cotangent.astype(jnp.float32)
    weight_list = [None] * layer_count
    small_list = [None] * layer_count
    for layer_index in reversed(range(layer_count)):
        upstream, weight_grads, small_grads = layer_backward(
            stored_list[layer_index],
            upstream,
            task_cotangents[layer_index, 0].astype(jnp.float32),
            task_cotangents[layer_index, 1].astype(jnp.float32),
            layer_params[layer_index],
            masks_one,
            masks_two,
            pixel_count,
        )
        weight_list[layer_index] = weight_grads
        small_list[layer_index] = small_grads
    stacked = [
        jnp.stack([weight_list[layer_index][member] for layer_index in range(layer_count)])
        for member in range(5)
    ]
    weight_sums = weight_totals(stacked[0], stacked[1], stacked[2], stacked[3], stacked[4])
    small_sums = [
        jnp.stack([small_list[layer_index][member] for layer_index in range(layer_count)])
        for member in range(6)
    ]
    return (
        current,
        jnp.stack(task_list),
        upstream,
        weight_sums[0],
        weight_sums[1],
        weight_sums[2],
        weight_sums[3],
        weight_sums[4],
        small_sums[0],
        small_sums[1],
        small_sums[2],
        small_sums[3],
        small_sums[4],
        small_sums[5],
    )


lanes = 128
source_order = ((1, 0, 4), (2, 1, 5), (0, 3), (3, 2))


def kernel_params():
    return pltpu.CompilerParams(vmem_limit_bytes=56 * 2**20)


def whole(shape):
    return pl.BlockSpec(shape, lambda *_: (0,) * len(shape))


def contract_last(left, right):
    return lax.dot_general(
        left, right, (((1,), (1,)), ((), ())), preferred_element_type=jnp.float32
    )


def sigmoid(values):
    return 1.0 / (1.0 + jnp.exp(-values))


def heads_forward_kernel(v_ref, w_ref, mask_ref, pre_ref, act_ref, z_ref):
    tap = pl.program_id(0)
    head_count, pixels, mid = pre_ref.shape
    cols = (v_ref.shape[0] - pixels) // 2
    row_step = tap // 3
    col_step = lax.rem(tap, 3)
    window = v_ref[pl.ds(pl.multiple_of(row_step * cols, cols), pixels), :]
    weights = w_ref[...].reshape(head_count * mid, v_ref.shape[1])
    product = contract_last(window, weights)
    mask = mask_ref[0]

    @pl.when(tap < 3)
    def _():
        for head in range(head_count):
            part = slice(head * mid, (head + 1) * mid)
            z_ref[col_step, :, part] = mask * product[:, part]

    @pl.when(tap >= 3)
    def _():
        for head in range(head_count):
            part = slice(head * mid, (head + 1) * mid)
            z_ref[col_step, :, part] += mask * product[:, part]

    @pl.when(tap == 8)
    def _():
        for head in range(head_count):
            part = slice(head * mid, (head + 1) * mid)
            total = (
                z_ref[1, :, part]
                + pltpu.roll(z_ref[0, :, part], 1, 0)
                + pltpu.roll(z_ref[2, :, part], pixels - 1, 0)
            )
            pre_ref[head] = total
            act_ref[head] = (total * sigmoid(total)).astype(jnp.bfloat16)


def heads_forward(extended, weights, mask):
    head_count, _, mid, feat = weights.shape
    pixels = mask.shape[1]
    return pl.pallas_call(
        heads_forward_kernel,
        grid=(9,),
        in_specs=[
            whole(extended.shape),
            pl.BlockSpec((head_count, 1, mid, feat), lambda t: (0, t, 0, 0)),
            pl.BlockSpec((1, pixels, lanes), lambda t: (t, 0, 0)),
        ],
        out_specs=[whole((head_count, pixels, mid))] * 2,
        out_shape=[
            jax.ShapeDtypeStruct((head_count, pixels, mid), jnp.float32),
            jax.ShapeDtypeStruct((head_count, pixels, mid), jnp.bfloat16),
        ],
        scratch_shapes=[pltpu.VMEM((3, pixels, head_count * mid), jnp.float32)],
        compiler_params=kernel_params(),
        cost_estimate=pl.CostEstimate(
            flops=2 * pixels * weights.size, bytes_accessed=2 * weights.size, transcendentals=0
        ),
    )(extended, weights, mask)


def tapped_conv(window_of, weights_of, mask_ref, pixels, mid, dilation):
    totals = [None, None, None]
    for row_step in range(3):
        product = contract_last(window_of(row_step), weights_of(row_step))
        for col_step in range(3):
            part = mask_ref[row_step * 3 + col_step] * product[:, col_step * mid : (col_step + 1) * mid]
            totals[col_step] = part if totals[col_step] is None else totals[col_step] + part
    return (
        totals[1]
        + pltpu.roll(totals[0], dilation, 0)
        + pltpu.roll(totals[2], pixels - dilation, 0)
    )


def messages_forward_kernel(low_ref, main_ref, high_ref, wa_ref, wb_ref, mask_ref, out_ref, lhs_ref):
    step = pl.program_id(0)
    parts, _, pixels, mid = main_ref.shape
    cols = low_ref.shape[2]

    def load(slot, source):
        for part in range(parts):
            chan = slice(part * mid, (part + 1) * mid)
            lhs_ref[slot, 0:cols, chan] = low_ref[part, source]
            lhs_ref[slot, cols : cols + pixels, chan] = main_ref[part, source]
            lhs_ref[slot, cols + pixels :, chan] = high_ref[part, source]

    def run(slot, w_ref, place):
        out_ref[place] = tapped_conv(
            lambda r: lhs_ref[slot, r * cols : r * cols + pixels, :],
            lambda r: w_ref[0, 3 * r : 3 * r + 3].reshape(3 * mid, parts * mid),
            mask_ref,
            pixels,
            mid,
            1,
        )

    for index, places in enumerate(((0, 4), (1, 5), (3, 2))):

        @pl.when(step == index)
        def _(index=index, places=places):
            if index < 2:
                load(0, index + 1)
                run(0, wa_ref, places[0])
                run(0, wb_ref, places[1])
            else:
                load(0, 0)
                load(1, 3)
                run(0, wa_ref, places[0])
                run(1, wb_ref, places[1])


def messages_forward(low, main, high, weights, mask):
    pixels = mask.shape[1]
    pairs, taps, mid, width = weights.shape
    cols = low.shape[2]
    return pl.pallas_call(
        messages_forward_kernel,
        grid=(3,),
        in_specs=[
            whole(low.shape),
            whole(main.shape),
            whole(high.shape),
            pl.BlockSpec((1, taps, mid, width), lambda i: (i + i // 2, 0, 0, 0)),
            pl.BlockSpec((1, taps, mid, width), lambda i: (4 + i - 4 * (i // 2), 0, 0, 0)),
            whole(mask.shape),
        ],
        out_specs=whole((pairs, pixels, mid)),
        out_shape=jax.ShapeDtypeStruct((pairs, pixels, mid), jnp.float32),
        scratch_shapes=[pltpu.VMEM((2, pixels + 2 * cols, width), jnp.bfloat16)],
        compiler_params=kernel_params(),
        cost_estimate=pl.CostEstimate(
            flops=2 * pixels * weights.size, bytes_accessed=2 * weights.size, transcendentals=0
        ),
    )(low, main, high, weights, weights, mask)


def dilated_forward_kernel(v_ref, w_ref, mask_ref, out_ref):
    pixels, mid = out_ref.shape
    cols = (v_ref.shape[0] - pixels) // 4
    out_ref[...] = tapped_conv(
        lambda r: v_ref[2 * r * cols : 2 * r * cols + pixels, :],
        lambda r: w_ref[3 * r : 3 * r + 3].reshape(3 * mid, v_ref.shape[1]),
        mask_ref,
        pixels,
        mid,
        2,
    )


def dilated_forward(extended, weights, mask):
    pixels, mid = mask.shape[1], weights.shape[1]
    return pl.pallas_call(
        dilated_forward_kernel,
        out_shape=jax.ShapeDtypeStruct((pixels, mid), jnp.float32),
        compiler_params=kernel_params(),
    )(extended, weights, mask)


def fill_taps(im_ref, slot, grad, mask_ref, pixels, cols, dilation):
    rows, mid = grad.shape
    wide = grad.astype(jnp.float32)
    shifted_by = (pltpu.roll(wide, rows - dilation, 0), wide, pltpu.roll(wide, dilation, 0))
    for tap, (row_step, col_step) in enumerate(tap_offsets):
        start = (1 - row_step) * dilation * cols
        part = shifted_by[col_step + 1][start : start + pixels]
        im_ref[slot, :, tap * mid : (tap + 1) * mid] = (part * mask_ref[tap]).astype(jnp.bfloat16)


def heads_backward_kernel(low_ref, main_ref, high_ref, w_ref, mask_ref, out_ref, im_ref):
    step = pl.program_id(0)
    head_count, pixels, mid = main_ref.shape
    cols = low_ref.shape[1]

    @pl.when(step == 0)
    def _():
        for head in range(head_count):
            grad = jnp.concatenate([low_ref[head], main_ref[head], high_ref[head]], axis=0)
            fill_taps(im_ref, head, grad, mask_ref, pixels, cols, 1)

    total = None
    for head in range(head_count):
        product = jnp.dot(
            im_ref[head],
            w_ref[head].reshape(9 * mid, w_ref.shape[3]),
            preferred_element_type=jnp.float32,
        )
        total = product if total is None else total + product
    out_ref[0] = total.astype(jnp.bfloat16)


def heads_backward(low, main, high, weights, mask, parts):
    head_count, taps, mid, feat = weights.shape
    pixels = mask.shape[1]
    width = feat // parts
    return pl.pallas_call(
        heads_backward_kernel,
        grid=(parts,),
        in_specs=[
            whole(low.shape),
            whole(main.shape),
            whole(high.shape),
            pl.BlockSpec((head_count, taps, mid, width), lambda j: (0, 0, 0, j)),
            whole(mask.shape),
        ],
        out_specs=pl.BlockSpec((1, pixels, width), lambda j: (j, 0, 0)),
        out_shape=jax.ShapeDtypeStruct((parts, pixels, width), jnp.bfloat16),
        scratch_shapes=[pltpu.VMEM((head_count, pixels, taps * mid), jnp.bfloat16)],
        compiler_params=kernel_params(),
        cost_estimate=pl.CostEstimate(
            flops=2 * pixels * weights.size, bytes_accessed=2 * weights.size, transcendentals=0
        ),
    )(low, main, high, weights, mask)


def messages_backward_kernel(low_ref, main_ref, high_ref, wa_ref, wb_ref, mask_ref, out_ref, im_ref):
    step = pl.program_id(0)
    parts, _, pixels, mid = out_ref.shape
    cols = low_ref.shape[1]

    def product(slot, pair, w_ref):
        grad = jnp.concatenate([low_ref[pair], main_ref[pair], high_ref[pair]], axis=0)
        fill_taps(im_ref, slot, grad, mask_ref, pixels, cols, 1)
        return jnp.dot(
            im_ref[slot],
            w_ref[0].reshape(9 * mid, parts * mid),
            preferred_element_type=jnp.float32,
        )

    def store(source, total):
        for part in range(parts):
            out_ref[part, source] = total[:, part * mid : (part + 1) * mid].astype(jnp.bfloat16)

    for index, pairs in enumerate(((0, 4), (1, 5), (3, 2))):

        @pl.when(step == index)
        def _(index=index, pairs=pairs):
            first = product(0, pairs[0], wa_ref)
            second = product(1, pairs[1], wb_ref)
            if index < 2:
                store(index + 1, first + second)
            else:
                store(0, first)
                store(3, second)


def messages_backward(low, main, high, weights, mask, parts):
    pixels = mask.shape[1]
    pairs, taps, mid, width = weights.shape
    return pl.pallas_call(
        messages_backward_kernel,
        grid=(3,),
        in_specs=[
            whole(low.shape),
            whole(main.shape),
            whole(high.shape),
            pl.BlockSpec((1, taps, mid, width), lambda i: (i + i // 2, 0, 0, 0)),
            pl.BlockSpec((1, taps, mid, width), lambda i: (4 + i - 4 * (i // 2), 0, 0, 0)),
            whole(mask.shape),
        ],
        out_specs=whole((parts, 4, pixels, mid)),
        out_shape=jax.ShapeDtypeStruct((parts, 4, pixels, mid), jnp.bfloat16),
        scratch_shapes=[pltpu.VMEM((2, pixels, taps * mid), jnp.bfloat16)],
        compiler_params=kernel_params(),
        cost_estimate=pl.CostEstimate(
            flops=2 * pixels * weights.size, bytes_accessed=2 * weights.size, transcendentals=0
        ),
    )(low, main, high, weights, weights, mask)


def dilated_backward_kernel(g_ref, w_ref, mask_ref, out_ref, im_ref):
    parts, pixels, mid = out_ref.shape
    cols = (g_ref.shape[0] - pixels) // 4
    fill_taps(im_ref, 0, g_ref[...], mask_ref, pixels, cols, 2)
    total = jnp.dot(
        im_ref[0], w_ref[...].reshape(9 * mid, parts * mid), preferred_element_type=jnp.float32
    )
    for part in range(parts):
        out_ref[part] = total[:, part * mid : (part + 1) * mid].astype(jnp.bfloat16)


def dilated_backward(extended, weights, mask, parts):
    pixels, mid = mask.shape[1], weights.shape[1]
    return pl.pallas_call(
        dilated_backward_kernel,
        out_shape=jax.ShapeDtypeStruct((parts, pixels, mid), jnp.bfloat16),
        scratch_shapes=[pltpu.VMEM((1, pixels, 9 * mid), jnp.bfloat16)],
        compiler_params=kernel_params(),
    )(extended, weights, mask)


def tap_rows(lhs_ref, start, window, mask_ref, pixels, cols):
    count = window.shape[0]
    size = window.shape[1]
    wide = window.astype(jnp.float32)
    shifted_by = (pltpu.roll(wide, 1, 1), wide, pltpu.roll(wide, size - 1, 1))
    for tap, (row_step, col_step) in enumerate(tap_offsets):
        left = (1 + row_step) * cols
        part = shifted_by[col_step + 1][:, left : left + pixels]
        lhs_ref[start + tap * count : start + (tap + 1) * count, :] = (
            part * mask_ref[0, tap : tap + 1, :]
        ).astype(jnp.bfloat16)


def heads_weight_kernel(before_ref, v_ref, after_ref, g_ref, mask_ref, out_ref, lhs_ref, acc_ref):
    step = pl.program_id(0)
    head_count, taps, chans, mid = out_ref.shape
    pixels = v_ref.shape[2]
    cols = before_ref.shape[2]
    window = jnp.concatenate([before_ref[0], v_ref[0], after_ref[0]], axis=1)
    tap_rows(lhs_ref, 0, window, mask_ref, pixels, cols)
    grads = jnp.concatenate([g_ref[0, head] for head in range(head_count)], axis=1)
    product = jnp.dot(lhs_ref[...], grads, preferred_element_type=jnp.float32)

    @pl.when(step == 0)
    def _():
        acc_ref[...] = product

    @pl.when(step > 0)
    def _():
        acc_ref[...] += product

    @pl.when(step == pl.num_programs(0) - 1)
    def _():
        for head in range(head_count):
            for tap in range(taps):
                out_ref[head, tap] = acc_ref[
                    tap * chans : (tap + 1) * chans, head * mid : (head + 1) * mid
                ]


def heads_weight(values, grads, mask, cols):
    count, chans, pixels = values.shape
    _, head_count, _, mid = grads.shape
    last = count - 1
    tail = pixels // cols - 1
    return pl.pallas_call(
        heads_weight_kernel,
        grid=(count,),
        in_specs=[
            pl.BlockSpec((1, chans, cols), lambda i: (jnp.maximum(i - 1, 0), 0, tail)),
            pl.BlockSpec((1, chans, pixels), lambda i: (i, 0, 0)),
            pl.BlockSpec((1, chans, cols), lambda i: (jnp.minimum(i + 1, last), 0, 0)),
            pl.BlockSpec((1, head_count, pixels, mid), lambda i: (i, 0, 0, 0)),
            pl.BlockSpec((1, 9, pixels), lambda i: (i, 0, 0)),
        ],
        out_specs=whole((head_count, 9, chans, mid)),
        out_shape=jax.ShapeDtypeStruct((head_count, 9, chans, mid), jnp.float32),
        scratch_shapes=[
            pltpu.VMEM((9 * chans, pixels), jnp.bfloat16),
            pltpu.VMEM((9 * chans, head_count * mid), jnp.float32),
        ],
        compiler_params=kernel_params(),
        cost_estimate=pl.CostEstimate(
            flops=18 * chans * count * pixels * head_count * mid,
            bytes_accessed=4 * 9 * chans * head_count * mid,
            transcendentals=0,
        ),
    )(values, values, values, grads, mask)


def messages_weight_kernel(before_ref, v_ref, after_ref, g_ref, mask_ref, out_ref, lhs_ref, *acc_refs):
    step = pl.program_id(0)
    pairs, taps, chans, mid = out_ref.shape
    pixels = v_ref.shape[3]
    cols = before_ref.shape[3]
    for index, (source, *members) in enumerate(source_order):
        window = jnp.concatenate(
            [before_ref[0, source], v_ref[0, source], after_ref[0, source]], axis=1
        )
        tap_rows(lhs_ref, index * taps * chans, window, mask_ref, pixels, cols)
        grads = jnp.concatenate([g_ref[0, pair] for pair in members], axis=1)
        product = jnp.dot(
            lhs_ref[index * taps * chans : (index + 1) * taps * chans, :],
            grads,
            preferred_element_type=jnp.float32,
        )
        acc_ref = acc_refs[index]

        @pl.when(step == 0)
        def _(acc_ref=acc_ref, product=product):
            acc_ref[...] = product

        @pl.when(step > 0)
        def _(acc_ref=acc_ref, product=product):
            acc_ref[...] += product

    @pl.when(step == pl.num_programs(0) - 1)
    def _():
        for index, (source, *members) in enumerate(source_order):
            for place, pair in enumerate(members):
                for tap in range(taps):
                    out_ref[pair, tap] = acc_refs[index][
                        tap * chans : (tap + 1) * chans, place * mid : (place + 1) * mid
                    ]


def messages_weight(values, grads, mask, cols):
    count, sources, chans, pixels = values.shape
    _, pairs, _, mid = grads.shape
    last = count - 1
    tail = pixels // cols - 1
    return pl.pallas_call(
        messages_weight_kernel,
        grid=(count,),
        in_specs=[
            pl.BlockSpec((1, sources, chans, cols), lambda i: (jnp.maximum(i - 1, 0), 0, 0, tail)),
            pl.BlockSpec((1, sources, chans, pixels), lambda i: (i, 0, 0, 0)),
            pl.BlockSpec((1, sources, chans, cols), lambda i: (jnp.minimum(i + 1, last), 0, 0, 0)),
            pl.BlockSpec((1, pairs, pixels, mid), lambda i: (i, 0, 0, 0)),
            pl.BlockSpec((1, 9, pixels), lambda i: (i, 0, 0)),
        ],
        out_specs=whole((pairs, 9, chans, mid)),
        out_shape=jax.ShapeDtypeStruct((pairs, 9, chans, mid), jnp.float32),
        scratch_shapes=[pltpu.VMEM((sources * 9 * chans, pixels), jnp.bfloat16)]
        + [
            pltpu.VMEM((9 * chans, (len(entry) - 1) * mid), jnp.float32) for entry in source_order
        ],
        compiler_params=kernel_params(),
        cost_estimate=pl.CostEstimate(
            flops=18 * chans * count * pixels * pairs * mid,
            bytes_accessed=4 * 9 * chans * pairs * mid,
            transcendentals=0,
        ),
    )(values, values, values, grads, mask)


MESH = pl.DeviceIdType.MESH


def greet(blocks, parts):
    barrier = pltpu.get_barrier_semaphore()
    blk, ch = lax.axis_index(BLK), lax.axis_index(CH)
    for step in range(1, blocks):
        pl.semaphore_signal(
            barrier, inc=1, device_id={BLK: lax.rem(blk + step, blocks)}, device_id_type=MESH
        )
    for step in range(1, parts):
        pl.semaphore_signal(
            barrier, inc=1, device_id={CH: lax.rem(ch + step, parts)}, device_id_type=MESH
        )
    pl.semaphore_wait(barrier, blocks + parts - 2)


def send_slots(source_of, target_ref, send_sem, recv_sem, axis, count):
    me = lax.axis_index(axis)
    copies = []
    for step in range(1, count):
        peer = lax.rem(me + step, count)
        copy = pltpu.make_async_remote_copy(
            src_ref=source_of(peer),
            dst_ref=target_ref.at[me],
            send_sem=send_sem.at[step],
            recv_sem=recv_sem.at[me],
            device_id={axis: peer},
            device_id_type=MESH,
        )
        copy.start()
        copies.append(copy)

    def finish():
        for step in range(1, count):
            peer = lax.rem(me + step, count)
            pltpu.make_async_remote_copy(
                src_ref=target_ref.at[peer],
                dst_ref=target_ref.at[peer],
                send_sem=send_sem.at[step],
                recv_sem=recv_sem.at[peer],
                device_id={axis: peer},
                device_id_type=MESH,
            ).wait_recv()
        for copy in copies:
            copy.wait_send()

    return finish


def block_totals(first, second, stat_ref, send_sem, recv_sem, blocks):
    me = lax.axis_index(BLK)
    stat_ref[me, 0:1] = first
    stat_ref[me, 1:2] = second
    send_slots(lambda _: stat_ref.at[me], stat_ref, send_sem, recv_sem, BLK, blocks)()
    total = stat_ref[0]
    for block in range(1, blocks):
        total = total + stat_ref[block]
    return total[0:1], total[1:2]


def fold(values):
    rows, width = values.shape
    return values.reshape(rows // 8, 8, width).sum(axis=0)


def row_loop(rows, block, body, carry):
    def step(index, state):
        return body(pl.ds(pl.multiple_of(index * block, block), block), state)

    return lax.fori_loop(0, rows // block, step, carry)


def moments(ref, block):
    rows, width = ref.shape

    def body(part, state):
        values = ref[part, :]
        return state[0] + fold(values), state[1] + fold(values * values)

    zero = jnp.zeros((8, width), jnp.float32)
    total, square = row_loop(rows, block, body, (zero, zero))
    return total.sum(axis=0, keepdims=True), square.sum(axis=0, keepdims=True)


def halo_copies(ref, edge, pixels, send_sem, recv_sem, blocks):
    me = lax.axis_index(BLK)

    def copy(source, target, side, peer):
        return pltpu.make_async_remote_copy(
            src_ref=ref.at[pl.ds(source, edge)],
            dst_ref=ref.at[pl.ds(target, edge)],
            send_sem=send_sem.at[side],
            recv_sem=recv_sem.at[side],
            device_id={BLK: peer},
            device_id_type=MESH,
        )

    up = copy(pixels, 0, 0, lax.rem(me + 1, blocks))
    down = copy(edge, edge + pixels, 1, lax.rem(me + blocks - 1, blocks))

    @pl.when(me < blocks - 1)
    def _():
        up.start()

    @pl.when(me > 0)
    def _():
        down.start()

    @pl.when(me == 0)
    def _():
        ref[0:edge, :] = jnp.zeros((edge, ref.shape[1]), ref.dtype)

    @pl.when(me == blocks - 1)
    def _():
        ref[edge + pixels :, :] = jnp.zeros((edge, ref.shape[1]), ref.dtype)

    def finish():
        @pl.when(me > 0)
        def _():
            up.wait_recv()
            down.wait_send()

        @pl.when(me < blocks - 1)
        def _():
            down.wait_recv()
            up.wait_send()

    return finish


def trunk_forward_kernel(
    blocks,
    parts,
    cur_ref,
    wr_ref,
    wd_ref,
    we_ref,
    mask_ref,
    gain1_ref,
    bias1_ref,
    gain2_ref,
    bias2_ref,
    gain3_ref,
    bias3_ref,
    out_ref,
    ext_out_ref,
    full_ref,
    normed1_ref,
    inverse1_ref,
    normed2_ref,
    inverse2_ref,
    normed3_ref,
    inverse3_ref,
    pre1_ref,
    pre3_ref,
    ext_ref,
    z_ref,
    gath_ref,
    stat1_ref,
    stat2_ref,
    stat3_ref,
    term1_ref,
    term3_ref,
    stat_send,
    stat_recv,
    halo_send,
    halo_recv,
    part_send,
    part_recv,
):
    pixels, feat = cur_ref.shape
    mid = normed1_ref.shape[1]
    wide = normed3_ref.shape[1]
    edge = (ext_ref.shape[0] - pixels) // 2
    ch = lax.axis_index(CH)
    pixel_count = float(pixels * blocks)
    greet(blocks, parts)

    def terms(total, square):
        mean_value = total / pixel_count
        variance = square / pixel_count - mean_value * mean_value
        return mean_value, lax.rsqrt(variance + epsilon)

    pre1_ref[...] = contract_last(cur_ref[...], wr_ref[...])
    total, square = moments(pre1_ref, 64)
    mean_value, inverse = terms(
        *block_totals(total, square, stat1_ref, stat_send.at[0], stat_recv.at[0], blocks)
    )
    term1_ref[0:1] = mean_value
    term1_ref[1:2] = inverse

    def first(part, state):
        value = gain1_ref[...] * ((pre1_ref[part, :] - mean_value) * inverse) + bias1_ref[...]
        pre1_ref[part, :] = value * sigmoid(value)
        return state

    own_mid = pl.ds(pl.multiple_of(ch * mid, mid), mid)
    normed1_ref[...] = (pre1_ref[:, own_mid] - term1_ref[0:1, own_mid]) * term1_ref[1:2, own_mid]
    inverse1_ref[...] = term1_ref[1:2, own_mid]
    row_loop(pixels, 64, first, 0)
    ext_ref[edge : edge + pixels, :] = pre1_ref[...].astype(jnp.bfloat16)
    wait_halo = halo_copies(ext_ref, edge, pixels, halo_send, halo_recv, blocks)

    half = edge // 2
    for row_step in (1, 0, 2):
        if row_step == 0:
            wait_halo()
        top = 2 * row_step * half
        product = contract_last(
            ext_ref[top : top + pixels, :],
            wd_ref[3 * row_step : 3 * row_step + 3].reshape(3 * mid, parts * mid),
        )
        for col_step in range(3):
            part = mask_ref[row_step * 3 + col_step] * product[:, col_step * mid : (col_step + 1) * mid]
            if row_step == 1:
                z_ref[col_step] = part
            else:
                z_ref[col_step] += part
    second_pre = (
        z_ref[1] + pltpu.roll(z_ref[0], 2, 0) + pltpu.roll(z_ref[2], pixels - 2, 0)
    )
    mean_value, inverse = terms(
        *block_totals(
            jnp.sum(second_pre, axis=0, keepdims=True),
            jnp.sum(second_pre * second_pre, axis=0, keepdims=True),
            stat2_ref,
            stat_send.at[1],
            stat_recv.at[1],
            blocks,
        )
    )
    normed = (second_pre - mean_value) * inverse
    normed2_ref[...] = normed
    inverse2_ref[...] = inverse
    value = gain2_ref[...] * normed + bias2_ref[...]
    gath_ref[ch] = (value * sigmoid(value)).astype(jnp.bfloat16)
    wait_parts = send_slots(
        lambda _: gath_ref.at[ch], gath_ref, part_send, part_recv, CH, parts
    )
    ext_out_ref[...] = ext_ref[...]
    wait_parts()
    for part in range(parts):
        full_ref[:, part * mid : (part + 1) * mid] = gath_ref[part]
    for part in range(parts):
        lane = slice(part * wide, (part + 1) * wide)
        pre3_ref[:, lane] = jnp.dot(
            full_ref[...], we_ref[:, lane], preferred_element_type=jnp.float32
        )
    total, square = moments(pre3_ref, 16)
    mean_value, inverse = terms(
        *block_totals(total, square, stat3_ref, stat_send.at[2], stat_recv.at[2], blocks)
    )
    term3_ref[0:1] = mean_value
    term3_ref[1:2] = inverse

    def last(part, state):
        value = (
            gain3_ref[...] * ((pre3_ref[part, :] - mean_value) * inverse)
            + bias3_ref[...]
            + cur_ref[part, :].astype(jnp.float32)
        )
        out_ref[part, :] = (value * sigmoid(value)).astype(jnp.bfloat16)
        return state

    row_loop(pixels, 16, last, 0)
    own_wide = pl.ds(pl.multiple_of(ch * wide, wide), wide)
    normed3_ref[...] = (pre3_ref[:, own_wide] - term3_ref[0:1, own_wide]) * term3_ref[1:2, own_wide]
    inverse3_ref[...] = term3_ref[1:2, own_wide]


def trunk_params(key):
    return pltpu.CompilerParams(
        vmem_limit_bytes=60 * 2**20, collective_id=key, has_side_effects=True
    )


def trunk_forward(blocks, parts, cols, current, reduce_w, dilated_w, expand_w, mask, norms):
    pixels, feat = current.shape
    narrow = reduce_w.shape[0]
    mid, wide = narrow // parts, feat // parts
    edge = 2 * cols
    f32, low = jnp.float32, jnp.bfloat16
    shape = jax.ShapeDtypeStruct
    rows = edge * 2 + pixels
    return pl.pallas_call(
        functools.partial(trunk_forward_kernel, blocks, parts),
        out_shape=[
            shape((pixels, feat), low),
            shape((rows, narrow), low),
            shape((pixels, narrow), low),
            shape((pixels, mid), f32),
            shape((1, mid), f32),
            shape((pixels, mid), f32),
            shape((1, mid), f32),
            shape((pixels, wide), f32),
            shape((1, wide), f32),
        ],
        scratch_shapes=[
            pltpu.VMEM((pixels, narrow), f32),
            pltpu.VMEM((pixels, feat), f32),
            pltpu.VMEM((rows, narrow), low),
            pltpu.VMEM((3, pixels, mid), f32),
            pltpu.VMEM((parts, pixels, mid), low),
            pltpu.VMEM((blocks, 2, narrow), f32),
            pltpu.VMEM((blocks, 2, mid), f32),
            pltpu.VMEM((blocks, 2, feat), f32),
            pltpu.VMEM((2, narrow), f32),
            pltpu.VMEM((2, feat), f32),
            pltpu.SemaphoreType.DMA((3, blocks)),
            pltpu.SemaphoreType.DMA((3, blocks)),
            pltpu.SemaphoreType.DMA((2,)),
            pltpu.SemaphoreType.DMA((2,)),
            pltpu.SemaphoreType.DMA((parts,)),
            pltpu.SemaphoreType.DMA((parts,)),
        ],
        compiler_params=trunk_params(1),
        cost_estimate=pl.CostEstimate(
            flops=2 * pixels * (2 * narrow * feat + 9 * mid * narrow),
            bytes_accessed=20 * 2**20,
            transcendentals=0,
        ),
    )(current, reduce_w, dilated_w, expand_w, mask, *norms)


def slope_of(values):
    gate = sigmoid(values)
    return gate * (1.0 + values * (1.0 - gate))


def sum_slots(ref, count):
    total = ref[0].astype(jnp.float32)
    for slot in range(1, count):
        total = total + ref[slot].astype(jnp.float32)
    return total


def trunk_backward_kernel(
    blocks,
    parts,
    up_ref,
    heads_ref,
    cur_ref,
    normed3_ref,
    inverse3_ref,
    gain3_ref,
    bias3_ref,
    we_ref,
    full_ref,
    normed2_ref,
    inverse2_ref,
    gain2_ref,
    bias2_ref,
    wd_ref,
    mask_f_ref,
    mask_b_ref,
    ext_ref,
    normed1_ref,
    inverse1_ref,
    gain1_ref,
    bias1_ref,
    wr_ref,
    out_ref,
    expand_ref,
    dilated_ref,
    reduce_ref,
    wide_ref,
    second_ref,
    first_ref,
    third_ref,
    grad_ref,
    im_ref,
    send2_ref,
    recv2_ref,
    send1_ref,
    recv1_ref,
    gath_ref,
    low_ref,
    ex_send_ref,
    ex_recv_ref,
    di_send_ref,
    di_recv_ref,
    re_send_ref,
    re_recv_ref,
    stat3_ref,
    stat2_ref,
    stat1_ref,
    stat_send,
    stat_recv,
    halo_send,
    halo_recv,
    part_send,
    part_recv,
    sum_send,
    sum_recv,
):
    pixels, wide = up_ref.shape
    mid = normed1_ref.shape[1]
    narrow = mid * parts
    feat = cur_ref.shape[1]
    edge = (grad_ref.shape[0] - pixels) // 2
    half = edge // 2
    blk = lax.axis_index(BLK)
    ch = lax.axis_index(CH)
    pixel_count = float(pixels * blocks)
    low = jnp.bfloat16
    greet(blocks, parts)
    own_wide = pl.ds(pl.multiple_of(ch * wide, wide), wide)

    def start(part, state):
        normed = normed3_ref[part, :]
        summed = (
            gain3_ref[...] * normed + bias3_ref[...] + cur_ref[part, own_wide].astype(jnp.float32)
        )
        value = (up_ref[part, :] + heads_ref[part, :].astype(jnp.float32)) * slope_of(summed)
        out_ref[part, :] = value
        return state[0] + fold(value), state[1] + fold(value * normed)

    zero = jnp.zeros((8, wide), jnp.float32)
    bias_sum, gain_sum = row_loop(pixels, 32, start, (zero, zero))
    bias_grad, gain_grad = block_totals(
        bias_sum.sum(axis=0, keepdims=True),
        gain_sum.sum(axis=0, keepdims=True),
        stat3_ref,
        stat_send.at[0],
        stat_recv.at[0],
        blocks,
    )
    wide_ref[0:1] = gain_grad
    wide_ref[1:2] = bias_grad
    scale = gain3_ref[...] * inverse3_ref[...]
    bias_part = bias_grad / pixel_count
    gain_part = gain_grad / pixel_count

    def third(part, state):
        third_ref[part, :] = (
            scale * (out_ref[part, :] - bias_part - normed3_ref[part, :] * gain_part)
        ).astype(low)
        return state

    row_loop(pixels, 32, third, 0)
    product = contract_last(third_ref[...], we_ref[...])
    for part in range(parts):
        send2_ref[part] = product[:, part * mid : (part + 1) * mid].astype(low)
    recv2_ref[ch] = send2_ref[ch]
    wait_parts = send_slots(
        lambda peer: send2_ref.at[peer], recv2_ref, part_send.at[0], part_recv.at[0], CH, parts
    )
    size = narrow // blocks
    product = lax.dot_general(
        full_ref[...], third_ref[...], (((0,), (0,)), ((), ())), preferred_element_type=jnp.float32
    )
    for block in range(blocks):
        ex_send_ref[block] = product[block * size : (block + 1) * size].astype(low)
    ex_recv_ref[blk] = ex_send_ref[blk]
    wait_expand = send_slots(
        lambda peer: ex_send_ref.at[peer], ex_recv_ref, sum_send.at[0], sum_recv.at[0], BLK, blocks
    )
    wait_parts()

    def narrow_norm(recv_ref, normed_ref, inverse_ref, gain_ref, bias_ref, stat_ref, phase, sums_ref):
        normed = normed_ref[...]
        value = sum_slots(recv_ref, parts) * slope_of(gain_ref[...] * normed + bias_ref[...])
        bias_grad, gain_grad = block_totals(
            jnp.sum(value, axis=0, keepdims=True),
            jnp.sum(value * normed, axis=0, keepdims=True),
            stat_ref,
            stat_send.at[phase],
            stat_recv.at[phase],
            blocks,
        )
        sums_ref[0:1] = gain_grad
        sums_ref[1:2] = bias_grad
        return (
            gain_ref[...]
            * inverse_ref[...]
            * (value - bias_grad / pixel_count - normed * (gain_grad / pixel_count))
        )

    grad = narrow_norm(
        recv2_ref, normed2_ref, inverse2_ref, gain2_ref, bias2_ref, stat2_ref, 1, second_ref
    )
    grad_ref[edge : edge + pixels, :] = grad.astype(low)
    wait_halo = halo_copies(grad_ref, edge, pixels, halo_send, halo_recv, blocks)
    own = grad_ref[edge : edge + pixels, :].astype(jnp.float32)
    turned = (pltpu.roll(own, pixels - 2, 0), own, pltpu.roll(own, 2, 0))
    for row_step in range(3):
        side = jnp.concatenate(
            [
                (mask_f_ref[row_step * 3 + col_step] * turned[col_step]).astype(low)
                for col_step in range(3)
            ],
            axis=1,
        )
        top = 2 * row_step * half
        product = lax.dot_general(
            ext_ref[top : top + pixels, :],
            side,
            (((0,), (0,)), ((), ())),
            preferred_element_type=jnp.float32,
        )
        for block in range(blocks):
            for col_step in range(3):
                di_send_ref[block, row_step * 3 + col_step] = product[
                    block * size : (block + 1) * size, col_step * mid : (col_step + 1) * mid
                ].astype(low)
    di_recv_ref[blk] = di_send_ref[blk]
    wait_halo()
    fill_taps(im_ref, 0, grad_ref[...], mask_b_ref, pixels, half, 2)
    product = jnp.dot(
        im_ref[0], wd_ref[...].reshape(9 * mid, narrow), preferred_element_type=jnp.float32
    )
    for part in range(parts):
        send1_ref[part] = product[:, part * mid : (part + 1) * mid].astype(low)
    recv1_ref[ch] = send1_ref[ch]
    wait_parts = send_slots(
        lambda peer: send1_ref.at[peer], recv1_ref, part_send.at[1], part_recv.at[1], CH, parts
    )
    wait_dilated = send_slots(
        lambda peer: di_send_ref.at[peer], di_recv_ref, sum_send.at[1], sum_recv.at[1], BLK, blocks
    )
    wait_parts()
    grad = narrow_norm(
        recv1_ref, normed1_ref, inverse1_ref, gain1_ref, bias1_ref, stat1_ref, 2, first_ref
    )
    gath_ref[ch] = grad.astype(low)
    wait_parts = send_slots(
        lambda _: gath_ref.at[ch], gath_ref, part_send.at[2], part_recv.at[2], CH, parts
    )
    product = lax.dot_general(
        cur_ref[...], gath_ref[ch], (((0,), (0,)), ((), ())), preferred_element_type=jnp.float32
    )
    size = feat // blocks
    for block in range(blocks):
        re_send_ref[block] = product[block * size : (block + 1) * size].astype(low)
    re_recv_ref[blk] = re_send_ref[blk]
    wait_reduce = send_slots(
        lambda peer: re_send_ref.at[peer], re_recv_ref, sum_send.at[2], sum_recv.at[2], BLK, blocks
    )
    wait_parts()
    for part in range(parts):
        low_ref[:, part * mid : (part + 1) * mid] = gath_ref[part]
    out_ref[...] += jnp.dot(low_ref[...], wr_ref[:, own_wide], preferred_element_type=jnp.float32)
    wait_expand()
    expand_ref[...] = sum_slots(ex_recv_ref, blocks)
    wait_dilated()
    dilated_ref[...] = sum_slots(di_recv_ref, blocks)
    wait_reduce()
    reduce_ref[...] = sum_slots(re_recv_ref, blocks)


def trunk_backward(blocks, parts, operands):
    pixels, wide = operands[0].shape
    feat = wide * parts
    mid = operands[9].shape[1]
    narrow = mid * parts
    rows = operands[16].shape[0]
    f32, low = jnp.float32, jnp.bfloat16
    shape = jax.ShapeDtypeStruct
    small, large = narrow // blocks, feat // blocks
    return pl.pallas_call(
        functools.partial(trunk_backward_kernel, blocks, parts),
        out_shape=[
            shape((pixels, wide), f32),
            shape((small, wide), f32),
            shape((9, small, mid), f32),
            shape((large, mid), f32),
            shape((2, wide), f32),
            shape((2, mid), f32),
            shape((2, mid), f32),
        ],
        scratch_shapes=[
            pltpu.VMEM((pixels, wide), low),
            pltpu.VMEM((rows, mid), low),
            pltpu.VMEM((1, pixels, 9 * mid), low),
            pltpu.VMEM((parts, pixels, mid), low),
            pltpu.VMEM((parts, pixels, mid), low),
            pltpu.VMEM((parts, pixels, mid), low),
            pltpu.VMEM((parts, pixels, mid), low),
            pltpu.VMEM((parts, pixels, mid), low),
            pltpu.VMEM((pixels, narrow), low),
            pltpu.VMEM((blocks, small, wide), low),
            pltpu.VMEM((blocks, small, wide), low),
            pltpu.VMEM((blocks, 9, small, mid), low),
            pltpu.VMEM((blocks, 9, small, mid), low),
            pltpu.VMEM((blocks, large, mid), low),
            pltpu.VMEM((blocks, large, mid), low),
            pltpu.VMEM((blocks, 2, wide), f32),
            pltpu.VMEM((blocks, 2, mid), f32),
            pltpu.VMEM((blocks, 2, mid), f32),
            pltpu.SemaphoreType.DMA((3, blocks)),
            pltpu.SemaphoreType.DMA((3, blocks)),
            pltpu.SemaphoreType.DMA((2,)),
            pltpu.SemaphoreType.DMA((2,)),
            pltpu.SemaphoreType.DMA((3, parts)),
            pltpu.SemaphoreType.DMA((3, parts)),
            pltpu.SemaphoreType.DMA((3, blocks)),
            pltpu.SemaphoreType.DMA((3, blocks)),
        ],
        compiler_params=trunk_params(2),
        cost_estimate=pl.CostEstimate(
            flops=4 * pixels * (2 * narrow * wide + 9 * mid * narrow),
            bytes_accessed=20 * 2**20,
            transcendentals=0,
        ),
    )(*operands)


def neighbour_rows(low_part, high_part):
    count = lax.axis_size(BLK)
    forward = [(i, i + 1) for i in range(count - 1)]
    backward = [(target, source) for source, target in forward]
    return lax.ppermute(low_part, BLK, forward), lax.ppermute(high_part, BLK, backward)


def gather_parts(values):
    return lax.all_gather(values, CH, axis=0, tiled=False)


def reduce_parts(values):
    return lax.psum_scatter(values, CH, scatter_dimension=0, tiled=False)


def own_slice(values, size, axis):
    return lax.dynamic_slice_in_dim(values, lax.axis_index(CH) * size, size, axis)


def gather_weights(weights, axis):
    blocks = lax.axis_size(BLK)
    parts = lax.axis_size(CH)
    other = 3 - axis
    size = weights.shape[other] // blocks
    mine = lax.dynamic_slice_in_dim(weights, lax.axis_index(BLK) * size, size, other)
    everything = lax.all_gather(mine, (BLK, CH), axis=0, tiled=False)
    everything = everything.reshape((blocks, parts) + mine.shape)
    layers = weights.shape[0]
    if axis == 1:
        return everything.transpose(2, 1, 3, 0, 4).reshape(
            layers, parts * weights.shape[1], weights.shape[2]
        )
    return everything.transpose(2, 0, 3, 1, 4).reshape(
        layers, weights.shape[1], parts * weights.shape[2]
    )


def canvas_masks(canvas_ids, dilation):
    rows, cols = canvas_ids.shape
    padded = jnp.pad(canvas_ids, 2, constant_values=-1)
    result = []
    for row_step, col_step in tap_offsets:
        top = 2 + row_step * dilation
        left = 2 + col_step * dilation
        result.append(padded[top : top + rows, left : left + cols] == canvas_ids)
    return jnp.stack(result).astype(jnp.float32)


def spread(mask):
    taps, rows, cols = mask.shape
    return jnp.broadcast_to(mask.reshape(taps, rows * cols, 1), (taps, rows * cols, lanes))


def mask_set(canvas_ids, row_count, dilation):
    everything = canvas_masks(canvas_ids, dilation)
    own = lax.dynamic_slice_in_dim(everything, lax.axis_index(BLK) * row_count, row_count, 1)
    turned = jnp.stack(
        [jnp.roll(own[tap], step[1] * dilation, axis=1) for tap, step in enumerate(tap_offsets)]
    )
    return everything, own, spread(turned), spread(own[::-1])


def shards(
    features_in,
    w_reduce,
    w_dilated,
    w_expand,
    w_heads,
    w_messages,
    norm_gain,
    norm_bias,
    wide_gain,
    wide_bias,
    gate_gain,
    gate_bias,
    canvas_ids,
    output_cotangent,
    task_cotangents,
):
    rows, cols, wide = features_in.shape
    pixels = rows * cols
    blocks = lax.axis_size(BLK)
    parts = lax.axis_size(CH)
    pixel_count = float(pixels * blocks)
    layers = w_reduce.shape[0]
    mid = w_reduce.shape[1]
    feat = wide * parts
    narrow = mid * parts
    low = jnp.bfloat16
    all_masks, _, forward_one, backward_one = mask_set(canvas_ids, rows, 1)
    _, _, forward_two, backward_two = mask_set(canvas_ids, rows, 2)
    chunk_masks = all_masks.reshape(9, blocks, pixels).transpose(1, 0, 2)

    reduce_full = gather_weights(w_reduce, 1)
    expand_full = gather_weights(w_expand, 2)
    small = jnp.concatenate(
        [norm_gain[:, 0], norm_bias[:, 0]], axis=0
    )
    small_full = gather_parts(small).transpose(1, 0, 2).reshape(2, layers, narrow)
    wide_full = (
        gather_parts(jnp.concatenate([wide_gain, wide_bias], axis=0))
        .transpose(1, 0, 2)
        .reshape(2, layers, feat)
    )
    current = gather_parts(features_in.reshape(pixels, wide)).transpose(1, 0, 2).reshape(pixels, feat)
    dilated_t = w_dilated.transpose(0, 2, 1, 3)
    heads_t = w_heads.transpose(0, 1, 3, 2, 4)
    messages_t = w_messages.transpose(0, 1, 3, 2, 4)

    kept = []
    task_list = []
    for layer in range(layers):
        keep = types.SimpleNamespace(input=current)
        (
            current,
            keep.first_ext,
            keep.second_full,
            keep.normed1,
            keep.inverse1,
            keep.normed2,
            keep.inverse2,
            keep.normed3,
            keep.inverse3,
        ) = trunk_forward(
            blocks,
            parts,
            cols,
            current,
            reduce_full[layer],
            dilated_t[layer],
            expand_full[layer],
            forward_two,
            (
                small_full[0, layer][None],
                small_full[1, layer][None],
                norm_gain[layer, 1][None],
                norm_bias[layer, 1][None],
                wide_full[0, layer][None],
                wide_full[1, layer][None],
            ),
        )
        keep.output = current
        kept.append(keep)
    output = own_slice(current, wide, 1).reshape(rows, cols, wide)

    partial_heads = []
    gate_grads = []
    for layer in range(layers):
        keep = kept[layer]
        out_full = keep.output
        before, after = neighbour_rows(out_full[-cols:], out_full[:cols])
        extended = jnp.concatenate([before, out_full, after], axis=0)
        heads_pre, features = heads_forward(extended, heads_t[layer], forward_one)
        keep.heads_pre = heads_pre
        features_all = gather_parts(features)
        before, after = neighbour_rows(features_all[:, :, -cols:], features_all[:, :, :cols])
        messages = messages_forward(before, features_all, after, messages_t[layer], forward_one)
        values = features.astype(jnp.float32)
        maps = [values[0], None, None, values[3]]
        cotangents = [
            task_cotangents[layer, 0].reshape(pixels, mid).astype(jnp.float32),
            None,
            None,
            task_cotangents[layer, 1].reshape(pixels, mid).astype(jnp.float32),
        ]
        head_grads = [cotangents[0], jnp.zeros_like(cotangents[0]), jnp.zeros_like(cotangents[0]), cotangents[3]]
        message_grads, gain_terms, bias_terms = [], [], []
        for pair, (source, target) in enumerate(message_pairs):
            gate = jax.nn.sigmoid(gate_gain[layer, pair] * values[target] + gate_bias[layer, pair])
            maps[target] = maps[target] + gate * messages[pair]
            message_grads.append((cotangents[target] * gate).astype(low))
            slope = cotangents[target] * messages[pair] * gate * (1.0 - gate)
            gain_terms.append(jnp.sum(slope * values[target], axis=0))
            bias_terms.append(jnp.sum(slope, axis=0))
            head_grads[target] = head_grads[target] + slope * gate_gain[layer, pair]
        task_list.append(jnp.stack([maps[0], maps[3]]).astype(low).reshape(2, rows, cols, mid))
        gate_grads.append(jnp.stack([jnp.stack(gain_terms), jnp.stack(bias_terms)]))
        message_low = jnp.stack(message_grads)
        before, after = neighbour_rows(message_low[:, -cols:], message_low[:, :cols])
        source_sums = reduce_parts(
            messages_backward(before, message_low, after, messages_t[layer], backward_one, parts)
        )
        chans = narrow // blocks
        feature_cols = features_all.transpose(1, 0, 3, 2).reshape(4, blocks, chans, pixels)
        feature_cols = feature_cols.transpose(1, 0, 2, 3)
        feature_cols = lax.all_to_all(feature_cols, BLK, 0, 0)
        grads_all = lax.all_gather(message_low, BLK, axis=0, tiled=False)
        keep.messages_grad = messages_weight(feature_cols, grads_all, chunk_masks, cols)
        head_total = jnp.stack(head_grads) + source_sums.astype(jnp.float32)
        heads_low = (head_total * silu_slope(heads_pre)).astype(low)
        before, after = neighbour_rows(heads_low[:, -cols:], heads_low[:, :cols])
        partial_heads.append(
            reduce_parts(
                heads_backward(before, heads_low, after, heads_t[layer], backward_one, parts)
            )
        )
        chans = feat // blocks
        value_cols = out_full.T.reshape(blocks, chans, pixels)
        value_cols = lax.all_to_all(value_cols, BLK, 0, 0)
        grads_all = lax.all_gather(heads_low, BLK, axis=0, tiled=False)
        keep.heads_grad = heads_weight(value_cols, grads_all, chunk_masks, cols)

    gate_sums = lax.psum(jnp.stack(gate_grads), BLK)

    upstream = output_cotangent.reshape(pixels, wide).astype(jnp.float32)
    for layer in reversed(range(layers)):
        keep = kept[layer]
        (
            upstream,
            keep.expand_grad,
            keep.dilated_grad,
            keep.reduce_grad,
            keep.wide_sums,
            keep.second_sums,
            keep.first_sums,
        ) = trunk_backward(
            blocks,
            parts,
            (
                upstream,
                partial_heads[layer],
                keep.input,
                keep.normed3,
                keep.inverse3,
                wide_gain[layer][None],
                wide_bias[layer][None],
                w_expand[layer],
                keep.second_full,
                keep.normed2,
                keep.inverse2,
                norm_gain[layer, 1][None],
                norm_bias[layer, 1][None],
                dilated_t[layer],
                forward_two,
                backward_two,
                keep.first_ext,
                keep.normed1,
                keep.inverse1,
                norm_gain[layer, 0][None],
                norm_bias[layer, 0][None],
                reduce_full[layer],
            ),
        )

    def stacked(of):
        return jnp.stack([of(keep) for keep in kept])

    narrow_sums = stacked(lambda keep: jnp.stack([keep.first_sums, keep.second_sums]))
    wide_sums = stacked(lambda keep: keep.wide_sums)
    return (
        output,
        jnp.stack(task_list),
        upstream.reshape(rows, cols, wide),
        stacked(lambda keep: keep.reduce_grad),
        stacked(lambda keep: keep.dilated_grad),
        stacked(lambda keep: keep.expand_grad),
        stacked(lambda keep: keep.heads_grad),
        stacked(lambda keep: keep.messages_grad),
        narrow_sums[:, :, 0],
        narrow_sums[:, :, 1],
        wide_sums[:, 0],
        wide_sums[:, 1],
        gate_sums[:, 0],
        gate_sums[:, 1],
    )


def route(*args):
    mid = args[1].shape[1]
    if mid % lanes == 0 and args[0].shape[1] % lanes == 0:
        return shards(*args)
    return plain_shards(*args)


def solution(mesh):
    placed = (
        P(BLK, None, CH),
        P(None, CH, None),
        P(None, CH, None, None),
        P(None, None, CH),
        P(None, None, CH, None, None),
        P(None, None, CH, None, None),
        P(None, None, CH),
        P(None, None, CH),
        P(None, CH),
        P(None, CH),
        P(None, None, CH),
        P(None, None, CH),
        P(),
        P(BLK, None, CH),
        P(None, None, BLK, None, CH),
    )
    return jax.shard_map(
        route,
        mesh=mesh,
        in_specs=placed,
        out_specs=(
            P(BLK, None, CH),
            P(None, None, BLK, None, CH),
            P(BLK, None, CH),
            P(None, BLK, CH),
            P(None, None, BLK, CH),
            P(None, BLK, CH),
            P(None, None, None, BLK, CH),
            P(None, None, None, BLK, CH),
            P(None, None, CH),
            P(None, None, CH),
            P(None, CH),
            P(None, CH),
            P(None, None, CH),
            P(None, None, CH),
        ),
        check_vma=False,
    )
```

```python
import functools
import types

import jax
import jax.numpy as jnp
from jax import lax
from jax.experimental import pallas as pl
from jax.experimental.pallas import tpu as pltpu
from jax.sharding import PartitionSpec as P

epsilon = 1e-05
BLK = "blk"
CH = "ch"
tap_offsets = tuple(((row_step, col_step) for row_step in (-1, 0, 1) for col_step in (-1, 0, 1)))
message_pairs = ((1, 0), (2, 0), (3, 0), (0, 3), (1, 3), (2, 3))


def extended_2(block, sides, width):
    for axis, dim in sides:
        count = lax.axis_size(axis)
        forward = [(i, i + 1) for i in range(count - 1)]
        backward = [(target, source) for source, target in forward]
        low = lax.ppermute(
            lax.slice_in_dim(block, block.shape[dim] - width, None, axis=dim), axis, forward
        )
        high = lax.ppermute(lax.slice_in_dim(block, 0, width, axis=dim), axis, backward)
        block = jnp.concatenate([low, block, high], axis=dim)
    return block


def silu_slope(values):
    sigmoid_value = jax.nn.sigmoid(values)
    return sigmoid_value * (1.0 + values * (1.0 - sigmoid_value))


def gather_channels(values):
    return lax.all_gather(values, CH, axis=3, tiled=True)


def reduce_channels(values):
    return lax.psum_scatter(
        values.astype(jnp.bfloat16), CH, scatter_dimension=3, tiled=True
    ).astype(jnp.float32)


def extend_rows(values, halo_width):
    return extended_2(values, ((BLK, 0),), halo_width)


def pixel_totals(first_sum, second_sum):
    return lax.psum((first_sum, second_sum), BLK)


def weight_totals(reduce_grad, dilated_grad, expand_grad, heads_grad, messages_grad):
    return (
        lax.psum_scatter(
            reduce_grad.astype(jnp.bfloat16), BLK, scatter_dimension=1, tiled=True
        ).astype(jnp.float32),
        lax.psum_scatter(
            dilated_grad.astype(jnp.bfloat16), BLK, scatter_dimension=2, tiled=True
        ).astype(jnp.float32),
        lax.psum_scatter(
            expand_grad.astype(jnp.bfloat16), BLK, scatter_dimension=1, tiled=True
        ).astype(jnp.float32),
        lax.psum_scatter(
            heads_grad.astype(jnp.bfloat16), BLK, scatter_dimension=3, tiled=True
        ).astype(jnp.float32),
        lax.psum_scatter(
            messages_grad.astype(jnp.bfloat16), BLK, scatter_dimension=3, tiled=True
        ).astype(jnp.float32),
    )


def widen(values, halo_width):
    return extend_rows(gather_channels(values), halo_width)


def local_masks(canvas_ids, row_count, dilation):
    col_count = canvas_ids.shape[1]
    padded = jnp.pad(canvas_ids, 2, constant_values=-1)
    start = lax.axis_index(BLK) * row_count
    window = lax.dynamic_slice(padded, (start, jnp.int32(0)), (row_count + 4, col_count + 4))
    centre = window[2 : 2 + row_count, 2 : 2 + col_count]
    result = []
    for row_step, col_step in tap_offsets:
        top = 2 + row_step * dilation
        left = 2 + col_step * dilation
        result.append(window[top : top + row_count, left : left + col_count] == centre)
    return jnp.stack(result)


def shifted(padded, halo_width, dilation, row_step, col_step, row_count, col_count):
    top = halo_width + row_step * dilation
    left = dilation + col_step * dilation
    return padded[top : top + row_count, left : left + col_count]


def conv_forward(extended, halo_width, dilation, weights, tap_masks):
    row_count = extended.shape[0] - 2 * halo_width
    col_count = extended.shape[1]
    padded = jnp.pad(extended, ((0, 0), (dilation, dilation), (0, 0)))
    running = jnp.zeros((row_count, col_count, weights.shape[0], weights.shape[1]), jnp.float32)
    for tap_index, (row_step, col_step) in enumerate(tap_offsets):
        window = shifted(padded, halo_width, dilation, row_step, col_step, row_count, col_count)
        product = jnp.einsum(
            "rwc,koc->rwko", window, weights[:, :, tap_index], preferred_element_type=jnp.float32
        )
        running = running + jnp.where(tap_masks[tap_index][:, :, None, None], product, 0.0)
    return running


def conv_weight_grad(extended, halo_width, dilation, gradient, tap_masks):
    row_count = extended.shape[0] - 2 * halo_width
    col_count = extended.shape[1]
    padded = jnp.pad(extended, ((0, 0), (dilation, dilation), (0, 0)))
    result = []
    for tap_index, (row_step, col_step) in enumerate(tap_offsets):
        window = shifted(padded, halo_width, dilation, row_step, col_step, row_count, col_count)
        masked = jnp.where(
            tap_masks[tap_index][:, :, None, None], gradient, jnp.zeros((), gradient.dtype)
        )
        result.append(
            jnp.einsum("rwc,rwko->kco", window, masked, preferred_element_type=jnp.float32)
        )
    return jnp.stack(result, axis=1)


def conv_input_grad(grad_extended, halo_width, dilation, weights, tap_masks):
    row_count = grad_extended.shape[0] - 2 * halo_width
    col_count = grad_extended.shape[1]
    padded = jnp.pad(grad_extended, ((0, 0), (dilation, dilation), (0, 0), (0, 0)))
    running = jnp.zeros((row_count, col_count, weights.shape[3]), jnp.float32)
    for tap_index, (row_step, col_step) in enumerate(tap_offsets):
        window = shifted(padded, halo_width, dilation, -row_step, -col_step, row_count, col_count)
        product = jnp.einsum(
            "rwko,koc->rwc", window, weights[:, :, tap_index], preferred_element_type=jnp.float32
        )
        running = running + jnp.where(tap_masks[8 - tap_index][:, :, None], product, 0.0)
    return running


def norm_forward(hidden, gain, bias, pixel_count):
    total_sum, square_sum = pixel_totals(
        jnp.sum(hidden, axis=(0, 1)), jnp.sum(hidden * hidden, axis=(0, 1))
    )
    mean_value = total_sum / pixel_count
    variance = square_sum / pixel_count - mean_value * mean_value
    inverse = lax.rsqrt(variance + epsilon)
    normed = (hidden - mean_value) * inverse
    return (gain * normed + bias, normed, inverse)


def norm_backward(upstream, normed, inverse, gain, pixel_count):
    bias_grad, gain_grad = pixel_totals(
        jnp.sum(upstream, axis=(0, 1)), jnp.sum(upstream * normed, axis=(0, 1))
    )
    hidden_grad = (
        gain * inverse * (upstream - bias_grad / pixel_count - normed * gain_grad / pixel_count)
    )
    return (hidden_grad, gain_grad, bias_grad)


def layer_forward(inputs, params, masks_one, masks_two, pixel_count):
    (
        reduce_w,
        dilated_w,
        expand_w,
        heads_w,
        messages_w,
        narrow_gain,
        narrow_bias,
        wide_g,
        wide_b,
        gate_g,
        gate_b,
    ) = params
    stored = types.SimpleNamespace()
    inputs_full = gather_channels(inputs[:, :, None, :])[:, :, 0, :]
    first_pre = jnp.einsum("rwc,oc->rwo", inputs_full, reduce_w, preferred_element_type=jnp.float32)
    first_norm, first_normed, first_inverse = norm_forward(
        first_pre, narrow_gain[0], narrow_bias[0], pixel_count
    )
    first_act = jax.nn.silu(first_norm).astype(jnp.bfloat16)
    first_ext = widen(first_act[:, :, None, :], 2)[:, :, 0, :]
    second_pre = conv_forward(first_ext, 2, 2, dilated_w[None], masks_two)[:, :, 0, :]
    second_norm, second_normed, second_inverse = norm_forward(
        second_pre, narrow_gain[1], narrow_bias[1], pixel_count
    )
    second_act = jax.nn.silu(second_norm).astype(jnp.bfloat16)
    second_full = gather_channels(second_act[:, :, None, :])[:, :, 0, :]
    third_pre = jnp.einsum("rwc,co->rwo", second_full, expand_w, preferred_element_type=jnp.float32)
    third_norm, third_normed, third_inverse = norm_forward(third_pre, wide_g, wide_b, pixel_count)
    summed = third_norm + inputs.astype(jnp.float32)
    output = jax.nn.silu(summed).astype(jnp.bfloat16)
    output_ext = widen(output[:, :, None, :], 1)[:, :, 0, :]
    heads_pre = conv_forward(output_ext, 1, 1, heads_w, masks_one)
    features = jax.nn.silu(heads_pre).astype(jnp.bfloat16)
    features_ext = widen(features, 1)
    feature_values = features.astype(jnp.float32)
    depth_map = feature_values[:, :, 0]
    segment_map = feature_values[:, :, 3]
    message_list = []
    for pair_index, (source, target) in enumerate(message_pairs):
        message = conv_forward(
            features_ext[:, :, source], 1, 1, messages_w[pair_index][None], masks_one
        )[:, :, 0]
        gate_value = jax.nn.sigmoid(
            gate_g[pair_index] * feature_values[:, :, target] + gate_b[pair_index]
        )
        message_list.append(message)
        if target == 0:
            depth_map = depth_map + gate_value * message
        else:
            segment_map = segment_map + gate_value * message
    stored.inputs_full = inputs_full
    stored.first_norm = first_norm
    stored.first_normed = first_normed
    stored.first_inverse = first_inverse
    stored.first_ext = first_ext
    stored.second_norm = second_norm
    stored.second_normed = second_normed
    stored.second_inverse = second_inverse
    stored.second_full = second_full
    stored.third_normed = third_normed
    stored.third_inverse = third_inverse
    stored.summed = summed
    stored.output_ext = output_ext
    stored.heads_pre = heads_pre
    stored.features = feature_values
    stored.features_ext = features_ext
    stored.messages = message_list
    return (output, depth_map, segment_map, stored)


def layer_backward(
    stored, upstream, depth_grad, segment_grad, params, masks_one, masks_two, pixel_count
):
    (
        reduce_w,
        dilated_w,
        expand_w,
        heads_w,
        messages_w,
        narrow_gain,
        narrow_bias,
        wide_g,
        wide_b,
        gate_g,
        gate_b,
    ) = params
    feature_values = stored.features
    zero_map = jnp.zeros_like(depth_grad)
    feature_grads = [depth_grad, zero_map, zero_map, segment_grad]
    message_grads = []
    gain_terms = []
    bias_terms = []
    for pair_index, (source, target) in enumerate(message_pairs):
        target_grad = depth_grad if target == 0 else segment_grad
        gate_value = jax.nn.sigmoid(
            gate_g[pair_index] * feature_values[:, :, target] + gate_b[pair_index]
        )
        message_grads.append(target_grad * gate_value)
        slope = target_grad * stored.messages[pair_index] * gate_value * (1.0 - gate_value)
        gain_terms.append(jnp.sum(slope * feature_values[:, :, target], axis=(0, 1)))
        bias_terms.append(jnp.sum(slope, axis=(0, 1)))
        feature_grads[target] = feature_grads[target] + slope * gate_g[pair_index]
    gate_gain_grad, gate_bias_grad = pixel_totals(jnp.stack(gain_terms), jnp.stack(bias_terms))
    message_stack = jnp.stack(message_grads, axis=2).astype(jnp.bfloat16)
    message_ext = extend_rows(message_stack, 1)
    weight_parts = []
    source_partials = [None, None, None, None]
    for pair_index, (source, target) in enumerate(message_pairs):
        weight_parts.append(
            conv_weight_grad(
                stored.features_ext[:, :, source],
                1,
                1,
                message_stack[:, :, pair_index : pair_index + 1],
                masks_one,
            )
        )
        partial_grad = conv_input_grad(
            message_ext[:, :, pair_index : pair_index + 1],
            1,
            1,
            messages_w[pair_index][None],
            masks_one,
        )
        if source_partials[source] is None:
            source_partials[source] = partial_grad
        else:
            source_partials[source] = source_partials[source] + partial_grad
    messages_w_grad = jnp.concatenate(weight_parts, axis=0)
    source_sums = reduce_channels(jnp.stack(source_partials, axis=2))
    features_total = jnp.stack(feature_grads, axis=2) + source_sums
    heads_grad = (features_total * silu_slope(stored.heads_pre)).astype(jnp.bfloat16)
    heads_w_grad = conv_weight_grad(stored.output_ext, 1, 1, heads_grad, masks_one)
    heads_ext = extend_rows(heads_grad, 1)
    output_partial = conv_input_grad(heads_ext, 1, 1, heads_w, masks_one)
    output_total = upstream + reduce_channels(output_partial[:, :, None, :])[:, :, 0, :]
    summed_grad = output_total * silu_slope(stored.summed)
    third_grad, wide_gain_grad, wide_bias_grad = norm_backward(
        summed_grad, stored.third_normed, stored.third_inverse, wide_g, pixel_count
    )
    third_low = third_grad.astype(jnp.bfloat16)
    expand_w_grad = jnp.einsum(
        "rwc,rwo->co", stored.second_full, third_low, preferred_element_type=jnp.float32
    )
    second_partial = jnp.einsum(
        "rwo,co->rwc", third_low, expand_w, preferred_element_type=jnp.float32
    )
    second_act_grad = reduce_channels(second_partial[:, :, None, :])[:, :, 0, :]
    second_grad, second_gain_grad, second_bias_grad = norm_backward(
        second_act_grad * silu_slope(stored.second_norm),
        stored.second_normed,
        stored.second_inverse,
        narrow_gain[1],
        pixel_count,
    )
    second_low = second_grad.astype(jnp.bfloat16)[:, :, None, :]
    dilated_w_grad = conv_weight_grad(stored.first_ext, 2, 2, second_low, masks_two)[0]
    second_ext = extend_rows(second_low, 2)
    first_partial = conv_input_grad(second_ext, 2, 2, dilated_w[None], masks_two)
    first_act_grad = reduce_channels(first_partial[:, :, None, :])[:, :, 0, :]
    first_grad, first_gain_grad, first_bias_grad = norm_backward(
        first_act_grad * silu_slope(stored.first_norm),
        stored.first_normed,
        stored.first_inverse,
        narrow_gain[0],
        pixel_count,
    )
    first_low = first_grad.astype(jnp.bfloat16)
    reduce_w_grad = jnp.einsum(
        "rwc,rwo->co", stored.inputs_full, first_low, preferred_element_type=jnp.float32
    )
    inputs_partial = jnp.einsum(
        "rwo,oc->rwc", first_low, reduce_w, preferred_element_type=jnp.float32
    )
    inputs_grad = reduce_channels(inputs_partial[:, :, None, :])[:, :, 0, :] + summed_grad
    weight_grads = (reduce_w_grad, dilated_w_grad, expand_w_grad, heads_w_grad, messages_w_grad)
    small_grads = (
        jnp.stack([first_gain_grad, second_gain_grad]),
        jnp.stack([first_bias_grad, second_bias_grad]),
        wide_gain_grad,
        wide_bias_grad,
        gate_gain_grad,
        gate_bias_grad,
    )
    return (inputs_grad, weight_grads, small_grads)


def plain_shards(
    features_in,
    w_reduce,
    w_dilated,
    w_expand,
    w_heads,
    w_messages,
    norm_gain,
    norm_bias,
    wide_gain,
    wide_bias,
    gate_gain,
    gate_bias,
    canvas_ids,
    output_cotangent,
    task_cotangents,
):
    row_count = features_in.shape[0]
    col_count = features_in.shape[1]
    pixel_count = float(row_count * col_count * lax.axis_size(BLK))
    masks_one = local_masks(canvas_ids, row_count, 1)
    masks_two = local_masks(canvas_ids, row_count, 2)
    layer_count = w_reduce.shape[0]
    layer_params = []
    for layer_index in range(layer_count):
        layer_params.append(
            (
                w_reduce[layer_index],
                w_dilated[layer_index],
                w_expand[layer_index],
                w_heads[layer_index],
                w_messages[layer_index],
                norm_gain[layer_index],
                norm_bias[layer_index],
                wide_gain[layer_index],
                wide_bias[layer_index],
                gate_gain[layer_index],
                gate_bias[layer_index],
            )
        )
    current = features_in
    stored_list = []
    task_list = []
    for layer_index in range(layer_count):
        current, depth_map, segment_map, stored = layer_forward(
            current, layer_params[layer_index], masks_one, masks_two, pixel_count
        )
        stored_list.append(stored)
        task_list.append(jnp.stack([depth_map, segment_map]).astype(jnp.bfloat16))
    upstream = output_cotangent.astype(jnp.float32)
    weight_list = [None] * layer_count
    small_list = [None] * layer_count
    for layer_index in reversed(range(layer_count)):
        upstream, weight_grads, small_grads = layer_backward(
            stored_list[layer_index],
            upstream,
            task_cotangents[layer_index, 0].astype(jnp.float32),
            task_cotangents[layer_index, 1].astype(jnp.float32),
            layer_params[layer_index],
            masks_one,
            masks_two,
            pixel_count,
        )
        weight_list[layer_index] = weight_grads
        small_list[layer_index] = small_grads
    stacked = [
        jnp.stack([weight_list[layer_index][member] for layer_index in range(layer_count)])
        for member in range(5)
    ]
    weight_sums = weight_totals(stacked[0], stacked[1], stacked[2], stacked[3], stacked[4])
    small_sums = [
        jnp.stack([small_list[layer_index][member] for layer_index in range(layer_count)])
        for member in range(6)
    ]
    return (
        current,
        jnp.stack(task_list),
        upstream,
        weight_sums[0],
        weight_sums[1],
        weight_sums[2],
        weight_sums[3],
        weight_sums[4],
        small_sums[0],
        small_sums[1],
        small_sums[2],
        small_sums[3],
        small_sums[4],
        small_sums[5],
    )


lanes = 128
source_order = ((1, 0, 4), (2, 1, 5), (0, 3), (3, 2))


def whole(shape):
    return pl.BlockSpec(shape, lambda *_: (0,) * len(shape))


def contract_last(left, right):
    return lax.dot_general(
        left, right, (((1,), (1,)), ((), ())), preferred_element_type=jnp.float32
    )


def sigmoid(values):
    return 1.0 / (1.0 + jnp.exp(-values))


MESH = pl.DeviceIdType.MESH
groups = ((1, 2), (0, 3))
group_pairs = ((0, 4, 1, 5), (3, 2))


def remote(source, target, send_sem, recv_sem, axis, peer):
    return pltpu.make_async_remote_copy(
        src_ref=source,
        dst_ref=target,
        send_sem=send_sem,
        recv_sem=recv_sem,
        device_id={axis: peer},
        device_id_type=MESH,
    )


def comm_params(key):
    return pltpu.CompilerParams(
        vmem_limit_bytes=60 * 2**20, collective_id=key, has_side_effects=True
    )


def announce(targets):
    barrier = pltpu.get_barrier_semaphore()
    for axis, peer in targets:
        pl.semaphore_signal(barrier, inc=1, device_id={axis: peer}, device_id_type=MESH)
    pl.semaphore_wait(barrier, len(targets))


def near_blocks(blocks):
    me = lax.axis_index(BLK)
    sibling = me + 1 - 2 * lax.rem(me, 2)
    return sibling, [lax.rem(me + 2 * step, blocks) for step in range(1, blocks // 2)]


def others(axis, count):
    me = lax.axis_index(axis)
    return [lax.rem(me + step, count) for step in range(1, count)]


def gather_job(source, target, sems, blocks):
    near_send, slot_recv, pass_send, local_sem = sems
    me = lax.axis_index(BLK)
    sibling, peers = near_blocks(blocks)
    own = pltpu.make_async_copy(source, target.at[me], local_sem.at[0])

    def near(step, peer):
        return remote(
            source, target.at[me], near_send.at[step], slot_recv.at[me], BLK, peer
        )

    def passing(step, peer):
        return remote(
            target.at[peer], target.at[peer], pass_send.at[step], slot_recv.at[peer], BLK, sibling
        )

    def start():
        own.start()
        for step, peer in enumerate(peers + [sibling]):
            near(step, peer).start()

    def forward():
        for step, peer in enumerate(peers):
            copy = passing(step, peer)
            copy.wait_recv()
            copy.start()

    def finish():
        for step in range(blocks // 2):
            passing(0, lax.rem(sibling + 2 * step, blocks)).wait_recv()
        for step, peer in enumerate(peers + [sibling]):
            near(step, peer).wait_send()
        for step, peer in enumerate(peers):
            passing(step, peer).wait_send()
        own.wait()

    return start, forward, finish


def swap_job(source, target, sems, blocks):
    slot_send, slot_recv, _, local_sem = sems
    me = lax.axis_index(BLK)
    width = source.shape[1] // blocks

    def part_of(block):
        return source.at[:, pl.ds(pl.multiple_of(block * width, width), width)]

    own = pltpu.make_async_copy(part_of(me), target.at[me], local_sem.at[0])

    def copy(step, peer, slot):
        return remote(
            part_of(peer), target.at[slot], slot_send.at[step], slot_recv.at[slot], BLK, peer
        )

    def start():
        for step, peer in enumerate(others(BLK, blocks)):
            copy(step, peer, me).start()
        own.start()

    def finish():
        for step, peer in enumerate(others(BLK, blocks)):
            copy(step, peer, peer).wait_recv()
            copy(step, peer, me).wait_send()
        own.wait()

    return start, lambda: None, finish


job_kinds = (gather_job, swap_job)
gather_kind, swap_kind = 0, 1


def job_target(kind, source, blocks):
    if kind == gather_kind:
        return jax.ShapeDtypeStruct((blocks,) + source.shape, source.dtype)
    return jax.ShapeDtypeStruct(
        (blocks, source.shape[0], source.shape[1] // blocks), source.dtype
    )


def job_sems(blocks):
    dma = pltpu.SemaphoreType.DMA
    return [dma((blocks,)), dma((blocks,)), dma((blocks,)), dma((1,))]


def job_call(kernel, jobs, blocks, in_specs, out_specs, out_shape, scratch_shapes, **options):
    anywhere = pl.BlockSpec(memory_space=pl.ANY)
    n_in, n_out, n_scratch = len(in_specs), len(out_specs), len(scratch_shapes)
    count = len(jobs)

    def wrapped(*refs):
        ins, refs = refs[:n_in], refs[n_in:]
        sources, refs = refs[:count], refs[count:]
        outs, refs = refs[:n_out], refs[n_out:]
        targets, refs = refs[:count], refs[count:]
        scratch, sems = refs[:n_scratch], refs[n_scratch:]
        running = [
            job_kinds[kind](
                sources[place], targets[place], sems[4 * place : 4 * place + 4], blocks
            )
            for place, (kind, _) in enumerate(jobs)
        ]
        kernel(running, *ins, *outs, *scratch)

    def call(*operands):
        result = pl.pallas_call(
            wrapped,
            in_specs=list(in_specs) + [anywhere] * count,
            out_specs=list(out_specs) + [anywhere] * count,
            out_shape=list(out_shape) + [job_target(kind, source, blocks) for kind, source in jobs],
            scratch_shapes=list(scratch_shapes) + job_sems(blocks) * count,
            **options,
        )(*operands, *[source for _, source in jobs])
        return result[:n_out], result[n_out:]

    return call


def weights_job(wr_ref, we_ref, layer, fulls, sems, blocks, parts):
    part_send, part_recv, near_send, near_recv, pass_send, local_sem = sems
    _, mid, feat = wr_ref.shape
    _, narrow, wide = we_ref.shape
    cw, rw = feat // blocks, narrow // blocks
    blk, ch = lax.axis_index(BLK), lax.axis_index(CH)
    sibling, peers = near_blocks(blocks)

    def cut(index, size):
        return pl.ds(pl.multiple_of(index * size, size), size)

    def source(array):
        if array == 0:
            return wr_ref.at[layer, :, cut(blk, cw)]
        return we_ref.at[layer, cut(blk, rw), :]

    def share(array, part):
        if array == 0:
            return fulls[0].at[cut(part, mid), cut(blk, cw)]
        return fulls[1].at[cut(blk, rw), cut(part, wide)]

    def stripe(array, block):
        if array == 0:
            return fulls[0].at[:, cut(block, cw)]
        return fulls[1].at[cut(block, rw), :]

    def own(array):
        return pltpu.make_async_copy(source(array), share(array, ch), local_sem.at[array])

    def part_copy(array, step, peer, slot):
        return remote(
            source(array),
            share(array, slot),
            part_send.at[array, step],
            part_recv.at[array, slot],
            CH,
            peer,
        )

    def near_copy(array, step, peer):
        return remote(
            stripe(array, blk),
            stripe(array, blk),
            near_send.at[array, step],
            near_recv.at[array, blk],
            BLK,
            peer,
        )

    def passing(array, step, peer):
        return remote(
            stripe(array, peer),
            stripe(array, peer),
            pass_send.at[array, step],
            near_recv.at[array, peer],
            BLK,
            sibling,
        )

    def start():
        for array in range(2):
            own(array).start()
            for step, peer in enumerate(others(CH, parts)):
                part_copy(array, step, peer, ch).start()

    def spread():
        for array in range(2):
            for step, peer in enumerate(others(CH, parts)):
                part_copy(array, step, peer, peer).wait_recv()
            own(array).wait()
            for step, peer in enumerate(peers + [sibling]):
                near_copy(array, step, peer).start()

    def forward(array):
        for step, peer in enumerate(peers):
            copy = passing(array, step, peer)
            copy.wait_recv()
            copy.start()

    def finish():
        for array in range(2):
            for step in range(blocks // 2):
                passing(array, 0, lax.rem(sibling + 2 * step, blocks)).wait_recv()
            for step, peer in enumerate(others(CH, parts)):
                part_copy(array, step, peer, ch).wait_send()
            for step, peer in enumerate(peers + [sibling]):
                near_copy(array, step, peer).wait_send()
            for step, peer in enumerate(peers):
                passing(array, step, peer).wait_send()

    return start, spread, forward, finish


def weights_sems(blocks, parts):
    dma = pltpu.SemaphoreType.DMA
    near = blocks // 2
    return [
        dma((2, parts)),
        dma((2, parts)),
        dma((2, near)),
        dma((2, blocks)),
        dma((2, near)),
        dma((2,)),
    ]


def prologue_kernel(
    blocks,
    parts,
    feat_ref,
    wr_ref,
    we_ref,
    narrow_ref,
    wide_ref,
    ids_ref,
    cur_ref,
    full_r,
    full_e,
    narrow_out,
    wide_out,
    f1_ref,
    b1_ref,
    f2_ref,
    b2_ref,
    cols_ref,
    line_send,
    line_recv,
    small_send,
    small_recv,
    local_sem,
    *sems,
):
    pixels, wide = feat_ref.shape
    blk, ch = lax.axis_index(BLK), lax.axis_index(CH)
    sibling, peers = near_blocks(blocks)
    smalls = ((narrow_ref, narrow_out), (wide_ref, wide_out))

    def lane_part(index):
        return cur_ref.at[:, pl.ds(pl.multiple_of(index * wide, wide), wide)]

    start, spread, forward, finish = weights_job(
        wr_ref, we_ref, 0, (full_r, full_e), sems, blocks, parts
    )
    own = pltpu.make_async_copy(feat_ref, lane_part(ch), local_sem.at[0])
    own.start()
    announce(
        [(CH, peer) for peer in others(CH, parts)]
        + [(BLK, peer) for peer in [sibling] + peers]
    )
    start()

    right, left = lax.rem(ch + 1, parts), lax.rem(ch + parts - 1, parts)

    def sides(hop):
        return (
            (0, lax.rem(ch + parts - hop, parts), right, ch - hop >= 0, ch < parts - 1),
            (1, lax.rem(ch + hop, parts), left, ch + hop < parts, ch > 0),
        )

    def line_copy(block, side, hop, peer):
        return remote(
            feat_ref if hop == 0 else lane_part(block),
            lane_part(block),
            line_send.at[side, hop],
            line_recv.at[block],
            CH,
            peer,
        )

    def line_hop(hop):
        for side, block, peer, valid, goes in sides(hop):
            if hop > 0:

                @pl.when(valid)
                def _():
                    line_copy(block, side, hop, peer).wait_recv()

            if hop < parts - 1:

                @pl.when(valid & goes)
                def _():
                    line_copy(block, side, hop, peer).start()

    def small_copy(place, step, peer, slot):
        source, target = smalls[place]
        return remote(
            source,
            target.at[slot],
            small_send.at[place, step],
            small_recv.at[place, slot],
            CH,
            peer,
        )

    def small_own(place):
        source, target = smalls[place]
        return pltpu.make_async_copy(source, target.at[ch], local_sem.at[1 + place])

    line_hop(0)
    for place in range(2):
        small_own(place).start()
        for step, peer in enumerate(others(CH, parts)):
            small_copy(place, step, peer, ch).start()
    spread()

    rows = f1_ref.shape[1] // lanes
    for f_ref, b_ref, reach in ((f1_ref, b1_ref, 1), (f2_ref, b2_ref, 2)):
        for row in range(rows):
            place = 2 + blk * rows + row
            for tap, (row_step, col_step) in enumerate(tap_offsets):
                a, b = row_step * reach, col_step * reach
                here = ids_ref[place, 4 - b : 4 - b + lanes, :]
                there = ids_ref[place + a, 4 : 4 + lanes, :]
                f_ref[tap, row * lanes : (row + 1) * lanes] = jnp.where(
                    (here == there) & (here >= 0), 1.0, 0.0
                )
                here = ids_ref[place, 4 : 4 + lanes, :]
                there = ids_ref[place - a, 4 - b : 4 - b + lanes, :]
                b_ref[tap, row * lanes : (row + 1) * lanes] = jnp.where(here == there, 1.0, 0.0)
    lane = lax.broadcasted_iota(jnp.int32, (lanes, lanes), 1)

    def all_rows(row, state):
        here = ids_ref[2 + row, 4 : 4 + lanes, :]
        value = jnp.zeros((lanes, lanes), jnp.float32)
        for tap, (row_step, col_step) in enumerate(tap_offsets):
            there = ids_ref[2 + row + row_step, 4 + col_step : 4 + col_step + lanes, :]
            value = jnp.where((lane == tap) & (here == there), 1.0, value)
        cols_ref[pl.ds(pl.multiple_of(row * lanes, lanes), lanes), :] = value
        return state

    lax.fori_loop(0, ids_ref.shape[0] - 4, all_rows, 0)
    for hop in range(1, parts):
        line_hop(hop)
        if hop <= 2:
            forward(hop - 1)
    for array in range(parts - 1, 2):
        forward(array)
    finish()
    for hop in range(parts - 1):
        for side, block, peer, valid, goes in sides(hop):

            @pl.when(valid & goes)
            def _():
                line_copy(block, side, hop, peer).wait_send()

    for place in range(2):
        for step, peer in enumerate(others(CH, parts)):
            small_copy(place, step, peer, peer).wait_recv()
            small_copy(place, step, peer, ch).wait_send()
        small_own(place).wait()
    own.wait()


def prologue(blocks, parts, features, reduce_w, expand_w, narrow_terms, wide_terms, canvas_ids):
    layers, mid, feat = reduce_w.shape
    pixels, wide = features.shape
    narrow = mid * parts
    f32, low = jnp.float32, jnp.bfloat16
    shape = jax.ShapeDtypeStruct
    padded = jnp.pad(canvas_ids, ((2, 2), (4, 4)), constant_values=-1)
    ids = jnp.broadcast_to(padded[:, :, None], padded.shape + (lanes,))
    anywhere = pl.BlockSpec(memory_space=pl.ANY)
    inside = pl.BlockSpec(memory_space=pltpu.VMEM)
    dma = pltpu.SemaphoreType.DMA
    mask = shape((9, pixels, lanes), f32)
    return pl.pallas_call(
        functools.partial(prologue_kernel, blocks, parts),
        in_specs=[anywhere] * 5 + [inside],
        out_specs=[anywhere] * 5 + [inside] * 5,
        out_shape=[
            shape((pixels, feat), low),
            shape((narrow, feat), low),
            shape((narrow, feat), low),
            shape((parts,) + narrow_terms.shape, f32),
            shape((parts,) + wide_terms.shape, f32),
            mask,
            mask,
            mask,
            mask,
            shape((pixels * blocks, lanes), f32),
        ],
        scratch_shapes=[
            dma((2, parts)),
            dma((parts,)),
            dma((2, parts)),
            dma((2, parts)),
            dma((3,)),
        ]
        + weights_sems(blocks, parts),
        compiler_params=comm_params(5),
        cost_estimate=pl.CostEstimate(flops=10**6, bytes_accessed=10**8, transcendentals=0),
    )(features, reduce_w, expand_w, narrow_terms, wide_terms, ids)


def greet_line(blocks):
    barrier = pltpu.get_barrier_semaphore()
    me = lax.axis_index(BLK)
    for peer in (lax.rem(me + 1, blocks), lax.rem(me + blocks - 1, blocks)):
        pl.semaphore_signal(barrier, inc=1, device_id={BLK: peer}, device_id_type=MESH)
    pl.semaphore_wait(barrier, 2)


def greet_blocks(blocks):
    announce([(BLK, peer) for peer in others(BLK, blocks)])


def edge_copies(main_ref, low_ref, high_ref, edge, send_sem, recv_sem, blocks):
    me = lax.axis_index(BLK)
    lead = (slice(None),) * (len(main_ref.shape) - 2)
    pixels = main_ref.shape[-2]
    up = remote(
        main_ref.at[lead + (pl.ds(pixels - edge, edge),)],
        low_ref,
        send_sem.at[0],
        recv_sem.at[0],
        BLK,
        lax.rem(me + 1, blocks),
    )
    down = remote(
        main_ref.at[lead + (pl.ds(0, edge),)],
        high_ref,
        send_sem.at[1],
        recv_sem.at[1],
        BLK,
        lax.rem(me + blocks - 1, blocks),
    )

    def start():
        @pl.when(me < blocks - 1)
        def _():
            up.start()

        @pl.when(me > 0)
        def _():
            down.start()

    def finish(zero=True):
        @pl.when(me > 0)
        def _():
            up.wait_recv()
            down.wait_send()

        @pl.when(me < blocks - 1)
        def _():
            down.wait_recv()
            up.wait_send()

        if zero:

            @pl.when(me == 0)
            def _():
                low_ref[...] = jnp.zeros(low_ref.shape, low_ref.dtype)

            @pl.when(me == blocks - 1)
            def _():
                high_ref[...] = jnp.zeros(high_ref.shape, high_ref.dtype)

    return start, finish


def heads_forward_kernel(
    blocks,
    main_ref,
    w_ref,
    mask_ref,
    pre_ref,
    act_ref,
    ext_ref,
    z_ref,
    local_sem,
    halo_send,
    halo_recv,
):
    step = pl.program_id(0)
    head_count, pixels, mid = pre_ref.shape
    cols = (ext_ref.shape[0] - pixels) // 2
    feat = ext_ref.shape[1]
    start, finish = edge_copies(
        main_ref,
        ext_ref.at[pl.ds(0, cols)],
        ext_ref.at[pl.ds(cols + pixels, cols)],
        cols,
        halo_send,
        halo_recv,
        blocks,
    )
    own = pltpu.make_async_copy(main_ref, ext_ref.at[pl.ds(cols, pixels)], local_sem.at[0])

    @pl.when(step == 0)
    def _():
        own.start()
        greet_line(blocks)
        start()
        own.wait()

    @pl.when(step == 3)
    def _():
        finish()

    row_step = jnp.where(step < 3, 1, jnp.where(step < 6, 0, 2))
    col_step = lax.rem(step, 3)
    window = ext_ref[pl.ds(pl.multiple_of(row_step * cols, cols), pixels), :]
    product = contract_last(window, w_ref[0].reshape(head_count * mid, feat))
    mask = mask_ref[0]

    @pl.when(step < 3)
    def _():
        for head in range(head_count):
            part = slice(head * mid, (head + 1) * mid)
            z_ref[col_step, :, part] = mask * product[:, part]

    @pl.when(step >= 3)
    def _():
        for head in range(head_count):
            part = slice(head * mid, (head + 1) * mid)
            z_ref[col_step, :, part] += mask * product[:, part]

    @pl.when(step == 8)
    def _():
        for head in range(head_count):
            part = slice(head * mid, (head + 1) * mid)
            total = (
                z_ref[1, :, part]
                + pltpu.roll(z_ref[0, :, part], 1, 0)
                + pltpu.roll(z_ref[2, :, part], pixels - 1, 0)
            )
            pre_ref[head] = total
            act_ref[head] = (total * sigmoid(total)).astype(jnp.bfloat16)


def tap_at(step):
    return jnp.where(step < 3, step + 3, jnp.where(step < 6, step - 3, step))


def heads_forward(blocks, layer, cols, main, weights, mask):
    _, head_count, _, mid, feat = weights.shape
    pixels = mask.shape[1]
    anywhere = pl.BlockSpec(memory_space=pl.ANY)
    dma = pltpu.SemaphoreType.DMA
    return pl.pallas_call(
        functools.partial(heads_forward_kernel, blocks),
        grid=(9,),
        in_specs=[
            anywhere,
            pl.BlockSpec((1, head_count, 1, mid, feat), lambda t: (layer, 0, tap_at(t), 0, 0)),
            pl.BlockSpec((1, pixels, lanes), lambda t: (tap_at(t), 0, 0)),
        ],
        out_specs=[whole((head_count, pixels, mid))] * 2,
        out_shape=[
            jax.ShapeDtypeStruct((head_count, pixels, mid), jnp.float32),
            jax.ShapeDtypeStruct((head_count, pixels, mid), jnp.bfloat16),
        ],
        scratch_shapes=[
            pltpu.VMEM((pixels + 2 * cols, feat), jnp.bfloat16),
            pltpu.VMEM((3, pixels, head_count * mid), jnp.float32),
            dma((1,)),
            dma((2,)),
            dma((2,)),
        ],
        compiler_params=comm_params(6 + layer),
        cost_estimate=pl.CostEstimate(
            flops=18 * pixels * head_count * mid * feat,
            bytes_accessed=18 * head_count * mid * feat,
            transcendentals=0,
        ),
    )(main, weights, mask)


def fill_taps(im_ref, slot, grad, mask_ref, pixels, cols, dilation):
    rows, mid = grad.shape
    wide = grad.astype(jnp.float32)
    shifted_by = (pltpu.roll(wide, rows - dilation, 0), wide, pltpu.roll(wide, dilation, 0))
    for tap, (row_step, col_step) in enumerate(tap_offsets):
        start = (1 - row_step) * dilation * cols
        part = shifted_by[col_step + 1][start : start + pixels]
        im_ref[slot, :, tap * mid : (tap + 1) * mid] = (part * mask_ref[tap]).astype(jnp.bfloat16)


def messages_kernel(
    blocks,
    layer,
    jobs,
    feat_ref,
    w_hbm,
    cot_ref,
    gain_ref,
    bias_ref,
    f_ref,
    b_ref,
    maps_ref,
    local_ref,
    sums_ref,
    grad_ref,
    part_ref,
    cols_out,
    main_ref,
    low_ref,
    high_ref,
    cot_low,
    cot_high,
    w_ref,
    lhs_ref,
    z_ref,
    im_ref,
    pack_ref,
    w_sem,
    local_sem,
    halo_send,
    halo_recv,
    cot_send,
    cot_recv,
    slot_send,
    slot_recv,
):
    parts, heads, pixels, mid = feat_ref.shape
    cols = low_ref.shape[2]
    pairs = w_ref.shape[0]
    me, ch = lax.axis_index(BLK), lax.axis_index(CH)
    low = jnp.bfloat16
    loads = [
        pltpu.make_async_copy(w_hbm.at[layer, pair], w_ref.at[pair], w_sem.at[pair])
        for pair in range(pairs)
    ]
    main_copy = pltpu.make_async_copy(feat_ref, main_ref, local_sem.at[0])
    main_copy.start()
    for pair in (0, 4, 1, 5, 3, 2):
        loads[pair].start()
    announce([(BLK, peer) for peer in others(BLK, blocks)])
    start, finish = edge_copies(feat_ref, low_ref, high_ref, cols, halo_send, halo_recv, blocks)
    start()
    cot_start, cot_finish = edge_copies(
        cot_ref, cot_low, cot_high, cols, cot_send, cot_recv, blocks
    )
    cot_start()
    main_copy.wait()
    size = parts * mid // blocks
    for block in range(blocks):
        part, first = block * size // mid, block * size % mid
        for index, (one, two) in enumerate(groups):
            pack_ref[block, index] = jnp.concatenate(
                [main_ref[part, one][:, first : first + size], main_ref[part, two][:, first : first + size]],
                axis=1,
            )
    for index, peer in enumerate(others(BLK, blocks)):
        remote(
            pack_ref.at[peer], cols_out.at[me], slot_send.at[index], slot_recv.at[me], BLK, peer
        ).start()
    keep = pltpu.make_async_copy(pack_ref.at[me], cols_out.at[me], local_sem.at[1])
    keep.start()
    for job in jobs:
        job[0]()

    for source in range(heads):
        for part in range(parts):
            lhs_ref[source, cols : cols + pixels, part * mid : (part + 1) * mid] = main_ref[part, source]
    order = (0, 4, 1, 5, 3, 2)

    def taps(pair, row_step):
        source = message_pairs[pair][0]
        product = contract_last(
            lhs_ref[source, row_step * cols : row_step * cols + pixels, :],
            w_ref[pair, 3 * row_step : 3 * row_step + 3].reshape(3 * mid, parts * mid),
        )
        for col_step in range(3):
            value = f_ref[row_step * 3 + col_step] * product[:, col_step * mid : (col_step + 1) * mid]
            if row_step == 1:
                z_ref[pair, col_step] = value
            else:
                z_ref[pair, col_step] += value

    for pair in order:
        loads[pair].wait()
        taps(pair, 1)
    finish()
    for source in range(heads):
        for part in range(parts):
            chan = slice(part * mid, (part + 1) * mid)
            lhs_ref[source, 0:cols, chan] = low_ref[part, source]
            lhs_ref[source, cols + pixels :, chan] = high_ref[part, source]
    for pair in order:
        taps(pair, 0)
        taps(pair, 2)
    cot_finish()
    values = {}
    cots = {}
    for place, target in enumerate((0, 3)):
        values[target] = main_ref[ch, target].astype(jnp.float32)
        cots[target] = cot_ref[place].astype(jnp.float32)
    for place, target in enumerate((0, 3)):
        value, cot = values[target], cots[target]
        total, slopes = value, cot
        for pair in range(pairs):
            if message_pairs[pair][1] != target:
                continue
            message = (
                z_ref[pair, 1]
                + pltpu.roll(z_ref[pair, 0], 1, 0)
                + pltpu.roll(z_ref[pair, 2], pixels - 1, 0)
            )
            gain, bias = gain_ref[layer, pair : pair + 1], bias_ref[layer, pair : pair + 1]
            gate = sigmoid(gain * value + bias)
            total = total + gate * message
            grad_ref[pair] = (cot * gate).astype(low)
            slope = cot * message * gate * (1.0 - gate)
            sums_ref[pair : pair + 1] = jnp.sum(slope * value, axis=0, keepdims=True)
            sums_ref[pairs + pair : pairs + pair + 1] = jnp.sum(slope, axis=0, keepdims=True)
            slopes = slopes + slope * gain
        maps_ref[place] = total.astype(low)
        local_ref[place] = slopes

    def product_of(pair, slot):
        source, target = message_pairs[pair]
        place = 0 if target == 0 else 1
        gain, bias = gain_ref[layer, pair : pair + 1], bias_ref[layer, pair : pair + 1]

        def border(cot, feat):
            return (
                cot[place].astype(jnp.float32)
                * sigmoid(gain * feat[ch, target].astype(jnp.float32) + bias)
            ).astype(low)

        grad = jnp.concatenate(
            [border(cot_low, low_ref), grad_ref[pair], border(cot_high, high_ref)], axis=0
        )
        fill_taps(im_ref, slot, grad, b_ref, pixels, cols, 1)
        return jnp.dot(
            im_ref[slot],
            w_ref[pair].reshape(9 * mid, parts * mid),
            preferred_element_type=jnp.float32,
        )

    for source, *members in source_order:
        total = product_of(members[0], 0)
        for pair in members[1:]:
            total = total + product_of(pair, 1)
        for part in range(parts):
            part_ref[part, source] = total[:, part * mid : (part + 1) * mid].astype(low)
    for job in jobs:
        job[1]()
    for index, peer in enumerate(others(BLK, blocks)):
        copy = remote(
            pack_ref.at[peer], cols_out.at[peer], slot_send.at[index], slot_recv.at[peer], BLK, peer
        )
        copy.wait_recv()
        copy.wait_send()
    keep.wait()
    for job in jobs:
        job[2]()


def messages_both(blocks, layer, jobs, cols, features, weights, cotangents, gains, biases, forward, backward):
    parts, heads, pixels, mid = features.shape
    pairs = weights.shape[1]
    narrow = parts * mid
    f32, low = jnp.float32, jnp.bfloat16
    shape = jax.ShapeDtypeStruct
    anywhere = pl.BlockSpec(memory_space=pl.ANY)
    inside = pl.BlockSpec(memory_space=pltpu.VMEM)
    dma = pltpu.SemaphoreType.DMA
    wide = 2 * narrow // blocks
    return job_call(
        functools.partial(messages_kernel, blocks, layer),
        jobs,
        blocks,
        in_specs=[anywhere, anywhere] + [inside] * 5,
        out_specs=[inside] * 5 + [anywhere],
        out_shape=[
            shape((2, pixels, mid), low),
            shape((2, pixels, mid), f32),
            shape((2 * pairs, mid), f32),
            shape((pairs, pixels, mid), low),
            shape((parts, heads, pixels, mid), low),
            shape((blocks, 2, pixels, wide), low),
        ],
        scratch_shapes=[
            pltpu.VMEM((parts, heads, pixels, mid), low),
            pltpu.VMEM((parts, heads, cols, mid), low),
            pltpu.VMEM((parts, heads, cols, mid), low),
            pltpu.VMEM((2, cols, mid), low),
            pltpu.VMEM((2, cols, mid), low),
            pltpu.VMEM((pairs, 9, mid, narrow), low),
            pltpu.VMEM((heads, pixels + 2 * cols, narrow), low),
            pltpu.VMEM((pairs, 3, pixels, mid), f32),
            pltpu.VMEM((2, pixels, 9 * mid), low),
            pltpu.VMEM((blocks, 2, pixels, wide), low),
            dma((pairs,)),
            dma((2,)),
            dma((2,)),
            dma((2,)),
            dma((2,)),
            dma((2,)),
            dma((blocks,)),
            dma((blocks,)),
        ],
        compiler_params=comm_params(10 + layer),
        cost_estimate=pl.CostEstimate(
            flops=36 * pixels * pairs * mid * narrow,
            bytes_accessed=18 * pairs * mid * narrow,
            transcendentals=0,
        ),
    )(features, weights, cotangents, gains, biases, forward, backward)


def heads_backward_kernel(
    blocks,
    jobs,
    main_ref,
    w_ref,
    mask_ref,
    out_ref,
    low_ref,
    high_ref,
    im_ref,
    halo_send,
    halo_recv,
):
    step = pl.program_id(0)
    head_count, pixels, mid = main_ref.shape
    cols = low_ref.shape[1]

    @pl.when(step == 0)
    def _():
        start, finish = edge_copies(main_ref, low_ref, high_ref, cols, halo_send, halo_recv, blocks)
        if jobs:
            greet_blocks(blocks)
        else:
            greet_line(blocks)
        start()
        for job in jobs:
            job[0]()
        finish()
        for head in range(head_count):
            grad = jnp.concatenate([low_ref[head], main_ref[head], high_ref[head]], axis=0)
            fill_taps(im_ref, head, grad, mask_ref, pixels, cols, 1)

    total = None
    for head in range(head_count):
        product = jnp.dot(
            im_ref[head],
            w_ref[0, head].reshape(9 * mid, w_ref.shape[4]),
            preferred_element_type=jnp.float32,
        )
        total = product if total is None else total + product
    out_ref[0] = total.astype(jnp.bfloat16)

    if jobs:

        @pl.when(step == pl.num_programs(0) - 1)
        def _():
            for job in jobs:
                job[1]()
            for job in jobs:
                job[2]()


def heads_backward(blocks, layer, jobs, cols, main, weights, mask, parts):
    _, head_count, taps, mid, feat = weights.shape
    pixels = mask.shape[1]
    width = feat // parts
    dma = pltpu.SemaphoreType.DMA
    return job_call(
        functools.partial(heads_backward_kernel, blocks),
        jobs,
        blocks,
        grid=(parts,),
        in_specs=[
            whole(main.shape),
            pl.BlockSpec((1, head_count, taps, mid, width), lambda j: (layer, 0, 0, 0, j)),
            whole(mask.shape),
        ],
        out_specs=[pl.BlockSpec((1, pixels, width), lambda j: (j, 0, 0))],
        out_shape=[jax.ShapeDtypeStruct((parts, pixels, width), jnp.bfloat16)],
        scratch_shapes=[
            pltpu.VMEM((head_count, cols, mid), jnp.bfloat16),
            pltpu.VMEM((head_count, cols, mid), jnp.bfloat16),
            pltpu.VMEM((head_count, pixels, taps * mid), jnp.bfloat16),
            dma((2,)),
            dma((2,)),
        ],
        compiler_params=comm_params(20 + layer),
        cost_estimate=pl.CostEstimate(
            flops=18 * pixels * head_count * mid * feat,
            bytes_accessed=18 * head_count * mid * feat,
            transcendentals=0,
        ),
    )(main, weights, mask)


def weight_kernel(
    blocks,
    lists,
    store,
    jobs,
    before_ref,
    v_ref,
    after_ref,
    g_ref,
    cols_ref,
    out_ref,
    lhs_ref,
    *acc_refs,
):
    step = pl.program_id(0)
    pixels, chans = v_ref.shape[2:]
    cols = lanes
    if jobs:

        @pl.when(step == 0)
        def _():
            greet_blocks(blocks)
            for job in jobs:
                job[0]()

    masks = cols_ref[...]
    for index, members in enumerate(lists):
        window = jnp.concatenate(
            [before_ref[0, index], v_ref[0, index], after_ref[0, index]], axis=0
        ).astype(jnp.float32)
        size = window.shape[0]
        shifted_by = (pltpu.roll(window, 1, 0), window, pltpu.roll(window, size - 1, 0))
        for tap, (row_step, col_step) in enumerate(tap_offsets):
            top = (1 + row_step) * cols
            part = shifted_by[col_step + 1][top : top + pixels]
            lhs_ref[:, tap * chans : (tap + 1) * chans] = (
                part * masks[:, tap : tap + 1]
            ).astype(jnp.bfloat16)
        grads = jnp.concatenate([g_ref[0, member] for member in members], axis=1)
        product = lax.dot_general(
            lhs_ref[...], grads, (((0,), (0,)), ((), ())), preferred_element_type=jnp.float32
        )
        acc_ref = acc_refs[index]

        @pl.when(step == 0)
        def _(acc_ref=acc_ref, product=product):
            acc_ref[...] = product

        @pl.when(step > 0)
        def _(acc_ref=acc_ref, product=product):
            acc_ref[...] += product

    @pl.when(step == blocks - 1)
    def _():
        store(out_ref, acc_refs)
        for job in jobs:
            job[1]()
        for job in jobs:
            job[2]()


def weight_gradient(key, blocks, jobs, lists, store, out_shape, values, grads, mask_cols):
    _, count, pixels, chans = values.shape
    _, members, _, mid = grads.shape
    f32, low = jnp.float32, jnp.bfloat16
    tail = pixels // lanes - 1
    return job_call(
        functools.partial(weight_kernel, blocks, lists, store),
        jobs,
        blocks,
        grid=(blocks,),
        in_specs=[
            pl.BlockSpec((1, count, lanes, chans), lambda i: (jnp.maximum(i - 1, 0), 0, tail, 0)),
            pl.BlockSpec((1, count, pixels, chans), lambda i: (i, 0, 0, 0)),
            pl.BlockSpec(
                (1, count, lanes, chans), lambda i: (jnp.minimum(i + 1, blocks - 1), 0, 0, 0)
            ),
            pl.BlockSpec((1, members, pixels, mid), lambda i: (i, 0, 0, 0)),
            pl.BlockSpec((pixels, lanes), lambda i: (i, 0)),
        ],
        out_specs=[whole(out_shape)],
        out_shape=[jax.ShapeDtypeStruct(out_shape, f32)],
        scratch_shapes=[pltpu.VMEM((pixels, 9 * chans), low)]
        + [pltpu.VMEM((9 * chans, len(entry) * mid), f32) for entry in lists],
        compiler_params=comm_params(key)
        if jobs
        else pltpu.CompilerParams(vmem_limit_bytes=60 * 2**20),
        cost_estimate=pl.CostEstimate(
            flops=18 * chans * pixels * blocks * mid * sum(len(entry) for entry in lists),
            bytes_accessed=10**7,
            transcendentals=0,
        ),
    )(values, values, values, grads, mask_cols)


def heads_store(out_ref, acc_refs):
    head_count, taps, chans, mid = out_ref.shape
    for head in range(head_count):
        for tap in range(taps):
            out_ref[head, tap] = acc_refs[0][
                tap * chans : (tap + 1) * chans, head * mid : (head + 1) * mid
            ]


def messages_store(out_ref, acc_refs):
    _, taps, size, mid = out_ref.shape
    for index, members in enumerate(group_pairs):
        for place, pair in enumerate(members):
            side = groups[index].index(message_pairs[pair][0])
            for tap in range(taps):
                start = (2 * tap + side) * size
                out_ref[pair, tap] = acc_refs[index][
                    start : start + size, place * mid : (place + 1) * mid
                ]


def greet(blocks, parts):
    barrier = pltpu.get_barrier_semaphore()
    blk, ch = lax.axis_index(BLK), lax.axis_index(CH)
    for step in range(1, blocks):
        pl.semaphore_signal(
            barrier, inc=1, device_id={BLK: lax.rem(blk + step, blocks)}, device_id_type=MESH
        )
    for step in range(1, parts):
        pl.semaphore_signal(
            barrier, inc=1, device_id={CH: lax.rem(ch + step, parts)}, device_id_type=MESH
        )
    pl.semaphore_wait(barrier, blocks + parts - 2)


def send_slots(source_of, target_ref, send_sem, recv_sem, axis, count):
    me = lax.axis_index(axis)
    copies = []
    for step in range(1, count):
        peer = lax.rem(me + step, count)
        copy = pltpu.make_async_remote_copy(
            src_ref=source_of(peer),
            dst_ref=target_ref.at[me],
            send_sem=send_sem.at[step],
            recv_sem=recv_sem.at[me],
            device_id={axis: peer},
            device_id_type=MESH,
        )
        copy.start()
        copies.append(copy)

    def finish():
        for step in range(1, count):
            peer = lax.rem(me + step, count)
            pltpu.make_async_remote_copy(
                src_ref=target_ref.at[peer],
                dst_ref=target_ref.at[peer],
                send_sem=send_sem.at[step],
                recv_sem=recv_sem.at[peer],
                device_id={axis: peer},
                device_id_type=MESH,
            ).wait_recv()
        for copy in copies:
            copy.wait_send()

    return finish


def block_totals(first, second, stat_ref, send_sem, recv_sem, blocks):
    me = lax.axis_index(BLK)
    stat_ref[me, 0:1] = first
    stat_ref[me, 1:2] = second
    send_slots(lambda _: stat_ref.at[me], stat_ref, send_sem, recv_sem, BLK, blocks)()
    total = stat_ref[0]
    for block in range(1, blocks):
        total = total + stat_ref[block]
    return total[0:1], total[1:2]


def fold(values):
    rows, width = values.shape
    return values.reshape(rows // 8, 8, width).sum(axis=0)


def row_loop(rows, block, body, carry):
    def step(index, state):
        return body(pl.ds(pl.multiple_of(index * block, block), block), state)

    return lax.fori_loop(0, rows // block, step, carry)


def moments(ref, block):
    rows, width = ref.shape

    def body(part, state):
        values = ref[part, :]
        return state[0] + fold(values), state[1] + fold(values * values)

    zero = jnp.zeros((8, width), jnp.float32)
    total, square = row_loop(rows, block, body, (zero, zero))
    return total.sum(axis=0, keepdims=True), square.sum(axis=0, keepdims=True)


def halo_copies(ref, edge, pixels, send_sem, recv_sem, blocks):
    me = lax.axis_index(BLK)

    def copy(source, target, side, peer):
        return pltpu.make_async_remote_copy(
            src_ref=ref.at[pl.ds(source, edge)],
            dst_ref=ref.at[pl.ds(target, edge)],
            send_sem=send_sem.at[side],
            recv_sem=recv_sem.at[side],
            device_id={BLK: peer},
            device_id_type=MESH,
        )

    up = copy(pixels, 0, 0, lax.rem(me + 1, blocks))
    down = copy(edge, edge + pixels, 1, lax.rem(me + blocks - 1, blocks))

    @pl.when(me < blocks - 1)
    def _():
        up.start()

    @pl.when(me > 0)
    def _():
        down.start()

    @pl.when(me == 0)
    def _():
        ref[0:edge, :] = jnp.zeros((edge, ref.shape[1]), ref.dtype)

    @pl.when(me == blocks - 1)
    def _():
        ref[edge + pixels :, :] = jnp.zeros((edge, ref.shape[1]), ref.dtype)

    def finish():
        @pl.when(me > 0)
        def _():
            up.wait_recv()
            down.wait_send()

        @pl.when(me < blocks - 1)
        def _():
            down.wait_recv()
            up.wait_send()

    return finish


def trunk_forward_kernel(
    blocks,
    parts,
    fetch,
    jobs,
    cur_ref,
    wr_ref,
    wd_ref,
    we_ref,
    mask_ref,
    gain1_ref,
    bias1_ref,
    gain2_ref,
    bias2_ref,
    gain3_ref,
    bias3_ref,
    *refs,
):
    if fetch:
        raw_r, raw_e, *refs = refs
    out_ref, ext_out_ref, full_ref, normed1_ref, inverse1_ref, normed2_ref, inverse2_ref = refs[:7]
    normed3_ref, inverse3_ref = refs[7:9]
    refs = refs[9:]
    if fetch:
        full_r, full_e, *refs = refs
    pre1_ref, pre3_ref, ext_ref, z_ref, gath_ref, stat1_ref, stat2_ref, stat3_ref = refs[:8]
    term1_ref, term3_ref, stat_send, stat_recv, halo_send, halo_recv, part_send, part_recv = refs[8:16]
    pixels, feat = cur_ref.shape
    mid = normed1_ref.shape[1]
    wide = normed3_ref.shape[1]
    edge = (ext_ref.shape[0] - pixels) // 2
    ch = lax.axis_index(CH)
    pixel_count = float(pixels * blocks)
    greet(blocks, parts)
    for job in jobs:
        job[0]()
    if fetch:
        start, spread, forward, finish = weights_job(
            raw_r, raw_e, fetch, (full_r, full_e), refs[16:], blocks, parts
        )
        start()

    def terms(total, square):
        mean_value = total / pixel_count
        variance = square / pixel_count - mean_value * mean_value
        return mean_value, lax.rsqrt(variance + epsilon)

    pre1_ref[...] = contract_last(cur_ref[...], wr_ref[...])
    total, square = moments(pre1_ref, 64)
    mean_value, inverse = terms(
        *block_totals(total, square, stat1_ref, stat_send.at[0], stat_recv.at[0], blocks)
    )
    term1_ref[0:1] = mean_value
    term1_ref[1:2] = inverse

    def first(part, state):
        value = gain1_ref[...] * ((pre1_ref[part, :] - mean_value) * inverse) + bias1_ref[...]
        pre1_ref[part, :] = value * sigmoid(value)
        return state

    if fetch:
        spread()
    own_mid = pl.ds(pl.multiple_of(ch * mid, mid), mid)
    normed1_ref[...] = (pre1_ref[:, own_mid] - term1_ref[0:1, own_mid]) * term1_ref[1:2, own_mid]
    inverse1_ref[...] = term1_ref[1:2, own_mid]
    row_loop(pixels, 64, first, 0)
    ext_ref[edge : edge + pixels, :] = pre1_ref[...].astype(jnp.bfloat16)
    wait_halo = halo_copies(ext_ref, edge, pixels, halo_send, halo_recv, blocks)

    half = edge // 2
    for row_step in (1, 0, 2):
        if row_step == 0:
            wait_halo()
        top = 2 * row_step * half
        product = contract_last(
            ext_ref[top : top + pixels, :],
            wd_ref[3 * row_step : 3 * row_step + 3].reshape(3 * mid, parts * mid),
        )
        for col_step in range(3):
            part = mask_ref[row_step * 3 + col_step] * product[:, col_step * mid : (col_step + 1) * mid]
            if row_step == 1:
                z_ref[col_step] = part
            else:
                z_ref[col_step] += part
    second_pre = (
        z_ref[1] + pltpu.roll(z_ref[0], 2, 0) + pltpu.roll(z_ref[2], pixels - 2, 0)
    )
    mean_value, inverse = terms(
        *block_totals(
            jnp.sum(second_pre, axis=0, keepdims=True),
            jnp.sum(second_pre * second_pre, axis=0, keepdims=True),
            stat2_ref,
            stat_send.at[1],
            stat_recv.at[1],
            blocks,
        )
    )
    normed = (second_pre - mean_value) * inverse
    normed2_ref[...] = normed
    inverse2_ref[...] = inverse
    value = gain2_ref[...] * normed + bias2_ref[...]
    gath_ref[ch] = (value * sigmoid(value)).astype(jnp.bfloat16)
    wait_parts = send_slots(
        lambda _: gath_ref.at[ch], gath_ref, part_send, part_recv, CH, parts
    )
    ext_out_ref[...] = ext_ref[...]
    wait_parts()
    for part in range(parts):
        full_ref[:, part * mid : (part + 1) * mid] = gath_ref[part]
    for part in range(parts):
        lane = slice(part * wide, (part + 1) * wide)
        pre3_ref[:, lane] = jnp.dot(
            full_ref[...], we_ref[:, lane], preferred_element_type=jnp.float32
        )
    total, square = moments(pre3_ref, 16)
    mean_value, inverse = terms(
        *block_totals(total, square, stat3_ref, stat_send.at[2], stat_recv.at[2], blocks)
    )
    term3_ref[0:1] = mean_value
    term3_ref[1:2] = inverse

    def last(part, state):
        value = (
            gain3_ref[...] * ((pre3_ref[part, :] - mean_value) * inverse)
            + bias3_ref[...]
            + cur_ref[part, :].astype(jnp.float32)
        )
        out_ref[part, :] = (value * sigmoid(value)).astype(jnp.bfloat16)
        return state

    row_loop(pixels, 16, last, 0)
    own_wide = pl.ds(pl.multiple_of(ch * wide, wide), wide)
    if fetch:
        for array in range(2):
            forward(array)
    for job in jobs:
        job[1]()
    normed3_ref[...] = (pre3_ref[:, own_wide] - term3_ref[0:1, own_wide]) * term3_ref[1:2, own_wide]
    inverse3_ref[...] = term3_ref[1:2, own_wide]
    if fetch:
        finish()
    for job in jobs:
        job[2]()


def trunk_forward(
    blocks, parts, cols, layer, jobs, current, reduce_w, dilated_w, expand_w, mask, norms, raw
):
    pixels, feat = current.shape
    narrow = reduce_w.shape[0]
    mid, wide = narrow // parts, feat // parts
    edge = 2 * cols
    f32, low = jnp.float32, jnp.bfloat16
    shape = jax.ShapeDtypeStruct
    rows = edge * 2 + pixels
    inside = pl.BlockSpec(memory_space=pltpu.VMEM)
    anywhere = pl.BlockSpec(memory_space=pl.ANY)
    fetch = layer + 1 if raw else 0
    return job_call(
        functools.partial(trunk_forward_kernel, blocks, parts, fetch),
        jobs,
        blocks,
        in_specs=[inside] * 11 + [anywhere] * len(raw),
        out_specs=[inside] * 9 + [anywhere] * len(raw),
        out_shape=[
            shape((pixels, feat), low),
            shape((rows, narrow), low),
            shape((pixels, narrow), low),
            shape((pixels, mid), f32),
            shape((1, mid), f32),
            shape((pixels, mid), f32),
            shape((1, mid), f32),
            shape((pixels, wide), f32),
            shape((1, wide), f32),
        ]
        + [shape((narrow, feat), low)] * len(raw),
        scratch_shapes=[
            pltpu.VMEM((pixels, narrow), f32),
            pltpu.VMEM((pixels, feat), f32),
            pltpu.VMEM((rows, narrow), low),
            pltpu.VMEM((3, pixels, mid), f32),
            pltpu.VMEM((parts, pixels, mid), low),
            pltpu.VMEM((blocks, 2, narrow), f32),
            pltpu.VMEM((blocks, 2, mid), f32),
            pltpu.VMEM((blocks, 2, feat), f32),
            pltpu.VMEM((2, narrow), f32),
            pltpu.VMEM((2, feat), f32),
            pltpu.SemaphoreType.DMA((3, blocks)),
            pltpu.SemaphoreType.DMA((3, blocks)),
            pltpu.SemaphoreType.DMA((2,)),
            pltpu.SemaphoreType.DMA((2,)),
            pltpu.SemaphoreType.DMA((parts,)),
            pltpu.SemaphoreType.DMA((parts,)),
        ]
        + (weights_sems(blocks, parts) if raw else []),
        compiler_params=comm_params(50 + layer),
        cost_estimate=pl.CostEstimate(
            flops=2 * pixels * (2 * narrow * feat + 9 * mid * narrow),
            bytes_accessed=150 * 2**20,
            transcendentals=0,
        ),
    )(current, reduce_w, dilated_w, expand_w, mask, *norms, *raw)


def slope_of(values):
    gate = sigmoid(values)
    return gate * (1.0 + values * (1.0 - gate))


def sum_slots(ref, count):
    total = ref[0].astype(jnp.float32)
    for slot in range(1, count):
        total = total + ref[slot].astype(jnp.float32)
    return total


def trunk_backward_kernel(
    blocks,
    parts,
    up_ref,
    heads_ref,
    cur_ref,
    normed3_ref,
    inverse3_ref,
    gain3_ref,
    bias3_ref,
    we_ref,
    full_ref,
    normed2_ref,
    inverse2_ref,
    gain2_ref,
    bias2_ref,
    wd_ref,
    mask_f_ref,
    mask_b_ref,
    ext_ref,
    normed1_ref,
    inverse1_ref,
    gain1_ref,
    bias1_ref,
    wr_ref,
    gate_ref,
    out_ref,
    expand_ref,
    dilated_ref,
    reduce_ref,
    wide_ref,
    second_ref,
    first_ref,
    gate_out,
    third_ref,
    grad_ref,
    im_ref,
    send2_ref,
    recv2_ref,
    send1_ref,
    recv1_ref,
    gath_ref,
    low_ref,
    ex_send_ref,
    ex_recv_ref,
    di_send_ref,
    di_recv_ref,
    re_send_ref,
    re_recv_ref,
    stat3_ref,
    stat2_ref,
    stat1_ref,
    gates_ref,
    stat_send,
    stat_recv,
    halo_send,
    halo_recv,
    part_send,
    part_recv,
    sum_send,
    sum_recv,
):
    pixels, wide = up_ref.shape
    mid = normed1_ref.shape[1]
    narrow = mid * parts
    feat = cur_ref.shape[1]
    edge = (grad_ref.shape[0] - pixels) // 2
    half = edge // 2
    blk = lax.axis_index(BLK)
    ch = lax.axis_index(CH)
    pixel_count = float(pixels * blocks)
    low = jnp.bfloat16
    greet(blocks, parts)
    own_wide = pl.ds(pl.multiple_of(ch * wide, wide), wide)
    gates_ref[blk] = gate_ref[...]
    wait_gates = send_slots(
        lambda _: gates_ref.at[blk], gates_ref, stat_send.at[3], stat_recv.at[3], BLK, blocks
    )

    def start(part, state):
        normed = normed3_ref[part, :]
        summed = (
            gain3_ref[...] * normed + bias3_ref[...] + cur_ref[part, own_wide].astype(jnp.float32)
        )
        value = (up_ref[part, :] + heads_ref[part, :].astype(jnp.float32)) * slope_of(summed)
        out_ref[part, :] = value
        return state[0] + fold(value), state[1] + fold(value * normed)

    zero = jnp.zeros((8, wide), jnp.float32)
    bias_sum, gain_sum = row_loop(pixels, 32, start, (zero, zero))
    bias_grad, gain_grad = block_totals(
        bias_sum.sum(axis=0, keepdims=True),
        gain_sum.sum(axis=0, keepdims=True),
        stat3_ref,
        stat_send.at[0],
        stat_recv.at[0],
        blocks,
    )
    wide_ref[0:1] = gain_grad
    wide_ref[1:2] = bias_grad
    scale = gain3_ref[...] * inverse3_ref[...]
    bias_part = bias_grad / pixel_count
    gain_part = gain_grad / pixel_count

    def third(part, state):
        third_ref[part, :] = (
            scale * (out_ref[part, :] - bias_part - normed3_ref[part, :] * gain_part)
        ).astype(low)
        return state

    row_loop(pixels, 32, third, 0)
    product = contract_last(third_ref[...], we_ref[...])
    for part in range(parts):
        send2_ref[part] = product[:, part * mid : (part + 1) * mid].astype(low)
    recv2_ref[ch] = send2_ref[ch]
    wait_parts = send_slots(
        lambda peer: send2_ref.at[peer], recv2_ref, part_send.at[0], part_recv.at[0], CH, parts
    )
    size = narrow // blocks
    product = lax.dot_general(
        full_ref[...], third_ref[...], (((0,), (0,)), ((), ())), preferred_element_type=jnp.float32
    )
    for block in range(blocks):
        ex_send_ref[block] = product[block * size : (block + 1) * size].astype(low)
    ex_recv_ref[blk] = ex_send_ref[blk]
    wait_expand = send_slots(
        lambda peer: ex_send_ref.at[peer], ex_recv_ref, sum_send.at[0], sum_recv.at[0], BLK, blocks
    )
    wait_parts()

    def narrow_norm(recv_ref, normed_ref, inverse_ref, gain_ref, bias_ref, stat_ref, phase, sums_ref):
        normed = normed_ref[...]
        value = sum_slots(recv_ref, parts) * slope_of(gain_ref[...] * normed + bias_ref[...])
        bias_grad, gain_grad = block_totals(
            jnp.sum(value, axis=0, keepdims=True),
            jnp.sum(value * normed, axis=0, keepdims=True),
            stat_ref,
            stat_send.at[phase],
            stat_recv.at[phase],
            blocks,
        )
        sums_ref[0:1] = gain_grad
        sums_ref[1:2] = bias_grad
        return (
            gain_ref[...]
            * inverse_ref[...]
            * (value - bias_grad / pixel_count - normed * (gain_grad / pixel_count))
        )

    grad = narrow_norm(
        recv2_ref, normed2_ref, inverse2_ref, gain2_ref, bias2_ref, stat2_ref, 1, second_ref
    )
    grad_ref[edge : edge + pixels, :] = grad.astype(low)
    wait_halo = halo_copies(grad_ref, edge, pixels, halo_send, halo_recv, blocks)
    own = grad_ref[edge : edge + pixels, :].astype(jnp.float32)
    turned = (pltpu.roll(own, pixels - 2, 0), own, pltpu.roll(own, 2, 0))
    for row_step in range(3):
        side = jnp.concatenate(
            [
                (mask_f_ref[row_step * 3 + col_step] * turned[col_step]).astype(low)
                for col_step in range(3)
            ],
            axis=1,
        )
        top = 2 * row_step * half
        product = lax.dot_general(
            ext_ref[top : top + pixels, :],
            side,
            (((0,), (0,)), ((), ())),
            preferred_element_type=jnp.float32,
        )
        for block in range(blocks):
            for col_step in range(3):
                di_send_ref[block, row_step * 3 + col_step] = product[
                    block * size : (block + 1) * size, col_step * mid : (col_step + 1) * mid
                ].astype(low)
    di_recv_ref[blk] = di_send_ref[blk]
    wait_halo()
    fill_taps(im_ref, 0, grad_ref[...], mask_b_ref, pixels, half, 2)
    product = jnp.dot(
        im_ref[0], wd_ref[...].reshape(9 * mid, narrow), preferred_element_type=jnp.float32
    )
    for part in range(parts):
        send1_ref[part] = product[:, part * mid : (part + 1) * mid].astype(low)
    recv1_ref[ch] = send1_ref[ch]
    wait_parts = send_slots(
        lambda peer: send1_ref.at[peer], recv1_ref, part_send.at[1], part_recv.at[1], CH, parts
    )
    wait_dilated = send_slots(
        lambda peer: di_send_ref.at[peer], di_recv_ref, sum_send.at[1], sum_recv.at[1], BLK, blocks
    )
    wait_parts()
    grad = narrow_norm(
        recv1_ref, normed1_ref, inverse1_ref, gain1_ref, bias1_ref, stat1_ref, 2, first_ref
    )
    gath_ref[ch] = grad.astype(low)
    wait_parts = send_slots(
        lambda _: gath_ref.at[ch], gath_ref, part_send.at[2], part_recv.at[2], CH, parts
    )
    product = lax.dot_general(
        cur_ref[...], gath_ref[ch], (((0,), (0,)), ((), ())), preferred_element_type=jnp.float32
    )
    size = feat // blocks
    for block in range(blocks):
        re_send_ref[block] = product[block * size : (block + 1) * size].astype(low)
    re_recv_ref[blk] = re_send_ref[blk]
    wait_reduce = send_slots(
        lambda peer: re_send_ref.at[peer], re_recv_ref, sum_send.at[2], sum_recv.at[2], BLK, blocks
    )
    wait_parts()
    for part in range(parts):
        low_ref[:, part * mid : (part + 1) * mid] = gath_ref[part]
    out_ref[...] += jnp.dot(low_ref[...], wr_ref[:, own_wide], preferred_element_type=jnp.float32)
    wait_gates()
    gate_out[...] = sum_slots(gates_ref, blocks)
    wait_expand()
    expand_ref[...] = sum_slots(ex_recv_ref, blocks)
    wait_dilated()
    dilated_ref[...] = sum_slots(di_recv_ref, blocks)
    wait_reduce()
    reduce_ref[...] = sum_slots(re_recv_ref, blocks)


def trunk_backward(blocks, parts, operands):
    pixels, wide = operands[0].shape
    feat = wide * parts
    mid = operands[9].shape[1]
    narrow = mid * parts
    rows = operands[16].shape[0]
    f32, low = jnp.float32, jnp.bfloat16
    shape = jax.ShapeDtypeStruct
    small, large = narrow // blocks, feat // blocks
    return pl.pallas_call(
        functools.partial(trunk_backward_kernel, blocks, parts),
        out_shape=[
            shape((pixels, wide), f32),
            shape((small, wide), f32),
            shape((9, small, mid), f32),
            shape((large, mid), f32),
            shape((2, wide), f32),
            shape((2, mid), f32),
            shape((2, mid), f32),
            shape(operands[-1].shape, f32),
        ],
        scratch_shapes=[
            pltpu.VMEM((pixels, wide), low),
            pltpu.VMEM((rows, mid), low),
            pltpu.VMEM((1, pixels, 9 * mid), low),
            pltpu.VMEM((parts, pixels, mid), low),
            pltpu.VMEM((parts, pixels, mid), low),
            pltpu.VMEM((parts, pixels, mid), low),
            pltpu.VMEM((parts, pixels, mid), low),
            pltpu.VMEM((parts, pixels, mid), low),
            pltpu.VMEM((pixels, narrow), low),
            pltpu.VMEM((blocks, small, wide), low),
            pltpu.VMEM((blocks, small, wide), low),
            pltpu.VMEM((blocks, 9, small, mid), low),
            pltpu.VMEM((blocks, 9, small, mid), low),
            pltpu.VMEM((blocks, large, mid), low),
            pltpu.VMEM((blocks, large, mid), low),
            pltpu.VMEM((blocks, 2, wide), f32),
            pltpu.VMEM((blocks, 2, mid), f32),
            pltpu.VMEM((blocks, 2, mid), f32),
            pltpu.VMEM((blocks,) + operands[-1].shape, f32),
            pltpu.SemaphoreType.DMA((4, blocks)),
            pltpu.SemaphoreType.DMA((4, blocks)),
            pltpu.SemaphoreType.DMA((2,)),
            pltpu.SemaphoreType.DMA((2,)),
            pltpu.SemaphoreType.DMA((3, parts)),
            pltpu.SemaphoreType.DMA((3, parts)),
            pltpu.SemaphoreType.DMA((3, blocks)),
            pltpu.SemaphoreType.DMA((3, blocks)),
        ],
        compiler_params=comm_params(2),
        cost_estimate=pl.CostEstimate(
            flops=4 * pixels * (2 * narrow * wide + 9 * mid * narrow),
            bytes_accessed=200 * 2**20,
            transcendentals=0,
        ),
    )(*operands)


def gather_parts(values):
    return lax.all_gather(values, CH, axis=0, tiled=False)


def reduce_parts(values):
    return lax.psum_scatter(values, CH, scatter_dimension=0, tiled=False)


def own_slice(values, size, axis):
    return lax.dynamic_slice_in_dim(values, lax.axis_index(CH) * size, size, axis)


def shards(
    features_in,
    w_reduce,
    w_dilated,
    w_expand,
    w_heads,
    w_messages,
    norm_gain,
    norm_bias,
    wide_gain,
    wide_bias,
    gate_gain,
    gate_bias,
    canvas_ids,
    output_cotangent,
    task_cotangents,
):
    rows, cols, wide = features_in.shape
    pixels = rows * cols
    blocks = lax.axis_size(BLK)
    parts = lax.axis_size(CH)
    layers = w_reduce.shape[0]
    mid = w_reduce.shape[1]
    feat = wide * parts
    narrow = mid * parts
    low = jnp.bfloat16
    dilated_t = w_dilated.transpose(0, 2, 1, 3)
    heads_t = w_heads.transpose(0, 1, 3, 2, 4)
    messages_t = w_messages.transpose(0, 1, 3, 2, 4)
    current, *rest = prologue(
        blocks,
        parts,
        features_in.reshape(pixels, wide),
        w_reduce,
        w_expand,
        jnp.concatenate([norm_gain[:, 0], norm_bias[:, 0]], axis=0),
        jnp.concatenate([wide_gain, wide_bias], axis=0),
        canvas_ids,
    )
    reduce_full, expand_full = [rest[0]], [rest[1]]
    narrow_all, wide_all, forward_one, backward_one, forward_two, backward_two, mask_cols = rest[2:]
    narrow_all = narrow_all.transpose(1, 0, 2).reshape(2, layers, narrow)
    wide_all = wide_all.transpose(1, 0, 2).reshape(2, layers, feat)

    kept = []
    for layer in range(layers):
        keep = types.SimpleNamespace(input=current)
        results, swapped = trunk_forward(
            blocks,
            parts,
            cols,
            layer,
            [(swap_kind, current)] if layer else [],
            current,
            reduce_full[layer],
            dilated_t[layer],
            expand_full[layer],
            forward_two,
            (
                narrow_all[0, layer][None],
                narrow_all[1, layer][None],
                norm_gain[layer, 1][None],
                norm_bias[layer, 1][None],
                wide_all[0, layer][None],
                wide_all[1, layer][None],
            ),
            (w_reduce, w_expand) if layer + 1 < layers else (),
        )
        (
            current,
            keep.first_ext,
            keep.second_full,
            keep.normed1,
            keep.inverse1,
            keep.normed2,
            keep.inverse2,
            keep.normed3,
            keep.inverse3,
            *fetched,
        ) = results
        if fetched:
            reduce_full.append(fetched[0])
            expand_full.append(fetched[1])
        if layer:
            kept[-1].values = swapped[0]
            current, kept[-1].features = lax.optimization_barrier((current, kept[-1].features))
        keep.output = current
        keep.heads_pre, features = heads_forward(blocks, layer, cols, current, heads_t, forward_one)
        current, features = lax.optimization_barrier((current, features))
        keep.features = gather_parts(features)
        kept.append(keep)
    output = own_slice(current, wide, 1).reshape(rows, cols, wide)

    for layer in range(layers):
        keep = kept[layer]
        jobs = [(gather_kind, keep_before.message_low) for keep_before in kept[:layer][-1:]]
        if layer == 0:
            jobs = [(swap_kind, kept[-1].output)]
        results, moved = messages_both(
            blocks,
            layer,
            jobs,
            cols,
            keep.features,
            messages_t,
            task_cotangents[layer].reshape(2, pixels, mid),
            gate_gain,
            gate_bias,
            forward_one,
            backward_one,
        )
        keep.maps, keep.local, keep.gate_sums, keep.message_low, partial, keep.message_values = results
        if layer == 0:
            kept[-1].values = moved[0]
        else:
            kept[layer - 1].message_all = moved[0]
        keep.source_sums = reduce_parts(partial)

    def heads_low_of(keep):
        sums = keep.source_sums.astype(jnp.float32)
        total = jnp.stack([sums[0] + keep.local[0], sums[1], sums[2], sums[3] + keep.local[1]])
        return (total * silu_slope(keep.heads_pre)).astype(low)

    def messages_weight(layer, jobs):
        keep = kept[layer]
        (keep.messages_grad,), moved = weight_gradient(
            30 + layer,
            blocks,
            jobs,
            group_pairs,
            messages_store,
            (6, 9, narrow // blocks, mid),
            keep.message_values,
            keep.message_all,
            mask_cols,
        )
        return moved

    def heads_weight(layer):
        keep = kept[layer]
        (keep.heads_grad,), _ = weight_gradient(
            40 + layer,
            blocks,
            [],
            (tuple(range(4)),),
            heads_store,
            (4, 9, feat // blocks, mid),
            keep.values[:, None],
            keep.heads_all,
            mask_cols,
        )

    for layer in range(layers):
        keep = kept[layer]
        keep.heads_low = heads_low_of(keep)
        jobs = [(gather_kind, kept[-1].message_low)] if layer == 0 else []
        (partial,), moved = heads_backward(
            blocks, layer, jobs, cols, keep.heads_low, heads_t, backward_one, parts
        )
        if layer == 0:
            kept[-1].message_all = moved[0]
        keep.heads_partial = reduce_parts(partial)
        (keep.heads_all,) = messages_weight(layer, [(gather_kind, keep.heads_low)])
        if layer + 1 < layers:
            kept[layer + 1].source_sums, keep.messages_grad = lax.optimization_barrier(
                (kept[layer + 1].source_sums, keep.messages_grad)
            )
    heads_weight(0)

    upstream = output_cotangent.reshape(pixels, wide).astype(jnp.float32)
    for layer in reversed(range(layers)):
        keep = kept[layer]
        (
            upstream,
            keep.expand_grad,
            keep.dilated_grad,
            keep.reduce_grad,
            keep.wide_sums,
            keep.second_sums,
            keep.first_sums,
            keep.gates,
        ) = trunk_backward(
            blocks,
            parts,
            (
                upstream,
                keep.heads_partial,
                keep.input,
                keep.normed3,
                keep.inverse3,
                wide_gain[layer][None],
                wide_bias[layer][None],
                w_expand[layer],
                keep.second_full,
                keep.normed2,
                keep.inverse2,
                norm_gain[layer, 1][None],
                norm_bias[layer, 1][None],
                dilated_t[layer],
                forward_two,
                backward_two,
                keep.first_ext,
                keep.normed1,
                keep.inverse1,
                norm_gain[layer, 0][None],
                norm_bias[layer, 0][None],
                reduce_full[layer],
                keep.gate_sums,
            ),
        )

    for layer in range(1, layers):
        heads_weight(layer)

    def stacked(of):
        return jnp.stack([of(keep) for keep in kept])

    narrow_sums = stacked(lambda keep: jnp.stack([keep.first_sums, keep.second_sums]))
    wide_sums = stacked(lambda keep: keep.wide_sums)
    gate_sums = stacked(lambda keep: keep.gates.reshape(2, 6, mid))
    return (
        output,
        stacked(lambda keep: keep.maps.reshape(2, rows, cols, mid)),
        upstream.reshape(rows, cols, wide),
        stacked(lambda keep: keep.reduce_grad),
        stacked(lambda keep: keep.dilated_grad),
        stacked(lambda keep: keep.expand_grad),
        stacked(lambda keep: keep.heads_grad),
        stacked(lambda keep: keep.messages_grad),
        narrow_sums[:, :, 0],
        narrow_sums[:, :, 1],
        wide_sums[:, 0],
        wide_sums[:, 1],
        gate_sums[:, 0],
        gate_sums[:, 1],
    )


def route(*args):
    mid = args[1].shape[1]
    blocks, parts = lax.axis_size(BLK), lax.axis_size(CH)
    whole_tiles = args[1].shape[0] == 2 and mid % lanes == 0 and args[0].shape[1] == lanes and parts >= 2
    if whole_tiles and blocks % 2 == 0 and 2 * mid * parts == lanes * blocks:
        return shards(*args)
    return plain_shards(*args)


def solution(mesh):
    placed = (
        P(BLK, None, CH),
        P(None, CH, None),
        P(None, CH, None, None),
        P(None, None, CH),
        P(None, None, CH, None, None),
        P(None, None, CH, None, None),
        P(None, None, CH),
        P(None, None, CH),
        P(None, CH),
        P(None, CH),
        P(None, None, CH),
        P(None, None, CH),
        P(),
        P(BLK, None, CH),
        P(None, None, BLK, None, CH),
    )
    return jax.shard_map(
        route,
        mesh=mesh,
        in_specs=placed,
        out_specs=(
            P(BLK, None, CH),
            P(None, None, BLK, None, CH),
            P(BLK, None, CH),
            P(None, BLK, CH),
            P(None, None, BLK, CH),
            P(None, BLK, CH),
            P(None, None, None, BLK, CH),
            P(None, None, None, BLK, CH),
            P(None, None, CH),
            P(None, None, CH),
            P(None, CH),
            P(None, CH),
            P(None, None, CH),
            P(None, None, CH),
        ),
        check_vma=False,
    )
```

```python
import functools
import types

import jax
import jax.numpy as jnp
from jax import lax
from jax.experimental import pallas as pl
from jax.experimental.pallas import tpu as pltpu
from jax.sharding import PartitionSpec as P

epsilon = 1e-05
BLK = "blk"
CH = "ch"
tap_offsets = tuple(((row_step, col_step) for row_step in (-1, 0, 1) for col_step in (-1, 0, 1)))
message_pairs = ((1, 0), (2, 0), (3, 0), (0, 3), (1, 3), (2, 3))


def extended_2(block, sides, width):
    for axis, dim in sides:
        count = lax.axis_size(axis)
        forward = [(i, i + 1) for i in range(count - 1)]
        backward = [(target, source) for source, target in forward]
        low = lax.ppermute(
            lax.slice_in_dim(block, block.shape[dim] - width, None, axis=dim), axis, forward
        )
        high = lax.ppermute(lax.slice_in_dim(block, 0, width, axis=dim), axis, backward)
        block = jnp.concatenate([low, block, high], axis=dim)
    return block


def silu_slope(values):
    sigmoid_value = jax.nn.sigmoid(values)
    return sigmoid_value * (1.0 + values * (1.0 - sigmoid_value))


def gather_channels(values):
    return lax.all_gather(values, CH, axis=3, tiled=True)


def reduce_channels(values):
    return lax.psum_scatter(
        values.astype(jnp.bfloat16), CH, scatter_dimension=3, tiled=True
    ).astype(jnp.float32)


def extend_rows(values, halo_width):
    return extended_2(values, ((BLK, 0),), halo_width)


def pixel_totals(first_sum, second_sum):
    return lax.psum((first_sum, second_sum), BLK)


def weight_totals(reduce_grad, dilated_grad, expand_grad, heads_grad, messages_grad):
    return (
        lax.psum_scatter(
            reduce_grad.astype(jnp.bfloat16), BLK, scatter_dimension=1, tiled=True
        ).astype(jnp.float32),
        lax.psum_scatter(
            dilated_grad.astype(jnp.bfloat16), BLK, scatter_dimension=2, tiled=True
        ).astype(jnp.float32),
        lax.psum_scatter(
            expand_grad.astype(jnp.bfloat16), BLK, scatter_dimension=1, tiled=True
        ).astype(jnp.float32),
        lax.psum_scatter(
            heads_grad.astype(jnp.bfloat16), BLK, scatter_dimension=3, tiled=True
        ).astype(jnp.float32),
        lax.psum_scatter(
            messages_grad.astype(jnp.bfloat16), BLK, scatter_dimension=3, tiled=True
        ).astype(jnp.float32),
    )


def widen(values, halo_width):
    return extend_rows(gather_channels(values), halo_width)


def local_masks(canvas_ids, row_count, dilation):
    col_count = canvas_ids.shape[1]
    padded = jnp.pad(canvas_ids, 2, constant_values=-1)
    start = lax.axis_index(BLK) * row_count
    window = lax.dynamic_slice(padded, (start, jnp.int32(0)), (row_count + 4, col_count + 4))
    centre = window[2 : 2 + row_count, 2 : 2 + col_count]
    result = []
    for row_step, col_step in tap_offsets:
        top = 2 + row_step * dilation
        left = 2 + col_step * dilation
        result.append(window[top : top + row_count, left : left + col_count] == centre)
    return jnp.stack(result)


def shifted(padded, halo_width, dilation, row_step, col_step, row_count, col_count):
    top = halo_width + row_step * dilation
    left = dilation + col_step * dilation
    return padded[top : top + row_count, left : left + col_count]


def conv_forward(extended, halo_width, dilation, weights, tap_masks):
    row_count = extended.shape[0] - 2 * halo_width
    col_count = extended.shape[1]
    padded = jnp.pad(extended, ((0, 0), (dilation, dilation), (0, 0)))
    running = jnp.zeros((row_count, col_count, weights.shape[0], weights.shape[1]), jnp.float32)
    for tap_index, (row_step, col_step) in enumerate(tap_offsets):
        window = shifted(padded, halo_width, dilation, row_step, col_step, row_count, col_count)
        product = jnp.einsum(
            "rwc,koc->rwko", window, weights[:, :, tap_index], preferred_element_type=jnp.float32
        )
        running = running + jnp.where(tap_masks[tap_index][:, :, None, None], product, 0.0)
    return running


def conv_weight_grad(extended, halo_width, dilation, gradient, tap_masks):
    row_count = extended.shape[0] - 2 * halo_width
    col_count = extended.shape[1]
    padded = jnp.pad(extended, ((0, 0), (dilation, dilation), (0, 0)))
    result = []
    for tap_index, (row_step, col_step) in enumerate(tap_offsets):
        window = shifted(padded, halo_width, dilation, row_step, col_step, row_count, col_count)
        masked = jnp.where(
            tap_masks[tap_index][:, :, None, None], gradient, jnp.zeros((), gradient.dtype)
        )
        result.append(
            jnp.einsum("rwc,rwko->kco", window, masked, preferred_element_type=jnp.float32)
        )
    return jnp.stack(result, axis=1)


def conv_input_grad(grad_extended, halo_width, dilation, weights, tap_masks):
    row_count = grad_extended.shape[0] - 2 * halo_width
    col_count = grad_extended.shape[1]
    padded = jnp.pad(grad_extended, ((0, 0), (dilation, dilation), (0, 0), (0, 0)))
    running = jnp.zeros((row_count, col_count, weights.shape[3]), jnp.float32)
    for tap_index, (row_step, col_step) in enumerate(tap_offsets):
        window = shifted(padded, halo_width, dilation, -row_step, -col_step, row_count, col_count)
        product = jnp.einsum(
            "rwko,koc->rwc", window, weights[:, :, tap_index], preferred_element_type=jnp.float32
        )
        running = running + jnp.where(tap_masks[8 - tap_index][:, :, None], product, 0.0)
    return running


def norm_forward(hidden, gain, bias, pixel_count):
    total_sum, square_sum = pixel_totals(
        jnp.sum(hidden, axis=(0, 1)), jnp.sum(hidden * hidden, axis=(0, 1))
    )
    mean_value = total_sum / pixel_count
    variance = square_sum / pixel_count - mean_value * mean_value
    inverse = lax.rsqrt(variance + epsilon)
    normed = (hidden - mean_value) * inverse
    return (gain * normed + bias, normed, inverse)


def norm_backward(upstream, normed, inverse, gain, pixel_count):
    bias_grad, gain_grad = pixel_totals(
        jnp.sum(upstream, axis=(0, 1)), jnp.sum(upstream * normed, axis=(0, 1))
    )
    hidden_grad = (
        gain * inverse * (upstream - bias_grad / pixel_count - normed * gain_grad / pixel_count)
    )
    return (hidden_grad, gain_grad, bias_grad)


def layer_forward(inputs, params, masks_one, masks_two, pixel_count):
    (
        reduce_w,
        dilated_w,
        expand_w,
        heads_w,
        messages_w,
        narrow_gain,
        narrow_bias,
        wide_g,
        wide_b,
        gate_g,
        gate_b,
    ) = params
    stored = types.SimpleNamespace()
    inputs_full = gather_channels(inputs[:, :, None, :])[:, :, 0, :]
    first_pre = jnp.einsum("rwc,oc->rwo", inputs_full, reduce_w, preferred_element_type=jnp.float32)
    first_norm, first_normed, first_inverse = norm_forward(
        first_pre, narrow_gain[0], narrow_bias[0], pixel_count
    )
    first_act = jax.nn.silu(first_norm).astype(jnp.bfloat16)
    first_ext = widen(first_act[:, :, None, :], 2)[:, :, 0, :]
    second_pre = conv_forward(first_ext, 2, 2, dilated_w[None], masks_two)[:, :, 0, :]
    second_norm, second_normed, second_inverse = norm_forward(
        second_pre, narrow_gain[1], narrow_bias[1], pixel_count
    )
    second_act = jax.nn.silu(second_norm).astype(jnp.bfloat16)
    second_full = gather_channels(second_act[:, :, None, :])[:, :, 0, :]
    third_pre = jnp.einsum("rwc,co->rwo", second_full, expand_w, preferred_element_type=jnp.float32)
    third_norm, third_normed, third_inverse = norm_forward(third_pre, wide_g, wide_b, pixel_count)
    summed = third_norm + inputs.astype(jnp.float32)
    output = jax.nn.silu(summed).astype(jnp.bfloat16)
    output_ext = widen(output[:, :, None, :], 1)[:, :, 0, :]
    heads_pre = conv_forward(output_ext, 1, 1, heads_w, masks_one)
    features = jax.nn.silu(heads_pre).astype(jnp.bfloat16)
    features_ext = widen(features, 1)
    feature_values = features.astype(jnp.float32)
    depth_map = feature_values[:, :, 0]
    segment_map = feature_values[:, :, 3]
    message_list = []
    for pair_index, (source, target) in enumerate(message_pairs):
        message = conv_forward(
            features_ext[:, :, source], 1, 1, messages_w[pair_index][None], masks_one
        )[:, :, 0]
        gate_value = jax.nn.sigmoid(
            gate_g[pair_index] * feature_values[:, :, target] + gate_b[pair_index]
        )
        message_list.append(message)
        if target == 0:
            depth_map = depth_map + gate_value * message
        else:
            segment_map = segment_map + gate_value * message
    stored.inputs_full = inputs_full
    stored.first_norm = first_norm
    stored.first_normed = first_normed
    stored.first_inverse = first_inverse
    stored.first_ext = first_ext
    stored.second_norm = second_norm
    stored.second_normed = second_normed
    stored.second_inverse = second_inverse
    stored.second_full = second_full
    stored.third_normed = third_normed
    stored.third_inverse = third_inverse
    stored.summed = summed
    stored.output_ext = output_ext
    stored.heads_pre = heads_pre
    stored.features = feature_values
    stored.features_ext = features_ext
    stored.messages = message_list
    return (output, depth_map, segment_map, stored)


def layer_backward(
    stored, upstream, depth_grad, segment_grad, params, masks_one, masks_two, pixel_count
):
    (
        reduce_w,
        dilated_w,
        expand_w,
        heads_w,
        messages_w,
        narrow_gain,
        narrow_bias,
        wide_g,
        wide_b,
        gate_g,
        gate_b,
    ) = params
    feature_values = stored.features
    zero_map = jnp.zeros_like(depth_grad)
    feature_grads = [depth_grad, zero_map, zero_map, segment_grad]
    message_grads = []
    gain_terms = []
    bias_terms = []
    for pair_index, (source, target) in enumerate(message_pairs):
        target_grad = depth_grad if target == 0 else segment_grad
        gate_value = jax.nn.sigmoid(
            gate_g[pair_index] * feature_values[:, :, target] + gate_b[pair_index]
        )
        message_grads.append(target_grad * gate_value)
        slope = target_grad * stored.messages[pair_index] * gate_value * (1.0 - gate_value)
        gain_terms.append(jnp.sum(slope * feature_values[:, :, target], axis=(0, 1)))
        bias_terms.append(jnp.sum(slope, axis=(0, 1)))
        feature_grads[target] = feature_grads[target] + slope * gate_g[pair_index]
    gate_gain_grad, gate_bias_grad = pixel_totals(jnp.stack(gain_terms), jnp.stack(bias_terms))
    message_stack = jnp.stack(message_grads, axis=2).astype(jnp.bfloat16)
    message_ext = extend_rows(message_stack, 1)
    weight_parts = []
    source_partials = [None, None, None, None]
    for pair_index, (source, target) in enumerate(message_pairs):
        weight_parts.append(
            conv_weight_grad(
                stored.features_ext[:, :, source],
                1,
                1,
                message_stack[:, :, pair_index : pair_index + 1],
                masks_one,
            )
        )
        partial_grad = conv_input_grad(
            message_ext[:, :, pair_index : pair_index + 1],
            1,
            1,
            messages_w[pair_index][None],
            masks_one,
        )
        if source_partials[source] is None:
            source_partials[source] = partial_grad
        else:
            source_partials[source] = source_partials[source] + partial_grad
    messages_w_grad = jnp.concatenate(weight_parts, axis=0)
    source_sums = reduce_channels(jnp.stack(source_partials, axis=2))
    features_total = jnp.stack(feature_grads, axis=2) + source_sums
    heads_grad = (features_total * silu_slope(stored.heads_pre)).astype(jnp.bfloat16)
    heads_w_grad = conv_weight_grad(stored.output_ext, 1, 1, heads_grad, masks_one)
    heads_ext = extend_rows(heads_grad, 1)
    output_partial = conv_input_grad(heads_ext, 1, 1, heads_w, masks_one)
    output_total = upstream + reduce_channels(output_partial[:, :, None, :])[:, :, 0, :]
    summed_grad = output_total * silu_slope(stored.summed)
    third_grad, wide_gain_grad, wide_bias_grad = norm_backward(
        summed_grad, stored.third_normed, stored.third_inverse, wide_g, pixel_count
    )
    third_low = third_grad.astype(jnp.bfloat16)
    expand_w_grad = jnp.einsum(
        "rwc,rwo->co", stored.second_full, third_low, preferred_element_type=jnp.float32
    )
    second_partial = jnp.einsum(
        "rwo,co->rwc", third_low, expand_w, preferred_element_type=jnp.float32
    )
    second_act_grad = reduce_channels(second_partial[:, :, None, :])[:, :, 0, :]
    second_grad, second_gain_grad, second_bias_grad = norm_backward(
        second_act_grad * silu_slope(stored.second_norm),
        stored.second_normed,
        stored.second_inverse,
        narrow_gain[1],
        pixel_count,
    )
    second_low = second_grad.astype(jnp.bfloat16)[:, :, None, :]
    dilated_w_grad = conv_weight_grad(stored.first_ext, 2, 2, second_low, masks_two)[0]
    second_ext = extend_rows(second_low, 2)
    first_partial = conv_input_grad(second_ext, 2, 2, dilated_w[None], masks_two)
    first_act_grad = reduce_channels(first_partial[:, :, None, :])[:, :, 0, :]
    first_grad, first_gain_grad, first_bias_grad = norm_backward(
        first_act_grad * silu_slope(stored.first_norm),
        stored.first_normed,
        stored.first_inverse,
        narrow_gain[0],
        pixel_count,
    )
    first_low = first_grad.astype(jnp.bfloat16)
    reduce_w_grad = jnp.einsum(
        "rwc,rwo->co", stored.inputs_full, first_low, preferred_element_type=jnp.float32
    )
    inputs_partial = jnp.einsum(
        "rwo,oc->rwc", first_low, reduce_w, preferred_element_type=jnp.float32
    )
    inputs_grad = reduce_channels(inputs_partial[:, :, None, :])[:, :, 0, :] + summed_grad
    weight_grads = (reduce_w_grad, dilated_w_grad, expand_w_grad, heads_w_grad, messages_w_grad)
    small_grads = (
        jnp.stack([first_gain_grad, second_gain_grad]),
        jnp.stack([first_bias_grad, second_bias_grad]),
        wide_gain_grad,
        wide_bias_grad,
        gate_gain_grad,
        gate_bias_grad,
    )
    return (inputs_grad, weight_grads, small_grads)


def plain_shards(
    features_in,
    w_reduce,
    w_dilated,
    w_expand,
    w_heads,
    w_messages,
    norm_gain,
    norm_bias,
    wide_gain,
    wide_bias,
    gate_gain,
    gate_bias,
    canvas_ids,
    output_cotangent,
    task_cotangents,
):
    row_count = features_in.shape[0]
    col_count = features_in.shape[1]
    pixel_count = float(row_count * col_count * lax.axis_size(BLK))
    masks_one = local_masks(canvas_ids, row_count, 1)
    masks_two = local_masks(canvas_ids, row_count, 2)
    layer_count = w_reduce.shape[0]
    layer_params = []
    for layer_index in range(layer_count):
        layer_params.append(
            (
                w_reduce[layer_index],
                w_dilated[layer_index],
                w_expand[layer_index],
                w_heads[layer_index],
                w_messages[layer_index],
                norm_gain[layer_index],
                norm_bias[layer_index],
                wide_gain[layer_index],
                wide_bias[layer_index],
                gate_gain[layer_index],
                gate_bias[layer_index],
            )
        )
    current = features_in
    stored_list = []
    task_list = []
    for layer_index in range(layer_count):
        current, depth_map, segment_map, stored = layer_forward(
            current, layer_params[layer_index], masks_one, masks_two, pixel_count
        )
        stored_list.append(stored)
        task_list.append(jnp.stack([depth_map, segment_map]).astype(jnp.bfloat16))
    upstream = output_cotangent.astype(jnp.float32)
    weight_list = [None] * layer_count
    small_list = [None] * layer_count
    for layer_index in reversed(range(layer_count)):
        upstream, weight_grads, small_grads = layer_backward(
            stored_list[layer_index],
            upstream,
            task_cotangents[layer_index, 0].astype(jnp.float32),
            task_cotangents[layer_index, 1].astype(jnp.float32),
            layer_params[layer_index],
            masks_one,
            masks_two,
            pixel_count,
        )
        weight_list[layer_index] = weight_grads
        small_list[layer_index] = small_grads
    stacked = [
        jnp.stack([weight_list[layer_index][member] for layer_index in range(layer_count)])
        for member in range(5)
    ]
    weight_sums = weight_totals(stacked[0], stacked[1], stacked[2], stacked[3], stacked[4])
    small_sums = [
        jnp.stack([small_list[layer_index][member] for layer_index in range(layer_count)])
        for member in range(6)
    ]
    return (
        current,
        jnp.stack(task_list),
        upstream,
        weight_sums[0],
        weight_sums[1],
        weight_sums[2],
        weight_sums[3],
        weight_sums[4],
        small_sums[0],
        small_sums[1],
        small_sums[2],
        small_sums[3],
        small_sums[4],
        small_sums[5],
    )


lanes = 128
source_order = ((1, 0, 4), (2, 1, 5), (0, 3), (3, 2))


def whole(shape):
    return pl.BlockSpec(shape, lambda *_: (0,) * len(shape))


def contract_last(left, right):
    return lax.dot_general(
        left, right, (((1,), (1,)), ((), ())), preferred_element_type=jnp.float32
    )


def sigmoid(values):
    return 1.0 / (1.0 + jnp.exp(-values))


def masked(values, bits, place):
    taken = (bits & (1 << place)) != 0
    width = values.shape[1]
    parts = [
        jnp.where(taken, values[:, start : start + lanes], 0.0) for start in range(0, width, lanes)
    ]
    return parts[0] if len(parts) == 1 else jnp.concatenate(parts, axis=1)


MESH = pl.DeviceIdType.MESH
groups = ((1, 2), (0, 3))
targets = (0, 3)
group_pairs = ((0, 4, 1, 5), (3, 2))


def remote(source, target, send_sem, recv_sem, axis, peer):
    return pltpu.make_async_remote_copy(
        src_ref=source,
        dst_ref=target,
        send_sem=send_sem,
        recv_sem=recv_sem,
        device_id={axis: peer},
        device_id_type=MESH,
    )


def comm_params(key):
    return pltpu.CompilerParams(
        vmem_limit_bytes=60 * 2**20, collective_id=key, has_side_effects=True
    )


def announce(targets):
    barrier = pltpu.get_barrier_semaphore()
    for axis, peer in targets:
        pl.semaphore_signal(barrier, inc=1, device_id={axis: peer}, device_id_type=MESH)
    pl.semaphore_wait(barrier, len(targets))


def near_blocks(blocks):
    me = lax.axis_index(BLK)
    sibling = me + 1 - 2 * lax.rem(me, 2)
    return sibling, [lax.rem(me + 2 * step, blocks) for step in range(1, blocks // 2)]


def others(axis, count):
    me = lax.axis_index(axis)
    return [lax.rem(me + step, count) for step in range(1, count)]


def gather_job(source, target, sems, blocks):
    near_send, slot_recv, pass_send, local_sem = sems
    me = lax.axis_index(BLK)
    sibling, peers = near_blocks(blocks)
    own = pltpu.make_async_copy(source, target.at[me], local_sem.at[0])

    def near(step, peer):
        return remote(
            source, target.at[me], near_send.at[step], slot_recv.at[me], BLK, peer
        )

    def passing(step, peer):
        return remote(
            target.at[peer], target.at[peer], pass_send.at[step], slot_recv.at[peer], BLK, sibling
        )

    def start():
        own.start()
        for step, peer in enumerate(peers + [sibling]):
            near(step, peer).start()

    def forward():
        for step, peer in enumerate(peers):
            copy = passing(step, peer)
            copy.wait_recv()
            copy.start()

    def finish():
        for step in range(blocks // 2):
            passing(0, lax.rem(sibling + 2 * step, blocks)).wait_recv()
        for step, peer in enumerate(peers + [sibling]):
            near(step, peer).wait_send()
        for step, peer in enumerate(peers):
            passing(step, peer).wait_send()
        own.wait()

    return start, forward, finish


def swap_job(source, target, sems, blocks):
    slot_send, slot_recv, _, local_sem = sems
    me = lax.axis_index(BLK)
    width = source.shape[1] // blocks

    def part_of(block):
        return source.at[:, pl.ds(pl.multiple_of(block * width, width), width)]

    own = pltpu.make_async_copy(part_of(me), target.at[me], local_sem.at[0])

    def copy(step, peer, slot):
        return remote(
            part_of(peer), target.at[slot], slot_send.at[step], slot_recv.at[slot], BLK, peer
        )

    def start():
        for step, peer in enumerate(others(BLK, blocks)):
            copy(step, peer, me).start()
        own.start()

    def finish():
        for step, peer in enumerate(others(BLK, blocks)):
            copy(step, peer, peer).wait_recv()
            copy(step, peer, me).wait_send()
        own.wait()

    return start, lambda: None, finish


def slot_job(source, target, sems, blocks):
    slot_send, slot_recv, _, local_sem = sems
    me = lax.axis_index(BLK)
    own = pltpu.make_async_copy(source.at[me], target.at[me], local_sem.at[0])

    def copy(step, peer, slot):
        return remote(
            source.at[peer], target.at[slot], slot_send.at[step], slot_recv.at[slot], BLK, peer
        )

    def start():
        for step, peer in enumerate(others(BLK, blocks)):
            copy(step, peer, me).start()
        own.start()

    def finish():
        for step, peer in enumerate(others(BLK, blocks)):
            copy(step, peer, peer).wait_recv()
            copy(step, peer, me).wait_send()
        own.wait()

    return start, lambda: None, finish


job_kinds = (gather_job, swap_job, slot_job)
gather_kind, swap_kind, slot_kind = 0, 1, 2


def job_target(kind, source, blocks):
    if kind == gather_kind:
        return jax.ShapeDtypeStruct((blocks,) + source.shape, source.dtype)
    if kind == slot_kind:
        return jax.ShapeDtypeStruct(source.shape, source.dtype)
    return jax.ShapeDtypeStruct(
        (blocks, source.shape[0], source.shape[1] // blocks), source.dtype
    )


def job_sems(blocks):
    dma = pltpu.SemaphoreType.DMA
    return [dma((blocks,)), dma((blocks,)), dma((blocks,)), dma((1,))]


def job_call(kernel, jobs, blocks, in_specs, out_specs, out_shape, scratch_shapes, **options):
    anywhere = pl.BlockSpec(memory_space=pl.ANY)
    n_in, n_out, n_scratch = len(in_specs), len(out_specs), len(scratch_shapes)
    count = len(jobs)

    def wrapped(*refs):
        ins, refs = refs[:n_in], refs[n_in:]
        sources, refs = refs[:count], refs[count:]
        outs, refs = refs[:n_out], refs[n_out:]
        targets, refs = refs[:count], refs[count:]
        scratch, sems = refs[:n_scratch], refs[n_scratch:]
        running = [
            job_kinds[kind](
                sources[place], targets[place], sems[4 * place : 4 * place + 4], blocks
            )
            for place, (kind, _) in enumerate(jobs)
        ]
        kernel(running, *ins, *outs, *scratch)

    def call(*operands):
        result = pl.pallas_call(
            wrapped,
            in_specs=list(in_specs) + [anywhere] * count,
            out_specs=list(out_specs) + [anywhere] * count,
            out_shape=list(out_shape) + [job_target(kind, source, blocks) for kind, source in jobs],
            scratch_shapes=list(scratch_shapes) + job_sems(blocks) * count,
            **options,
        )(*operands, *[source for _, source in jobs])
        return result[:n_out], result[n_out:]

    return call


def weights_job(wr_ref, we_ref, layer, fulls, sems, blocks, parts):
    part_send, part_recv, near_send, near_recv, pass_send, local_sem = sems
    _, mid, feat = wr_ref.shape
    _, narrow, wide = we_ref.shape
    cw, rw = feat // blocks, narrow // blocks
    blk, ch = lax.axis_index(BLK), lax.axis_index(CH)
    sibling, peers = near_blocks(blocks)

    def cut(index, size):
        return pl.ds(pl.multiple_of(index * size, size), size)

    def source(array):
        if array == 0:
            return wr_ref.at[layer, :, cut(blk, cw)]
        return we_ref.at[layer, cut(blk, rw), :]

    def share(array, part):
        if array == 0:
            return fulls[0].at[cut(part, mid), cut(blk, cw)]
        return fulls[1].at[cut(blk, rw), cut(part, wide)]

    def stripe(array, block):
        if array == 0:
            return fulls[0].at[:, cut(block, cw)]
        return fulls[1].at[cut(block, rw), :]

    def own(array):
        return pltpu.make_async_copy(source(array), share(array, ch), local_sem.at[array])

    def part_copy(array, step, peer, slot):
        return remote(
            source(array),
            share(array, slot),
            part_send.at[array, step],
            part_recv.at[array, slot],
            CH,
            peer,
        )

    def near_copy(array, step, peer):
        return remote(
            stripe(array, blk),
            stripe(array, blk),
            near_send.at[array, step],
            near_recv.at[array, blk],
            BLK,
            peer,
        )

    def passing(array, step, peer):
        return remote(
            stripe(array, peer),
            stripe(array, peer),
            pass_send.at[array, step],
            near_recv.at[array, peer],
            BLK,
            sibling,
        )

    def start():
        for array in range(2):
            own(array).start()
            for step, peer in enumerate(others(CH, parts)):
                part_copy(array, step, peer, ch).start()

    def spread():
        for array in range(2):
            for step, peer in enumerate(others(CH, parts)):
                part_copy(array, step, peer, peer).wait_recv()
            own(array).wait()
            for step, peer in enumerate(peers + [sibling]):
                near_copy(array, step, peer).start()

    def forward(array):
        for step, peer in enumerate(peers):
            copy = passing(array, step, peer)
            copy.wait_recv()
            copy.start()

    def finish():
        for array in range(2):
            for step in range(blocks // 2):
                passing(array, 0, lax.rem(sibling + 2 * step, blocks)).wait_recv()
            for step, peer in enumerate(others(CH, parts)):
                part_copy(array, step, peer, ch).wait_send()
            for step, peer in enumerate(peers + [sibling]):
                near_copy(array, step, peer).wait_send()
            for step, peer in enumerate(peers):
                passing(array, step, peer).wait_send()

    return start, spread, forward, finish


def weights_sems(blocks, parts):
    dma = pltpu.SemaphoreType.DMA
    near = blocks // 2
    return [
        dma((2, parts)),
        dma((2, parts)),
        dma((2, near)),
        dma((2, blocks)),
        dma((2, near)),
        dma((2,)),
    ]


def prologue_kernel(
    blocks,
    parts,
    feat_ref,
    wr_ref,
    we_ref,
    narrow_ref,
    wide_ref,
    ids_ref,
    cur_ref,
    full_r,
    full_e,
    narrow_out,
    wide_out,
    own_ref,
    all_ref,
    line_send,
    line_recv,
    small_send,
    small_recv,
    local_sem,
    *sems,
):
    pixels, wide = feat_ref.shape
    blk, ch = lax.axis_index(BLK), lax.axis_index(CH)
    sibling, peers = near_blocks(blocks)
    smalls = ((narrow_ref, narrow_out), (wide_ref, wide_out))

    def lane_part(index):
        return cur_ref.at[:, pl.ds(pl.multiple_of(index * wide, wide), wide)]

    start, spread, forward, finish = weights_job(
        wr_ref, we_ref, 0, (full_r, full_e), sems, blocks, parts
    )
    own = pltpu.make_async_copy(feat_ref, lane_part(ch), local_sem.at[0])
    own.start()
    announce(
        [(CH, peer) for peer in others(CH, parts)]
        + [(BLK, peer) for peer in [sibling] + peers]
    )
    start()

    right, left = lax.rem(ch + 1, parts), lax.rem(ch + parts - 1, parts)

    def sides(hop):
        return (
            (0, lax.rem(ch + parts - hop, parts), right, ch - hop >= 0, ch < parts - 1),
            (1, lax.rem(ch + hop, parts), left, ch + hop < parts, ch > 0),
        )

    def line_copy(block, side, hop, peer):
        return remote(
            feat_ref if hop == 0 else lane_part(block),
            lane_part(block),
            line_send.at[side, hop],
            line_recv.at[block],
            CH,
            peer,
        )

    def line_hop(hop):
        for side, block, peer, valid, goes in sides(hop):
            if hop > 0:

                @pl.when(valid)
                def _():
                    line_copy(block, side, hop, peer).wait_recv()

            if hop < parts - 1:

                @pl.when(valid & goes)
                def _():
                    line_copy(block, side, hop, peer).start()

    def small_copy(place, step, peer, slot):
        source, target = smalls[place]
        return remote(
            source,
            target.at[slot],
            small_send.at[place, step],
            small_recv.at[place, slot],
            CH,
            peer,
        )

    def small_own(place):
        source, target = smalls[place]
        return pltpu.make_async_copy(source, target.at[ch], local_sem.at[1 + place])

    line_hop(0)
    for place in range(2):
        small_own(place).start()
        for step, peer in enumerate(others(CH, parts)):
            small_copy(place, step, peer, ch).start()
    spread()

    rows = own_ref.shape[1] // lanes

    def same(row, row_move, col_move, other_move):
        here = ids_ref[row, 4 + other_move : 4 + other_move + lanes, :]
        there = ids_ref[row + row_move, 4 + col_move : 4 + col_move + lanes, :]
        return here, here == there

    def own_row(row, state):
        place = 2 + blk * rows + row
        for word, reach in enumerate((1, 2)):
            bits = jnp.zeros((lanes, lanes), jnp.int32)
            for tap, (row_step, col_step) in enumerate(tap_offsets):
                a, b = row_step * reach, col_step * reach
                here, equal = same(place, a, 0, -b)
                bits = bits | jnp.where(equal & (here >= 0), 1 << tap, 0)
                _, equal = same(place, -a, -b, 0)
                bits = bits | jnp.where(equal, 1 << (9 + tap), 0)
            own_ref[word, pl.ds(pl.multiple_of(row * lanes, lanes), lanes), :] = bits
        return state

    lax.fori_loop(0, rows, own_row, 0)

    def any_row(row, state):
        bits = jnp.zeros((lanes, lanes), jnp.int32)
        for tap, (row_step, col_step) in enumerate(tap_offsets):
            _, equal = same(2 + row, row_step, col_step, 0)
            bits = bits | jnp.where(equal, 1 << tap, 0)
        all_ref[pl.ds(pl.multiple_of(row * lanes, lanes), lanes), :] = bits
        return state

    lax.fori_loop(0, ids_ref.shape[0] - 4, any_row, 0)
    for hop in range(1, parts):
        line_hop(hop)
        if hop <= 2:
            forward(hop - 1)
    for array in range(parts - 1, 2):
        forward(array)
    finish()
    for hop in range(parts - 1):
        for side, block, peer, valid, goes in sides(hop):

            @pl.when(valid & goes)
            def _():
                line_copy(block, side, hop, peer).wait_send()

    for place in range(2):
        for step, peer in enumerate(others(CH, parts)):
            small_copy(place, step, peer, peer).wait_recv()
            small_copy(place, step, peer, ch).wait_send()
        small_own(place).wait()
    own.wait()


def prologue(blocks, parts, features, reduce_w, expand_w, narrow_terms, wide_terms, canvas_ids):
    layers, mid, feat = reduce_w.shape
    pixels, wide = features.shape
    narrow = mid * parts
    f32, low = jnp.float32, jnp.bfloat16
    shape = jax.ShapeDtypeStruct
    padded = jnp.pad(canvas_ids, ((2, 2), (4, 4)), constant_values=-1)
    ids = jnp.broadcast_to(padded[:, :, None], padded.shape + (lanes,))
    anywhere = pl.BlockSpec(memory_space=pl.ANY)
    inside = pl.BlockSpec(memory_space=pltpu.VMEM)
    dma = pltpu.SemaphoreType.DMA
    return pl.pallas_call(
        functools.partial(prologue_kernel, blocks, parts),
        in_specs=[anywhere] * 5 + [inside],
        out_specs=[anywhere] * 5 + [inside] * 2,
        out_shape=[
            shape((pixels, feat), low),
            shape((narrow, feat), low),
            shape((narrow, feat), low),
            shape((parts,) + narrow_terms.shape, f32),
            shape((parts,) + wide_terms.shape, f32),
            shape((2, pixels, lanes), jnp.int32),
            shape((pixels * blocks, lanes), jnp.int32),
        ],
        scratch_shapes=[
            dma((2, parts)),
            dma((parts,)),
            dma((2, parts)),
            dma((2, parts)),
            dma((3,)),
        ]
        + weights_sems(blocks, parts),
        compiler_params=comm_params(5),
        cost_estimate=pl.CostEstimate(flops=10**6, bytes_accessed=10**8, transcendentals=0),
    )(features, reduce_w, expand_w, narrow_terms, wide_terms, ids)


def greet_line(blocks):
    barrier = pltpu.get_barrier_semaphore()
    me = lax.axis_index(BLK)
    for peer in (lax.rem(me + 1, blocks), lax.rem(me + blocks - 1, blocks)):
        pl.semaphore_signal(barrier, inc=1, device_id={BLK: peer}, device_id_type=MESH)
    pl.semaphore_wait(barrier, 2)


def greet_blocks(blocks):
    announce([(BLK, peer) for peer in others(BLK, blocks)])


def edge_copies(main_ref, low_ref, high_ref, edge, send_sem, recv_sem, blocks):
    me = lax.axis_index(BLK)
    lead = (slice(None),) * (len(main_ref.shape) - 2)
    pixels = main_ref.shape[-2]
    up = remote(
        main_ref.at[lead + (pl.ds(pixels - edge, edge),)],
        low_ref,
        send_sem.at[0],
        recv_sem.at[0],
        BLK,
        lax.rem(me + 1, blocks),
    )
    down = remote(
        main_ref.at[lead + (pl.ds(0, edge),)],
        high_ref,
        send_sem.at[1],
        recv_sem.at[1],
        BLK,
        lax.rem(me + blocks - 1, blocks),
    )

    def start():
        @pl.when(me < blocks - 1)
        def _():
            up.start()

        @pl.when(me > 0)
        def _():
            down.start()

    def finish(zero=True):
        @pl.when(me > 0)
        def _():
            up.wait_recv()
            down.wait_send()

        @pl.when(me < blocks - 1)
        def _():
            down.wait_recv()
            up.wait_send()

        if zero:

            @pl.when(me == 0)
            def _():
                low_ref[...] = jnp.zeros(low_ref.shape, low_ref.dtype)

            @pl.when(me == blocks - 1)
            def _():
                high_ref[...] = jnp.zeros(high_ref.shape, high_ref.dtype)

    return start, finish


def heads_forward_kernel(blocks, parts, fetch, main_ref, w_ref, mask_ref, *refs):
    if fetch:
        raw_r, raw_e, *refs = refs
    pre_ref, act_ref, ends_ref, *refs = refs
    if fetch:
        full_r, full_e, *refs = refs
    ext_ref, z_ref, local_sem, halo_send, halo_recv, *sems = refs
    step = pl.program_id(0)
    head_count, pixels, mid = pre_ref.shape
    cols = (ext_ref.shape[0] - pixels) // 2
    feat = ext_ref.shape[1]
    start, finish = edge_copies(
        main_ref,
        ext_ref.at[pl.ds(0, cols)],
        ext_ref.at[pl.ds(cols + pixels, cols)],
        cols,
        halo_send,
        halo_recv,
        blocks,
    )
    own = pltpu.make_async_copy(main_ref, ext_ref.at[pl.ds(cols, pixels)], local_sem.at[0])
    if fetch:
        first, spread, forward, last = weights_job(
            raw_r, raw_e, fetch, (full_r, full_e), sems, blocks, parts
        )

    @pl.when(step == 0)
    def _():
        own.start()
        if fetch:
            greet(blocks, parts)
        else:
            greet_line(blocks)
        start()
        if fetch:
            first()
        own.wait()

    @pl.when(step == 3)
    def _():
        finish()
        if fetch:
            spread()

    row_step = jnp.where(step < 3, 1, jnp.where(step < 6, 0, 2))
    col_step = lax.rem(step, 3)
    window = ext_ref[pl.ds(pl.multiple_of(row_step * cols, cols), pixels), :]
    product = contract_last(window, w_ref[0].reshape(head_count * mid, feat))
    product = masked(product, mask_ref[0], tap_at(step))

    @pl.when(step < 3)
    def _():
        z_ref[col_step] = product

    @pl.when(step >= 3)
    def _():
        z_ref[col_step] += product

    @pl.when(step == 8)
    def _():
        for head in range(head_count):
            part = slice(head * mid, (head + 1) * mid)
            total = (
                z_ref[1, :, part]
                + pltpu.roll(z_ref[0, :, part], 1, 0)
                + pltpu.roll(z_ref[2, :, part], pixels - 1, 0)
            )
            pre_ref[head] = total
            value = (total * sigmoid(total)).astype(jnp.bfloat16)
            act_ref[head] = value
            if head in targets:
                ends_ref[targets.index(head)] = value
        if fetch:
            for array in range(2):
                forward(array)
            last()


def tap_at(step):
    return jnp.where(step < 3, step + 3, jnp.where(step < 6, step - 3, step))


def heads_forward(blocks, parts, layer, cols, main, weights, mask, raw):
    _, head_count, _, mid, feat = weights.shape
    pixels = main.shape[0]
    f32, low = jnp.float32, jnp.bfloat16
    shape = jax.ShapeDtypeStruct
    anywhere = pl.BlockSpec(memory_space=pl.ANY)
    dma = pltpu.SemaphoreType.DMA
    narrow = mid * parts
    return pl.pallas_call(
        functools.partial(heads_forward_kernel, blocks, parts, layer + 1 if raw else 0),
        grid=(9,),
        in_specs=[
            anywhere,
            pl.BlockSpec((1, head_count, 1, mid, feat), lambda t: (layer, 0, tap_at(t), 0, 0)),
            pl.BlockSpec((1, pixels, lanes), lambda t: (0, 0, 0)),
        ]
        + [anywhere] * len(raw),
        out_specs=[whole((head_count, pixels, mid))] * 2
        + [whole((2, pixels, mid))]
        + [anywhere] * len(raw),
        out_shape=[
            shape((head_count, pixels, mid), f32),
            shape((head_count, pixels, mid), low),
            shape((2, pixels, mid), low),
        ]
        + [shape((narrow, feat), low)] * len(raw),
        scratch_shapes=[
            pltpu.VMEM((pixels + 2 * cols, feat), low),
            pltpu.VMEM((3, pixels, head_count * mid), f32),
            dma((1,)),
            dma((2,)),
            dma((2,)),
        ]
        + (weights_sems(blocks, parts) if raw else []),
        compiler_params=comm_params(6 + layer),
        cost_estimate=pl.CostEstimate(
            flops=18 * pixels * head_count * mid * feat,
            bytes_accessed=18 * head_count * mid * feat,
            transcendentals=0,
        ),
    )(main, weights, mask, *raw)


def fill_taps(im_ref, slot, grad, bits, pixels, cols, dilation):
    rows, mid = grad.shape
    wide = grad.astype(jnp.float32)
    shifted_by = (pltpu.roll(wide, rows - dilation, 0), wide, pltpu.roll(wide, dilation, 0))
    for tap, (row_step, col_step) in enumerate(tap_offsets):
        start = (1 - row_step) * dilation * cols
        part = shifted_by[col_step + 1][start : start + pixels]
        im_ref[slot, :, tap * mid : (tap + 1) * mid] = masked(part, bits, 9 + tap).astype(
            jnp.bfloat16
        )


def messages_kernel(
    blocks,
    layer,
    jobs,
    feat_ref,
    w_hbm,
    cot_ref,
    gain_ref,
    bias_ref,
    mask_ref,
    maps_ref,
    local_ref,
    sums_ref,
    part_ref,
    pack_ref,
    main_ref,
    low_ref,
    high_ref,
    cot_low,
    cot_high,
    w_ref,
    lhs_ref,
    z_ref,
    im_ref,
    grad_ref,
    w_sem,
    local_sem,
    halo_send,
    halo_recv,
    cot_send,
    cot_recv,
):
    parts, heads, pixels, mid = feat_ref.shape
    cols = low_ref.shape[2]
    pairs = w_ref.shape[0]
    me, ch = lax.axis_index(BLK), lax.axis_index(CH)
    low = jnp.bfloat16
    loads = [
        pltpu.make_async_copy(w_hbm.at[layer, pair], w_ref.at[pair], w_sem.at[pair])
        for pair in range(pairs)
    ]
    main_copy = pltpu.make_async_copy(feat_ref, main_ref, local_sem.at[0])
    main_copy.start()
    for pair in (0, 4, 1, 5, 3, 2):
        loads[pair].start()
    greet_blocks(blocks)
    start, finish = edge_copies(feat_ref, low_ref, high_ref, cols, halo_send, halo_recv, blocks)
    start()
    cot_start, cot_finish = edge_copies(
        cot_ref, cot_low, cot_high, cols, cot_send, cot_recv, blocks
    )
    cot_start()
    main_copy.wait()
    size = parts * mid // blocks
    for block in range(blocks):
        part, first = block * size // mid, block * size % mid
        for index, (one, two) in enumerate(groups):
            pack_ref[block, index] = jnp.concatenate(
                [main_ref[part, one][:, first : first + size], main_ref[part, two][:, first : first + size]],
                axis=1,
            )
    for source in range(heads):
        for part in range(parts):
            lhs_ref[source, cols : cols + pixels, part * mid : (part + 1) * mid] = main_ref[part, source]
    order = (0, 4, 1, 5, 3, 2)
    bits = mask_ref[0]

    def taps(pair, row_step):
        source = message_pairs[pair][0]
        product = contract_last(
            lhs_ref[source, row_step * cols : row_step * cols + pixels, :],
            w_ref[pair, 3 * row_step : 3 * row_step + 3].reshape(3 * mid, parts * mid),
        )
        for col_step in range(3):
            value = masked(
                product[:, col_step * mid : (col_step + 1) * mid], bits, row_step * 3 + col_step
            )
            if row_step == 1:
                z_ref[pair, col_step] = value
            else:
                z_ref[pair, col_step] += value

    for pair in order:
        loads[pair].wait()
        taps(pair, 1)
    finish()
    cot_finish()
    for job in jobs:
        job[0]()
    for source in range(heads):
        for part in range(parts):
            chan = slice(part * mid, (part + 1) * mid)
            lhs_ref[source, 0:cols, chan] = low_ref[part, source]
            lhs_ref[source, cols + pixels :, chan] = high_ref[part, source]
    for pair in order:
        taps(pair, 0)
        taps(pair, 2)
    values = {}
    cots = {}
    for place, target in enumerate((0, 3)):
        values[target] = main_ref[ch, target].astype(jnp.float32)
        cots[target] = cot_ref[place].astype(jnp.float32)
    for place, target in enumerate((0, 3)):
        value, cot = values[target], cots[target]
        total, slopes = value, cot
        for pair in range(pairs):
            if message_pairs[pair][1] != target:
                continue
            message = (
                z_ref[pair, 1]
                + pltpu.roll(z_ref[pair, 0], 1, 0)
                + pltpu.roll(z_ref[pair, 2], pixels - 1, 0)
            )
            gain, bias = gain_ref[layer, pair : pair + 1], bias_ref[layer, pair : pair + 1]
            gate = sigmoid(gain * value + bias)
            total = total + gate * message
            grad_ref[pair] = (cot * gate).astype(low)
            slope = cot * message * gate * (1.0 - gate)
            sums_ref[pair : pair + 1] = jnp.sum(slope * value, axis=0, keepdims=True)
            sums_ref[pairs + pair : pairs + pair + 1] = jnp.sum(slope, axis=0, keepdims=True)
            slopes = slopes + slope * gain
        maps_ref[place] = total.astype(low)
        local_ref[place] = slopes

    def product_of(pair, slot):
        source, target = message_pairs[pair]
        place = 0 if target == 0 else 1
        gain, bias = gain_ref[layer, pair : pair + 1], bias_ref[layer, pair : pair + 1]

        def border(cot, feat):
            return (
                cot[place].astype(jnp.float32)
                * sigmoid(gain * feat[ch, target].astype(jnp.float32) + bias)
            ).astype(low)

        grad = jnp.concatenate(
            [border(cot_low, low_ref), grad_ref[pair], border(cot_high, high_ref)], axis=0
        )
        fill_taps(im_ref, slot, grad, bits, pixels, cols, 1)
        return jnp.dot(
            im_ref[slot],
            w_ref[pair].reshape(9 * mid, parts * mid),
            preferred_element_type=jnp.float32,
        )

    for source, *members in source_order:
        total = product_of(members[0], 0)
        for pair in members[1:]:
            total = total + product_of(pair, 1)
        for part in range(parts):
            part_ref[part, source] = total[:, part * mid : (part + 1) * mid].astype(low)
    for job in jobs:
        job[1]()
    for job in jobs:
        job[2]()


def messages_both(blocks, layer, jobs, cols, features, weights, cotangents, gains, biases, mask):
    parts, heads, pixels, mid = features.shape
    pairs = weights.shape[1]
    narrow = parts * mid
    f32, low = jnp.float32, jnp.bfloat16
    shape = jax.ShapeDtypeStruct
    anywhere = pl.BlockSpec(memory_space=pl.ANY)
    inside = pl.BlockSpec(memory_space=pltpu.VMEM)
    dma = pltpu.SemaphoreType.DMA
    wide = 2 * narrow // blocks
    return job_call(
        functools.partial(messages_kernel, blocks, layer),
        jobs,
        blocks,
        in_specs=[anywhere, anywhere] + [inside] * 4,
        out_specs=[inside] * 5,
        out_shape=[
            shape((2, pixels, mid), low),
            shape((2, pixels, mid), f32),
            shape((2 * pairs, mid), f32),
            shape((parts, heads, pixels, mid), low),
            shape((blocks, 2, pixels, wide), low),
        ],
        scratch_shapes=[
            pltpu.VMEM((parts, heads, pixels, mid), low),
            pltpu.VMEM((parts, heads, cols, mid), low),
            pltpu.VMEM((parts, heads, cols, mid), low),
            pltpu.VMEM((2, cols, mid), low),
            pltpu.VMEM((2, cols, mid), low),
            pltpu.VMEM((pairs, 9, mid, narrow), low),
            pltpu.VMEM((heads, pixels + 2 * cols, narrow), low),
            pltpu.VMEM((pairs, 3, pixels, mid), f32),
            pltpu.VMEM((2, pixels, 9 * mid), low),
            pltpu.VMEM((pairs, pixels, mid), low),
            dma((pairs,)),
            dma((1,)),
            dma((2,)),
            dma((2,)),
            dma((2,)),
            dma((2,)),
        ],
        compiler_params=comm_params(10 + layer),
        cost_estimate=pl.CostEstimate(
            flops=36 * pixels * pairs * mid * narrow,
            bytes_accessed=18 * pairs * mid * narrow,
            transcendentals=0,
        ),
    )(features, weights, cotangents, gains, biases, mask)


def heads_backward_kernel(
    blocks,
    jobs,
    main_ref,
    w_ref,
    mask_ref,
    out_ref,
    low_ref,
    high_ref,
    im_ref,
    halo_send,
    halo_recv,
):
    step = pl.program_id(0)
    head_count, pixels, mid = main_ref.shape
    cols = low_ref.shape[1]

    @pl.when(step == 0)
    def _():
        start, finish = edge_copies(main_ref, low_ref, high_ref, cols, halo_send, halo_recv, blocks)
        if jobs:
            greet_blocks(blocks)
        else:
            greet_line(blocks)
        start()
        finish()
        for job in jobs:
            job[0]()
        for head in range(head_count):
            grad = jnp.concatenate([low_ref[head], main_ref[head], high_ref[head]], axis=0)
            fill_taps(im_ref, head, grad, mask_ref[0], pixels, cols, 1)

    total = None
    for head in range(head_count):
        product = jnp.dot(
            im_ref[head],
            w_ref[0, head].reshape(9 * mid, w_ref.shape[4]),
            preferred_element_type=jnp.float32,
        )
        total = product if total is None else total + product
    out_ref[0] = total.astype(jnp.bfloat16)

    if jobs:

        @pl.when(step == pl.num_programs(0) - 1)
        def _():
            for job in jobs:
                job[1]()
            for job in jobs:
                job[2]()


def heads_backward(blocks, layer, jobs, cols, main, weights, mask, parts):
    _, head_count, taps, mid, feat = weights.shape
    pixels = main.shape[1]
    width = feat // parts
    dma = pltpu.SemaphoreType.DMA
    return job_call(
        functools.partial(heads_backward_kernel, blocks),
        jobs,
        blocks,
        grid=(parts,),
        in_specs=[
            whole(main.shape),
            pl.BlockSpec((1, head_count, taps, mid, width), lambda j: (layer, 0, 0, 0, j)),
            pl.BlockSpec((1, pixels, lanes), lambda j: (0, 0, 0)),
        ],
        out_specs=[pl.BlockSpec((1, pixels, width), lambda j: (j, 0, 0))],
        out_shape=[jax.ShapeDtypeStruct((parts, pixels, width), jnp.bfloat16)],
        scratch_shapes=[
            pltpu.VMEM((head_count, cols, mid), jnp.bfloat16),
            pltpu.VMEM((head_count, cols, mid), jnp.bfloat16),
            pltpu.VMEM((head_count, pixels, taps * mid), jnp.bfloat16),
            dma((2,)),
            dma((2,)),
        ],
        compiler_params=comm_params(20 + layer),
        cost_estimate=pl.CostEstimate(
            flops=18 * pixels * head_count * mid * feat,
            bytes_accessed=18 * head_count * mid * feat,
            transcendentals=0,
        ),
    )(main, weights, mask)


def weight_kernel(blocks, lists, load, store, jobs, before_ref, v_ref, after_ref, bits_ref, *refs):
    count = len(lists)
    g_refs, (out_ref, lhs_ref, *acc_refs) = refs[: len(refs) - 2 - count], refs[-2 - count :]
    step = pl.program_id(0)
    pixels, chans = v_ref.shape[2:]
    cols = lanes
    if jobs:

        @pl.when(step == 0)
        def _():
            greet_blocks(blocks)
            for job in jobs:
                job[0]()

    bits = bits_ref[...]
    for index, members in enumerate(lists):
        window = jnp.concatenate(
            [before_ref[0, index], v_ref[0, index], after_ref[0, index]], axis=0
        ).astype(jnp.float32)
        size = window.shape[0]
        shifted_by = (pltpu.roll(window, 1, 0), window, pltpu.roll(window, size - 1, 0))
        for tap, (row_step, col_step) in enumerate(tap_offsets):
            top = (1 + row_step) * cols
            part = shifted_by[col_step + 1][top : top + pixels]
            lhs_ref[:, tap * chans : (tap + 1) * chans] = masked(part, bits, tap).astype(
                jnp.bfloat16
            )
        grads = jnp.concatenate([load(g_refs, member) for member in members], axis=1)
        product = lax.dot_general(
            lhs_ref[...], grads, (((0,), (0,)), ((), ())), preferred_element_type=jnp.float32
        )
        acc_ref = acc_refs[index]

        @pl.when(step == 0)
        def _(acc_ref=acc_ref, product=product):
            acc_ref[...] = product

        @pl.when(step > 0)
        def _(acc_ref=acc_ref, product=product):
            acc_ref[...] += product

    @pl.when(step == blocks - 1)
    def _():
        store(out_ref, acc_refs)
        for job in jobs:
            job[1]()
        for job in jobs:
            job[2]()


def weight_gradient(key, blocks, jobs, lists, load, store, out_shape, values, bits, grads, specs):
    _, count, pixels, chans = values.shape
    mid = out_shape[-1]
    f32, low = jnp.float32, jnp.bfloat16
    tail = pixels // lanes - 1
    return job_call(
        functools.partial(weight_kernel, blocks, lists, load, store),
        jobs,
        blocks,
        grid=(blocks,),
        in_specs=[
            pl.BlockSpec((1, count, lanes, chans), lambda i: (jnp.maximum(i - 1, 0), 0, tail, 0)),
            pl.BlockSpec((1, count, pixels, chans), lambda i: (i, 0, 0, 0)),
            pl.BlockSpec(
                (1, count, lanes, chans), lambda i: (jnp.minimum(i + 1, blocks - 1), 0, 0, 0)
            ),
            pl.BlockSpec((pixels, lanes), lambda i: (i, 0)),
        ]
        + specs,
        out_specs=[whole(out_shape)],
        out_shape=[jax.ShapeDtypeStruct(out_shape, f32)],
        scratch_shapes=[pltpu.VMEM((pixels, 9 * chans), low)]
        + [pltpu.VMEM((9 * chans, len(entry) * mid), f32) for entry in lists],
        compiler_params=comm_params(key)
        if jobs
        else pltpu.CompilerParams(vmem_limit_bytes=60 * 2**20),
        cost_estimate=pl.CostEstimate(
            flops=18 * chans * pixels * blocks * mid * sum(len(entry) for entry in lists),
            bytes_accessed=10**7,
            transcendentals=0,
        ),
    )(values, values, values, bits, *grads)


def heads_load(refs, head):
    return refs[0][0, head]


def messages_load(layer):
    def load(refs, pair):
        cot_ref, feat_ref, gain_ref, bias_ref = refs
        place = targets.index(message_pairs[pair][1])
        gain, bias = gain_ref[layer, pair : pair + 1], bias_ref[layer, pair : pair + 1]
        gate = sigmoid(gain * feat_ref[0, place].astype(jnp.float32) + bias)
        return (cot_ref[0, 0, place].astype(jnp.float32) * gate).astype(jnp.bfloat16)

    return load


def heads_store(out_ref, acc_refs):
    head_count, taps, chans, mid = out_ref.shape
    for head in range(head_count):
        for tap in range(taps):
            out_ref[head, tap] = acc_refs[0][
                tap * chans : (tap + 1) * chans, head * mid : (head + 1) * mid
            ]


def messages_store(out_ref, acc_refs):
    _, taps, size, mid = out_ref.shape
    for index, members in enumerate(group_pairs):
        for place, pair in enumerate(members):
            side = groups[index].index(message_pairs[pair][0])
            for tap in range(taps):
                start = (2 * tap + side) * size
                out_ref[pair, tap] = acc_refs[index][
                    start : start + size, place * mid : (place + 1) * mid
                ]


def greet(blocks, parts):
    barrier = pltpu.get_barrier_semaphore()
    blk, ch = lax.axis_index(BLK), lax.axis_index(CH)
    for step in range(1, blocks):
        pl.semaphore_signal(
            barrier, inc=1, device_id={BLK: lax.rem(blk + step, blocks)}, device_id_type=MESH
        )
    for step in range(1, parts):
        pl.semaphore_signal(
            barrier, inc=1, device_id={CH: lax.rem(ch + step, parts)}, device_id_type=MESH
        )
    pl.semaphore_wait(barrier, blocks + parts - 2)


def send_slots(source_of, target_ref, send_sem, recv_sem, axis, count):
    me = lax.axis_index(axis)
    copies = []
    for step in range(1, count):
        peer = lax.rem(me + step, count)
        copy = pltpu.make_async_remote_copy(
            src_ref=source_of(peer),
            dst_ref=target_ref.at[me],
            send_sem=send_sem.at[step],
            recv_sem=recv_sem.at[me],
            device_id={axis: peer},
            device_id_type=MESH,
        )
        copy.start()
        copies.append(copy)

    def finish():
        for step in range(1, count):
            peer = lax.rem(me + step, count)
            pltpu.make_async_remote_copy(
                src_ref=target_ref.at[peer],
                dst_ref=target_ref.at[peer],
                send_sem=send_sem.at[step],
                recv_sem=recv_sem.at[peer],
                device_id={axis: peer},
                device_id_type=MESH,
            ).wait_recv()
        for copy in copies:
            copy.wait_send()

    return finish


def block_totals(first, second, stat_ref, send_sem, recv_sem, blocks):
    me = lax.axis_index(BLK)
    stat_ref[me, 0:1] = first
    stat_ref[me, 1:2] = second
    send_slots(lambda _: stat_ref.at[me], stat_ref, send_sem, recv_sem, BLK, blocks)()
    total = stat_ref[0]
    for block in range(1, blocks):
        total = total + stat_ref[block]
    return total[0:1], total[1:2]


def fold(values):
    rows, width = values.shape
    return values.reshape(rows // 8, 8, width).sum(axis=0)


def row_loop(rows, block, body, carry):
    def step(index, state):
        return body(pl.ds(pl.multiple_of(index * block, block), block), state)

    return lax.fori_loop(0, rows // block, step, carry)


def moments(ref, block):
    rows, width = ref.shape

    def body(part, state):
        values = ref[part, :]
        return state[0] + fold(values), state[1] + fold(values * values)

    zero = jnp.zeros((8, width), jnp.float32)
    total, square = row_loop(rows, block, body, (zero, zero))
    return total.sum(axis=0, keepdims=True), square.sum(axis=0, keepdims=True)


def halo_copies(ref, edge, pixels, send_sem, recv_sem, blocks):
    me = lax.axis_index(BLK)

    def copy(source, target, side, peer):
        return pltpu.make_async_remote_copy(
            src_ref=ref.at[pl.ds(source, edge)],
            dst_ref=ref.at[pl.ds(target, edge)],
            send_sem=send_sem.at[side],
            recv_sem=recv_sem.at[side],
            device_id={BLK: peer},
            device_id_type=MESH,
        )

    up = copy(pixels, 0, 0, lax.rem(me + 1, blocks))
    down = copy(edge, edge + pixels, 1, lax.rem(me + blocks - 1, blocks))

    @pl.when(me < blocks - 1)
    def _():
        up.start()

    @pl.when(me > 0)
    def _():
        down.start()

    @pl.when(me == 0)
    def _():
        ref[0:edge, :] = jnp.zeros((edge, ref.shape[1]), ref.dtype)

    @pl.when(me == blocks - 1)
    def _():
        ref[edge + pixels :, :] = jnp.zeros((edge, ref.shape[1]), ref.dtype)

    def finish():
        @pl.when(me > 0)
        def _():
            up.wait_recv()
            down.wait_send()

        @pl.when(me < blocks - 1)
        def _():
            down.wait_recv()
            up.wait_send()

    return finish


def trunk_forward_kernel(
    blocks,
    parts,
    fetch,
    jobs,
    cur_ref,
    wr_ref,
    wd_ref,
    we_ref,
    mask_ref,
    gain1_ref,
    bias1_ref,
    gain2_ref,
    bias2_ref,
    gain3_ref,
    bias3_ref,
    *refs,
):
    if fetch:
        raw_r, raw_e, *refs = refs
    out_ref, ext_out_ref, full_ref, normed1_ref, inverse1_ref, normed2_ref, inverse2_ref = refs[:7]
    normed3_ref, inverse3_ref = refs[7:9]
    refs = refs[9:]
    if fetch:
        full_r, full_e, *refs = refs
    pre1_ref, pre3_ref, ext_ref, z_ref, gath_ref, stat1_ref, stat2_ref, stat3_ref = refs[:8]
    term1_ref, term3_ref, stat_send, stat_recv, halo_send, halo_recv, part_send, part_recv = refs[8:16]
    pixels, feat = cur_ref.shape
    mid = normed1_ref.shape[1]
    wide = normed3_ref.shape[1]
    edge = (ext_ref.shape[0] - pixels) // 2
    ch = lax.axis_index(CH)
    pixel_count = float(pixels * blocks)
    greet(blocks, parts)
    for job in jobs:
        job[0]()
    if fetch:
        start, spread, forward, finish = weights_job(
            raw_r, raw_e, fetch, (full_r, full_e), refs[16:], blocks, parts
        )
        start()

    def terms(total, square):
        mean_value = total / pixel_count
        variance = square / pixel_count - mean_value * mean_value
        return mean_value, lax.rsqrt(variance + epsilon)

    pre1_ref[...] = contract_last(cur_ref[...], wr_ref[...])
    total, square = moments(pre1_ref, 64)
    mean_value, inverse = terms(
        *block_totals(total, square, stat1_ref, stat_send.at[0], stat_recv.at[0], blocks)
    )
    term1_ref[0:1] = mean_value
    term1_ref[1:2] = inverse

    def first(part, state):
        value = gain1_ref[...] * ((pre1_ref[part, :] - mean_value) * inverse) + bias1_ref[...]
        pre1_ref[part, :] = value * sigmoid(value)
        return state

    if fetch:
        spread()
    own_mid = pl.ds(pl.multiple_of(ch * mid, mid), mid)
    normed1_ref[...] = (pre1_ref[:, own_mid] - term1_ref[0:1, own_mid]) * term1_ref[1:2, own_mid]
    inverse1_ref[...] = term1_ref[1:2, own_mid]
    row_loop(pixels, 64, first, 0)
    ext_ref[edge : edge + pixels, :] = pre1_ref[...].astype(jnp.bfloat16)
    wait_halo = halo_copies(ext_ref, edge, pixels, halo_send, halo_recv, blocks)

    half = edge // 2
    for row_step in (1, 0, 2):
        if row_step == 0:
            wait_halo()
        top = 2 * row_step * half
        product = contract_last(
            ext_ref[top : top + pixels, :],
            wd_ref[3 * row_step : 3 * row_step + 3].reshape(3 * mid, parts * mid),
        )
        for col_step in range(3):
            part = masked(
                product[:, col_step * mid : (col_step + 1) * mid],
                mask_ref[1],
                row_step * 3 + col_step,
            )
            if row_step == 1:
                z_ref[col_step] = part
            else:
                z_ref[col_step] += part
    second_pre = (
        z_ref[1] + pltpu.roll(z_ref[0], 2, 0) + pltpu.roll(z_ref[2], pixels - 2, 0)
    )
    mean_value, inverse = terms(
        *block_totals(
            jnp.sum(second_pre, axis=0, keepdims=True),
            jnp.sum(second_pre * second_pre, axis=0, keepdims=True),
            stat2_ref,
            stat_send.at[1],
            stat_recv.at[1],
            blocks,
        )
    )
    normed = (second_pre - mean_value) * inverse
    normed2_ref[...] = normed
    inverse2_ref[...] = inverse
    value = gain2_ref[...] * normed + bias2_ref[...]
    gath_ref[ch] = (value * sigmoid(value)).astype(jnp.bfloat16)
    wait_parts = send_slots(
        lambda _: gath_ref.at[ch], gath_ref, part_send, part_recv, CH, parts
    )
    ext_out_ref[...] = ext_ref[...]
    wait_parts()
    for part in range(parts):
        full_ref[:, part * mid : (part + 1) * mid] = gath_ref[part]
    for part in range(parts):
        lane = slice(part * wide, (part + 1) * wide)
        pre3_ref[:, lane] = jnp.dot(
            full_ref[...], we_ref[:, lane], preferred_element_type=jnp.float32
        )
    total, square = moments(pre3_ref, 16)
    mean_value, inverse = terms(
        *block_totals(total, square, stat3_ref, stat_send.at[2], stat_recv.at[2], blocks)
    )
    term3_ref[0:1] = mean_value
    term3_ref[1:2] = inverse

    def last(part, state):
        value = (
            gain3_ref[...] * ((pre3_ref[part, :] - mean_value) * inverse)
            + bias3_ref[...]
            + cur_ref[part, :].astype(jnp.float32)
        )
        out_ref[part, :] = (value * sigmoid(value)).astype(jnp.bfloat16)
        return state

    row_loop(pixels, 16, last, 0)
    own_wide = pl.ds(pl.multiple_of(ch * wide, wide), wide)
    if fetch:
        for array in range(2):
            forward(array)
    for job in jobs:
        job[1]()
    normed3_ref[...] = (pre3_ref[:, own_wide] - term3_ref[0:1, own_wide]) * term3_ref[1:2, own_wide]
    inverse3_ref[...] = term3_ref[1:2, own_wide]
    if fetch:
        finish()
    for job in jobs:
        job[2]()


def trunk_forward(
    blocks, parts, cols, layer, jobs, current, reduce_w, dilated_w, expand_w, mask, norms, raw
):
    pixels, feat = current.shape
    narrow = reduce_w.shape[0]
    mid, wide = narrow // parts, feat // parts
    edge = 2 * cols
    f32, low = jnp.float32, jnp.bfloat16
    shape = jax.ShapeDtypeStruct
    rows = edge * 2 + pixels
    inside = pl.BlockSpec(memory_space=pltpu.VMEM)
    anywhere = pl.BlockSpec(memory_space=pl.ANY)
    fetch = layer + 1 if raw else 0
    return job_call(
        functools.partial(trunk_forward_kernel, blocks, parts, fetch),
        jobs,
        blocks,
        in_specs=[inside] * 11 + [anywhere] * len(raw),
        out_specs=[inside] * 9 + [anywhere] * len(raw),
        out_shape=[
            shape((pixels, feat), low),
            shape((rows, narrow), low),
            shape((pixels, narrow), low),
            shape((pixels, mid), f32),
            shape((1, mid), f32),
            shape((pixels, mid), f32),
            shape((1, mid), f32),
            shape((pixels, wide), f32),
            shape((1, wide), f32),
        ]
        + [shape((narrow, feat), low)] * len(raw),
        scratch_shapes=[
            pltpu.VMEM((pixels, narrow), f32),
            pltpu.VMEM((pixels, feat), f32),
            pltpu.VMEM((rows, narrow), low),
            pltpu.VMEM((3, pixels, mid), f32),
            pltpu.VMEM((parts, pixels, mid), low),
            pltpu.VMEM((blocks, 2, narrow), f32),
            pltpu.VMEM((blocks, 2, mid), f32),
            pltpu.VMEM((blocks, 2, feat), f32),
            pltpu.VMEM((2, narrow), f32),
            pltpu.VMEM((2, feat), f32),
            pltpu.SemaphoreType.DMA((3, blocks)),
            pltpu.SemaphoreType.DMA((3, blocks)),
            pltpu.SemaphoreType.DMA((2,)),
            pltpu.SemaphoreType.DMA((2,)),
            pltpu.SemaphoreType.DMA((parts,)),
            pltpu.SemaphoreType.DMA((parts,)),
        ]
        + (weights_sems(blocks, parts) if raw else []),
        compiler_params=comm_params(50 + layer),
        cost_estimate=pl.CostEstimate(
            flops=2 * pixels * (2 * narrow * feat + 9 * mid * narrow),
            bytes_accessed=150 * 2**20,
            transcendentals=0,
        ),
    )(current, reduce_w, dilated_w, expand_w, mask, *norms, *raw)


def slope_of(values):
    gate = sigmoid(values)
    return gate * (1.0 + values * (1.0 - gate))


def sum_slots(ref, count):
    total = ref[0].astype(jnp.float32)
    for slot in range(1, count):
        total = total + ref[slot].astype(jnp.float32)
    return total


def trunk_backward_kernel(
    blocks,
    parts,
    up_ref,
    heads_ref,
    cur_ref,
    normed3_ref,
    inverse3_ref,
    gain3_ref,
    bias3_ref,
    we_ref,
    full_ref,
    normed2_ref,
    inverse2_ref,
    gain2_ref,
    bias2_ref,
    wd_ref,
    mask_ref,
    ext_ref,
    normed1_ref,
    inverse1_ref,
    gain1_ref,
    bias1_ref,
    wr_ref,
    gate_ref,
    out_ref,
    expand_ref,
    dilated_ref,
    reduce_ref,
    wide_ref,
    second_ref,
    first_ref,
    gate_out,
    third_ref,
    grad_ref,
    im_ref,
    send2_ref,
    recv2_ref,
    send1_ref,
    recv1_ref,
    gath_ref,
    low_ref,
    ex_send_ref,
    ex_recv_ref,
    di_send_ref,
    di_recv_ref,
    re_send_ref,
    re_recv_ref,
    stat3_ref,
    stat2_ref,
    stat1_ref,
    gates_ref,
    stat_send,
    stat_recv,
    halo_send,
    halo_recv,
    part_send,
    part_recv,
    sum_send,
    sum_recv,
):
    pixels, wide = up_ref.shape
    mid = normed1_ref.shape[1]
    narrow = mid * parts
    feat = cur_ref.shape[1]
    edge = (grad_ref.shape[0] - pixels) // 2
    half = edge // 2
    blk = lax.axis_index(BLK)
    ch = lax.axis_index(CH)
    pixel_count = float(pixels * blocks)
    low = jnp.bfloat16
    greet(blocks, parts)
    own_wide = pl.ds(pl.multiple_of(ch * wide, wide), wide)
    gates_ref[blk] = gate_ref[...]
    wait_gates = send_slots(
        lambda _: gates_ref.at[blk], gates_ref, stat_send.at[3], stat_recv.at[3], BLK, blocks
    )

    def start(part, state):
        normed = normed3_ref[part, :]
        summed = (
            gain3_ref[...] * normed + bias3_ref[...] + cur_ref[part, own_wide].astype(jnp.float32)
        )
        value = (up_ref[part, :] + heads_ref[part, :].astype(jnp.float32)) * slope_of(summed)
        out_ref[part, :] = value
        return state[0] + fold(value), state[1] + fold(value * normed)

    zero = jnp.zeros((8, wide), jnp.float32)
    bias_sum, gain_sum = row_loop(pixels, 32, start, (zero, zero))
    bias_grad, gain_grad = block_totals(
        bias_sum.sum(axis=0, keepdims=True),
        gain_sum.sum(axis=0, keepdims=True),
        stat3_ref,
        stat_send.at[0],
        stat_recv.at[0],
        blocks,
    )
    wide_ref[0:1] = gain_grad
    wide_ref[1:2] = bias_grad
    scale = gain3_ref[...] * inverse3_ref[...]
    bias_part = bias_grad / pixel_count
    gain_part = gain_grad / pixel_count

    def third(part, state):
        third_ref[part, :] = (
            scale * (out_ref[part, :] - bias_part - normed3_ref[part, :] * gain_part)
        ).astype(low)
        return state

    row_loop(pixels, 32, third, 0)
    product = contract_last(third_ref[...], we_ref[...])
    for part in range(parts):
        send2_ref[part] = product[:, part * mid : (part + 1) * mid].astype(low)
    recv2_ref[ch] = send2_ref[ch]
    wait_parts = send_slots(
        lambda peer: send2_ref.at[peer], recv2_ref, part_send.at[0], part_recv.at[0], CH, parts
    )
    size = narrow // blocks
    product = lax.dot_general(
        full_ref[...], third_ref[...], (((0,), (0,)), ((), ())), preferred_element_type=jnp.float32
    )
    for block in range(blocks):
        ex_send_ref[block] = product[block * size : (block + 1) * size].astype(low)
    ex_recv_ref[blk] = ex_send_ref[blk]
    wait_expand = send_slots(
        lambda peer: ex_send_ref.at[peer], ex_recv_ref, sum_send.at[0], sum_recv.at[0], BLK, blocks
    )
    wait_parts()

    def narrow_norm(recv_ref, normed_ref, inverse_ref, gain_ref, bias_ref, stat_ref, phase, sums_ref):
        normed = normed_ref[...]
        value = sum_slots(recv_ref, parts) * slope_of(gain_ref[...] * normed + bias_ref[...])
        bias_grad, gain_grad = block_totals(
            jnp.sum(value, axis=0, keepdims=True),
            jnp.sum(value * normed, axis=0, keepdims=True),
            stat_ref,
            stat_send.at[phase],
            stat_recv.at[phase],
            blocks,
        )
        sums_ref[0:1] = gain_grad
        sums_ref[1:2] = bias_grad
        return (
            gain_ref[...]
            * inverse_ref[...]
            * (value - bias_grad / pixel_count - normed * (gain_grad / pixel_count))
        )

    grad = narrow_norm(
        recv2_ref, normed2_ref, inverse2_ref, gain2_ref, bias2_ref, stat2_ref, 1, second_ref
    )
    grad_ref[edge : edge + pixels, :] = grad.astype(low)
    wait_halo = halo_copies(grad_ref, edge, pixels, halo_send, halo_recv, blocks)
    own = grad_ref[edge : edge + pixels, :].astype(jnp.float32)
    turned = (pltpu.roll(own, pixels - 2, 0), own, pltpu.roll(own, 2, 0))
    for row_step in range(3):
        side = jnp.concatenate(
            [
                masked(turned[col_step], mask_ref[1], row_step * 3 + col_step).astype(low)
                for col_step in range(3)
            ],
            axis=1,
        )
        top = 2 * row_step * half
        product = lax.dot_general(
            ext_ref[top : top + pixels, :],
            side,
            (((0,), (0,)), ((), ())),
            preferred_element_type=jnp.float32,
        )
        for block in range(blocks):
            for col_step in range(3):
                di_send_ref[block, row_step * 3 + col_step] = product[
                    block * size : (block + 1) * size, col_step * mid : (col_step + 1) * mid
                ].astype(low)
    di_recv_ref[blk] = di_send_ref[blk]
    wait_halo()
    fill_taps(im_ref, 0, grad_ref[...], mask_ref[1], pixels, half, 2)
    product = jnp.dot(
        im_ref[0], wd_ref[...].reshape(9 * mid, narrow), preferred_element_type=jnp.float32
    )
    for part in range(parts):
        send1_ref[part] = product[:, part * mid : (part + 1) * mid].astype(low)
    recv1_ref[ch] = send1_ref[ch]
    wait_parts = send_slots(
        lambda peer: send1_ref.at[peer], recv1_ref, part_send.at[1], part_recv.at[1], CH, parts
    )
    wait_dilated = send_slots(
        lambda peer: di_send_ref.at[peer], di_recv_ref, sum_send.at[1], sum_recv.at[1], BLK, blocks
    )
    wait_parts()
    grad = narrow_norm(
        recv1_ref, normed1_ref, inverse1_ref, gain1_ref, bias1_ref, stat1_ref, 2, first_ref
    )
    gath_ref[ch] = grad.astype(low)
    wait_parts = send_slots(
        lambda _: gath_ref.at[ch], gath_ref, part_send.at[2], part_recv.at[2], CH, parts
    )
    product = lax.dot_general(
        cur_ref[...], gath_ref[ch], (((0,), (0,)), ((), ())), preferred_element_type=jnp.float32
    )
    size = feat // blocks
    for block in range(blocks):
        re_send_ref[block] = product[block * size : (block + 1) * size].astype(low)
    re_recv_ref[blk] = re_send_ref[blk]
    wait_reduce = send_slots(
        lambda peer: re_send_ref.at[peer], re_recv_ref, sum_send.at[2], sum_recv.at[2], BLK, blocks
    )
    wait_parts()
    for part in range(parts):
        low_ref[:, part * mid : (part + 1) * mid] = gath_ref[part]
    out_ref[...] += jnp.dot(low_ref[...], wr_ref[:, own_wide], preferred_element_type=jnp.float32)
    wait_gates()
    gate_out[...] = sum_slots(gates_ref, blocks)
    wait_expand()
    expand_ref[...] = sum_slots(ex_recv_ref, blocks)
    wait_dilated()
    dilated_ref[...] = sum_slots(di_recv_ref, blocks)
    wait_reduce()
    reduce_ref[...] = sum_slots(re_recv_ref, blocks)


def trunk_backward(blocks, parts, operands):
    pixels, wide = operands[0].shape
    feat = wide * parts
    mid = operands[9].shape[1]
    narrow = mid * parts
    rows = operands[15].shape[0]
    f32, low = jnp.float32, jnp.bfloat16
    shape = jax.ShapeDtypeStruct
    small, large = narrow // blocks, feat // blocks
    return pl.pallas_call(
        functools.partial(trunk_backward_kernel, blocks, parts),
        out_shape=[
            shape((pixels, wide), f32),
            shape((small, wide), f32),
            shape((9, small, mid), f32),
            shape((large, mid), f32),
            shape((2, wide), f32),
            shape((2, mid), f32),
            shape((2, mid), f32),
            shape(operands[-1].shape, f32),
        ],
        scratch_shapes=[
            pltpu.VMEM((pixels, wide), low),
            pltpu.VMEM((rows, mid), low),
            pltpu.VMEM((1, pixels, 9 * mid), low),
            pltpu.VMEM((parts, pixels, mid), low),
            pltpu.VMEM((parts, pixels, mid), low),
            pltpu.VMEM((parts, pixels, mid), low),
            pltpu.VMEM((parts, pixels, mid), low),
            pltpu.VMEM((parts, pixels, mid), low),
            pltpu.VMEM((pixels, narrow), low),
            pltpu.VMEM((blocks, small, wide), low),
            pltpu.VMEM((blocks, small, wide), low),
            pltpu.VMEM((blocks, 9, small, mid), low),
            pltpu.VMEM((blocks, 9, small, mid), low),
            pltpu.VMEM((blocks, large, mid), low),
            pltpu.VMEM((blocks, large, mid), low),
            pltpu.VMEM((blocks, 2, wide), f32),
            pltpu.VMEM((blocks, 2, mid), f32),
            pltpu.VMEM((blocks, 2, mid), f32),
            pltpu.VMEM((blocks,) + operands[-1].shape, f32),
            pltpu.SemaphoreType.DMA((4, blocks)),
            pltpu.SemaphoreType.DMA((4, blocks)),
            pltpu.SemaphoreType.DMA((2,)),
            pltpu.SemaphoreType.DMA((2,)),
            pltpu.SemaphoreType.DMA((3, parts)),
            pltpu.SemaphoreType.DMA((3, parts)),
            pltpu.SemaphoreType.DMA((3, blocks)),
            pltpu.SemaphoreType.DMA((3, blocks)),
        ],
        compiler_params=comm_params(2),
        cost_estimate=pl.CostEstimate(
            flops=4 * pixels * (2 * narrow * wide + 9 * mid * narrow),
            bytes_accessed=200 * 2**20,
            transcendentals=0,
        ),
    )(*operands)


def gather_parts(values):
    return lax.all_gather(values, CH, axis=0, tiled=False)


def reduce_parts(values):
    return lax.psum_scatter(values, CH, scatter_dimension=0, tiled=False)


def own_slice(values, size, axis):
    return lax.dynamic_slice_in_dim(values, lax.axis_index(CH) * size, size, axis)


def shards(
    features_in,
    w_reduce,
    w_dilated,
    w_expand,
    w_heads,
    w_messages,
    norm_gain,
    norm_bias,
    wide_gain,
    wide_bias,
    gate_gain,
    gate_bias,
    canvas_ids,
    output_cotangent,
    task_cotangents,
):
    rows, cols, wide = features_in.shape
    pixels = rows * cols
    blocks = lax.axis_size(BLK)
    parts = lax.axis_size(CH)
    layers = w_reduce.shape[0]
    mid = w_reduce.shape[1]
    feat = wide * parts
    narrow = mid * parts
    low = jnp.bfloat16
    dilated_t = w_dilated.transpose(0, 2, 1, 3)
    heads_t = w_heads.transpose(0, 1, 3, 2, 4)
    messages_t = w_messages.transpose(0, 1, 3, 2, 4)
    current, *rest = prologue(
        blocks,
        parts,
        features_in.reshape(pixels, wide),
        w_reduce,
        w_expand,
        jnp.concatenate([norm_gain[:, 0], norm_bias[:, 0]], axis=0),
        jnp.concatenate([wide_gain, wide_bias], axis=0),
        canvas_ids,
    )
    reduce_full, expand_full = [rest[0]], [rest[1]]
    narrow_all, wide_all, bits, all_bits = rest[2:]
    narrow_all = narrow_all.transpose(1, 0, 2).reshape(2, layers, narrow)
    wide_all = wide_all.transpose(1, 0, 2).reshape(2, layers, feat)

    kept = []
    for layer in range(layers):
        keep = types.SimpleNamespace(input=current)
        results, _ = trunk_forward(
            blocks,
            parts,
            cols,
            layer,
            [],
            current,
            reduce_full[layer],
            dilated_t[layer],
            expand_full[layer],
            bits,
            (
                narrow_all[0, layer][None],
                narrow_all[1, layer][None],
                norm_gain[layer, 1][None],
                norm_bias[layer, 1][None],
                wide_all[0, layer][None],
                wide_all[1, layer][None],
            ),
            (),
        )
        (
            current,
            keep.first_ext,
            keep.second_full,
            keep.normed1,
            keep.inverse1,
            keep.normed2,
            keep.inverse2,
            keep.normed3,
            keep.inverse3,
        ) = results
        if layer:
            current, kept[-1].features = lax.optimization_barrier((current, kept[-1].features))
        keep.output = current
        keep.heads_pre, features, keep.ends, *fetched = heads_forward(
            blocks,
            parts,
            layer,
            cols,
            current,
            heads_t,
            bits,
            (w_reduce, w_expand) if layer + 1 < layers else (),
        )
        if fetched:
            reduce_full.append(fetched[0])
            expand_full.append(fetched[1])
        current, features = lax.optimization_barrier((current, features))
        keep.features = gather_parts(features)
        kept.append(keep)
    output = own_slice(current, wide, 1).reshape(rows, cols, wide)

    cotangents = task_cotangents.reshape(layers, 2, pixels, mid)
    for layer in range(layers):
        keep = kept[layer]
        if layer == 0:
            jobs = [(gather_kind, cotangents), (gather_kind, keep.ends)]
        else:
            jobs = [(gather_kind, keep.ends), (swap_kind, kept[0].output)]
        (keep.maps, keep.local, keep.gate_sums, partial, keep.message_values), moved = messages_both(
            blocks,
            layer,
            jobs,
            cols,
            keep.features,
            messages_t,
            cotangents[layer],
            gate_gain,
            gate_bias,
            bits,
        )
        if layer == 0:
            cotangents_all, keep.ends_all = moved
        else:
            keep.ends_all, kept[0].values = moved
        keep.source_sums = reduce_parts(partial)

    def heads_low_of(keep):
        sums = keep.source_sums.astype(jnp.float32)
        total = jnp.stack([sums[0] + keep.local[0], sums[1], sums[2], sums[3] + keep.local[1]])
        return (total * silu_slope(keep.heads_pre)).astype(low)

    def messages_weight(layer, jobs):
        keep = kept[layer]
        (keep.messages_grad,), moved = weight_gradient(
            30 + layer,
            blocks,
            jobs,
            group_pairs,
            messages_load(layer),
            messages_store,
            (6, 9, narrow // blocks, mid),
            keep.message_values,
            all_bits,
            (cotangents_all, keep.ends_all, gate_gain, gate_bias),
            [
                pl.BlockSpec((1, 1, 2, pixels, mid), lambda i: (i, layer, 0, 0, 0)),
                pl.BlockSpec((1, 2, pixels, mid), lambda i: (i, 0, 0, 0)),
                whole(gate_gain.shape),
                whole(gate_bias.shape),
            ],
        )
        return moved

    def heads_weight(layer, jobs):
        keep = kept[layer]
        (keep.heads_grad,), moved = weight_gradient(
            40 + layer,
            blocks,
            jobs,
            (tuple(range(4)),),
            heads_load,
            heads_store,
            (4, 9, feat // blocks, mid),
            keep.values[:, None],
            all_bits,
            (keep.heads_all,),
            [pl.BlockSpec((1, 4, pixels, mid), lambda i: (i, 0, 0, 0))],
        )
        return moved

    for layer in range(layers):
        keep = kept[layer]
        keep.heads_low = heads_low_of(keep)
        jobs = [(slot_kind, each.message_values) for each in kept] if layer == 0 else []
        (partial,), moved = heads_backward(
            blocks, layer, jobs, cols, keep.heads_low, heads_t, bits, parts
        )
        if layer == 0:
            for each, values in zip(kept, moved):
                each.message_values = values
        keep.heads_partial = reduce_parts(partial)
        if layer + 1 < layers:
            kept[layer + 1].source_sums, partial = lax.optimization_barrier(
                (kept[layer + 1].source_sums, partial)
            )
    kept[0].message_values, partial = lax.optimization_barrier((kept[0].message_values, partial))
    (kept[0].heads_all,) = messages_weight(0, [(gather_kind, kept[0].heads_low)])
    kept[1].message_values, kept[0].heads_all = lax.optimization_barrier(
        (kept[1].message_values, kept[0].heads_all)
    )
    (kept[1].heads_all,) = messages_weight(1, [(gather_kind, kept[1].heads_low)])
    (kept[1].values,) = heads_weight(0, [(swap_kind, kept[1].output)])
    kept[1].heads_partial, kept[0].heads_grad = lax.optimization_barrier(
        (kept[1].heads_partial, kept[0].heads_grad)
    )

    upstream = output_cotangent.reshape(pixels, wide).astype(jnp.float32)
    for layer in reversed(range(layers)):
        keep = kept[layer]
        (
            upstream,
            keep.expand_grad,
            keep.dilated_grad,
            keep.reduce_grad,
            keep.wide_sums,
            keep.second_sums,
            keep.first_sums,
            keep.gates,
        ) = trunk_backward(
            blocks,
            parts,
            (
                upstream,
                keep.heads_partial,
                keep.input,
                keep.normed3,
                keep.inverse3,
                wide_gain[layer][None],
                wide_bias[layer][None],
                w_expand[layer],
                keep.second_full,
                keep.normed2,
                keep.inverse2,
                norm_gain[layer, 1][None],
                norm_bias[layer, 1][None],
                dilated_t[layer],
                bits,
                keep.first_ext,
                keep.normed1,
                keep.inverse1,
                norm_gain[layer, 0][None],
                norm_bias[layer, 0][None],
                reduce_full[layer],
                keep.gate_sums,
            ),
        )

    heads_weight(1, [])

    def stacked(of):
        return jnp.stack([of(keep) for keep in kept])

    narrow_sums = stacked(lambda keep: jnp.stack([keep.first_sums, keep.second_sums]))
    wide_sums = stacked(lambda keep: keep.wide_sums)
    gate_sums = stacked(lambda keep: keep.gates.reshape(2, 6, mid))
    return (
        output,
        stacked(lambda keep: keep.maps.reshape(2, rows, cols, mid)),
        upstream.reshape(rows, cols, wide),
        stacked(lambda keep: keep.reduce_grad),
        stacked(lambda keep: keep.dilated_grad),
        stacked(lambda keep: keep.expand_grad),
        stacked(lambda keep: keep.heads_grad),
        stacked(lambda keep: keep.messages_grad),
        narrow_sums[:, :, 0],
        narrow_sums[:, :, 1],
        wide_sums[:, 0],
        wide_sums[:, 1],
        gate_sums[:, 0],
        gate_sums[:, 1],
    )


def route(*args):
    mid = args[1].shape[1]
    blocks, parts = lax.axis_size(BLK), lax.axis_size(CH)
    whole_tiles = args[1].shape[0] == 2 and mid % lanes == 0 and args[0].shape[1] == lanes and parts >= 2
    if whole_tiles and blocks % 2 == 0 and 2 * mid * parts == lanes * blocks:
        return shards(*args)
    return plain_shards(*args)


def solution(mesh):
    placed = (
        P(BLK, None, CH),
        P(None, CH, None),
        P(None, CH, None, None),
        P(None, None, CH),
        P(None, None, CH, None, None),
        P(None, None, CH, None, None),
        P(None, None, CH),
        P(None, None, CH),
        P(None, CH),
        P(None, CH),
        P(None, None, CH),
        P(None, None, CH),
        P(),
        P(BLK, None, CH),
        P(None, None, BLK, None, CH),
    )
    return jax.shard_map(
        route,
        mesh=mesh,
        in_specs=placed,
        out_specs=(
            P(BLK, None, CH),
            P(None, None, BLK, None, CH),
            P(BLK, None, CH),
            P(None, BLK, CH),
            P(None, None, BLK, CH),
            P(None, BLK, CH),
            P(None, None, None, BLK, CH),
            P(None, None, None, BLK, CH),
            P(None, None, CH),
            P(None, None, CH),
            P(None, CH),
            P(None, CH),
            P(None, None, CH),
            P(None, None, CH),
        ),
        check_vma=False,
    )
```

```python
import functools
import types

import jax
import jax.numpy as jnp
from jax import lax
from jax.experimental import pallas as pl
from jax.experimental.pallas import tpu as pltpu
from jax.sharding import PartitionSpec as P

epsilon = 1e-05
BLK = "blk"
CH = "ch"
tap_offsets = tuple(((row_step, col_step) for row_step in (-1, 0, 1) for col_step in (-1, 0, 1)))
message_pairs = ((1, 0), (2, 0), (3, 0), (0, 3), (1, 3), (2, 3))


def extended_2(block, sides, width):
    for axis, dim in sides:
        count = lax.axis_size(axis)
        forward = [(i, i + 1) for i in range(count - 1)]
        backward = [(target, source) for source, target in forward]
        low = lax.ppermute(
            lax.slice_in_dim(block, block.shape[dim] - width, None, axis=dim), axis, forward
        )
        high = lax.ppermute(lax.slice_in_dim(block, 0, width, axis=dim), axis, backward)
        block = jnp.concatenate([low, block, high], axis=dim)
    return block


def silu_slope(values):
    sigmoid_value = jax.nn.sigmoid(values)
    return sigmoid_value * (1.0 + values * (1.0 - sigmoid_value))


def gather_channels(values):
    return lax.all_gather(values, CH, axis=3, tiled=True)


def reduce_channels(values):
    return lax.psum_scatter(
        values.astype(jnp.bfloat16), CH, scatter_dimension=3, tiled=True
    ).astype(jnp.float32)


def extend_rows(values, halo_width):
    return extended_2(values, ((BLK, 0),), halo_width)


def pixel_totals(first_sum, second_sum):
    return lax.psum((first_sum, second_sum), BLK)


def weight_totals(reduce_grad, dilated_grad, expand_grad, heads_grad, messages_grad):
    return (
        lax.psum_scatter(
            reduce_grad.astype(jnp.bfloat16), BLK, scatter_dimension=1, tiled=True
        ).astype(jnp.float32),
        lax.psum_scatter(
            dilated_grad.astype(jnp.bfloat16), BLK, scatter_dimension=2, tiled=True
        ).astype(jnp.float32),
        lax.psum_scatter(
            expand_grad.astype(jnp.bfloat16), BLK, scatter_dimension=1, tiled=True
        ).astype(jnp.float32),
        lax.psum_scatter(
            heads_grad.astype(jnp.bfloat16), BLK, scatter_dimension=3, tiled=True
        ).astype(jnp.float32),
        lax.psum_scatter(
            messages_grad.astype(jnp.bfloat16), BLK, scatter_dimension=3, tiled=True
        ).astype(jnp.float32),
    )


def widen(values, halo_width):
    return extend_rows(gather_channels(values), halo_width)


def local_masks(canvas_ids, row_count, dilation):
    col_count = canvas_ids.shape[1]
    padded = jnp.pad(canvas_ids, 2, constant_values=-1)
    start = lax.axis_index(BLK) * row_count
    window = lax.dynamic_slice(padded, (start, jnp.int32(0)), (row_count + 4, col_count + 4))
    centre = window[2 : 2 + row_count, 2 : 2 + col_count]
    result = []
    for row_step, col_step in tap_offsets:
        top = 2 + row_step * dilation
        left = 2 + col_step * dilation
        result.append(window[top : top + row_count, left : left + col_count] == centre)
    return jnp.stack(result)


def shifted(padded, halo_width, dilation, row_step, col_step, row_count, col_count):
    top = halo_width + row_step * dilation
    left = dilation + col_step * dilation
    return padded[top : top + row_count, left : left + col_count]


def conv_forward(extended, halo_width, dilation, weights, tap_masks):
    row_count = extended.shape[0] - 2 * halo_width
    col_count = extended.shape[1]
    padded = jnp.pad(extended, ((0, 0), (dilation, dilation), (0, 0)))
    running = jnp.zeros((row_count, col_count, weights.shape[0], weights.shape[1]), jnp.float32)
    for tap_index, (row_step, col_step) in enumerate(tap_offsets):
        window = shifted(padded, halo_width, dilation, row_step, col_step, row_count, col_count)
        product = jnp.einsum(
            "rwc,koc->rwko", window, weights[:, :, tap_index], preferred_element_type=jnp.float32
        )
        running = running + jnp.where(tap_masks[tap_index][:, :, None, None], product, 0.0)
    return running


def conv_weight_grad(extended, halo_width, dilation, gradient, tap_masks):
    row_count = extended.shape[0] - 2 * halo_width
    col_count = extended.shape[1]
    padded = jnp.pad(extended, ((0, 0), (dilation, dilation), (0, 0)))
    result = []
    for tap_index, (row_step, col_step) in enumerate(tap_offsets):
        window = shifted(padded, halo_width, dilation, row_step, col_step, row_count, col_count)
        masked = jnp.where(
            tap_masks[tap_index][:, :, None, None], gradient, jnp.zeros((), gradient.dtype)
        )
        result.append(
            jnp.einsum("rwc,rwko->kco", window, masked, preferred_element_type=jnp.float32)
        )
    return jnp.stack(result, axis=1)


def conv_input_grad(grad_extended, halo_width, dilation, weights, tap_masks):
    row_count = grad_extended.shape[0] - 2 * halo_width
    col_count = grad_extended.shape[1]
    padded = jnp.pad(grad_extended, ((0, 0), (dilation, dilation), (0, 0), (0, 0)))
    running = jnp.zeros((row_count, col_count, weights.shape[3]), jnp.float32)
    for tap_index, (row_step, col_step) in enumerate(tap_offsets):
        window = shifted(padded, halo_width, dilation, -row_step, -col_step, row_count, col_count)
        product = jnp.einsum(
            "rwko,koc->rwc", window, weights[:, :, tap_index], preferred_element_type=jnp.float32
        )
        running = running + jnp.where(tap_masks[8 - tap_index][:, :, None], product, 0.0)
    return running


def norm_forward(hidden, gain, bias, pixel_count):
    total_sum, square_sum = pixel_totals(
        jnp.sum(hidden, axis=(0, 1)), jnp.sum(hidden * hidden, axis=(0, 1))
    )
    mean_value = total_sum / pixel_count
    variance = square_sum / pixel_count - mean_value * mean_value
    inverse = lax.rsqrt(variance + epsilon)
    normed = (hidden - mean_value) * inverse
    return (gain * normed + bias, normed, inverse)


def norm_backward(upstream, normed, inverse, gain, pixel_count):
    bias_grad, gain_grad = pixel_totals(
        jnp.sum(upstream, axis=(0, 1)), jnp.sum(upstream * normed, axis=(0, 1))
    )
    hidden_grad = (
        gain * inverse * (upstream - bias_grad / pixel_count - normed * gain_grad / pixel_count)
    )
    return (hidden_grad, gain_grad, bias_grad)


def layer_forward(inputs, params, masks_one, masks_two, pixel_count):
    (
        reduce_w,
        dilated_w,
        expand_w,
        heads_w,
        messages_w,
        narrow_gain,
        narrow_bias,
        wide_g,
        wide_b,
        gate_g,
        gate_b,
    ) = params
    stored = types.SimpleNamespace()
    inputs_full = gather_channels(inputs[:, :, None, :])[:, :, 0, :]
    first_pre = jnp.einsum("rwc,oc->rwo", inputs_full, reduce_w, preferred_element_type=jnp.float32)
    first_norm, first_normed, first_inverse = norm_forward(
        first_pre, narrow_gain[0], narrow_bias[0], pixel_count
    )
    first_act = jax.nn.silu(first_norm).astype(jnp.bfloat16)
    first_ext = widen(first_act[:, :, None, :], 2)[:, :, 0, :]
    second_pre = conv_forward(first_ext, 2, 2, dilated_w[None], masks_two)[:, :, 0, :]
    second_norm, second_normed, second_inverse = norm_forward(
        second_pre, narrow_gain[1], narrow_bias[1], pixel_count
    )
    second_act = jax.nn.silu(second_norm).astype(jnp.bfloat16)
    second_full = gather_channels(second_act[:, :, None, :])[:, :, 0, :]
    third_pre = jnp.einsum("rwc,co->rwo", second_full, expand_w, preferred_element_type=jnp.float32)
    third_norm, third_normed, third_inverse = norm_forward(third_pre, wide_g, wide_b, pixel_count)
    summed = third_norm + inputs.astype(jnp.float32)
    output = jax.nn.silu(summed).astype(jnp.bfloat16)
    output_ext = widen(output[:, :, None, :], 1)[:, :, 0, :]
    heads_pre = conv_forward(output_ext, 1, 1, heads_w, masks_one)
    features = jax.nn.silu(heads_pre).astype(jnp.bfloat16)
    features_ext = widen(features, 1)
    feature_values = features.astype(jnp.float32)
    depth_map = feature_values[:, :, 0]
    segment_map = feature_values[:, :, 3]
    message_list = []
    for pair_index, (source, target) in enumerate(message_pairs):
        message = conv_forward(
            features_ext[:, :, source], 1, 1, messages_w[pair_index][None], masks_one
        )[:, :, 0]
        gate_value = jax.nn.sigmoid(
            gate_g[pair_index] * feature_values[:, :, target] + gate_b[pair_index]
        )
        message_list.append(message)
        if target == 0:
            depth_map = depth_map + gate_value * message
        else:
            segment_map = segment_map + gate_value * message
    stored.inputs_full = inputs_full
    stored.first_norm = first_norm
    stored.first_normed = first_normed
    stored.first_inverse = first_inverse
    stored.first_ext = first_ext
    stored.second_norm = second_norm
    stored.second_normed = second_normed
    stored.second_inverse = second_inverse
    stored.second_full = second_full
    stored.third_normed = third_normed
    stored.third_inverse = third_inverse
    stored.summed = summed
    stored.output_ext = output_ext
    stored.heads_pre = heads_pre
    stored.features = feature_values
    stored.features_ext = features_ext
    stored.messages = message_list
    return (output, depth_map, segment_map, stored)


def layer_backward(
    stored, upstream, depth_grad, segment_grad, params, masks_one, masks_two, pixel_count
):
    (
        reduce_w,
        dilated_w,
        expand_w,
        heads_w,
        messages_w,
        narrow_gain,
        narrow_bias,
        wide_g,
        wide_b,
        gate_g,
        gate_b,
    ) = params
    feature_values = stored.features
    zero_map = jnp.zeros_like(depth_grad)
    feature_grads = [depth_grad, zero_map, zero_map, segment_grad]
    message_grads = []
    gain_terms = []
    bias_terms = []
    for pair_index, (source, target) in enumerate(message_pairs):
        target_grad = depth_grad if target == 0 else segment_grad
        gate_value = jax.nn.sigmoid(
            gate_g[pair_index] * feature_values[:, :, target] + gate_b[pair_index]
        )
        message_grads.append(target_grad * gate_value)
        slope = target_grad * stored.messages[pair_index] * gate_value * (1.0 - gate_value)
        gain_terms.append(jnp.sum(slope * feature_values[:, :, target], axis=(0, 1)))
        bias_terms.append(jnp.sum(slope, axis=(0, 1)))
        feature_grads[target] = feature_grads[target] + slope * gate_g[pair_index]
    gate_gain_grad, gate_bias_grad = pixel_totals(jnp.stack(gain_terms), jnp.stack(bias_terms))
    message_stack = jnp.stack(message_grads, axis=2).astype(jnp.bfloat16)
    message_ext = extend_rows(message_stack, 1)
    weight_parts = []
    source_partials = [None, None, None, None]
    for pair_index, (source, target) in enumerate(message_pairs):
        weight_parts.append(
            conv_weight_grad(
                stored.features_ext[:, :, source],
                1,
                1,
                message_stack[:, :, pair_index : pair_index + 1],
                masks_one,
            )
        )
        partial_grad = conv_input_grad(
            message_ext[:, :, pair_index : pair_index + 1],
            1,
            1,
            messages_w[pair_index][None],
            masks_one,
        )
        if source_partials[source] is None:
            source_partials[source] = partial_grad
        else:
            source_partials[source] = source_partials[source] + partial_grad
    messages_w_grad = jnp.concatenate(weight_parts, axis=0)
    source_sums = reduce_channels(jnp.stack(source_partials, axis=2))
    features_total = jnp.stack(feature_grads, axis=2) + source_sums
    heads_grad = (features_total * silu_slope(stored.heads_pre)).astype(jnp.bfloat16)
    heads_w_grad = conv_weight_grad(stored.output_ext, 1, 1, heads_grad, masks_one)
    heads_ext = extend_rows(heads_grad, 1)
    output_partial = conv_input_grad(heads_ext, 1, 1, heads_w, masks_one)
    output_total = upstream + reduce_channels(output_partial[:, :, None, :])[:, :, 0, :]
    summed_grad = output_total * silu_slope(stored.summed)
    third_grad, wide_gain_grad, wide_bias_grad = norm_backward(
        summed_grad, stored.third_normed, stored.third_inverse, wide_g, pixel_count
    )
    third_low = third_grad.astype(jnp.bfloat16)
    expand_w_grad = jnp.einsum(
        "rwc,rwo->co", stored.second_full, third_low, preferred_element_type=jnp.float32
    )
    second_partial = jnp.einsum(
        "rwo,co->rwc", third_low, expand_w, preferred_element_type=jnp.float32
    )
    second_act_grad = reduce_channels(second_partial[:, :, None, :])[:, :, 0, :]
    second_grad, second_gain_grad, second_bias_grad = norm_backward(
        second_act_grad * silu_slope(stored.second_norm),
        stored.second_normed,
        stored.second_inverse,
        narrow_gain[1],
        pixel_count,
    )
    second_low = second_grad.astype(jnp.bfloat16)[:, :, None, :]
    dilated_w_grad = conv_weight_grad(stored.first_ext, 2, 2, second_low, masks_two)[0]
    second_ext = extend_rows(second_low, 2)
    first_partial = conv_input_grad(second_ext, 2, 2, dilated_w[None], masks_two)
    first_act_grad = reduce_channels(first_partial[:, :, None, :])[:, :, 0, :]
    first_grad, first_gain_grad, first_bias_grad = norm_backward(
        first_act_grad * silu_slope(stored.first_norm),
        stored.first_normed,
        stored.first_inverse,
        narrow_gain[0],
        pixel_count,
    )
    first_low = first_grad.astype(jnp.bfloat16)
    reduce_w_grad = jnp.einsum(
        "rwc,rwo->co", stored.inputs_full, first_low, preferred_element_type=jnp.float32
    )
    inputs_partial = jnp.einsum(
        "rwo,oc->rwc", first_low, reduce_w, preferred_element_type=jnp.float32
    )
    inputs_grad = reduce_channels(inputs_partial[:, :, None, :])[:, :, 0, :] + summed_grad
    weight_grads = (reduce_w_grad, dilated_w_grad, expand_w_grad, heads_w_grad, messages_w_grad)
    small_grads = (
        jnp.stack([first_gain_grad, second_gain_grad]),
        jnp.stack([first_bias_grad, second_bias_grad]),
        wide_gain_grad,
        wide_bias_grad,
        gate_gain_grad,
        gate_bias_grad,
    )
    return (inputs_grad, weight_grads, small_grads)


def plain_shards(
    features_in,
    w_reduce,
    w_dilated,
    w_expand,
    w_heads,
    w_messages,
    norm_gain,
    norm_bias,
    wide_gain,
    wide_bias,
    gate_gain,
    gate_bias,
    canvas_ids,
    output_cotangent,
    task_cotangents,
):
    row_count = features_in.shape[0]
    col_count = features_in.shape[1]
    pixel_count = float(row_count * col_count * lax.axis_size(BLK))
    masks_one = local_masks(canvas_ids, row_count, 1)
    masks_two = local_masks(canvas_ids, row_count, 2)
    layer_count = w_reduce.shape[0]
    layer_params = []
    for layer_index in range(layer_count):
        layer_params.append(
            (
                w_reduce[layer_index],
                w_dilated[layer_index],
                w_expand[layer_index],
                w_heads[layer_index],
                w_messages[layer_index],
                norm_gain[layer_index],
                norm_bias[layer_index],
                wide_gain[layer_index],
                wide_bias[layer_index],
                gate_gain[layer_index],
                gate_bias[layer_index],
            )
        )
    current = features_in
    stored_list = []
    task_list = []
    for layer_index in range(layer_count):
        current, depth_map, segment_map, stored = layer_forward(
            current, layer_params[layer_index], masks_one, masks_two, pixel_count
        )
        stored_list.append(stored)
        task_list.append(jnp.stack([depth_map, segment_map]).astype(jnp.bfloat16))
    upstream = output_cotangent.astype(jnp.float32)
    weight_list = [None] * layer_count
    small_list = [None] * layer_count
    for layer_index in reversed(range(layer_count)):
        upstream, weight_grads, small_grads = layer_backward(
            stored_list[layer_index],
            upstream,
            task_cotangents[layer_index, 0].astype(jnp.float32),
            task_cotangents[layer_index, 1].astype(jnp.float32),
            layer_params[layer_index],
            masks_one,
            masks_two,
            pixel_count,
        )
        weight_list[layer_index] = weight_grads
        small_list[layer_index] = small_grads
    stacked = [
        jnp.stack([weight_list[layer_index][member] for layer_index in range(layer_count)])
        for member in range(5)
    ]
    weight_sums = weight_totals(stacked[0], stacked[1], stacked[2], stacked[3], stacked[4])
    small_sums = [
        jnp.stack([small_list[layer_index][member] for layer_index in range(layer_count)])
        for member in range(6)
    ]
    return (
        current,
        jnp.stack(task_list),
        upstream,
        weight_sums[0],
        weight_sums[1],
        weight_sums[2],
        weight_sums[3],
        weight_sums[4],
        small_sums[0],
        small_sums[1],
        small_sums[2],
        small_sums[3],
        small_sums[4],
        small_sums[5],
    )


lanes = 128
source_order = ((1, 0, 4), (2, 1, 5), (0, 3), (3, 2))


def whole(shape):
    return pl.BlockSpec(shape, lambda *_: (0,) * len(shape))


def contract_last(left, right):
    return lax.dot_general(
        left, right, (((1,), (1,)), ((), ())), preferred_element_type=jnp.float32
    )


def sigmoid(values):
    return 1.0 / (1.0 + jnp.exp(-values))


def masked(values, bits, place):
    taken = (bits & (1 << place)) != 0
    width = values.shape[1]
    parts = [
        jnp.where(taken, values[:, start : start + lanes], 0.0) for start in range(0, width, lanes)
    ]
    return parts[0] if len(parts) == 1 else jnp.concatenate(parts, axis=1)


MESH = pl.DeviceIdType.MESH
groups = ((1, 2), (0, 3))
targets = (0, 3)
group_pairs = ((0, 4, 1, 5), (3, 2))


def remote(source, target, send_sem, recv_sem, axis, peer):
    return pltpu.make_async_remote_copy(
        src_ref=source,
        dst_ref=target,
        send_sem=send_sem,
        recv_sem=recv_sem,
        device_id={axis: peer},
        device_id_type=MESH,
    )


def comm_params(key):
    return pltpu.CompilerParams(
        vmem_limit_bytes=60 * 2**20, collective_id=key, has_side_effects=True
    )


def announce(targets):
    barrier = pltpu.get_barrier_semaphore()
    for axis, peer in targets:
        pl.semaphore_signal(barrier, inc=1, device_id={axis: peer}, device_id_type=MESH)
    pl.semaphore_wait(barrier, len(targets))


def near_blocks(blocks):
    me = lax.axis_index(BLK)
    sibling = me + 1 - 2 * lax.rem(me, 2)
    return sibling, [lax.rem(me + 2 * step, blocks) for step in range(1, blocks // 2)]


def others(axis, count):
    me = lax.axis_index(axis)
    return [lax.rem(me + step, count) for step in range(1, count)]


def gather_job(source, target, sems, blocks):
    near_send, slot_recv, pass_send, local_sem = sems
    me = lax.axis_index(BLK)
    sibling, peers = near_blocks(blocks)
    own = pltpu.make_async_copy(source, target.at[me], local_sem.at[0])

    def near(step, peer):
        return remote(
            source, target.at[me], near_send.at[step], slot_recv.at[me], BLK, peer
        )

    def passing(step, peer):
        return remote(
            target.at[peer], target.at[peer], pass_send.at[step], slot_recv.at[peer], BLK, sibling
        )

    def start():
        own.start()
        for step, peer in enumerate(peers + [sibling]):
            near(step, peer).start()

    def forward():
        for step, peer in enumerate(peers):
            copy = passing(step, peer)
            copy.wait_recv()
            copy.start()

    def finish():
        for step in range(blocks // 2):
            passing(0, lax.rem(sibling + 2 * step, blocks)).wait_recv()
        for step, peer in enumerate(peers + [sibling]):
            near(step, peer).wait_send()
        for step, peer in enumerate(peers):
            passing(step, peer).wait_send()
        own.wait()

    return start, forward, finish


def swap_job(source, target, sems, blocks):
    slot_send, slot_recv, _, local_sem = sems
    me = lax.axis_index(BLK)
    width = source.shape[1] // blocks

    def part_of(block):
        return source.at[:, pl.ds(pl.multiple_of(block * width, width), width)]

    own = pltpu.make_async_copy(part_of(me), target.at[me], local_sem.at[0])

    def copy(step, peer, slot):
        return remote(
            part_of(peer), target.at[slot], slot_send.at[step], slot_recv.at[slot], BLK, peer
        )

    def start():
        for step, peer in enumerate(others(BLK, blocks)):
            copy(step, peer, me).start()
        own.start()

    def finish():
        for step, peer in enumerate(others(BLK, blocks)):
            copy(step, peer, peer).wait_recv()
            copy(step, peer, me).wait_send()
        own.wait()

    return start, lambda: None, finish


def slot_job(source, target, sems, blocks):
    slot_send, slot_recv, _, local_sem = sems
    me = lax.axis_index(BLK)
    own = pltpu.make_async_copy(source.at[me], target.at[me], local_sem.at[0])

    def copy(step, peer, slot):
        return remote(
            source.at[peer], target.at[slot], slot_send.at[step], slot_recv.at[slot], BLK, peer
        )

    def start():
        for step, peer in enumerate(others(BLK, blocks)):
            copy(step, peer, me).start()
        own.start()

    def finish():
        for step, peer in enumerate(others(BLK, blocks)):
            copy(step, peer, peer).wait_recv()
            copy(step, peer, me).wait_send()
        own.wait()

    return start, lambda: None, finish


job_kinds = (gather_job, swap_job, slot_job)
gather_kind, swap_kind, slot_kind = 0, 1, 2


def job_target(kind, source, blocks):
    if kind == gather_kind:
        return jax.ShapeDtypeStruct((blocks,) + source.shape, source.dtype)
    if kind == slot_kind:
        return jax.ShapeDtypeStruct(source.shape, source.dtype)
    return jax.ShapeDtypeStruct(
        (blocks, source.shape[0], source.shape[1] // blocks), source.dtype
    )


def job_sems(blocks):
    dma = pltpu.SemaphoreType.DMA
    return [dma((blocks,)), dma((blocks,)), dma((blocks,)), dma((1,))]


def job_call(kernel, jobs, blocks, in_specs, out_specs, out_shape, scratch_shapes, **options):
    anywhere = pl.BlockSpec(memory_space=pl.ANY)
    n_in, n_out, n_scratch = len(in_specs), len(out_specs), len(scratch_shapes)
    count = len(jobs)

    def wrapped(*refs):
        ins, refs = refs[:n_in], refs[n_in:]
        sources, refs = refs[:count], refs[count:]
        outs, refs = refs[:n_out], refs[n_out:]
        targets, refs = refs[:count], refs[count:]
        scratch, sems = refs[:n_scratch], refs[n_scratch:]
        running = [
            job_kinds[kind](
                sources[place], targets[place], sems[4 * place : 4 * place + 4], blocks
            )
            for place, (kind, _) in enumerate(jobs)
        ]
        kernel(running, *ins, *outs, *scratch)

    def call(*operands):
        result = pl.pallas_call(
            wrapped,
            in_specs=list(in_specs) + [anywhere] * count,
            out_specs=list(out_specs) + [anywhere] * count,
            out_shape=list(out_shape) + [job_target(kind, source, blocks) for kind, source in jobs],
            scratch_shapes=list(scratch_shapes) + job_sems(blocks) * count,
            **options,
        )(*operands, *[source for _, source in jobs])
        return result[:n_out], result[n_out:]

    return call


def stripe_job(wr_ref, we_ref, layer, mine, sems, blocks, parts):
    part_send, part_recv, local_sem = sems
    _, mid, feat = wr_ref.shape
    _, narrow, wide = we_ref.shape
    blk, ch = lax.axis_index(BLK), lax.axis_index(CH)

    def cut(index, size):
        return pl.ds(pl.multiple_of(index * size, size), size)

    def source(array):
        if array == 0:
            return wr_ref.at[layer, :, cut(blk, feat // blocks)]
        return we_ref.at[layer, cut(blk, narrow // blocks), :]

    def share(array, part):
        if array == 0:
            return mine[0].at[cut(part, mid), :]
        return mine[1].at[:, cut(part, wide)]

    def own(array):
        return pltpu.make_async_copy(source(array), share(array, ch), local_sem.at[array])

    def copy(array, step, peer, slot):
        return remote(
            source(array),
            share(array, slot),
            part_send.at[array, step],
            part_recv.at[array, slot],
            CH,
            peer,
        )

    def start():
        for array in range(2):
            own(array).start()
            for step, peer in enumerate(others(CH, parts)):
                copy(array, step, peer, ch).start()

    def finish():
        for array in range(2):
            for step, peer in enumerate(others(CH, parts)):
                copy(array, step, peer, peer).wait_recv()
            own(array).wait()
            for step, peer in enumerate(others(CH, parts)):
                copy(array, step, peer, ch).wait_send()

    return start, finish


def stripe_sems(parts):
    dma = pltpu.SemaphoreType.DMA
    return [dma((2, parts)), dma((2, parts)), dma((2,))]


def stripe_shapes(parts, blocks, reduce_w, expand_w):
    _, mid, feat = reduce_w.shape
    narrow = mid * parts
    return [
        jax.ShapeDtypeStruct((narrow, feat // blocks), reduce_w.dtype),
        jax.ShapeDtypeStruct((narrow // blocks, feat), expand_w.dtype),
    ]


def spread_job(mine, fulls, sems, blocks):
    near_send, near_recv, pass_send, local_sem = sems
    blk = lax.axis_index(BLK)
    sibling, peers = near_blocks(blocks)
    sizes = (mine[0].shape[1], mine[1].shape[0])

    def stripe(array, block):
        part = pl.ds(pl.multiple_of(block * sizes[array], sizes[array]), sizes[array])
        return fulls[0].at[:, part] if array == 0 else fulls[1].at[part, :]

    def own(array):
        return pltpu.make_async_copy(mine[array], stripe(array, blk), local_sem.at[array])

    def near_copy(array, step, peer):
        return remote(
            mine[array],
            stripe(array, blk),
            near_send.at[array, step],
            near_recv.at[array, blk],
            BLK,
            peer,
        )

    def passing(array, step, peer):
        return remote(
            stripe(array, peer),
            stripe(array, peer),
            pass_send.at[array, step],
            near_recv.at[array, peer],
            BLK,
            sibling,
        )

    def start():
        for array in range(2):
            own(array).start()
            for step, peer in enumerate(peers + [sibling]):
                near_copy(array, step, peer).start()

    def forward(array):
        for step, peer in enumerate(peers):
            copy = passing(array, step, peer)
            copy.wait_recv()
            copy.start()

    def finish():
        for array in range(2):
            for step in range(blocks // 2):
                passing(array, 0, lax.rem(sibling + 2 * step, blocks)).wait_recv()
            for step, peer in enumerate(peers + [sibling]):
                near_copy(array, step, peer).wait_send()
            for step, peer in enumerate(peers):
                passing(array, step, peer).wait_send()
            own(array).wait()

    return start, forward, finish


def spread_sems(blocks):
    dma = pltpu.SemaphoreType.DMA
    near = blocks // 2
    return [dma((2, near)), dma((2, blocks)), dma((2, near)), dma((2,))]


def prologue_kernel(
    blocks,
    parts,
    feat_ref,
    wr_ref,
    we_ref,
    narrow_ref,
    wide_ref,
    ids_ref,
    cur_ref,
    mine_r,
    mine_e,
    full_r,
    full_e,
    narrow_out,
    wide_out,
    own_ref,
    all_ref,
    line_send,
    line_recv,
    small_send,
    small_recv,
    local_sem,
    *sems,
):
    pixels, wide = feat_ref.shape
    blk, ch = lax.axis_index(BLK), lax.axis_index(CH)
    sibling, peers = near_blocks(blocks)
    smalls = ((narrow_ref, narrow_out), (wide_ref, wide_out))

    def lane_part(index):
        return cur_ref.at[:, pl.ds(pl.multiple_of(index * wide, wide), wide)]

    start, gathered = stripe_job(wr_ref, we_ref, 0, (mine_r, mine_e), sems[:3], blocks, parts)
    spread, forward, finish = spread_job((mine_r, mine_e), (full_r, full_e), sems[3:], blocks)
    own = pltpu.make_async_copy(feat_ref, lane_part(ch), local_sem.at[0])
    own.start()
    announce(
        [(CH, peer) for peer in others(CH, parts)]
        + [(BLK, peer) for peer in [sibling] + peers]
    )
    start()

    right, left = lax.rem(ch + 1, parts), lax.rem(ch + parts - 1, parts)

    def sides(hop):
        return (
            (0, lax.rem(ch + parts - hop, parts), right, ch - hop >= 0, ch < parts - 1),
            (1, lax.rem(ch + hop, parts), left, ch + hop < parts, ch > 0),
        )

    def line_copy(block, side, hop, peer):
        return remote(
            feat_ref if hop == 0 else lane_part(block),
            lane_part(block),
            line_send.at[side, hop],
            line_recv.at[block],
            CH,
            peer,
        )

    def line_hop(hop):
        for side, block, peer, valid, goes in sides(hop):
            if hop > 0:

                @pl.when(valid)
                def _():
                    line_copy(block, side, hop, peer).wait_recv()

            if hop < parts - 1:

                @pl.when(valid & goes)
                def _():
                    line_copy(block, side, hop, peer).start()

    def small_copy(place, step, peer, slot):
        source, target = smalls[place]
        return remote(
            source,
            target.at[slot],
            small_send.at[place, step],
            small_recv.at[place, slot],
            CH,
            peer,
        )

    def small_own(place):
        source, target = smalls[place]
        return pltpu.make_async_copy(source, target.at[ch], local_sem.at[1 + place])

    line_hop(0)
    for place in range(2):
        small_own(place).start()
        for step, peer in enumerate(others(CH, parts)):
            small_copy(place, step, peer, ch).start()
    gathered()
    spread()

    rows = own_ref.shape[1] // lanes

    def same(row, row_move, col_move, other_move):
        here = ids_ref[row, 4 + other_move : 4 + other_move + lanes, :]
        there = ids_ref[row + row_move, 4 + col_move : 4 + col_move + lanes, :]
        return here, here == there

    def own_row(row, state):
        place = 2 + blk * rows + row
        for word, reach in enumerate((1, 2)):
            bits = jnp.zeros((lanes, lanes), jnp.int32)
            for tap, (row_step, col_step) in enumerate(tap_offsets):
                a, b = row_step * reach, col_step * reach
                here, equal = same(place, a, 0, -b)
                bits = bits | jnp.where(equal & (here >= 0), 1 << tap, 0)
                _, equal = same(place, -a, -b, 0)
                bits = bits | jnp.where(equal, 1 << (9 + tap), 0)
            own_ref[word, pl.ds(pl.multiple_of(row * lanes, lanes), lanes), :] = bits
        return state

    lax.fori_loop(0, rows, own_row, 0)

    def any_row(row, state):
        bits = jnp.zeros((lanes, lanes), jnp.int32)
        for tap, (row_step, col_step) in enumerate(tap_offsets):
            _, equal = same(2 + row, row_step, col_step, 0)
            bits = bits | jnp.where(equal, 1 << tap, 0)
        all_ref[pl.ds(pl.multiple_of(row * lanes, lanes), lanes), :] = bits
        return state

    lax.fori_loop(0, ids_ref.shape[0] - 4, any_row, 0)
    for hop in range(1, parts):
        line_hop(hop)
        if hop <= 2:
            forward(hop - 1)
    for array in range(parts - 1, 2):
        forward(array)
    finish()
    for hop in range(parts - 1):
        for side, block, peer, valid, goes in sides(hop):

            @pl.when(valid & goes)
            def _():
                line_copy(block, side, hop, peer).wait_send()

    for place in range(2):
        for step, peer in enumerate(others(CH, parts)):
            small_copy(place, step, peer, peer).wait_recv()
            small_copy(place, step, peer, ch).wait_send()
        small_own(place).wait()
    own.wait()


def prologue(blocks, parts, features, reduce_w, expand_w, narrow_terms, wide_terms, canvas_ids):
    layers, mid, feat = reduce_w.shape
    pixels, wide = features.shape
    narrow = mid * parts
    f32, low = jnp.float32, jnp.bfloat16
    shape = jax.ShapeDtypeStruct
    padded = jnp.pad(canvas_ids, ((2, 2), (4, 4)), constant_values=-1)
    ids = jnp.broadcast_to(padded[:, :, None], padded.shape + (lanes,))
    anywhere = pl.BlockSpec(memory_space=pl.ANY)
    inside = pl.BlockSpec(memory_space=pltpu.VMEM)
    dma = pltpu.SemaphoreType.DMA
    return pl.pallas_call(
        functools.partial(prologue_kernel, blocks, parts),
        in_specs=[anywhere] * 5 + [inside],
        out_specs=[anywhere] * 7 + [inside] * 2,
        out_shape=[
            shape((pixels, feat), low),
            *stripe_shapes(parts, blocks, reduce_w, expand_w),
            shape((narrow, feat), low),
            shape((narrow, feat), low),
            shape((parts,) + narrow_terms.shape, f32),
            shape((parts,) + wide_terms.shape, f32),
            shape((2, pixels, lanes), jnp.int32),
            shape((pixels * blocks, lanes), jnp.int32),
        ],
        scratch_shapes=[
            dma((2, parts)),
            dma((parts,)),
            dma((2, parts)),
            dma((2, parts)),
            dma((3,)),
        ]
        + stripe_sems(parts)
        + spread_sems(blocks),
        compiler_params=comm_params(5),
        cost_estimate=pl.CostEstimate(flops=10**6, bytes_accessed=10**8, transcendentals=0),
    )(features, reduce_w, expand_w, narrow_terms, wide_terms, ids)


def greet_line(blocks):
    barrier = pltpu.get_barrier_semaphore()
    me = lax.axis_index(BLK)
    for peer in (lax.rem(me + 1, blocks), lax.rem(me + blocks - 1, blocks)):
        pl.semaphore_signal(barrier, inc=1, device_id={BLK: peer}, device_id_type=MESH)
    pl.semaphore_wait(barrier, 2)


def greet_blocks(blocks):
    announce([(BLK, peer) for peer in others(BLK, blocks)])


def edge_copies(main_ref, low_ref, high_ref, edge, send_sem, recv_sem, blocks):
    me = lax.axis_index(BLK)
    lead = (slice(None),) * (len(main_ref.shape) - 2)
    pixels = main_ref.shape[-2]
    up = remote(
        main_ref.at[lead + (pl.ds(pixels - edge, edge),)],
        low_ref,
        send_sem.at[0],
        recv_sem.at[0],
        BLK,
        lax.rem(me + 1, blocks),
    )
    down = remote(
        main_ref.at[lead + (pl.ds(0, edge),)],
        high_ref,
        send_sem.at[1],
        recv_sem.at[1],
        BLK,
        lax.rem(me + blocks - 1, blocks),
    )

    def start():
        @pl.when(me < blocks - 1)
        def _():
            up.start()

        @pl.when(me > 0)
        def _():
            down.start()

    def finish(zero=True):
        @pl.when(me > 0)
        def _():
            up.wait_recv()
            down.wait_send()

        @pl.when(me < blocks - 1)
        def _():
            down.wait_recv()
            up.wait_send()

        if zero:

            @pl.when(me == 0)
            def _():
                low_ref[...] = jnp.zeros(low_ref.shape, low_ref.dtype)

            @pl.when(me == blocks - 1)
            def _():
                high_ref[...] = jnp.zeros(high_ref.shape, high_ref.dtype)

    return start, finish


def heads_forward_kernel(blocks, fetch, jobs, main_ref, w_ref, mask_ref, *refs):
    if fetch:
        mine_r, mine_e, *refs = refs
    pre_ref, act_ref, ends_ref, *refs = refs
    if fetch:
        full_r, full_e, *refs = refs
    ext_ref, z_ref, local_sem, halo_send, halo_recv, *sems = refs
    step = pl.program_id(0)
    head_count, pixels, mid = pre_ref.shape
    cols = (ext_ref.shape[0] - pixels) // 2
    feat = ext_ref.shape[1]
    start, finish = edge_copies(
        main_ref,
        ext_ref.at[pl.ds(0, cols)],
        ext_ref.at[pl.ds(cols + pixels, cols)],
        cols,
        halo_send,
        halo_recv,
        blocks,
    )
    own = pltpu.make_async_copy(main_ref, ext_ref.at[pl.ds(cols, pixels)], local_sem.at[0])
    if fetch:
        spread, forward, last = spread_job((mine_r, mine_e), (full_r, full_e), sems, blocks)

    @pl.when(step == 0)
    def _():
        own.start()
        if fetch or jobs:
            greet_blocks(blocks)
        else:
            greet_line(blocks)
        start()
        if fetch:
            spread()
        for job in jobs:
            job[0]()
        own.wait()

    @pl.when(step == 3)
    def _():
        finish()

    row_step = jnp.where(step < 3, 1, jnp.where(step < 6, 0, 2))
    col_step = lax.rem(step, 3)
    window = ext_ref[pl.ds(pl.multiple_of(row_step * cols, cols), pixels), :]
    product = contract_last(window, w_ref[0].reshape(head_count * mid, feat))
    product = masked(product, mask_ref[0], tap_at(step))

    @pl.when(step < 3)
    def _():
        z_ref[col_step] = product

    @pl.when(step >= 3)
    def _():
        z_ref[col_step] += product

    @pl.when(step == 8)
    def _():
        for head in range(head_count):
            part = slice(head * mid, (head + 1) * mid)
            total = (
                z_ref[1, :, part]
                + pltpu.roll(z_ref[0, :, part], 1, 0)
                + pltpu.roll(z_ref[2, :, part], pixels - 1, 0)
            )
            pre_ref[head] = total
            value = (total * sigmoid(total)).astype(jnp.bfloat16)
            act_ref[head] = value
            if head in targets:
                ends_ref[targets.index(head)] = value
        if fetch:
            for array in range(2):
                forward(array)
            last()
        for job in jobs:
            job[1]()
        for job in jobs:
            job[2]()


def tap_at(step):
    return jnp.where(step < 3, step + 3, jnp.where(step < 6, step - 3, step))


def heads_forward(blocks, layer, jobs, cols, main, weights, mask, mine):
    _, head_count, _, mid, feat = weights.shape
    pixels = main.shape[0]
    f32, low = jnp.float32, jnp.bfloat16
    shape = jax.ShapeDtypeStruct
    anywhere = pl.BlockSpec(memory_space=pl.ANY)
    dma = pltpu.SemaphoreType.DMA
    return job_call(
        functools.partial(heads_forward_kernel, blocks, bool(mine)),
        jobs,
        blocks,
        grid=(9,),
        in_specs=[
            anywhere,
            pl.BlockSpec((1, head_count, 1, mid, feat), lambda t: (layer, 0, tap_at(t), 0, 0)),
            pl.BlockSpec((1, pixels, lanes), lambda t: (0, 0, 0)),
        ]
        + [anywhere] * len(mine),
        out_specs=[whole((head_count, pixels, mid))] * 2
        + [whole((2, pixels, mid))]
        + [anywhere] * len(mine),
        out_shape=[
            shape((head_count, pixels, mid), f32),
            shape((head_count, pixels, mid), low),
            shape((2, pixels, mid), low),
        ]
        + [shape((mine[0].shape[0], feat), low) for _ in mine],
        scratch_shapes=[
            pltpu.VMEM((pixels + 2 * cols, feat), low),
            pltpu.VMEM((3, pixels, head_count * mid), f32),
            dma((1,)),
            dma((2,)),
            dma((2,)),
        ]
        + (spread_sems(blocks) if mine else []),
        compiler_params=comm_params(6 + layer),
        cost_estimate=pl.CostEstimate(
            flops=18 * pixels * head_count * mid * feat,
            bytes_accessed=18 * head_count * mid * feat,
            transcendentals=0,
        ),
    )(main, weights, mask, *mine)


def fill_taps(im_ref, slot, grad, bits, pixels, cols, dilation):
    rows, mid = grad.shape
    wide = grad.astype(jnp.float32)
    shifted_by = (pltpu.roll(wide, rows - dilation, 0), wide, pltpu.roll(wide, dilation, 0))
    for tap, (row_step, col_step) in enumerate(tap_offsets):
        start = (1 - row_step) * dilation * cols
        part = shifted_by[col_step + 1][start : start + pixels]
        im_ref[slot, :, tap * mid : (tap + 1) * mid] = masked(part, bits, 9 + tap).astype(
            jnp.bfloat16
        )


def messages_kernel(
    blocks,
    layer,
    jobs,
    feat_ref,
    w_hbm,
    cot_ref,
    gain_ref,
    bias_ref,
    mask_ref,
    maps_ref,
    local_ref,
    sums_ref,
    part_ref,
    pack_ref,
    main_ref,
    low_ref,
    high_ref,
    cot_low,
    cot_high,
    w_ref,
    lhs_ref,
    z_ref,
    im_ref,
    grad_ref,
    w_sem,
    local_sem,
    halo_send,
    halo_recv,
    cot_send,
    cot_recv,
):
    parts, heads, pixels, mid = feat_ref.shape
    cols = low_ref.shape[2]
    pairs = w_ref.shape[0]
    me, ch = lax.axis_index(BLK), lax.axis_index(CH)
    low = jnp.bfloat16
    loads = [
        pltpu.make_async_copy(w_hbm.at[layer, pair], w_ref.at[pair], w_sem.at[pair])
        for pair in range(pairs)
    ]
    main_copy = pltpu.make_async_copy(feat_ref, main_ref, local_sem.at[0])
    main_copy.start()
    for pair in (0, 4, 1, 5, 3, 2):
        loads[pair].start()
    greet_blocks(blocks)
    start, finish = edge_copies(feat_ref, low_ref, high_ref, cols, halo_send, halo_recv, blocks)
    start()
    cot_start, cot_finish = edge_copies(
        cot_ref, cot_low, cot_high, cols, cot_send, cot_recv, blocks
    )
    cot_start()
    main_copy.wait()
    size = parts * mid // blocks
    for block in range(blocks):
        part, first = block * size // mid, block * size % mid
        for index, (one, two) in enumerate(groups):
            pack_ref[block, index] = jnp.concatenate(
                [main_ref[part, one][:, first : first + size], main_ref[part, two][:, first : first + size]],
                axis=1,
            )
    for source in range(heads):
        for part in range(parts):
            lhs_ref[source, cols : cols + pixels, part * mid : (part + 1) * mid] = main_ref[part, source]
    order = (0, 4, 1, 5, 3, 2)
    bits = mask_ref[0]

    def taps(pair, row_step):
        source = message_pairs[pair][0]
        product = contract_last(
            lhs_ref[source, row_step * cols : row_step * cols + pixels, :],
            w_ref[pair, 3 * row_step : 3 * row_step + 3].reshape(3 * mid, parts * mid),
        )
        for col_step in range(3):
            value = masked(
                product[:, col_step * mid : (col_step + 1) * mid], bits, row_step * 3 + col_step
            )
            if row_step == 1:
                z_ref[pair, col_step] = value
            else:
                z_ref[pair, col_step] += value

    for pair in order:
        loads[pair].wait()
        taps(pair, 1)
    finish()
    cot_finish()
    for job in jobs:
        job[0]()
    for source in range(heads):
        for part in range(parts):
            chan = slice(part * mid, (part + 1) * mid)
            lhs_ref[source, 0:cols, chan] = low_ref[part, source]
            lhs_ref[source, cols + pixels :, chan] = high_ref[part, source]
    for pair in order:
        taps(pair, 0)
        taps(pair, 2)
    values = {}
    cots = {}
    for place, target in enumerate((0, 3)):
        values[target] = main_ref[ch, target].astype(jnp.float32)
        cots[target] = cot_ref[place].astype(jnp.float32)
    for place, target in enumerate((0, 3)):
        value, cot = values[target], cots[target]
        total, slopes = value, cot
        for pair in range(pairs):
            if message_pairs[pair][1] != target:
                continue
            message = (
                z_ref[pair, 1]
                + pltpu.roll(z_ref[pair, 0], 1, 0)
                + pltpu.roll(z_ref[pair, 2], pixels - 1, 0)
            )
            gain, bias = gain_ref[layer, pair : pair + 1], bias_ref[layer, pair : pair + 1]
            gate = sigmoid(gain * value + bias)
            total = total + gate * message
            grad_ref[pair] = (cot * gate).astype(low)
            slope = cot * message * gate * (1.0 - gate)
            sums_ref[pair : pair + 1] = jnp.sum(slope * value, axis=0, keepdims=True)
            sums_ref[pairs + pair : pairs + pair + 1] = jnp.sum(slope, axis=0, keepdims=True)
            slopes = slopes + slope * gain
        maps_ref[place] = total.astype(low)
        local_ref[place] = slopes

    def product_of(pair, slot):
        source, target = message_pairs[pair]
        place = 0 if target == 0 else 1
        gain, bias = gain_ref[layer, pair : pair + 1], bias_ref[layer, pair : pair + 1]

        def border(cot, feat):
            return (
                cot[place].astype(jnp.float32)
                * sigmoid(gain * feat[ch, target].astype(jnp.float32) + bias)
            ).astype(low)

        grad = jnp.concatenate(
            [border(cot_low, low_ref), grad_ref[pair], border(cot_high, high_ref)], axis=0
        )
        fill_taps(im_ref, slot, grad, bits, pixels, cols, 1)
        return jnp.dot(
            im_ref[slot],
            w_ref[pair].reshape(9 * mid, parts * mid),
            preferred_element_type=jnp.float32,
        )

    for source, *members in source_order:
        total = product_of(members[0], 0)
        for pair in members[1:]:
            total = total + product_of(pair, 1)
        for part in range(parts):
            part_ref[part, source] = total[:, part * mid : (part + 1) * mid].astype(low)
    for job in jobs:
        job[1]()
    for job in jobs:
        job[2]()


def messages_both(blocks, layer, jobs, cols, features, weights, cotangents, gains, biases, mask):
    parts, heads, pixels, mid = features.shape
    pairs = weights.shape[1]
    narrow = parts * mid
    f32, low = jnp.float32, jnp.bfloat16
    shape = jax.ShapeDtypeStruct
    anywhere = pl.BlockSpec(memory_space=pl.ANY)
    inside = pl.BlockSpec(memory_space=pltpu.VMEM)
    dma = pltpu.SemaphoreType.DMA
    wide = 2 * narrow // blocks
    return job_call(
        functools.partial(messages_kernel, blocks, layer),
        jobs,
        blocks,
        in_specs=[anywhere, anywhere] + [inside] * 4,
        out_specs=[inside] * 5,
        out_shape=[
            shape((2, pixels, mid), low),
            shape((2, pixels, mid), f32),
            shape((2 * pairs, mid), f32),
            shape((parts, heads, pixels, mid), low),
            shape((blocks, 2, pixels, wide), low),
        ],
        scratch_shapes=[
            pltpu.VMEM((parts, heads, pixels, mid), low),
            pltpu.VMEM((parts, heads, cols, mid), low),
            pltpu.VMEM((parts, heads, cols, mid), low),
            pltpu.VMEM((2, cols, mid), low),
            pltpu.VMEM((2, cols, mid), low),
            pltpu.VMEM((pairs, 9, mid, narrow), low),
            pltpu.VMEM((heads, pixels + 2 * cols, narrow), low),
            pltpu.VMEM((pairs, 3, pixels, mid), f32),
            pltpu.VMEM((2, pixels, 9 * mid), low),
            pltpu.VMEM((pairs, pixels, mid), low),
            dma((pairs,)),
            dma((1,)),
            dma((2,)),
            dma((2,)),
            dma((2,)),
            dma((2,)),
        ],
        compiler_params=comm_params(10 + layer),
        cost_estimate=pl.CostEstimate(
            flops=36 * pixels * pairs * mid * narrow,
            bytes_accessed=18 * pairs * mid * narrow,
            transcendentals=0,
        ),
    )(features, weights, cotangents, gains, biases, mask)


def heads_backward_kernel(
    blocks,
    jobs,
    main_ref,
    w_ref,
    mask_ref,
    out_ref,
    low_ref,
    high_ref,
    im_ref,
    halo_send,
    halo_recv,
):
    step = pl.program_id(0)
    head_count, pixels, mid = main_ref.shape
    cols = low_ref.shape[1]

    @pl.when(step == 0)
    def _():
        start, finish = edge_copies(main_ref, low_ref, high_ref, cols, halo_send, halo_recv, blocks)
        if jobs:
            greet_blocks(blocks)
        else:
            greet_line(blocks)
        start()
        finish()
        for job in jobs:
            job[0]()
        for head in range(head_count):
            grad = jnp.concatenate([low_ref[head], main_ref[head], high_ref[head]], axis=0)
            fill_taps(im_ref, head, grad, mask_ref[0], pixels, cols, 1)

    total = None
    for head in range(head_count):
        product = jnp.dot(
            im_ref[head],
            w_ref[0, head].reshape(9 * mid, w_ref.shape[4]),
            preferred_element_type=jnp.float32,
        )
        total = product if total is None else total + product
    out_ref[0] = total.astype(jnp.bfloat16)

    if jobs:

        @pl.when(step == pl.num_programs(0) - 1)
        def _():
            for job in jobs:
                job[1]()
            for job in jobs:
                job[2]()


def heads_backward(blocks, layer, jobs, cols, main, weights, mask, parts):
    _, head_count, taps, mid, feat = weights.shape
    pixels = main.shape[1]
    width = feat // parts
    dma = pltpu.SemaphoreType.DMA
    return job_call(
        functools.partial(heads_backward_kernel, blocks),
        jobs,
        blocks,
        grid=(parts,),
        in_specs=[
            whole(main.shape),
            pl.BlockSpec((1, head_count, taps, mid, width), lambda j: (layer, 0, 0, 0, j)),
            pl.BlockSpec((1, pixels, lanes), lambda j: (0, 0, 0)),
        ],
        out_specs=[pl.BlockSpec((1, pixels, width), lambda j: (j, 0, 0))],
        out_shape=[jax.ShapeDtypeStruct((parts, pixels, width), jnp.bfloat16)],
        scratch_shapes=[
            pltpu.VMEM((head_count, cols, mid), jnp.bfloat16),
            pltpu.VMEM((head_count, cols, mid), jnp.bfloat16),
            pltpu.VMEM((head_count, pixels, taps * mid), jnp.bfloat16),
            dma((2,)),
            dma((2,)),
        ],
        compiler_params=comm_params(20 + layer),
        cost_estimate=pl.CostEstimate(
            flops=18 * pixels * head_count * mid * feat,
            bytes_accessed=18 * head_count * mid * feat,
            transcendentals=0,
        ),
    )(main, weights, mask)


class WeightChunks:
    def __init__(self, blocks, layer, sources, gates, buffers, accs, lhs, sems):
        self.blocks, self.layer = blocks, layer
        (self.mv, self.cot, self.ends, self.hv, self.hg, self.bits) = sources
        self.gain, self.bias = gates
        (self.mv_buf, self.cot_buf, self.ends_buf, self.hv_buf, self.hg_buf, self.bits_buf) = buffers
        self.accs, self.lhs, self.sems = accs, lhs, sems
        self.done = 0
        self.pixels = self.hv.shape[1]

    def copies(self, heads, index):
        pixels, last = self.pixels, self.blocks - 1
        before, after = jnp.maximum(index - 1, 0), jnp.minimum(index + 1, last)
        slot = lax.rem(index, 2)
        values, buffer = (self.hv, self.hv_buf) if heads else (self.mv, self.mv_buf)
        lead = () if heads else (slice(None),)
        pairs = [
            (
                values.at[(before,) + lead + (pl.ds(pixels - lanes, lanes),)],
                buffer.at[(slot,) + lead + (pl.ds(0, lanes),)],
            ),
            (values.at[index], buffer.at[(slot,) + lead + (pl.ds(lanes, pixels),)]),
            (
                values.at[(after,) + lead + (pl.ds(0, lanes),)],
                buffer.at[(slot,) + lead + (pl.ds(lanes + pixels, lanes),)],
            ),
            (
                self.bits.at[pl.ds(pl.multiple_of(index * pixels, pixels), pixels)],
                self.bits_buf.at[slot],
            ),
        ]
        if heads:
            pairs.append((self.hg.at[index], self.hg_buf.at[slot]))
        else:
            pairs.append((self.cot.at[index], self.cot_buf.at[slot]))
            pairs.append((self.ends.at[index], self.ends_buf.at[slot]))
        return [
            pltpu.make_async_copy(source, target, self.sems.at[slot, place])
            for place, (source, target) in enumerate(pairs)
        ]

    def fetch(self, heads, index):
        for copy in self.copies(heads, index):
            copy.start()

    def begin(self):
        for acc in self.accs:
            acc[...] = jnp.zeros(acc.shape, acc.dtype)
        self.fetch(False, 0)

    def add(self, heads, index):
        slot = lax.rem(index, 2)
        pixels = self.pixels
        for copy in self.copies(heads, index):
            copy.wait()

        @pl.when(index + 1 < self.blocks)
        def _():
            self.fetch(heads, index + 1)

        if not heads:

            @pl.when(index + 1 == self.blocks)
            def _():
                self.fetch(True, 0)

        bits = self.bits_buf[slot]
        for place, members in enumerate((tuple(range(4)),) if heads else group_pairs):
            window = (self.hv_buf[slot] if heads else self.mv_buf[slot, place]).astype(jnp.float32)
            size, chans = window.shape
            shifted_by = (pltpu.roll(window, 1, 0), window, pltpu.roll(window, size - 1, 0))
            for tap, (row_step, col_step) in enumerate(tap_offsets):
                top = (1 + row_step) * lanes
                part = shifted_by[col_step + 1][top : top + pixels]
                self.lhs[:, tap * chans : (tap + 1) * chans] = masked(part, bits, tap).astype(
                    jnp.bfloat16
                )
            if heads:
                grads = [self.hg_buf[slot, member] for member in members]
            else:
                grads = [self.message_grad(slot, pair) for pair in members]
            acc = self.accs[2] if heads else self.accs[place]
            acc[...] += lax.dot_general(
                self.lhs[:, : 9 * chans],
                jnp.concatenate(grads, axis=1),
                (((0,), (0,)), ((), ())),
                preferred_element_type=jnp.float32,
            )

    def message_grad(self, slot, pair):
        place = targets.index(message_pairs[pair][1])
        gain = self.gain[self.layer, pair : pair + 1]
        bias = self.bias[self.layer, pair : pair + 1]
        gate = sigmoid(gain * self.ends_buf[slot, place].astype(jnp.float32) + bias)
        return (self.cot_buf[slot, place].astype(jnp.float32) * gate).astype(jnp.bfloat16)

    def run(self, count):
        while count:
            heads = self.done >= self.blocks
            start = self.done % self.blocks
            size = min(count, self.blocks - start)

            def step(index, state):
                self.add(heads, index)
                return state

            lax.fori_loop(start, start + size, step, 0)
            self.done += size
            count -= size


def exchange_kernel(blocks, jobs, done_ref):
    greet_blocks(blocks)
    for job in jobs:
        job[0]()
    for job in jobs:
        job[1]()
    for job in jobs:
        job[2]()
    done_ref[...] = jnp.zeros(done_ref.shape, done_ref.dtype)


def exchange(blocks, jobs):
    _, moved = job_call(
        functools.partial(exchange_kernel, blocks),
        jobs,
        blocks,
        in_specs=[],
        out_specs=[pl.BlockSpec(memory_space=pltpu.VMEM)],
        out_shape=[jax.ShapeDtypeStruct((8, lanes), jnp.float32)],
        scratch_shapes=[],
        compiler_params=comm_params(30),
        cost_estimate=pl.CostEstimate(flops=10**6, bytes_accessed=10**8, transcendentals=0),
    )()
    return moved


def heads_store(out_ref, acc_ref):
    head_count, taps, chans, mid = out_ref.shape
    for head in range(head_count):
        for tap in range(taps):
            out_ref[head, tap] = acc_ref[
                tap * chans : (tap + 1) * chans, head * mid : (head + 1) * mid
            ]


def messages_store(out_ref, acc_refs):
    _, taps, size, mid = out_ref.shape
    for index, members in enumerate(group_pairs):
        for place, pair in enumerate(members):
            side = groups[index].index(message_pairs[pair][0])
            for tap in range(taps):
                start = (2 * tap + side) * size
                out_ref[pair, tap] = acc_refs[index][
                    start : start + size, place * mid : (place + 1) * mid
                ]


def greet(blocks, parts):
    barrier = pltpu.get_barrier_semaphore()
    blk, ch = lax.axis_index(BLK), lax.axis_index(CH)
    for step in range(1, blocks):
        pl.semaphore_signal(
            barrier, inc=1, device_id={BLK: lax.rem(blk + step, blocks)}, device_id_type=MESH
        )
    for step in range(1, parts):
        pl.semaphore_signal(
            barrier, inc=1, device_id={CH: lax.rem(ch + step, parts)}, device_id_type=MESH
        )
    pl.semaphore_wait(barrier, blocks + parts - 2)


def send_slots(source_of, target_ref, send_sem, recv_sem, axis, count):
    me = lax.axis_index(axis)
    copies = []
    for step in range(1, count):
        peer = lax.rem(me + step, count)
        copy = pltpu.make_async_remote_copy(
            src_ref=source_of(peer),
            dst_ref=target_ref.at[me],
            send_sem=send_sem.at[step],
            recv_sem=recv_sem.at[me],
            device_id={axis: peer},
            device_id_type=MESH,
        )
        copy.start()
        copies.append(copy)

    def finish():
        for step in range(1, count):
            peer = lax.rem(me + step, count)
            pltpu.make_async_remote_copy(
                src_ref=target_ref.at[peer],
                dst_ref=target_ref.at[peer],
                send_sem=send_sem.at[step],
                recv_sem=recv_sem.at[peer],
                device_id={axis: peer},
                device_id_type=MESH,
            ).wait_recv()
        for copy in copies:
            copy.wait_send()

    return finish


def block_totals(first, second, stat_ref, send_sem, recv_sem, blocks, meanwhile=None):
    me = lax.axis_index(BLK)
    stat_ref[me, 0:1] = first
    stat_ref[me, 1:2] = second
    finish = send_slots(lambda _: stat_ref.at[me], stat_ref, send_sem, recv_sem, BLK, blocks)
    if meanwhile is not None:
        meanwhile()
    finish()
    total = stat_ref[0]
    for block in range(1, blocks):
        total = total + stat_ref[block]
    return total[0:1], total[1:2]


def fold(values):
    rows, width = values.shape
    return values.reshape(rows // 8, 8, width).sum(axis=0)


def row_loop(rows, block, body, carry):
    def step(index, state):
        return body(pl.ds(pl.multiple_of(index * block, block), block), state)

    return lax.fori_loop(0, rows // block, step, carry)


def moments(ref, block):
    rows, width = ref.shape

    def body(part, state):
        values = ref[part, :]
        return state[0] + fold(values), state[1] + fold(values * values)

    zero = jnp.zeros((8, width), jnp.float32)
    total, square = row_loop(rows, block, body, (zero, zero))
    return total.sum(axis=0, keepdims=True), square.sum(axis=0, keepdims=True)


def halo_copies(ref, edge, pixels, send_sem, recv_sem, blocks):
    me = lax.axis_index(BLK)

    def copy(source, target, side, peer):
        return pltpu.make_async_remote_copy(
            src_ref=ref.at[pl.ds(source, edge)],
            dst_ref=ref.at[pl.ds(target, edge)],
            send_sem=send_sem.at[side],
            recv_sem=recv_sem.at[side],
            device_id={BLK: peer},
            device_id_type=MESH,
        )

    up = copy(pixels, 0, 0, lax.rem(me + 1, blocks))
    down = copy(edge, edge + pixels, 1, lax.rem(me + blocks - 1, blocks))

    @pl.when(me < blocks - 1)
    def _():
        up.start()

    @pl.when(me > 0)
    def _():
        down.start()

    @pl.when(me == 0)
    def _():
        ref[0:edge, :] = jnp.zeros((edge, ref.shape[1]), ref.dtype)

    @pl.when(me == blocks - 1)
    def _():
        ref[edge + pixels :, :] = jnp.zeros((edge, ref.shape[1]), ref.dtype)

    def finish():
        @pl.when(me > 0)
        def _():
            up.wait_recv()
            down.wait_send()

        @pl.when(me < blocks - 1)
        def _():
            down.wait_recv()
            up.wait_send()

    return finish


def trunk_forward_kernel(
    blocks,
    parts,
    layer,
    fetch,
    jobs,
    cur_ref,
    wr_ref,
    wd_ref,
    we_ref,
    mask_ref,
    gain1_ref,
    bias1_ref,
    gain2_ref,
    bias2_ref,
    gain3_ref,
    bias3_ref,
    *refs,
):
    if fetch:
        raw_r, raw_e, *refs = refs
    out_ref, ext_out_ref, full_ref, normed1_ref, inverse1_ref, normed2_ref, inverse2_ref = refs[:7]
    normed3_ref, inverse3_ref = refs[7:9]
    refs = refs[9:]
    if fetch:
        full_r, full_e, *refs = refs
    pre1_ref, pre3_ref, ext_ref, z_ref, gath_ref, stat1_ref, stat2_ref, stat3_ref = refs[:8]
    term1_ref, term3_ref, stat_send, stat_recv, halo_send, halo_recv, part_send, part_recv = refs[8:16]
    pixels, feat = cur_ref.shape
    mid = normed1_ref.shape[1]
    wide = normed3_ref.shape[1]
    edge = (ext_ref.shape[0] - pixels) // 2
    ch = lax.axis_index(CH)
    pixel_count = float(pixels * blocks)
    greet(blocks, parts)
    if fetch:
        start, finish = stripe_job(
            raw_r, raw_e, fetch, (full_r, full_e), refs[16:], blocks, parts
        )

    def terms(total, square):
        mean_value = total / pixel_count
        variance = square / pixel_count - mean_value * mean_value
        return mean_value, lax.rsqrt(variance + epsilon)

    pre1_ref[...] = contract_last(cur_ref[...], wr_ref[...])
    total, square = moments(pre1_ref, 64)
    mean_value, inverse = terms(
        *block_totals(total, square, stat1_ref, stat_send.at[0], stat_recv.at[0], blocks)
    )
    term1_ref[0:1] = mean_value
    term1_ref[1:2] = inverse

    def first(part, state):
        value = gain1_ref[...] * ((pre1_ref[part, :] - mean_value) * inverse) + bias1_ref[...]
        pre1_ref[part, :] = value * sigmoid(value)
        return state

    own_mid = pl.ds(pl.multiple_of(ch * mid, mid), mid)
    normed1_ref[...] = (pre1_ref[:, own_mid] - term1_ref[0:1, own_mid]) * term1_ref[1:2, own_mid]
    inverse1_ref[...] = term1_ref[1:2, own_mid]
    row_loop(pixels, 64, first, 0)
    ext_ref[edge : edge + pixels, :] = pre1_ref[...].astype(jnp.bfloat16)
    wait_halo = halo_copies(ext_ref, edge, pixels, halo_send, halo_recv, blocks)

    half = edge // 2
    for row_step in (1, 0, 2):
        if row_step == 0:
            wait_halo()
        top = 2 * row_step * half
        product = contract_last(
            ext_ref[top : top + pixels, :],
            wd_ref[layer, 3 * row_step : 3 * row_step + 3].reshape(3 * mid, parts * mid),
        )
        for col_step in range(3):
            part = masked(
                product[:, col_step * mid : (col_step + 1) * mid],
                mask_ref[1],
                row_step * 3 + col_step,
            )
            if row_step == 1:
                z_ref[col_step] = part
            else:
                z_ref[col_step] += part
    second_pre = (
        z_ref[1] + pltpu.roll(z_ref[0], 2, 0) + pltpu.roll(z_ref[2], pixels - 2, 0)
    )
    mean_value, inverse = terms(
        *block_totals(
            jnp.sum(second_pre, axis=0, keepdims=True),
            jnp.sum(second_pre * second_pre, axis=0, keepdims=True),
            stat2_ref,
            stat_send.at[1],
            stat_recv.at[1],
            blocks,
        )
    )
    normed = (second_pre - mean_value) * inverse
    normed2_ref[...] = normed
    inverse2_ref[...] = inverse
    value = gain2_ref[...] * normed + bias2_ref[...]
    gath_ref[ch] = (value * sigmoid(value)).astype(jnp.bfloat16)
    wait_parts = send_slots(
        lambda _: gath_ref.at[ch], gath_ref, part_send, part_recv, CH, parts
    )
    for job in jobs:
        job[0]()
    ext_out_ref[...] = ext_ref[...]
    wait_parts()
    if fetch:
        start()
    for part in range(parts):
        full_ref[:, part * mid : (part + 1) * mid] = gath_ref[part]
    for part in range(parts):
        lane = slice(part * wide, (part + 1) * wide)
        pre3_ref[:, lane] = jnp.dot(
            full_ref[...], we_ref[:, lane], preferred_element_type=jnp.float32
        )
    total, square = moments(pre3_ref, 16)
    mean_value, inverse = terms(
        *block_totals(total, square, stat3_ref, stat_send.at[2], stat_recv.at[2], blocks)
    )
    term3_ref[0:1] = mean_value
    term3_ref[1:2] = inverse

    def last(part, state):
        value = (
            gain3_ref[...] * ((pre3_ref[part, :] - mean_value) * inverse)
            + bias3_ref[...]
            + cur_ref[part, :].astype(jnp.float32)
        )
        out_ref[part, :] = (value * sigmoid(value)).astype(jnp.bfloat16)
        return state

    row_loop(pixels, 16, last, 0)
    own_wide = pl.ds(pl.multiple_of(ch * wide, wide), wide)
    for job in jobs:
        job[1]()
    normed3_ref[...] = (pre3_ref[:, own_wide] - term3_ref[0:1, own_wide]) * term3_ref[1:2, own_wide]
    inverse3_ref[...] = term3_ref[1:2, own_wide]
    if fetch:
        finish()
    for job in jobs:
        job[2]()


def trunk_forward(
    blocks, parts, cols, layer, jobs, current, reduce_w, dilated_w, expand_w, mask, norms, raw
):
    pixels, feat = current.shape
    narrow = reduce_w.shape[0]
    mid, wide = narrow // parts, feat // parts
    edge = 2 * cols
    f32, low = jnp.float32, jnp.bfloat16
    shape = jax.ShapeDtypeStruct
    rows = edge * 2 + pixels
    inside = pl.BlockSpec(memory_space=pltpu.VMEM)
    anywhere = pl.BlockSpec(memory_space=pl.ANY)
    fetch = layer + 1 if raw else 0
    return job_call(
        functools.partial(trunk_forward_kernel, blocks, parts, layer, fetch),
        jobs,
        blocks,
        in_specs=[inside] * 11 + [anywhere] * len(raw),
        out_specs=[inside] * 9 + [anywhere] * len(raw),
        out_shape=[
            shape((pixels, feat), low),
            shape((rows, narrow), low),
            shape((pixels, narrow), low),
            shape((pixels, mid), f32),
            shape((1, mid), f32),
            shape((pixels, mid), f32),
            shape((1, mid), f32),
            shape((pixels, wide), f32),
            shape((1, wide), f32),
        ]
        + (stripe_shapes(parts, blocks, *raw) if raw else []),
        scratch_shapes=[
            pltpu.VMEM((pixels, narrow), f32),
            pltpu.VMEM((pixels, feat), f32),
            pltpu.VMEM((rows, narrow), low),
            pltpu.VMEM((3, pixels, mid), f32),
            pltpu.VMEM((parts, pixels, mid), low),
            pltpu.VMEM((blocks, 2, narrow), f32),
            pltpu.VMEM((blocks, 2, mid), f32),
            pltpu.VMEM((blocks, 2, feat), f32),
            pltpu.VMEM((2, narrow), f32),
            pltpu.VMEM((2, feat), f32),
            pltpu.SemaphoreType.DMA((3, blocks)),
            pltpu.SemaphoreType.DMA((3, blocks)),
            pltpu.SemaphoreType.DMA((2,)),
            pltpu.SemaphoreType.DMA((2,)),
            pltpu.SemaphoreType.DMA((parts,)),
            pltpu.SemaphoreType.DMA((parts,)),
        ]
        + (stripe_sems(parts) if raw else []),
        compiler_params=comm_params(50 + layer),
        cost_estimate=pl.CostEstimate(
            flops=2 * pixels * (2 * narrow * feat + 9 * mid * narrow),
            bytes_accessed=150 * 2**20,
            transcendentals=0,
        ),
    )(current, reduce_w, dilated_w, expand_w, mask, *norms, *raw)


def slope_of(values):
    gate = sigmoid(values)
    return gate * (1.0 + values * (1.0 - gate))


def sum_slots(ref, count):
    total = ref[0].astype(jnp.float32)
    for slot in range(1, count):
        total = total + ref[slot].astype(jnp.float32)
    return total


plan = (2, 4, 2, 4, 1, 3)


def trunk_backward_kernel(
    blocks,
    parts,
    layer,
    *refs,
):
    up_ref, heads_ref, cur_ref, normed3_ref, inverse3_ref = refs[:5]
    refs = refs[5:]
    gain3_ref, bias3_ref, we_ref, full_ref, normed2_ref = refs[:5]
    refs = refs[5:]
    inverse2_ref, gain2_ref, bias2_ref, wd_ref, mask_ref = refs[:5]
    refs = refs[5:]
    ext_ref, normed1_ref, inverse1_ref, gain1_ref, bias1_ref = refs[:5]
    refs = refs[5:]
    wr_ref, gate_ref = refs[:2]
    refs = refs[2:]
    sources, gates, refs = refs[:6], refs[6:8], refs[8:]
    out_ref, expand_ref, dilated_ref, reduce_ref, wide_ref = refs[:5]
    refs = refs[5:]
    second_ref, first_ref, gate_out = refs[:3]
    refs = refs[3:]
    messages_out, heads_out, *refs = refs
    third_ref, grad_ref, im_ref, send2_ref, recv2_ref = refs[:5]
    refs = refs[5:]
    send1_ref, recv1_ref, gath_ref, low_ref, ex_send_ref = refs[:5]
    refs = refs[5:]
    ex_recv_ref, di_send_ref, di_recv_ref, re_send_ref, re_recv_ref = refs[:5]
    refs = refs[5:]
    stat3_ref, stat2_ref, stat1_ref, gates_ref, stat_send = refs[:5]
    refs = refs[5:]
    stat_recv, halo_send, halo_recv, part_send, part_recv = refs[:5]
    refs = refs[5:]
    sum_send, sum_recv = refs[:2]
    refs = refs[2:]
    buffers, accs, (lhs_ref, chunk_sem) = refs[:6], refs[6:9], refs[9:]
    chunks = WeightChunks(blocks, layer, sources, gates, buffers, accs, lhs_ref, chunk_sem)
    pixels, wide = up_ref.shape
    mid = normed1_ref.shape[1]
    narrow = mid * parts
    feat = cur_ref.shape[1]
    edge = (grad_ref.shape[0] - pixels) // 2
    half = edge // 2
    blk = lax.axis_index(BLK)
    ch = lax.axis_index(CH)
    pixel_count = float(pixels * blocks)
    low = jnp.bfloat16
    greet(blocks, parts)
    chunks.begin()
    own_wide = pl.ds(pl.multiple_of(ch * wide, wide), wide)
    gates_ref[blk] = gate_ref[...]
    wait_gates = send_slots(
        lambda _: gates_ref.at[blk], gates_ref, stat_send.at[3], stat_recv.at[3], BLK, blocks
    )

    def start(part, state):
        normed = normed3_ref[part, :]
        summed = (
            gain3_ref[...] * normed + bias3_ref[...] + cur_ref[part, own_wide].astype(jnp.float32)
        )
        value = (up_ref[part, :] + heads_ref[part, :].astype(jnp.float32)) * slope_of(summed)
        out_ref[part, :] = value
        return state[0] + fold(value), state[1] + fold(value * normed)

    zero = jnp.zeros((8, wide), jnp.float32)
    bias_sum, gain_sum = row_loop(pixels, 32, start, (zero, zero))
    bias_grad, gain_grad = block_totals(
        bias_sum.sum(axis=0, keepdims=True),
        gain_sum.sum(axis=0, keepdims=True),
        stat3_ref,
        stat_send.at[0],
        stat_recv.at[0],
        blocks,
        lambda: chunks.run(plan[0]),
    )
    wide_ref[0:1] = gain_grad
    wide_ref[1:2] = bias_grad
    scale = gain3_ref[...] * inverse3_ref[...]
    bias_part = bias_grad / pixel_count
    gain_part = gain_grad / pixel_count

    def third(part, state):
        third_ref[part, :] = (
            scale * (out_ref[part, :] - bias_part - normed3_ref[part, :] * gain_part)
        ).astype(low)
        return state

    row_loop(pixels, 32, third, 0)
    product = contract_last(third_ref[...], we_ref[...])
    for part in range(parts):
        send2_ref[part] = product[:, part * mid : (part + 1) * mid].astype(low)
    recv2_ref[ch] = send2_ref[ch]
    wait_parts = send_slots(
        lambda peer: send2_ref.at[peer], recv2_ref, part_send.at[0], part_recv.at[0], CH, parts
    )
    size = narrow // blocks
    product = lax.dot_general(
        full_ref[...], third_ref[...], (((0,), (0,)), ((), ())), preferred_element_type=jnp.float32
    )
    for block in range(blocks):
        ex_send_ref[block] = product[block * size : (block + 1) * size].astype(low)
    ex_recv_ref[blk] = ex_send_ref[blk]
    wait_expand = send_slots(
        lambda peer: ex_send_ref.at[peer], ex_recv_ref, sum_send.at[0], sum_recv.at[0], BLK, blocks
    )
    chunks.run(plan[1])
    wait_parts()

    def narrow_norm(recv_ref, normed_ref, inverse_ref, gain_ref, bias_ref, stat_ref, phase, sums_ref):
        normed = normed_ref[...]
        value = sum_slots(recv_ref, parts) * slope_of(gain_ref[...] * normed + bias_ref[...])
        bias_grad, gain_grad = block_totals(
            jnp.sum(value, axis=0, keepdims=True),
            jnp.sum(value * normed, axis=0, keepdims=True),
            stat_ref,
            stat_send.at[phase],
            stat_recv.at[phase],
            blocks,
            lambda: chunks.run(plan[2 * phase]),
        )
        sums_ref[0:1] = gain_grad
        sums_ref[1:2] = bias_grad
        return (
            gain_ref[...]
            * inverse_ref[...]
            * (value - bias_grad / pixel_count - normed * (gain_grad / pixel_count))
        )

    grad = narrow_norm(
        recv2_ref, normed2_ref, inverse2_ref, gain2_ref, bias2_ref, stat2_ref, 1, second_ref
    )
    grad_ref[edge : edge + pixels, :] = grad.astype(low)
    wait_halo = halo_copies(grad_ref, edge, pixels, halo_send, halo_recv, blocks)
    own = grad_ref[edge : edge + pixels, :].astype(jnp.float32)
    turned = (pltpu.roll(own, pixels - 2, 0), own, pltpu.roll(own, 2, 0))
    for row_step in range(3):
        side = jnp.concatenate(
            [
                masked(turned[col_step], mask_ref[1], row_step * 3 + col_step).astype(low)
                for col_step in range(3)
            ],
            axis=1,
        )
        top = 2 * row_step * half
        product = lax.dot_general(
            ext_ref[top : top + pixels, :],
            side,
            (((0,), (0,)), ((), ())),
            preferred_element_type=jnp.float32,
        )
        for block in range(blocks):
            for col_step in range(3):
                di_send_ref[block, row_step * 3 + col_step] = product[
                    block * size : (block + 1) * size, col_step * mid : (col_step + 1) * mid
                ].astype(low)
    di_recv_ref[blk] = di_send_ref[blk]
    wait_halo()
    fill_taps(im_ref, 0, grad_ref[...], mask_ref[1], pixels, half, 2)
    product = jnp.dot(
        im_ref[0], wd_ref[layer].reshape(9 * mid, narrow), preferred_element_type=jnp.float32
    )
    for part in range(parts):
        send1_ref[part] = product[:, part * mid : (part + 1) * mid].astype(low)
    recv1_ref[ch] = send1_ref[ch]
    wait_parts = send_slots(
        lambda peer: send1_ref.at[peer], recv1_ref, part_send.at[1], part_recv.at[1], CH, parts
    )
    wait_dilated = send_slots(
        lambda peer: di_send_ref.at[peer], di_recv_ref, sum_send.at[1], sum_recv.at[1], BLK, blocks
    )
    chunks.run(plan[3])
    wait_parts()
    grad = narrow_norm(
        recv1_ref, normed1_ref, inverse1_ref, gain1_ref, bias1_ref, stat1_ref, 2, first_ref
    )
    gath_ref[ch] = grad.astype(low)
    wait_parts = send_slots(
        lambda _: gath_ref.at[ch], gath_ref, part_send.at[2], part_recv.at[2], CH, parts
    )
    product = lax.dot_general(
        cur_ref[...], gath_ref[ch], (((0,), (0,)), ((), ())), preferred_element_type=jnp.float32
    )
    size = feat // blocks
    for block in range(blocks):
        re_send_ref[block] = product[block * size : (block + 1) * size].astype(low)
    re_recv_ref[blk] = re_send_ref[blk]
    wait_reduce = send_slots(
        lambda peer: re_send_ref.at[peer], re_recv_ref, sum_send.at[2], sum_recv.at[2], BLK, blocks
    )
    chunks.run(plan[5])
    wait_parts()
    for part in range(parts):
        low_ref[:, part * mid : (part + 1) * mid] = gath_ref[part]
    out_ref[...] += jnp.dot(low_ref[...], wr_ref[:, own_wide], preferred_element_type=jnp.float32)
    chunks.run(2 * blocks - chunks.done)
    messages_store(messages_out, accs[:2])
    heads_store(heads_out, accs[2])
    wait_gates()
    gate_out[...] = sum_slots(gates_ref, blocks)
    wait_expand()
    expand_ref[...] = sum_slots(ex_recv_ref, blocks)
    wait_dilated()
    dilated_ref[...] = sum_slots(di_recv_ref, blocks)
    wait_reduce()
    reduce_ref[...] = sum_slots(re_recv_ref, blocks)


def trunk_backward(blocks, parts, layer, operands, sources, gates):
    pixels, wide = operands[0].shape
    feat = wide * parts
    mid = operands[9].shape[1]
    narrow = mid * parts
    rows = operands[15].shape[0]
    f32, low = jnp.float32, jnp.bfloat16
    shape = jax.ShapeDtypeStruct
    small, large = narrow // blocks, feat // blocks
    inside = pl.BlockSpec(memory_space=pltpu.VMEM)
    anywhere = pl.BlockSpec(memory_space=pl.ANY)
    rows_two = pixels + 2 * lanes
    return pl.pallas_call(
        functools.partial(trunk_backward_kernel, blocks, parts, layer),
        in_specs=[inside] * len(operands) + [anywhere] * len(sources) + [inside] * len(gates),
        out_shape=[
            shape((pixels, wide), f32),
            shape((small, wide), f32),
            shape((9, small, mid), f32),
            shape((large, mid), f32),
            shape((2, wide), f32),
            shape((2, mid), f32),
            shape((2, mid), f32),
            shape(operands[-1].shape, f32),
            shape((6, 9, small, mid), f32),
            shape((4, 9, large, mid), f32),
        ],
        scratch_shapes=[
            pltpu.VMEM((pixels, wide), low),
            pltpu.VMEM((rows, mid), low),
            pltpu.VMEM((1, pixels, 9 * mid), low),
            pltpu.VMEM((parts, pixels, mid), low),
            pltpu.VMEM((parts, pixels, mid), low),
            pltpu.VMEM((parts, pixels, mid), low),
            pltpu.VMEM((parts, pixels, mid), low),
            pltpu.VMEM((parts, pixels, mid), low),
            pltpu.VMEM((pixels, narrow), low),
            pltpu.VMEM((blocks, small, wide), low),
            pltpu.VMEM((blocks, small, wide), low),
            pltpu.VMEM((blocks, 9, small, mid), low),
            pltpu.VMEM((blocks, 9, small, mid), low),
            pltpu.VMEM((blocks, large, mid), low),
            pltpu.VMEM((blocks, large, mid), low),
            pltpu.VMEM((blocks, 2, wide), f32),
            pltpu.VMEM((blocks, 2, mid), f32),
            pltpu.VMEM((blocks, 2, mid), f32),
            pltpu.VMEM((blocks,) + operands[-1].shape, f32),
            pltpu.SemaphoreType.DMA((4, blocks)),
            pltpu.SemaphoreType.DMA((4, blocks)),
            pltpu.SemaphoreType.DMA((2,)),
            pltpu.SemaphoreType.DMA((2,)),
            pltpu.SemaphoreType.DMA((3, parts)),
            pltpu.SemaphoreType.DMA((3, parts)),
            pltpu.SemaphoreType.DMA((3, blocks)),
            pltpu.SemaphoreType.DMA((3, blocks)),
            pltpu.VMEM((2, 2, rows_two, 2 * small), low),
            pltpu.VMEM((2, 2, pixels, mid), low),
            pltpu.VMEM((2, 2, pixels, mid), low),
            pltpu.VMEM((2, rows_two, large), low),
            pltpu.VMEM((2, 4, pixels, mid), low),
            pltpu.VMEM((2, pixels, lanes), jnp.int32),
            pltpu.VMEM((18 * small, len(group_pairs[0]) * mid), f32),
            pltpu.VMEM((18 * small, len(group_pairs[1]) * mid), f32),
            pltpu.VMEM((9 * large, 4 * mid), f32),
            pltpu.VMEM((pixels, 9 * max(large, 2 * small)), low),
            pltpu.SemaphoreType.DMA((2, 6)),
        ],
        compiler_params=comm_params(60 + layer),
        cost_estimate=pl.CostEstimate(
            flops=4 * pixels * (2 * narrow * wide + 9 * mid * narrow) + 2 * 10**10,
            bytes_accessed=200 * 2**20,
            transcendentals=0,
        ),
    )(*operands, *sources, *gates)


def gather_parts(values):
    return lax.all_gather(values, CH, axis=0, tiled=False)


def reduce_parts(values):
    return lax.psum_scatter(values, CH, scatter_dimension=0, tiled=False)


def own_slice(values, size, axis):
    return lax.dynamic_slice_in_dim(values, lax.axis_index(CH) * size, size, axis)


def shards(
    features_in,
    w_reduce,
    w_dilated,
    w_expand,
    w_heads,
    w_messages,
    norm_gain,
    norm_bias,
    wide_gain,
    wide_bias,
    gate_gain,
    gate_bias,
    canvas_ids,
    output_cotangent,
    task_cotangents,
):
    rows, cols, wide = features_in.shape
    pixels = rows * cols
    blocks = lax.axis_size(BLK)
    parts = lax.axis_size(CH)
    layers = w_reduce.shape[0]
    mid = w_reduce.shape[1]
    feat = wide * parts
    narrow = mid * parts
    low = jnp.bfloat16
    dilated_t = w_dilated.transpose(0, 2, 1, 3)
    heads_t = w_heads.transpose(0, 1, 3, 2, 4)
    messages_t = w_messages.transpose(0, 1, 3, 2, 4)
    current, *rest = prologue(
        blocks,
        parts,
        features_in.reshape(pixels, wide),
        w_reduce,
        w_expand,
        jnp.concatenate([norm_gain[:, 0], norm_bias[:, 0]], axis=0),
        jnp.concatenate([wide_gain, wide_bias], axis=0),
        canvas_ids,
    )
    reduce_full, expand_full = [rest[2]], [rest[3]]
    narrow_all, wide_all, bits, all_bits = rest[4:]
    cotangents = task_cotangents.reshape(layers, 2, pixels, mid)
    narrow_all = narrow_all.transpose(1, 0, 2).reshape(2, layers, narrow)
    wide_all = wide_all.transpose(1, 0, 2).reshape(2, layers, feat)

    kept = []
    for layer in range(layers):
        keep = types.SimpleNamespace(input=current)
        results, (keep.cotangents,) = trunk_forward(
            blocks,
            parts,
            cols,
            layer,
            [(gather_kind, cotangents[layer])],
            current,
            reduce_full[layer],
            dilated_t,
            expand_full[layer],
            bits,
            (
                narrow_all[0, layer][None],
                narrow_all[1, layer][None],
                norm_gain[layer, 1][None],
                norm_bias[layer, 1][None],
                wide_all[0, layer][None],
                wide_all[1, layer][None],
            ),
            (w_reduce, w_expand) if layer + 1 < layers else (),
        )
        (
            current,
            keep.first_ext,
            keep.second_full,
            keep.normed1,
            keep.inverse1,
            keep.normed2,
            keep.inverse2,
            keep.normed3,
            keep.inverse3,
            *mine,
        ) = results
        if layer:
            current, kept[-1].features = lax.optimization_barrier((current, kept[-1].features))
        keep.output = current
        (keep.heads_pre, features, keep.ends, *fetched), moved = heads_forward(
            blocks,
            layer,
            [(swap_kind, kept[0].output)] if layer else [],
            cols,
            current,
            heads_t,
            bits,
            mine,
        )
        if layer:
            kept[0].values = moved[0]
        if fetched:
            reduce_full.append(fetched[0])
            expand_full.append(fetched[1])
        current, features = lax.optimization_barrier((current, features))
        keep.features = gather_parts(features)
        kept.append(keep)
    output = own_slice(current, wide, 1).reshape(rows, cols, wide)

    for layer in range(layers):
        keep = kept[layer]
        (keep.maps, keep.local, keep.gate_sums, partial, keep.message_values), moved = messages_both(
            blocks,
            layer,
            [(gather_kind, keep.ends)] + ([] if layer else [(swap_kind, kept[1].output)]),
            cols,
            keep.features,
            messages_t,
            cotangents[layer],
            gate_gain,
            gate_bias,
            bits,
        )
        keep.ends_all = moved[0]
        if layer == 0:
            kept[1].values = moved[1]
        keep.source_sums = reduce_parts(partial)

    def heads_low_of(keep):
        sums = keep.source_sums.astype(jnp.float32)
        total = jnp.stack([sums[0] + keep.local[0], sums[1], sums[2], sums[3] + keep.local[1]])
        return (total * silu_slope(keep.heads_pre)).astype(low)

    for layer in range(layers):
        keep = kept[layer]
        keep.heads_low = heads_low_of(keep)
        (partial,), (keep.message_values,) = heads_backward(
            blocks,
            layer,
            [(slot_kind, keep.message_values)],
            cols,
            keep.heads_low,
            heads_t,
            bits,
            parts,
        )
        keep.heads_partial = reduce_parts(partial)
        if layer + 1 < layers:
            kept[layer + 1].source_sums, partial = lax.optimization_barrier(
                (kept[layer + 1].source_sums, partial)
            )
    kept[0].heads_low, partial = lax.optimization_barrier((kept[0].heads_low, partial))
    kept[0].heads_all, kept[1].heads_all = exchange(
        blocks, [(gather_kind, keep.heads_low) for keep in kept]
    )

    upstream = output_cotangent.reshape(pixels, wide).astype(jnp.float32)
    for layer in reversed(range(layers)):
        keep = kept[layer]
        (
            upstream,
            keep.expand_grad,
            keep.dilated_grad,
            keep.reduce_grad,
            keep.wide_sums,
            keep.second_sums,
            keep.first_sums,
            keep.gates,
            keep.messages_grad,
            keep.heads_grad,
        ) = trunk_backward(
            blocks,
            parts,
            layer,
            (
                upstream,
                keep.heads_partial,
                keep.input,
                keep.normed3,
                keep.inverse3,
                wide_gain[layer][None],
                wide_bias[layer][None],
                w_expand[layer],
                keep.second_full,
                keep.normed2,
                keep.inverse2,
                norm_gain[layer, 1][None],
                norm_bias[layer, 1][None],
                dilated_t,
                bits,
                keep.first_ext,
                keep.normed1,
                keep.inverse1,
                norm_gain[layer, 0][None],
                norm_bias[layer, 0][None],
                reduce_full[layer],
                keep.gate_sums,
            ),
            (
                keep.message_values,
                keep.cotangents,
                keep.ends_all,
                keep.values,
                keep.heads_all,
                all_bits,
            ),
            (gate_gain, gate_bias),
        )


    def stacked(of):
        return jnp.stack([of(keep) for keep in kept])

    narrow_sums = stacked(lambda keep: jnp.stack([keep.first_sums, keep.second_sums]))
    wide_sums = stacked(lambda keep: keep.wide_sums)
    gate_sums = stacked(lambda keep: keep.gates.reshape(2, 6, mid))
    return (
        output,
        stacked(lambda keep: keep.maps.reshape(2, rows, cols, mid)),
        upstream.reshape(rows, cols, wide),
        stacked(lambda keep: keep.reduce_grad),
        stacked(lambda keep: keep.dilated_grad),
        stacked(lambda keep: keep.expand_grad),
        stacked(lambda keep: keep.heads_grad),
        stacked(lambda keep: keep.messages_grad),
        narrow_sums[:, :, 0],
        narrow_sums[:, :, 1],
        wide_sums[:, 0],
        wide_sums[:, 1],
        gate_sums[:, 0],
        gate_sums[:, 1],
    )


def route(*args):
    mid = args[1].shape[1]
    blocks, parts = lax.axis_size(BLK), lax.axis_size(CH)
    whole_tiles = args[1].shape[0] == 2 and mid % lanes == 0 and args[0].shape[1] == lanes and parts >= 2
    if whole_tiles and blocks % 2 == 0 and 2 * mid * parts == lanes * blocks:
        return shards(*args)
    return plain_shards(*args)


def solution(mesh):
    placed = (
        P(BLK, None, CH),
        P(None, CH, None),
        P(None, CH, None, None),
        P(None, None, CH),
        P(None, None, CH, None, None),
        P(None, None, CH, None, None),
        P(None, None, CH),
        P(None, None, CH),
        P(None, CH),
        P(None, CH),
        P(None, None, CH),
        P(None, None, CH),
        P(),
        P(BLK, None, CH),
        P(None, None, BLK, None, CH),
    )
    return jax.shard_map(
        route,
        mesh=mesh,
        in_specs=placed,
        out_specs=(
            P(BLK, None, CH),
            P(None, None, BLK, None, CH),
            P(BLK, None, CH),
            P(None, BLK, CH),
            P(None, None, BLK, CH),
            P(None, BLK, CH),
            P(None, None, None, BLK, CH),
            P(None, None, None, BLK, CH),
            P(None, None, CH),
            P(None, None, CH),
            P(None, CH),
            P(None, CH),
            P(None, None, CH),
            P(None, None, CH),
        ),
        check_vma=False,
    )
```

```python
import functools
import types

import jax
import jax.numpy as jnp
from jax import lax
from jax.experimental import pallas as pl
from jax.experimental.pallas import tpu as pltpu
from jax.sharding import PartitionSpec as P

epsilon = 1e-05
BLK = "blk"
CH = "ch"
tap_offsets = tuple(((row_step, col_step) for row_step in (-1, 0, 1) for col_step in (-1, 0, 1)))
message_pairs = ((1, 0), (2, 0), (3, 0), (0, 3), (1, 3), (2, 3))


def extended_2(block, sides, width):
    for axis, dim in sides:
        count = lax.axis_size(axis)
        forward = [(i, i + 1) for i in range(count - 1)]
        backward = [(target, source) for source, target in forward]
        low = lax.ppermute(
            lax.slice_in_dim(block, block.shape[dim] - width, None, axis=dim), axis, forward
        )
        high = lax.ppermute(lax.slice_in_dim(block, 0, width, axis=dim), axis, backward)
        block = jnp.concatenate([low, block, high], axis=dim)
    return block


def silu_slope(values):
    sigmoid_value = jax.nn.sigmoid(values)
    return sigmoid_value * (1.0 + values * (1.0 - sigmoid_value))


def gather_channels(values):
    return lax.all_gather(values, CH, axis=3, tiled=True)


def reduce_channels(values):
    return lax.psum_scatter(
        values.astype(jnp.bfloat16), CH, scatter_dimension=3, tiled=True
    ).astype(jnp.float32)


def extend_rows(values, halo_width):
    return extended_2(values, ((BLK, 0),), halo_width)


def pixel_totals(first_sum, second_sum):
    return lax.psum((first_sum, second_sum), BLK)


def weight_totals(reduce_grad, dilated_grad, expand_grad, heads_grad, messages_grad):
    return (
        lax.psum_scatter(
            reduce_grad.astype(jnp.bfloat16), BLK, scatter_dimension=1, tiled=True
        ).astype(jnp.float32),
        lax.psum_scatter(
            dilated_grad.astype(jnp.bfloat16), BLK, scatter_dimension=2, tiled=True
        ).astype(jnp.float32),
        lax.psum_scatter(
            expand_grad.astype(jnp.bfloat16), BLK, scatter_dimension=1, tiled=True
        ).astype(jnp.float32),
        lax.psum_scatter(
            heads_grad.astype(jnp.bfloat16), BLK, scatter_dimension=3, tiled=True
        ).astype(jnp.float32),
        lax.psum_scatter(
            messages_grad.astype(jnp.bfloat16), BLK, scatter_dimension=3, tiled=True
        ).astype(jnp.float32),
    )


def widen(values, halo_width):
    return extend_rows(gather_channels(values), halo_width)


def local_masks(canvas_ids, row_count, dilation):
    col_count = canvas_ids.shape[1]
    padded = jnp.pad(canvas_ids, 2, constant_values=-1)
    start = lax.axis_index(BLK) * row_count
    window = lax.dynamic_slice(padded, (start, jnp.int32(0)), (row_count + 4, col_count + 4))
    centre = window[2 : 2 + row_count, 2 : 2 + col_count]
    result = []
    for row_step, col_step in tap_offsets:
        top = 2 + row_step * dilation
        left = 2 + col_step * dilation
        result.append(window[top : top + row_count, left : left + col_count] == centre)
    return jnp.stack(result)


def shifted(padded, halo_width, dilation, row_step, col_step, row_count, col_count):
    top = halo_width + row_step * dilation
    left = dilation + col_step * dilation
    return padded[top : top + row_count, left : left + col_count]


def conv_forward(extended, halo_width, dilation, weights, tap_masks):
    row_count = extended.shape[0] - 2 * halo_width
    col_count = extended.shape[1]
    padded = jnp.pad(extended, ((0, 0), (dilation, dilation), (0, 0)))
    running = jnp.zeros((row_count, col_count, weights.shape[0], weights.shape[1]), jnp.float32)
    for tap_index, (row_step, col_step) in enumerate(tap_offsets):
        window = shifted(padded, halo_width, dilation, row_step, col_step, row_count, col_count)
        product = jnp.einsum(
            "rwc,koc->rwko", window, weights[:, :, tap_index], preferred_element_type=jnp.float32
        )
        running = running + jnp.where(tap_masks[tap_index][:, :, None, None], product, 0.0)
    return running


def conv_weight_grad(extended, halo_width, dilation, gradient, tap_masks):
    row_count = extended.shape[0] - 2 * halo_width
    col_count = extended.shape[1]
    padded = jnp.pad(extended, ((0, 0), (dilation, dilation), (0, 0)))
    result = []
    for tap_index, (row_step, col_step) in enumerate(tap_offsets):
        window = shifted(padded, halo_width, dilation, row_step, col_step, row_count, col_count)
        masked = jnp.where(
            tap_masks[tap_index][:, :, None, None], gradient, jnp.zeros((), gradient.dtype)
        )
        result.append(
            jnp.einsum("rwc,rwko->kco", window, masked, preferred_element_type=jnp.float32)
        )
    return jnp.stack(result, axis=1)


def conv_input_grad(grad_extended, halo_width, dilation, weights, tap_masks):
    row_count = grad_extended.shape[0] - 2 * halo_width
    col_count = grad_extended.shape[1]
    padded = jnp.pad(grad_extended, ((0, 0), (dilation, dilation), (0, 0), (0, 0)))
    running = jnp.zeros((row_count, col_count, weights.shape[3]), jnp.float32)
    for tap_index, (row_step, col_step) in enumerate(tap_offsets):
        window = shifted(padded, halo_width, dilation, -row_step, -col_step, row_count, col_count)
        product = jnp.einsum(
            "rwko,koc->rwc", window, weights[:, :, tap_index], preferred_element_type=jnp.float32
        )
        running = running + jnp.where(tap_masks[8 - tap_index][:, :, None], product, 0.0)
    return running


def norm_forward(hidden, gain, bias, pixel_count):
    total_sum, square_sum = pixel_totals(
        jnp.sum(hidden, axis=(0, 1)), jnp.sum(hidden * hidden, axis=(0, 1))
    )
    mean_value = total_sum / pixel_count
    variance = square_sum / pixel_count - mean_value * mean_value
    inverse = lax.rsqrt(variance + epsilon)
    normed = (hidden - mean_value) * inverse
    return (gain * normed + bias, normed, inverse)


def norm_backward(upstream, normed, inverse, gain, pixel_count):
    bias_grad, gain_grad = pixel_totals(
        jnp.sum(upstream, axis=(0, 1)), jnp.sum(upstream * normed, axis=(0, 1))
    )
    hidden_grad = (
        gain * inverse * (upstream - bias_grad / pixel_count - normed * gain_grad / pixel_count)
    )
    return (hidden_grad, gain_grad, bias_grad)


def layer_forward(inputs, params, masks_one, masks_two, pixel_count):
    (
        reduce_w,
        dilated_w,
        expand_w,
        heads_w,
        messages_w,
        narrow_gain,
        narrow_bias,
        wide_g,
        wide_b,
        gate_g,
        gate_b,
    ) = params
    stored = types.SimpleNamespace()
    inputs_full = gather_channels(inputs[:, :, None, :])[:, :, 0, :]
    first_pre = jnp.einsum("rwc,oc->rwo", inputs_full, reduce_w, preferred_element_type=jnp.float32)
    first_norm, first_normed, first_inverse = norm_forward(
        first_pre, narrow_gain[0], narrow_bias[0], pixel_count
    )
    first_act = jax.nn.silu(first_norm).astype(jnp.bfloat16)
    first_ext = widen(first_act[:, :, None, :], 2)[:, :, 0, :]
    second_pre = conv_forward(first_ext, 2, 2, dilated_w[None], masks_two)[:, :, 0, :]
    second_norm, second_normed, second_inverse = norm_forward(
        second_pre, narrow_gain[1], narrow_bias[1], pixel_count
    )
    second_act = jax.nn.silu(second_norm).astype(jnp.bfloat16)
    second_full = gather_channels(second_act[:, :, None, :])[:, :, 0, :]
    third_pre = jnp.einsum("rwc,co->rwo", second_full, expand_w, preferred_element_type=jnp.float32)
    third_norm, third_normed, third_inverse = norm_forward(third_pre, wide_g, wide_b, pixel_count)
    summed = third_norm + inputs.astype(jnp.float32)
    output = jax.nn.silu(summed).astype(jnp.bfloat16)
    output_ext = widen(output[:, :, None, :], 1)[:, :, 0, :]
    heads_pre = conv_forward(output_ext, 1, 1, heads_w, masks_one)
    features = jax.nn.silu(heads_pre).astype(jnp.bfloat16)
    features_ext = widen(features, 1)
    feature_values = features.astype(jnp.float32)
    depth_map = feature_values[:, :, 0]
    segment_map = feature_values[:, :, 3]
    message_list = []
    for pair_index, (source, target) in enumerate(message_pairs):
        message = conv_forward(
            features_ext[:, :, source], 1, 1, messages_w[pair_index][None], masks_one
        )[:, :, 0]
        gate_value = jax.nn.sigmoid(
            gate_g[pair_index] * feature_values[:, :, target] + gate_b[pair_index]
        )
        message_list.append(message)
        if target == 0:
            depth_map = depth_map + gate_value * message
        else:
            segment_map = segment_map + gate_value * message
    stored.inputs_full = inputs_full
    stored.first_norm = first_norm
    stored.first_normed = first_normed
    stored.first_inverse = first_inverse
    stored.first_ext = first_ext
    stored.second_norm = second_norm
    stored.second_normed = second_normed
    stored.second_inverse = second_inverse
    stored.second_full = second_full
    stored.third_normed = third_normed
    stored.third_inverse = third_inverse
    stored.summed = summed
    stored.output_ext = output_ext
    stored.heads_pre = heads_pre
    stored.features = feature_values
    stored.features_ext = features_ext
    stored.messages = message_list
    return (output, depth_map, segment_map, stored)


def layer_backward(
    stored, upstream, depth_grad, segment_grad, params, masks_one, masks_two, pixel_count
):
    (
        reduce_w,
        dilated_w,
        expand_w,
        heads_w,
        messages_w,
        narrow_gain,
        narrow_bias,
        wide_g,
        wide_b,
        gate_g,
        gate_b,
    ) = params
    feature_values = stored.features
    zero_map = jnp.zeros_like(depth_grad)
    feature_grads = [depth_grad, zero_map, zero_map, segment_grad]
    message_grads = []
    gain_terms = []
    bias_terms = []
    for pair_index, (source, target) in enumerate(message_pairs):
        target_grad = depth_grad if target == 0 else segment_grad
        gate_value = jax.nn.sigmoid(
            gate_g[pair_index] * feature_values[:, :, target] + gate_b[pair_index]
        )
        message_grads.append(target_grad * gate_value)
        slope = target_grad * stored.messages[pair_index] * gate_value * (1.0 - gate_value)
        gain_terms.append(jnp.sum(slope * feature_values[:, :, target], axis=(0, 1)))
        bias_terms.append(jnp.sum(slope, axis=(0, 1)))
        feature_grads[target] = feature_grads[target] + slope * gate_g[pair_index]
    gate_gain_grad, gate_bias_grad = pixel_totals(jnp.stack(gain_terms), jnp.stack(bias_terms))
    message_stack = jnp.stack(message_grads, axis=2).astype(jnp.bfloat16)
    message_ext = extend_rows(message_stack, 1)
    weight_parts = []
    source_partials = [None, None, None, None]
    for pair_index, (source, target) in enumerate(message_pairs):
        weight_parts.append(
            conv_weight_grad(
                stored.features_ext[:, :, source],
                1,
                1,
                message_stack[:, :, pair_index : pair_index + 1],
                masks_one,
            )
        )
        partial_grad = conv_input_grad(
            message_ext[:, :, pair_index : pair_index + 1],
            1,
            1,
            messages_w[pair_index][None],
            masks_one,
        )
        if source_partials[source] is None:
            source_partials[source] = partial_grad
        else:
            source_partials[source] = source_partials[source] + partial_grad
    messages_w_grad = jnp.concatenate(weight_parts, axis=0)
    source_sums = reduce_channels(jnp.stack(source_partials, axis=2))
    features_total = jnp.stack(feature_grads, axis=2) + source_sums
    heads_grad = (features_total * silu_slope(stored.heads_pre)).astype(jnp.bfloat16)
    heads_w_grad = conv_weight_grad(stored.output_ext, 1, 1, heads_grad, masks_one)
    heads_ext = extend_rows(heads_grad, 1)
    output_partial = conv_input_grad(heads_ext, 1, 1, heads_w, masks_one)
    output_total = upstream + reduce_channels(output_partial[:, :, None, :])[:, :, 0, :]
    summed_grad = output_total * silu_slope(stored.summed)
    third_grad, wide_gain_grad, wide_bias_grad = norm_backward(
        summed_grad, stored.third_normed, stored.third_inverse, wide_g, pixel_count
    )
    third_low = third_grad.astype(jnp.bfloat16)
    expand_w_grad = jnp.einsum(
        "rwc,rwo->co", stored.second_full, third_low, preferred_element_type=jnp.float32
    )
    second_partial = jnp.einsum(
        "rwo,co->rwc", third_low, expand_w, preferred_element_type=jnp.float32
    )
    second_act_grad = reduce_channels(second_partial[:, :, None, :])[:, :, 0, :]
    second_grad, second_gain_grad, second_bias_grad = norm_backward(
        second_act_grad * silu_slope(stored.second_norm),
        stored.second_normed,
        stored.second_inverse,
        narrow_gain[1],
        pixel_count,
    )
    second_low = second_grad.astype(jnp.bfloat16)[:, :, None, :]
    dilated_w_grad = conv_weight_grad(stored.first_ext, 2, 2, second_low, masks_two)[0]
    second_ext = extend_rows(second_low, 2)
    first_partial = conv_input_grad(second_ext, 2, 2, dilated_w[None], masks_two)
    first_act_grad = reduce_channels(first_partial[:, :, None, :])[:, :, 0, :]
    first_grad, first_gain_grad, first_bias_grad = norm_backward(
        first_act_grad * silu_slope(stored.first_norm),
        stored.first_normed,
        stored.first_inverse,
        narrow_gain[0],
        pixel_count,
    )
    first_low = first_grad.astype(jnp.bfloat16)
    reduce_w_grad = jnp.einsum(
        "rwc,rwo->co", stored.inputs_full, first_low, preferred_element_type=jnp.float32
    )
    inputs_partial = jnp.einsum(
        "rwo,oc->rwc", first_low, reduce_w, preferred_element_type=jnp.float32
    )
    inputs_grad = reduce_channels(inputs_partial[:, :, None, :])[:, :, 0, :] + summed_grad
    weight_grads = (reduce_w_grad, dilated_w_grad, expand_w_grad, heads_w_grad, messages_w_grad)
    small_grads = (
        jnp.stack([first_gain_grad, second_gain_grad]),
        jnp.stack([first_bias_grad, second_bias_grad]),
        wide_gain_grad,
        wide_bias_grad,
        gate_gain_grad,
        gate_bias_grad,
    )
    return (inputs_grad, weight_grads, small_grads)


def plain_shards(
    features_in,
    w_reduce,
    w_dilated,
    w_expand,
    w_heads,
    w_messages,
    norm_gain,
    norm_bias,
    wide_gain,
    wide_bias,
    gate_gain,
    gate_bias,
    canvas_ids,
    output_cotangent,
    task_cotangents,
):
    row_count = features_in.shape[0]
    col_count = features_in.shape[1]
    pixel_count = float(row_count * col_count * lax.axis_size(BLK))
    masks_one = local_masks(canvas_ids, row_count, 1)
    masks_two = local_masks(canvas_ids, row_count, 2)
    layer_count = w_reduce.shape[0]
    layer_params = []
    for layer_index in range(layer_count):
        layer_params.append(
            (
                w_reduce[layer_index],
                w_dilated[layer_index],
                w_expand[layer_index],
                w_heads[layer_index],
                w_messages[layer_index],
                norm_gain[layer_index],
                norm_bias[layer_index],
                wide_gain[layer_index],
                wide_bias[layer_index],
                gate_gain[layer_index],
                gate_bias[layer_index],
            )
        )
    current = features_in
    stored_list = []
    task_list = []
    for layer_index in range(layer_count):
        current, depth_map, segment_map, stored = layer_forward(
            current, layer_params[layer_index], masks_one, masks_two, pixel_count
        )
        stored_list.append(stored)
        task_list.append(jnp.stack([depth_map, segment_map]).astype(jnp.bfloat16))
    upstream = output_cotangent.astype(jnp.float32)
    weight_list = [None] * layer_count
    small_list = [None] * layer_count
    for layer_index in reversed(range(layer_count)):
        upstream, weight_grads, small_grads = layer_backward(
            stored_list[layer_index],
            upstream,
            task_cotangents[layer_index, 0].astype(jnp.float32),
            task_cotangents[layer_index, 1].astype(jnp.float32),
            layer_params[layer_index],
            masks_one,
            masks_two,
            pixel_count,
        )
        weight_list[layer_index] = weight_grads
        small_list[layer_index] = small_grads
    stacked = [
        jnp.stack([weight_list[layer_index][member] for layer_index in range(layer_count)])
        for member in range(5)
    ]
    weight_sums = weight_totals(stacked[0], stacked[1], stacked[2], stacked[3], stacked[4])
    small_sums = [
        jnp.stack([small_list[layer_index][member] for layer_index in range(layer_count)])
        for member in range(6)
    ]
    return (
        current,
        jnp.stack(task_list),
        upstream,
        weight_sums[0],
        weight_sums[1],
        weight_sums[2],
        weight_sums[3],
        weight_sums[4],
        small_sums[0],
        small_sums[1],
        small_sums[2],
        small_sums[3],
        small_sums[4],
        small_sums[5],
    )


lanes = 128
source_order = ((1, 0, 4), (2, 1, 5), (0, 3), (3, 2))


def whole(shape):
    return pl.BlockSpec(shape, lambda *_: (0,) * len(shape))


def contract_last(left, right):
    return lax.dot_general(
        left, right, (((1,), (1,)), ((), ())), preferred_element_type=jnp.float32
    )


def sigmoid(values):
    return 1.0 / (1.0 + jnp.exp(-values))


def masked(values, bits, place):
    taken = (bits & (1 << place)) != 0
    width = values.shape[1]
    parts = [
        jnp.where(taken, values[:, start : start + lanes], 0.0) for start in range(0, width, lanes)
    ]
    return parts[0] if len(parts) == 1 else jnp.concatenate(parts, axis=1)


MESH = pl.DeviceIdType.MESH
groups = ((1, 2), (0, 3))
targets = (0, 3)
group_pairs = ((0, 4, 1, 5), (3, 2))


def remote(source, target, send_sem, recv_sem, axis, peer):
    return pltpu.make_async_remote_copy(
        src_ref=source,
        dst_ref=target,
        send_sem=send_sem,
        recv_sem=recv_sem,
        device_id={axis: peer},
        device_id_type=MESH,
    )


def comm_params(key):
    return pltpu.CompilerParams(
        vmem_limit_bytes=60 * 2**20, collective_id=key, has_side_effects=True
    )


def announce(targets):
    barrier = pltpu.get_barrier_semaphore()
    for axis, peer in targets:
        pl.semaphore_signal(barrier, inc=1, device_id={axis: peer}, device_id_type=MESH)
    pl.semaphore_wait(barrier, len(targets))


def near_blocks():
    me = lax.axis_index(BLK)

    def turned(bit):
        return me + bit - 2 * bit * lax.rem(me // bit, 2)

    return turned(1), turned(2), turned(4)


def others(axis, count):
    me = lax.axis_index(axis)
    return [lax.rem(me + step, count) for step in range(1, count)]


def round_trip(own_source, target_of, half_of, sems):
    near_send, slot_recv, pass_send, local_sem = sems
    me = lax.axis_index(BLK)
    sibling, *peers = near_blocks()
    far = me + peers[0] - me + peers[1] - me
    own = pltpu.make_async_copy(own_source, target_of(me), local_sem.at[0])

    def near(step, peer):
        return remote(
            own_source, target_of(me), near_send.at[step], slot_recv.at[me], BLK, peer
        )

    def half(side, block, recv_sem, peer):
        part = half_of(block, side)
        return remote(part, part, near_send.at[3 + side], recv_sem, BLK, peer)

    def passing(step, block):
        part = target_of(block)
        return remote(part, part, pass_send.at[step], slot_recv.at[block], BLK, sibling)

    def start():
        own.start()
        for step, peer in enumerate(peers + [sibling]):
            near(step, peer).start()

    def sent_half(side):
        recv_sem = slot_recv.at[peers[0]] if side == 0 else local_sem.at[1]
        return half(side, peers[side], recv_sem, peers[1 - side])

    def middle():
        for side in range(2):
            copy = passing(side, peers[side])
            copy.wait_recv()
            sent_half(side).start()
            copy.start()

    def forward():
        half(0, far, slot_recv.at[far], sibling).wait_recv()
        half(1, far, local_sem.at[1], sibling).wait_recv()
        passing(2, far).start()

    def finish():
        for block in (sibling, sibling + peers[0] - me, sibling + peers[1] - me, sibling + far - me):
            passing(0, block).wait_recv()
        for step, peer in enumerate(peers + [sibling]):
            near(step, peer).wait_send()
        for side in range(2):
            sent_half(side).wait_send()
            passing(side, peers[side]).wait_send()
        passing(2, far).wait_send()
        own.wait()

    return start, middle, forward, finish


def gather_job(source, target, sems, blocks):
    count = source.shape[0] // 2
    return round_trip(
        source,
        lambda block: target.at[block],
        lambda block, side: target.at[block, pl.ds(side * count, count)],
        sems,
    )


def swap_job(source, target, sems, blocks):
    slot_send, slot_recv, _, local_sem = sems
    me = lax.axis_index(BLK)
    width = source.shape[1] // blocks

    def part_of(block):
        return source.at[:, pl.ds(pl.multiple_of(block * width, width), width)]

    own = pltpu.make_async_copy(part_of(me), target.at[me], local_sem.at[0])

    def copy(step, peer, slot):
        return remote(
            part_of(peer), target.at[slot], slot_send.at[step], slot_recv.at[slot], BLK, peer
        )

    def start():
        for step, peer in enumerate(others(BLK, blocks)):
            copy(step, peer, me).start()
        own.start()

    def finish():
        for step, peer in enumerate(others(BLK, blocks)):
            copy(step, peer, peer).wait_recv()
            copy(step, peer, me).wait_send()
        own.wait()

    return start, lambda: None, lambda: None, finish


def slot_job(source, target, sems, blocks):
    slot_send, slot_recv, _, local_sem = sems
    me = lax.axis_index(BLK)
    own = pltpu.make_async_copy(source.at[me], target.at[me], local_sem.at[0])

    def copy(step, peer, slot):
        return remote(
            source.at[peer], target.at[slot], slot_send.at[step], slot_recv.at[slot], BLK, peer
        )

    def start():
        for step, peer in enumerate(others(BLK, blocks)):
            copy(step, peer, me).start()
        own.start()

    def finish():
        for step, peer in enumerate(others(BLK, blocks)):
            copy(step, peer, peer).wait_recv()
            copy(step, peer, me).wait_send()
        own.wait()

    return start, lambda: None, lambda: None, finish


def line_job(source, target, sems, blocks):
    line_send, line_recv, _, local_sem = sems
    parts = target.shape[0]
    ch = lax.axis_index(CH)
    right, left = lax.rem(ch + 1, parts), lax.rem(ch + parts - 1, parts)
    own = pltpu.make_async_copy(source, target.at[ch], local_sem.at[0])

    def sides(hop):
        return (
            (0, lax.rem(ch + parts - hop, parts), right, ch - hop >= 0, ch < parts - 1),
            (1, lax.rem(ch + hop, parts), left, ch + hop < parts, ch > 0),
        )

    def copy(block, side, hop, peer):
        return remote(
            source if hop == 0 else target.at[block],
            target.at[block],
            line_send.at[side * (parts - 1) + hop],
            line_recv.at[block],
            CH,
            peer,
        )

    def move(hop):
        for side, block, peer, valid, goes in sides(hop):
            if hop > 0:

                @pl.when(valid)
                def _():
                    copy(block, side, hop, peer).wait_recv()

            if hop < parts - 1:

                @pl.when(valid & goes)
                def _():
                    copy(block, side, hop, peer).start()

    def start():
        own.start()
        move(0)

    def middle():
        move(1)

    def forward():
        for hop in range(2, parts - 1):
            move(hop)

    def finish():
        if parts > 2:
            move(parts - 1)
        for hop in range(parts - 1):
            for side, block, peer, valid, goes in sides(hop):

                @pl.when(valid & goes)
                def _():
                    copy(block, side, hop, peer).wait_send()

        own.wait()

    return start, middle, forward, finish


job_kinds = (gather_job, swap_job, slot_job, line_job)
gather_kind, swap_kind, slot_kind, line_kind = 0, 1, 2, 3


def job_target(kind, shape, dtype, blocks):
    if kind == gather_kind:
        shape = (blocks,) + shape
    elif kind == line_kind:
        shape = (lax.axis_size(CH),) + shape
    elif kind == swap_kind:
        shape = (blocks, shape[0], shape[1] // blocks)
    return jax.ShapeDtypeStruct(shape, dtype)


def job_sems(blocks):
    dma = pltpu.SemaphoreType.DMA
    return [dma((blocks,)), dma((blocks,)), dma((blocks,)), dma((2,))]


def job_call(kernel, jobs, blocks, in_specs, out_specs, out_shape, scratch_shapes, **options):
    anywhere = pl.BlockSpec(memory_space=pl.ANY)
    n_in, n_out, n_scratch = len(in_specs), len(out_specs), len(scratch_shapes)
    count = len(jobs)

    def wrapped(*refs):
        ins, refs = refs[:n_in], refs[n_in:]
        sources, refs = refs[:count], refs[count:]
        outs, refs = refs[:n_out], refs[n_out:]
        targets, refs = refs[:count], refs[count:]
        scratch, sems = refs[:n_scratch], refs[n_scratch:]
        running = [
            job_kinds[kind](
                sources[place].at[index[0]] if index else sources[place],
                targets[place],
                sems[4 * place : 4 * place + 4],
                blocks,
            )
            for place, (kind, _, *index) in enumerate(jobs)
        ]
        kernel(running, *ins, *outs, *scratch)

    def call(*operands):
        result = pl.pallas_call(
            wrapped,
            in_specs=list(in_specs) + [anywhere] * count,
            out_specs=list(out_specs) + [anywhere] * count,
            out_shape=list(out_shape) + [
                job_target(kind, source.shape[len(index) :], source.dtype, blocks)
                for kind, source, *index in jobs
            ],
            scratch_shapes=list(scratch_shapes) + job_sems(blocks) * count,
            **options,
        )(*operands, *[job[1] for job in jobs])
        return result[:n_out], result[n_out:]

    return call


def stripe_job(wr_ref, we_ref, layer, mine, sems, blocks, parts):
    part_send, part_recv, local_sem = sems
    _, mid, feat = wr_ref.shape
    _, narrow, wide = we_ref.shape
    blk, ch = lax.axis_index(BLK), lax.axis_index(CH)

    def cut(index, size):
        return pl.ds(pl.multiple_of(index * size, size), size)

    def source(array):
        if array == 0:
            return wr_ref.at[layer, :, cut(blk, feat // blocks)]
        return we_ref.at[layer, cut(blk, narrow // blocks), :]

    def share(array, part):
        if array == 0:
            return mine[0].at[cut(part, mid), :]
        return mine[1].at[:, cut(part, wide)]

    def own(array):
        return pltpu.make_async_copy(source(array), share(array, ch), local_sem.at[array])

    def copy(array, step, peer, slot):
        return remote(
            source(array),
            share(array, slot),
            part_send.at[array, step],
            part_recv.at[array, slot],
            CH,
            peer,
        )

    def start():
        for array in range(2):
            own(array).start()
            for step, peer in enumerate(others(CH, parts)):
                copy(array, step, peer, ch).start()

    def finish():
        for array in range(2):
            for step, peer in enumerate(others(CH, parts)):
                copy(array, step, peer, peer).wait_recv()
            own(array).wait()
            for step, peer in enumerate(others(CH, parts)):
                copy(array, step, peer, ch).wait_send()

    return start, finish


def stripe_sems(parts):
    dma = pltpu.SemaphoreType.DMA
    return [dma((2, parts)), dma((2, parts)), dma((2,))]


def stripe_shapes(parts, blocks, reduce_w, expand_w):
    _, mid, feat = reduce_w.shape
    narrow = mid * parts
    return [
        jax.ShapeDtypeStruct((narrow, feat // blocks), reduce_w.dtype),
        jax.ShapeDtypeStruct((narrow // blocks, feat), expand_w.dtype),
    ]


def spread_jobs(mine, fulls, sems, blocks):
    half_rows = mine[0].shape[0] // 2
    width, height = mine[0].shape[1], mine[1].shape[0]
    half_cols = mine[1].shape[1] // 2

    def cut(index, size):
        return pl.ds(pl.multiple_of(index * size, size), size)

    return [
        round_trip(
            mine[0],
            lambda block: fulls[0].at[:, cut(block, width)],
            lambda block, side: fulls[0].at[pl.ds(side * half_rows, half_rows), cut(block, width)],
            sems[:4],
        ),
        round_trip(
            mine[1],
            lambda block: fulls[1].at[cut(block, height), :],
            lambda block, side: fulls[1].at[cut(block, height), pl.ds(side * half_cols, half_cols)],
            sems[4:],
        ),
    ]


def prologue_kernel(
    blocks,
    parts,
    feat_ref,
    wr_ref,
    we_ref,
    *refs,
):
    small_refs, ids_ref, cur_ref, mine_r, mine_e = refs[:4], *refs[4:8]
    full_r, full_e, small_outs, own_ref, all_ref = *refs[8:10], refs[10:14], *refs[14:16]
    line_send, line_recv, small_send, small_recv, local_sem, *sems = refs[16:]
    pixels, wide = feat_ref.shape
    blk, ch = lax.axis_index(BLK), lax.axis_index(CH)
    smalls = tuple(zip(small_refs, small_outs))

    def lane_part(index):
        return cur_ref.at[:, pl.ds(pl.multiple_of(index * wide, wide), wide)]

    start, gathered = stripe_job(wr_ref, we_ref, 0, (mine_r, mine_e), sems[:3], blocks, parts)
    jobs = spread_jobs((mine_r, mine_e), (full_r, full_e), sems[3:], blocks)
    own = pltpu.make_async_copy(feat_ref, lane_part(ch), local_sem.at[0])
    own.start()
    announce(
        [(CH, peer) for peer in others(CH, parts)] + [(BLK, peer) for peer in near_blocks()]
    )
    start()

    right, left = lax.rem(ch + 1, parts), lax.rem(ch + parts - 1, parts)

    def sides(hop):
        return (
            (0, lax.rem(ch + parts - hop, parts), right, ch - hop >= 0, ch < parts - 1),
            (1, lax.rem(ch + hop, parts), left, ch + hop < parts, ch > 0),
        )

    def line_copy(block, side, hop, peer):
        return remote(
            feat_ref if hop == 0 else lane_part(block),
            lane_part(block),
            line_send.at[side, hop],
            line_recv.at[block],
            CH,
            peer,
        )

    def line_hop(hop):
        for side, block, peer, valid, goes in sides(hop):
            if hop > 0:

                @pl.when(valid)
                def _():
                    line_copy(block, side, hop, peer).wait_recv()

            if hop < parts - 1:

                @pl.when(valid & goes)
                def _():
                    line_copy(block, side, hop, peer).start()

    def small_copy(place, step, peer, slot):
        source, target = smalls[place]
        return remote(
            source,
            target.at[slot],
            small_send.at[place, step],
            small_recv.at[place, slot],
            CH,
            peer,
        )

    def small_own(place):
        source, target = smalls[place]
        return pltpu.make_async_copy(source, target.at[ch], local_sem.at[1 + place])

    line_hop(0)
    for place in range(4):
        small_own(place).start()
        for step, peer in enumerate(others(CH, parts)):
            small_copy(place, step, peer, ch).start()
    gathered()
    for job in jobs:
        job[0]()

    rows = own_ref.shape[1] // lanes
    lane = lax.broadcasted_iota(jnp.int32, (1, lanes), 1)

    def moved(values, step):
        turned = values if step == 0 else pltpu.roll(values, (lanes - step) % lanes, 1)
        return jnp.where((lane + step >= 0) & (lane + step < lanes), turned, -2)

    def spread(target, row, bits):
        block = jnp.broadcast_to(bits.astype(jnp.float32), (lanes, lanes)).T
        target[pl.ds(pl.multiple_of(row * lanes, lanes), lanes), :] = block.astype(jnp.int32)

    def own_row(row, state):
        place = 2 + blk * rows + row
        for word, reach in enumerate((1, 2)):
            bits = jnp.zeros((1, lanes), jnp.int32)
            for tap, (row_step, col_step) in enumerate(tap_offsets):
                a, b = row_step * reach, col_step * reach
                taken = moved(ids_ref[place], -b) == ids_ref[place + a]
                bits = bits | jnp.where(taken, 1 << tap, 0)
                taken = moved(ids_ref[place - a], -b) == ids_ref[place]
                bits = bits | jnp.where(taken, 1 << (9 + tap), 0)
            spread(own_ref.at[word], row, bits)
        return state

    lax.fori_loop(0, rows, own_row, 0)

    def any_row(row, state):
        bits = jnp.zeros((1, lanes), jnp.int32)
        for tap, (row_step, col_step) in enumerate(tap_offsets):
            taken = moved(ids_ref[2 + row + row_step], col_step) == ids_ref[2 + row]
            bits = bits | jnp.where(taken, 1 << tap, 0)
        spread(all_ref, row, bits)
        return state

    lax.fori_loop(0, ids_ref.shape[0] - 4, any_row, 0)
    for hop in range(1, parts):
        line_hop(hop)
        if hop <= 2:
            for job in jobs:
                job[hop]()
    if parts == 2:
        for job in jobs:
            job[2]()
    for job in jobs:
        job[3]()
    for hop in range(parts - 1):
        for side, block, peer, valid, goes in sides(hop):

            @pl.when(valid & goes)
            def _():
                line_copy(block, side, hop, peer).wait_send()

    for place in range(4):
        for step, peer in enumerate(others(CH, parts)):
            small_copy(place, step, peer, peer).wait_recv()
            small_copy(place, step, peer, ch).wait_send()
        small_own(place).wait()
    own.wait()


def prologue(blocks, parts, features, reduce_w, expand_w, terms, canvas_ids):
    layers, mid, feat = reduce_w.shape
    pixels, wide = features.shape
    narrow = mid * parts
    f32, low = jnp.float32, jnp.bfloat16
    shape = jax.ShapeDtypeStruct
    ids = jnp.pad(canvas_ids, ((2, 2), (0, 0)), constant_values=-1)[:, None]
    anywhere = pl.BlockSpec(memory_space=pl.ANY)
    inside = pl.BlockSpec(memory_space=pltpu.VMEM)
    dma = pltpu.SemaphoreType.DMA
    return pl.pallas_call(
        functools.partial(prologue_kernel, blocks, parts),
        in_specs=[anywhere] * 7 + [inside],
        out_specs=[anywhere] * 9 + [inside] * 2,
        out_shape=[
            shape((pixels, feat), low),
            *stripe_shapes(parts, blocks, reduce_w, expand_w),
            shape((narrow, feat), low),
            shape((narrow, feat), low),
            *[shape((parts,) + term.shape, f32) for term in terms],
            shape((2, pixels, lanes), jnp.int32),
            shape((pixels * blocks, lanes), jnp.int32),
        ],
        scratch_shapes=[
            dma((2, parts)),
            dma((parts,)),
            dma((4, parts)),
            dma((4, parts)),
            dma((5,)),
        ]
        + stripe_sems(parts)
        + job_sems(blocks) * 2,
        compiler_params=comm_params(5),
        cost_estimate=pl.CostEstimate(flops=10**6, bytes_accessed=10**8, transcendentals=0),
    )(features, reduce_w, expand_w, *terms, ids)


def greet_line(blocks):
    barrier = pltpu.get_barrier_semaphore()
    me = lax.axis_index(BLK)
    for peer in (lax.rem(me + 1, blocks), lax.rem(me + blocks - 1, blocks)):
        pl.semaphore_signal(barrier, inc=1, device_id={BLK: peer}, device_id_type=MESH)
    pl.semaphore_wait(barrier, 2)


def greet_blocks(blocks):
    announce([(BLK, peer) for peer in others(BLK, blocks)])


def edge_copies(main_ref, low_ref, high_ref, edge, send_sem, recv_sem, blocks):
    me = lax.axis_index(BLK)
    lead = (slice(None),) * (len(main_ref.shape) - 2)
    pixels = main_ref.shape[-2]
    up = remote(
        main_ref.at[lead + (pl.ds(pixels - edge, edge),)],
        low_ref,
        send_sem.at[0],
        recv_sem.at[0],
        BLK,
        lax.rem(me + 1, blocks),
    )
    down = remote(
        main_ref.at[lead + (pl.ds(0, edge),)],
        high_ref,
        send_sem.at[1],
        recv_sem.at[1],
        BLK,
        lax.rem(me + blocks - 1, blocks),
    )

    def start():
        @pl.when(me < blocks - 1)
        def _():
            up.start()

        @pl.when(me > 0)
        def _():
            down.start()

    def finish(zero=True):
        @pl.when(me > 0)
        def _():
            up.wait_recv()
            down.wait_send()

        @pl.when(me < blocks - 1)
        def _():
            down.wait_recv()
            up.wait_send()

        if zero:

            @pl.when(me == 0)
            def _():
                low_ref[...] = jnp.zeros(low_ref.shape, low_ref.dtype)

            @pl.when(me == blocks - 1)
            def _():
                high_ref[...] = jnp.zeros(high_ref.shape, high_ref.dtype)

    return start, finish


def heads_forward_kernel(blocks, fetch, jobs, main_ref, w_ref, mask_ref, *refs):
    if fetch:
        mine_r, mine_e, *refs = refs
    pre_ref, act_ref, ends_ref, *refs = refs
    if fetch:
        full_r, full_e, *refs = refs
    ext_ref, z_ref, local_sem, halo_send, halo_recv, *sems = refs
    step = pl.program_id(0)
    head_count, pixels, mid = pre_ref.shape
    cols = (ext_ref.shape[0] - pixels) // 2
    feat = ext_ref.shape[1]
    start, finish = edge_copies(
        main_ref,
        ext_ref.at[pl.ds(0, cols)],
        ext_ref.at[pl.ds(cols + pixels, cols)],
        cols,
        halo_send,
        halo_recv,
        blocks,
    )
    own = pltpu.make_async_copy(main_ref, ext_ref.at[pl.ds(cols, pixels)], local_sem.at[0])
    if fetch:
        jobs = jobs + spread_jobs((mine_r, mine_e), (full_r, full_e), sems, blocks)

    @pl.when(step == 0)
    def _():
        own.start()
        if jobs:
            greet_blocks(blocks)
        else:
            greet_line(blocks)
        start()
        for job in jobs:
            job[0]()
        own.wait()

    @pl.when(step == 3)
    def _():
        finish()

    if jobs:

        @pl.when(step == 7)
        def _():
            for job in jobs:
                job[1]()

    row_step = jnp.where(step < 3, 1, jnp.where(step < 6, 0, 2))
    col_step = lax.rem(step, 3)
    window = ext_ref[pl.ds(pl.multiple_of(row_step * cols, cols), pixels), :]
    product = contract_last(window, w_ref[0].reshape(head_count * mid, feat))
    product = masked(product, mask_ref[0], tap_at(step))

    @pl.when(step < 3)
    def _():
        z_ref[col_step] = product

    @pl.when(step >= 3)
    def _():
        z_ref[col_step] += product

    @pl.when(step == 8)
    def _():
        for head in range(head_count):
            part = slice(head * mid, (head + 1) * mid)
            total = (
                z_ref[1, :, part]
                + pltpu.roll(z_ref[0, :, part], 1, 0)
                + pltpu.roll(z_ref[2, :, part], pixels - 1, 0)
            )
            pre_ref[head] = total
            value = (total * sigmoid(total)).astype(jnp.bfloat16)
            act_ref[head] = value
            if head in targets:
                ends_ref[targets.index(head)] = value
        for job in jobs:
            job[2]()
        for job in jobs:
            job[3]()


def tap_at(step):
    return jnp.where(step < 3, step + 3, jnp.where(step < 6, step - 3, step))


def heads_forward(blocks, layer, jobs, cols, main, weights, mask, mine):
    _, head_count, _, mid, feat = weights.shape
    pixels = main.shape[0]
    f32, low = jnp.float32, jnp.bfloat16
    shape = jax.ShapeDtypeStruct
    anywhere = pl.BlockSpec(memory_space=pl.ANY)
    dma = pltpu.SemaphoreType.DMA
    return job_call(
        functools.partial(heads_forward_kernel, blocks, bool(mine)),
        jobs,
        blocks,
        grid=(9,),
        in_specs=[
            anywhere,
            pl.BlockSpec((1, head_count, 1, mid, feat), lambda t: (layer, 0, tap_at(t), 0, 0)),
            pl.BlockSpec((1, pixels, lanes), lambda t: (0, 0, 0)),
        ]
        + [anywhere] * len(mine),
        out_specs=[whole((head_count, pixels, mid))] * 2
        + [whole((2, pixels, mid))]
        + [anywhere] * len(mine),
        out_shape=[
            shape((head_count, pixels, mid), f32),
            shape((head_count, pixels, mid), low),
            shape((2, pixels, mid), low),
        ]
        + [shape((mine[0].shape[0], feat), low) for _ in mine],
        scratch_shapes=[
            pltpu.VMEM((pixels + 2 * cols, feat), low),
            pltpu.VMEM((3, pixels, head_count * mid), f32),
            dma((1,)),
            dma((2,)),
            dma((2,)),
        ]
        + (job_sems(blocks) * 2 if mine else []),
        compiler_params=comm_params(6 + layer),
        cost_estimate=pl.CostEstimate(
            flops=18 * pixels * head_count * mid * feat,
            bytes_accessed=18 * head_count * mid * feat,
            transcendentals=0,
        ),
    )(main, weights, mask, *mine)


def fill_taps(im_ref, slot, grad, bits, pixels, cols, dilation):
    rows, mid = grad.shape
    wide = grad.astype(jnp.float32)
    shifted_by = (pltpu.roll(wide, rows - dilation, 0), wide, pltpu.roll(wide, dilation, 0))
    for tap, (row_step, col_step) in enumerate(tap_offsets):
        start = (1 - row_step) * dilation * cols
        part = shifted_by[col_step + 1][start : start + pixels]
        im_ref[slot, :, tap * mid : (tap + 1) * mid] = masked(part, bits, 9 + tap).astype(
            jnp.bfloat16
        )


def messages_kernel(
    blocks,
    layer,
    ahead,
    jobs,
    feat_ref,
    w_hbm,
    cots_ref,
    gain_ref,
    bias_ref,
    mask_ref,
    maps_ref,
    local_ref,
    sums_ref,
    part_ref,
    values_ref,
    pack_ref,
    main_ref,
    low_ref,
    high_ref,
    cot_low,
    cot_high,
    w_ref,
    lhs_ref,
    z_ref,
    im_ref,
    grad_ref,
    *sems,
):
    w_sem, local_sem, halo_send, halo_recv, cot_send, cot_recv, *sems = sems
    parts, heads, pixels, mid = feat_ref.shape
    cot_ref = cots_ref.at[layer]
    cols = low_ref.shape[2]
    pairs = w_ref.shape[0]
    me, ch = lax.axis_index(BLK), lax.axis_index(CH)
    low = jnp.bfloat16
    loads = [
        pltpu.make_async_copy(w_hbm.at[layer, pair], w_ref.at[pair], w_sem.at[pair])
        for pair in range(pairs)
    ]
    main_copy = pltpu.make_async_copy(feat_ref, main_ref, local_sem.at[0])
    main_copy.start()
    for pair in (0, 4, 1, 5, 3, 2):
        loads[pair].start()
    greet(blocks, parts)
    early, jobs = jobs[:ahead], jobs[ahead:]
    for job in early:
        job[0]()
    start, finish = edge_copies(feat_ref, low_ref, high_ref, cols, halo_send, halo_recv, blocks)
    start()
    cot_start, cot_finish = edge_copies(
        cot_ref, cot_low, cot_high, cols, cot_send, cot_recv, blocks
    )
    cot_start()
    for job in jobs:
        job[0]()
    main_copy.wait()
    size = parts * mid // blocks
    for block in range(blocks):
        part, first = block * size // mid, block * size % mid
        for index, (one, two) in enumerate(groups):
            (pack_ref if sems else values_ref)[block, index] = jnp.concatenate(
                [main_ref[part, one][:, first : first + size], main_ref[part, two][:, first : first + size]],
                axis=1,
            )
    if sems:
        jobs = jobs + [slot_job(pack_ref, values_ref, sems, blocks)]
        jobs[-1][0]()
    for source in range(heads):
        for part in range(parts):
            lhs_ref[source, cols : cols + pixels, part * mid : (part + 1) * mid] = main_ref[part, source]
    order = (0, 4, 1, 5, 3, 2)
    bits = mask_ref[0]

    def taps(pair, row_step):
        source = message_pairs[pair][0]
        product = contract_last(
            lhs_ref[source, row_step * cols : row_step * cols + pixels, :],
            w_ref[pair, 3 * row_step : 3 * row_step + 3].reshape(3 * mid, parts * mid),
        )
        for col_step in range(3):
            value = masked(
                product[:, col_step * mid : (col_step + 1) * mid], bits, row_step * 3 + col_step
            )
            if row_step == 1:
                z_ref[pair, col_step] = value
            else:
                z_ref[pair, col_step] += value

    for pair in order:
        loads[pair].wait()
        taps(pair, 1)
    finish()
    cot_finish()
    for source in range(heads):
        for part in range(parts):
            chan = slice(part * mid, (part + 1) * mid)
            lhs_ref[source, 0:cols, chan] = low_ref[part, source]
            lhs_ref[source, cols + pixels :, chan] = high_ref[part, source]
    for pair in order:
        taps(pair, 0)
        taps(pair, 2)
    for job in early:
        job[1]()
    values = {}
    cots = {}
    for place, target in enumerate((0, 3)):
        values[target] = main_ref[ch, target].astype(jnp.float32)
        cots[target] = cot_ref[place].astype(jnp.float32)
    for place, target in enumerate((0, 3)):
        value, cot = values[target], cots[target]
        total, slopes = value, cot
        for pair in range(pairs):
            if message_pairs[pair][1] != target:
                continue
            message = (
                z_ref[pair, 1]
                + pltpu.roll(z_ref[pair, 0], 1, 0)
                + pltpu.roll(z_ref[pair, 2], pixels - 1, 0)
            )
            gain, bias = gain_ref[layer, pair : pair + 1], bias_ref[layer, pair : pair + 1]
            gate = sigmoid(gain * value + bias)
            total = total + gate * message
            grad_ref[pair] = (cot * gate).astype(low)
            slope = cot * message * gate * (1.0 - gate)
            sums_ref[pair : pair + 1] = jnp.sum(slope * value, axis=0, keepdims=True)
            sums_ref[pairs + pair : pairs + pair + 1] = jnp.sum(slope, axis=0, keepdims=True)
            slopes = slopes + slope * gain
        maps_ref[place] = total.astype(low)
        local_ref[place] = slopes

    for job in jobs:
        job[1]()

    def product_of(pair, slot):
        source, target = message_pairs[pair]
        place = 0 if target == 0 else 1
        gain, bias = gain_ref[layer, pair : pair + 1], bias_ref[layer, pair : pair + 1]

        def border(cot, feat):
            return (
                cot[place].astype(jnp.float32)
                * sigmoid(gain * feat[ch, target].astype(jnp.float32) + bias)
            ).astype(low)

        grad = jnp.concatenate(
            [border(cot_low, low_ref), grad_ref[pair], border(cot_high, high_ref)], axis=0
        )
        fill_taps(im_ref, slot, grad, bits, pixels, cols, 1)
        return jnp.dot(
            im_ref[slot],
            w_ref[pair].reshape(9 * mid, parts * mid),
            preferred_element_type=jnp.float32,
        )

    for count, (source, *members) in enumerate(source_order):
        if count == 2:
            for job in early:
                job[2]()
        total = product_of(members[0], 0)
        for pair in members[1:]:
            total = total + product_of(pair, 1)
        for part in range(parts):
            part_ref[part, source] = total[:, part * mid : (part + 1) * mid].astype(low)
    for job in jobs:
        job[2]()
    for job in early + jobs:
        job[3]()


def messages_both(blocks, layer, jobs, ahead, send, cols, features, weights, cotangents, gains, biases, mask):
    parts, heads, pixels, mid = features.shape
    pairs = weights.shape[1]
    narrow = parts * mid
    f32, low = jnp.float32, jnp.bfloat16
    shape = jax.ShapeDtypeStruct
    anywhere = pl.BlockSpec(memory_space=pl.ANY)
    inside = pl.BlockSpec(memory_space=pltpu.VMEM)
    dma = pltpu.SemaphoreType.DMA
    wide = 2 * narrow // blocks
    values = shape((blocks, 2, pixels, wide), low)
    return job_call(
        functools.partial(messages_kernel, blocks, layer, ahead),
        jobs,
        blocks,
        in_specs=[anywhere, anywhere] + [inside] * 4,
        out_specs=[inside] * 4 + [anywhere if send else inside],
        out_shape=[
            shape((2, pixels, mid), low),
            shape((2, pixels, mid), f32),
            shape((2 * pairs, mid), f32),
            shape((parts, heads, pixels, mid), low),
            values,
        ],
        scratch_shapes=[
            pltpu.VMEM(values.shape if send else (8, lanes), low),
            pltpu.VMEM((parts, heads, pixels, mid), low),
            pltpu.VMEM((parts, heads, cols, mid), low),
            pltpu.VMEM((parts, heads, cols, mid), low),
            pltpu.VMEM((2, cols, mid), low),
            pltpu.VMEM((2, cols, mid), low),
            pltpu.VMEM((pairs, 9, mid, narrow), low),
            pltpu.VMEM((heads, pixels + 2 * cols, narrow), low),
            pltpu.VMEM((pairs, 3, pixels, mid), f32),
            pltpu.VMEM((2, pixels, 9 * mid), low),
            pltpu.VMEM((pairs, pixels, mid), low),
            dma((pairs,)),
            dma((1,)),
            dma((2,)),
            dma((2,)),
            dma((2,)),
            dma((2,)),
        ]
        + (job_sems(blocks) if send else []),
        compiler_params=comm_params(10 + layer),
        cost_estimate=pl.CostEstimate(
            flops=36 * pixels * pairs * mid * narrow,
            bytes_accessed=18 * pairs * mid * narrow,
            transcendentals=0,
        ),
    )(features, weights, cotangents, gains, biases, mask)


def heads_backward_kernel(
    blocks,
    jobs,
    main_ref,
    w_ref,
    mask_ref,
    out_ref,
    low_ref,
    high_ref,
    im_ref,
    halo_send,
    halo_recv,
):
    step = pl.program_id(0)
    head_count, pixels, mid = main_ref.shape
    cols = low_ref.shape[1]

    @pl.when(step == 0)
    def _():
        start, finish = edge_copies(main_ref, low_ref, high_ref, cols, halo_send, halo_recv, blocks)
        if jobs:
            greet_blocks(blocks)
        else:
            greet_line(blocks)
        start()
        for job in jobs:
            job[0]()
        finish()
        for head in range(head_count):
            grad = jnp.concatenate([low_ref[head], main_ref[head], high_ref[head]], axis=0)
            fill_taps(im_ref, head, grad, mask_ref[0], pixels, cols, 1)

    total = None
    for head in range(head_count):
        product = jnp.dot(
            im_ref[head],
            w_ref[0, head].reshape(9 * mid, w_ref.shape[4]),
            preferred_element_type=jnp.float32,
        )
        total = product if total is None else total + product
    out_ref[0] = total.astype(jnp.bfloat16)

    if jobs:

        @pl.when(step == pl.num_programs(0) - 1)
        def _():
            for part in (1, 2, 3):
                for job in jobs:
                    job[part]()


def heads_backward(blocks, layer, jobs, cols, main, weights, mask, parts):
    _, head_count, taps, mid, feat = weights.shape
    pixels = main.shape[1]
    width = feat // parts
    dma = pltpu.SemaphoreType.DMA
    return job_call(
        functools.partial(heads_backward_kernel, blocks),
        jobs,
        blocks,
        grid=(parts,),
        in_specs=[
            whole(main.shape),
            pl.BlockSpec((1, head_count, taps, mid, width), lambda j: (layer, 0, 0, 0, j)),
            pl.BlockSpec((1, pixels, lanes), lambda j: (0, 0, 0)),
        ],
        out_specs=[pl.BlockSpec((1, pixels, width), lambda j: (j, 0, 0))],
        out_shape=[jax.ShapeDtypeStruct((parts, pixels, width), jnp.bfloat16)],
        scratch_shapes=[
            pltpu.VMEM((head_count, cols, mid), jnp.bfloat16),
            pltpu.VMEM((head_count, cols, mid), jnp.bfloat16),
            pltpu.VMEM((head_count, pixels, taps * mid), jnp.bfloat16),
            dma((2,)),
            dma((2,)),
        ],
        compiler_params=comm_params(20 + layer),
        cost_estimate=pl.CostEstimate(
            flops=18 * pixels * head_count * mid * feat,
            bytes_accessed=18 * head_count * mid * feat,
            transcendentals=0,
        ),
    )(main, weights, mask)


class WeightChunks:
    def __init__(self, blocks, layer, sources, gates, buffers, accs, lhs, sems):
        self.blocks, self.layer = blocks, layer
        (self.mv, self.cot, self.ends, self.hv, self.hg, self.bits) = sources
        self.gain, self.bias = gates
        (self.mv_buf, self.cot_buf, self.ends_buf, self.hv_buf, self.hg_buf, self.bits_buf) = buffers
        self.accs, self.lhs, self.sems = accs, lhs, sems
        self.done = 0
        self.pixels = self.hv.shape[1]

    def copies(self, heads, index):
        pixels, last = self.pixels, self.blocks - 1
        before, after = jnp.maximum(index - 1, 0), jnp.minimum(index + 1, last)
        slot = lax.rem(index, 2)
        values, buffer = (self.hv, self.hv_buf) if heads else (self.mv, self.mv_buf)
        lead = () if heads else (slice(None),)
        pairs = [
            (
                values.at[(before,) + lead + (pl.ds(pixels - lanes, lanes),)],
                buffer.at[(slot,) + lead + (pl.ds(0, lanes),)],
            ),
            (values.at[index], buffer.at[(slot,) + lead + (pl.ds(lanes, pixels),)]),
            (
                values.at[(after,) + lead + (pl.ds(0, lanes),)],
                buffer.at[(slot,) + lead + (pl.ds(lanes + pixels, lanes),)],
            ),
            (
                self.bits.at[pl.ds(pl.multiple_of(index * pixels, pixels), pixels)],
                self.bits_buf.at[slot],
            ),
        ]
        if heads:
            pairs.append((self.hg.at[index], self.hg_buf.at[slot]))
        else:
            pairs.append((self.cot.at[index], self.cot_buf.at[slot]))
            pairs.append((self.ends.at[index], self.ends_buf.at[slot]))
        return [
            pltpu.make_async_copy(source, target, self.sems.at[slot, place])
            for place, (source, target) in enumerate(pairs)
        ]

    def fetch(self, heads, index):
        for copy in self.copies(heads, index):
            copy.start()

    def begin(self):
        for acc in self.accs:
            acc[...] = jnp.zeros(acc.shape, acc.dtype)
        self.fetch(False, 0)

    def add(self, heads, index):
        slot = lax.rem(index, 2)
        pixels = self.pixels
        for copy in self.copies(heads, index):
            copy.wait()

        @pl.when(index + 1 < self.blocks)
        def _():
            self.fetch(heads, index + 1)

        if not heads:

            @pl.when(index + 1 == self.blocks)
            def _():
                self.fetch(True, 0)

        bits = self.bits_buf[slot]
        for place, members in enumerate((tuple(range(4)),) if heads else group_pairs):
            window = (self.hv_buf[slot] if heads else self.mv_buf[slot, place]).astype(jnp.float32)
            size, chans = window.shape
            shifted_by = (pltpu.roll(window, 1, 0), window, pltpu.roll(window, size - 1, 0))
            for tap, (row_step, col_step) in enumerate(tap_offsets):
                top = (1 + row_step) * lanes
                part = shifted_by[col_step + 1][top : top + pixels]
                self.lhs[:, tap * chans : (tap + 1) * chans] = masked(part, bits, tap).astype(
                    jnp.bfloat16
                )
            if heads:
                grads = [self.hg_buf[slot, member] for member in members]
            else:
                grads = [self.message_grad(slot, pair) for pair in members]
            acc = self.accs[2] if heads else self.accs[place]
            acc[...] += lax.dot_general(
                self.lhs[:, : 9 * chans],
                jnp.concatenate(grads, axis=1),
                (((0,), (0,)), ((), ())),
                preferred_element_type=jnp.float32,
            )

    def message_grad(self, slot, pair):
        place = targets.index(message_pairs[pair][1])
        gain = self.gain[self.layer, pair : pair + 1]
        bias = self.bias[self.layer, pair : pair + 1]
        gate = sigmoid(gain * self.ends_buf[slot, place].astype(jnp.float32) + bias)
        return (self.cot_buf[slot, place].astype(jnp.float32) * gate).astype(jnp.bfloat16)

    def run(self, count):
        while count:
            heads = self.done >= self.blocks
            start = self.done % self.blocks
            size = min(count, self.blocks - start)

            def step(index, state):
                self.add(heads, index)
                return state

            lax.fori_loop(start, start + size, step, 0)
            self.done += size
            count -= size


def exchange_kernel(blocks, jobs, done_ref):
    greet_blocks(blocks)
    for part in range(4):
        for job in jobs:
            job[part]()
    done_ref[...] = jnp.zeros(done_ref.shape, done_ref.dtype)


def exchange(blocks, jobs):
    _, moved = job_call(
        functools.partial(exchange_kernel, blocks),
        jobs,
        blocks,
        in_specs=[],
        out_specs=[pl.BlockSpec(memory_space=pltpu.VMEM)],
        out_shape=[jax.ShapeDtypeStruct((8, lanes), jnp.float32)],
        scratch_shapes=[],
        compiler_params=comm_params(30),
        cost_estimate=pl.CostEstimate(flops=10**6, bytes_accessed=10**8, transcendentals=0),
    )()
    return moved


def heads_store(out_ref, acc_ref):
    head_count, taps, chans, mid = out_ref.shape
    for head in range(head_count):
        for tap in range(taps):
            out_ref[head, tap] = acc_ref[
                tap * chans : (tap + 1) * chans, head * mid : (head + 1) * mid
            ]


def messages_store(out_ref, acc_refs):
    _, taps, size, mid = out_ref.shape
    for index, members in enumerate(group_pairs):
        for place, pair in enumerate(members):
            side = groups[index].index(message_pairs[pair][0])
            for tap in range(taps):
                start = (2 * tap + side) * size
                out_ref[pair, tap] = acc_refs[index][
                    start : start + size, place * mid : (place + 1) * mid
                ]


def greet(blocks, parts):
    barrier = pltpu.get_barrier_semaphore()
    blk, ch = lax.axis_index(BLK), lax.axis_index(CH)
    for step in range(1, blocks):
        pl.semaphore_signal(
            barrier, inc=1, device_id={BLK: lax.rem(blk + step, blocks)}, device_id_type=MESH
        )
    for step in range(1, parts):
        pl.semaphore_signal(
            barrier, inc=1, device_id={CH: lax.rem(ch + step, parts)}, device_id_type=MESH
        )
    pl.semaphore_wait(barrier, blocks + parts - 2)


def send_slots(source_of, target_ref, send_sem, recv_sem, axis, count):
    me = lax.axis_index(axis)
    copies = []
    for step in range(1, count):
        peer = lax.rem(me + step, count)
        copy = pltpu.make_async_remote_copy(
            src_ref=source_of(peer),
            dst_ref=target_ref.at[me],
            send_sem=send_sem.at[step],
            recv_sem=recv_sem.at[me],
            device_id={axis: peer},
            device_id_type=MESH,
        )
        copy.start()
        copies.append(copy)

    def finish():
        for step in range(1, count):
            peer = lax.rem(me + step, count)
            pltpu.make_async_remote_copy(
                src_ref=target_ref.at[peer],
                dst_ref=target_ref.at[peer],
                send_sem=send_sem.at[step],
                recv_sem=recv_sem.at[peer],
                device_id={axis: peer},
                device_id_type=MESH,
            ).wait_recv()
        for copy in copies:
            copy.wait_send()

    return finish


def block_totals(first, second, stat_ref, send_sem, recv_sem, blocks, meanwhile=None):
    me = lax.axis_index(BLK)
    stat_ref[me, 0:1] = first
    stat_ref[me, 1:2] = second
    finish = send_slots(lambda _: stat_ref.at[me], stat_ref, send_sem, recv_sem, BLK, blocks)
    if meanwhile is not None:
        meanwhile()
    finish()
    total = stat_ref[0]
    for block in range(1, blocks):
        total = total + stat_ref[block]
    return total[0:1], total[1:2]


def fold(values):
    rows, width = values.shape
    return values.reshape(rows // 8, 8, width).sum(axis=0)


def row_loop(rows, block, body, carry):
    def step(index, state):
        return body(pl.ds(pl.multiple_of(index * block, block), block), state)

    return lax.fori_loop(0, rows // block, step, carry)


def moments(ref, block):
    rows, width = ref.shape

    def body(part, state):
        values = ref[part, :]
        return state[0] + fold(values), state[1] + fold(values * values)

    zero = jnp.zeros((8, width), jnp.float32)
    total, square = row_loop(rows, block, body, (zero, zero))
    return total.sum(axis=0, keepdims=True), square.sum(axis=0, keepdims=True)


def halo_copies(ref, edge, pixels, send_sem, recv_sem, blocks):
    me = lax.axis_index(BLK)

    def copy(source, target, side, peer):
        return pltpu.make_async_remote_copy(
            src_ref=ref.at[pl.ds(source, edge)],
            dst_ref=ref.at[pl.ds(target, edge)],
            send_sem=send_sem.at[side],
            recv_sem=recv_sem.at[side],
            device_id={BLK: peer},
            device_id_type=MESH,
        )

    up = copy(pixels, 0, 0, lax.rem(me + 1, blocks))
    down = copy(edge, edge + pixels, 1, lax.rem(me + blocks - 1, blocks))

    @pl.when(me < blocks - 1)
    def _():
        up.start()

    @pl.when(me > 0)
    def _():
        down.start()

    @pl.when(me == 0)
    def _():
        ref[0:edge, :] = jnp.zeros((edge, ref.shape[1]), ref.dtype)

    @pl.when(me == blocks - 1)
    def _():
        ref[edge + pixels :, :] = jnp.zeros((edge, ref.shape[1]), ref.dtype)

    def finish():
        @pl.when(me > 0)
        def _():
            up.wait_recv()
            down.wait_send()

        @pl.when(me < blocks - 1)
        def _():
            down.wait_recv()
            up.wait_send()

    return finish


def trunk_forward_kernel(
    blocks,
    parts,
    layer,
    fetch,
    jobs,
    cur_ref,
    wr_ref,
    wd_ref,
    we_ref,
    mask_ref,
    gains_ref,
    biases_ref,
    wide_gains_ref,
    wide_biases_ref,
    *refs,
):
    if fetch:
        raw_r, raw_e, *refs = refs
    out_ref, ext_out_ref, full_ref, normed1_ref, inverse1_ref, normed2_ref, inverse2_ref = refs[:7]
    normed3_ref, inverse3_ref = refs[7:9]
    refs = refs[9:]
    if fetch:
        full_r, full_e, *refs = refs
    pre1_ref, pre3_ref, ext_ref, z_ref, gath_ref, stat1_ref, stat2_ref, stat3_ref = refs[:8]
    term1_ref, term3_ref, stat_send, stat_recv, halo_send, halo_recv, part_send, part_recv = refs[8:16]
    pixels, feat = cur_ref.shape
    mid = normed1_ref.shape[1]
    wide = normed3_ref.shape[1]
    edge = (ext_ref.shape[0] - pixels) // 2
    ch = lax.axis_index(CH)
    pixel_count = float(pixels * blocks)
    greet(blocks, parts)

    def whole_row(row_of):
        return jnp.concatenate([row_of(part) for part in range(parts)], axis=1)

    gain1 = whole_row(lambda part: gains_ref[part, layer, 0:1])
    bias1 = whole_row(lambda part: biases_ref[part, layer, 0:1])
    gain3 = whole_row(lambda part: wide_gains_ref[part, layer : layer + 1])
    bias3 = whole_row(lambda part: wide_biases_ref[part, layer : layer + 1])
    if fetch:
        start, finish = stripe_job(
            raw_r, raw_e, fetch, (full_r, full_e), refs[16:], blocks, parts
        )

    def terms(total, square):
        mean_value = total / pixel_count
        variance = square / pixel_count - mean_value * mean_value
        return mean_value, lax.rsqrt(variance + epsilon)

    pre1_ref[...] = contract_last(cur_ref[...], wr_ref[...])
    total, square = moments(pre1_ref, 64)
    mean_value, inverse = terms(
        *block_totals(total, square, stat1_ref, stat_send.at[0], stat_recv.at[0], blocks)
    )
    term1_ref[0:1] = mean_value
    term1_ref[1:2] = inverse

    def first(part, state):
        value = gain1 * ((pre1_ref[part, :] - mean_value) * inverse) + bias1
        pre1_ref[part, :] = value * sigmoid(value)
        return state

    own_mid = pl.ds(pl.multiple_of(ch * mid, mid), mid)
    normed1_ref[...] = (pre1_ref[:, own_mid] - term1_ref[0:1, own_mid]) * term1_ref[1:2, own_mid]
    inverse1_ref[...] = term1_ref[1:2, own_mid]
    row_loop(pixels, 64, first, 0)
    ext_ref[edge : edge + pixels, :] = pre1_ref[...].astype(jnp.bfloat16)
    wait_halo = halo_copies(ext_ref, edge, pixels, halo_send, halo_recv, blocks)

    half = edge // 2
    for row_step in (1, 0, 2):
        if row_step == 0:
            wait_halo()
        top = 2 * row_step * half
        product = contract_last(
            ext_ref[top : top + pixels, :],
            wd_ref[layer, 3 * row_step : 3 * row_step + 3].reshape(3 * mid, parts * mid),
        )
        for col_step in range(3):
            part = masked(
                product[:, col_step * mid : (col_step + 1) * mid],
                mask_ref[1],
                row_step * 3 + col_step,
            )
            if row_step == 1:
                z_ref[col_step] = part
            else:
                z_ref[col_step] += part
    second_pre = (
        z_ref[1] + pltpu.roll(z_ref[0], 2, 0) + pltpu.roll(z_ref[2], pixels - 2, 0)
    )
    mean_value, inverse = terms(
        *block_totals(
            jnp.sum(second_pre, axis=0, keepdims=True),
            jnp.sum(second_pre * second_pre, axis=0, keepdims=True),
            stat2_ref,
            stat_send.at[1],
            stat_recv.at[1],
            blocks,
        )
    )
    normed = (second_pre - mean_value) * inverse
    normed2_ref[...] = normed
    inverse2_ref[...] = inverse
    value = gains_ref[ch, layer, 1:2] * normed + biases_ref[ch, layer, 1:2]
    gath_ref[ch] = (value * sigmoid(value)).astype(jnp.bfloat16)
    wait_parts = send_slots(
        lambda _: gath_ref.at[ch], gath_ref, part_send, part_recv, CH, parts
    )
    for job in jobs:
        job[0]()
    ext_out_ref[...] = ext_ref[...]
    wait_parts()
    if fetch:
        start()
    for part in range(parts):
        full_ref[:, part * mid : (part + 1) * mid] = gath_ref[part]
    for part in range(parts):
        lane = slice(part * wide, (part + 1) * wide)
        pre3_ref[:, lane] = jnp.dot(
            full_ref[...], we_ref[:, lane], preferred_element_type=jnp.float32
        )
    for job in jobs:
        job[1]()
    total, square = moments(pre3_ref, 16)
    mean_value, inverse = terms(
        *block_totals(total, square, stat3_ref, stat_send.at[2], stat_recv.at[2], blocks)
    )
    term3_ref[0:1] = mean_value
    term3_ref[1:2] = inverse

    def last(part, state):
        value = (
            gain3 * ((pre3_ref[part, :] - mean_value) * inverse)
            + bias3
            + cur_ref[part, :].astype(jnp.float32)
        )
        out_ref[part, :] = (value * sigmoid(value)).astype(jnp.bfloat16)
        return state

    row_loop(pixels, 16, last, 0)
    own_wide = pl.ds(pl.multiple_of(ch * wide, wide), wide)
    for job in jobs:
        job[2]()
    normed3_ref[...] = (pre3_ref[:, own_wide] - term3_ref[0:1, own_wide]) * term3_ref[1:2, own_wide]
    inverse3_ref[...] = term3_ref[1:2, own_wide]
    if fetch:
        finish()
    for job in jobs:
        job[3]()


def trunk_forward(
    blocks, parts, cols, layer, jobs, current, reduce_w, dilated_w, expand_w, mask, norms, raw
):
    pixels, feat = current.shape
    narrow = reduce_w.shape[0]
    mid, wide = narrow // parts, feat // parts
    edge = 2 * cols
    f32, low = jnp.float32, jnp.bfloat16
    shape = jax.ShapeDtypeStruct
    rows = edge * 2 + pixels
    inside = pl.BlockSpec(memory_space=pltpu.VMEM)
    anywhere = pl.BlockSpec(memory_space=pl.ANY)
    fetch = layer + 1 if raw else 0
    return job_call(
        functools.partial(trunk_forward_kernel, blocks, parts, layer, fetch),
        jobs,
        blocks,
        in_specs=[inside] * 9 + [anywhere] * len(raw),
        out_specs=[inside] * 9 + [anywhere] * len(raw),
        out_shape=[
            shape((pixels, feat), low),
            shape((rows, narrow), low),
            shape((pixels, narrow), low),
            shape((pixels, mid), f32),
            shape((1, mid), f32),
            shape((pixels, mid), f32),
            shape((1, mid), f32),
            shape((pixels, wide), f32),
            shape((1, wide), f32),
        ]
        + (stripe_shapes(parts, blocks, *raw) if raw else []),
        scratch_shapes=[
            pltpu.VMEM((pixels, narrow), f32),
            pltpu.VMEM((pixels, feat), f32),
            pltpu.VMEM((rows, narrow), low),
            pltpu.VMEM((3, pixels, mid), f32),
            pltpu.VMEM((parts, pixels, mid), low),
            pltpu.VMEM((blocks, 2, narrow), f32),
            pltpu.VMEM((blocks, 2, mid), f32),
            pltpu.VMEM((blocks, 2, feat), f32),
            pltpu.VMEM((2, narrow), f32),
            pltpu.VMEM((2, feat), f32),
            pltpu.SemaphoreType.DMA((3, blocks)),
            pltpu.SemaphoreType.DMA((3, blocks)),
            pltpu.SemaphoreType.DMA((2,)),
            pltpu.SemaphoreType.DMA((2,)),
            pltpu.SemaphoreType.DMA((parts,)),
            pltpu.SemaphoreType.DMA((parts,)),
        ]
        + (stripe_sems(parts) if raw else []),
        compiler_params=comm_params(50 + layer),
        cost_estimate=pl.CostEstimate(
            flops=2 * pixels * (2 * narrow * feat + 9 * mid * narrow),
            bytes_accessed=150 * 2**20,
            transcendentals=0,
        ),
    )(current, reduce_w, dilated_w, expand_w, mask, *norms, *raw)


def slope_of(values):
    gate = sigmoid(values)
    return gate * (1.0 + values * (1.0 - gate))


def sum_slots(ref, count):
    total = ref[0].astype(jnp.float32)
    for slot in range(1, count):
        total = total + ref[slot].astype(jnp.float32)
    return total


plan = (2, 4, 2, 4, 1, 3)


def trunk_backward_kernel(
    blocks,
    parts,
    layer,
    jobs,
    *refs,
):
    up_ref, heads_ref, cur_ref, normed3_ref, inverse3_ref = refs[:5]
    refs = refs[5:]
    we_ref, full_ref, normed2_ref, inverse2_ref, wd_ref = refs[:5]
    refs = refs[5:]
    mask_ref, ext_ref, normed1_ref, inverse1_ref, wr_ref = refs[:5]
    refs = refs[5:]
    gate_ref, gains_ref, biases_ref, wide_gains_ref, wide_biases_ref = refs[:5]
    refs = refs[5:]
    sources, gates, refs = refs[:6], refs[6:8], refs[8:]
    out_ref, expand_ref, dilated_ref, reduce_ref, wide_ref = refs[:5]
    refs = refs[5:]
    second_ref, first_ref, gate_out = refs[:3]
    refs = refs[3:]
    messages_out, heads_out, *refs = refs
    third_ref, grad_ref, im_ref, send2_ref, recv2_ref = refs[:5]
    refs = refs[5:]
    send1_ref, recv1_ref, gath_ref, low_ref, ex_send_ref = refs[:5]
    refs = refs[5:]
    ex_recv_ref, di_send_ref, di_recv_ref, re_send_ref, re_recv_ref = refs[:5]
    refs = refs[5:]
    stat3_ref, stat2_ref, stat1_ref, gates_ref, stat_send = refs[:5]
    refs = refs[5:]
    stat_recv, halo_send, halo_recv, part_send, part_recv = refs[:5]
    refs = refs[5:]
    sum_send, sum_recv = refs[:2]
    refs = refs[2:]
    buffers, accs, (lhs_ref, chunk_sem) = refs[:6], refs[6:9], refs[9:]
    chunks = WeightChunks(blocks, layer, sources, gates, buffers, accs, lhs_ref, chunk_sem)
    pixels, wide = up_ref.shape
    mid = normed1_ref.shape[1]
    narrow = mid * parts
    feat = cur_ref.shape[1]
    edge = (grad_ref.shape[0] - pixels) // 2
    half = edge // 2
    blk = lax.axis_index(BLK)
    ch = lax.axis_index(CH)
    pixel_count = float(pixels * blocks)
    low = jnp.bfloat16
    gain3 = wide_gains_ref[layer : layer + 1]
    bias3 = wide_biases_ref[layer : layer + 1]
    greet(blocks, parts)
    chunks.begin()
    own_wide = pl.ds(pl.multiple_of(ch * wide, wide), wide)
    gates_ref[blk] = gate_ref[...]
    wait_gates = send_slots(
        lambda _: gates_ref.at[blk], gates_ref, stat_send.at[3], stat_recv.at[3], BLK, blocks
    )

    def start(part, state):
        normed = normed3_ref[part, :]
        summed = (
            gain3 * normed + bias3 + cur_ref[part, own_wide].astype(jnp.float32)
        )
        value = (up_ref[part, :] + heads_ref[part, :].astype(jnp.float32)) * slope_of(summed)
        out_ref[part, :] = value
        return state[0] + fold(value), state[1] + fold(value * normed)

    zero = jnp.zeros((8, wide), jnp.float32)
    bias_sum, gain_sum = row_loop(pixels, 32, start, (zero, zero))
    bias_grad, gain_grad = block_totals(
        bias_sum.sum(axis=0, keepdims=True),
        gain_sum.sum(axis=0, keepdims=True),
        stat3_ref,
        stat_send.at[0],
        stat_recv.at[0],
        blocks,
        lambda: chunks.run(plan[0]),
    )
    wide_ref[0:1] = gain_grad
    wide_ref[1:2] = bias_grad
    scale = gain3 * inverse3_ref[...]
    bias_part = bias_grad / pixel_count
    gain_part = gain_grad / pixel_count

    def third(part, state):
        third_ref[part, :] = (
            scale * (out_ref[part, :] - bias_part - normed3_ref[part, :] * gain_part)
        ).astype(low)
        return state

    row_loop(pixels, 32, third, 0)
    product = contract_last(third_ref[...], we_ref[layer])
    for part in range(parts):
        send2_ref[part] = product[:, part * mid : (part + 1) * mid].astype(low)
    recv2_ref[ch] = send2_ref[ch]
    wait_parts = send_slots(
        lambda peer: send2_ref.at[peer], recv2_ref, part_send.at[0], part_recv.at[0], CH, parts
    )
    size = narrow // blocks
    product = lax.dot_general(
        full_ref[...], third_ref[...], (((0,), (0,)), ((), ())), preferred_element_type=jnp.float32
    )
    for block in range(blocks):
        ex_send_ref[block] = product[block * size : (block + 1) * size].astype(low)
    ex_recv_ref[blk] = ex_send_ref[blk]
    wait_expand = send_slots(
        lambda peer: ex_send_ref.at[peer], ex_recv_ref, sum_send.at[0], sum_recv.at[0], BLK, blocks
    )
    chunks.run(plan[1])
    wait_parts()

    def narrow_norm(recv_ref, normed_ref, inverse_ref, norm, stat_ref, phase, sums_ref):
        gain = gains_ref[layer, norm : norm + 1]
        bias = biases_ref[layer, norm : norm + 1]
        normed = normed_ref[...]
        value = sum_slots(recv_ref, parts) * slope_of(gain * normed + bias)
        bias_grad, gain_grad = block_totals(
            jnp.sum(value, axis=0, keepdims=True),
            jnp.sum(value * normed, axis=0, keepdims=True),
            stat_ref,
            stat_send.at[phase],
            stat_recv.at[phase],
            blocks,
            lambda: chunks.run(plan[2 * phase]),
        )
        sums_ref[0:1] = gain_grad
        sums_ref[1:2] = bias_grad
        return (
            gain
            * inverse_ref[...]
            * (value - bias_grad / pixel_count - normed * (gain_grad / pixel_count))
        )

    grad = narrow_norm(
        recv2_ref, normed2_ref, inverse2_ref, 1, stat2_ref, 1, second_ref
    )
    grad_ref[edge : edge + pixels, :] = grad.astype(low)
    wait_halo = halo_copies(grad_ref, edge, pixels, halo_send, halo_recv, blocks)
    own = grad_ref[edge : edge + pixels, :].astype(jnp.float32)
    turned = (pltpu.roll(own, pixels - 2, 0), own, pltpu.roll(own, 2, 0))
    for row_step in range(3):
        side = jnp.concatenate(
            [
                masked(turned[col_step], mask_ref[1], row_step * 3 + col_step).astype(low)
                for col_step in range(3)
            ],
            axis=1,
        )
        top = 2 * row_step * half
        product = lax.dot_general(
            ext_ref[top : top + pixels, :],
            side,
            (((0,), (0,)), ((), ())),
            preferred_element_type=jnp.float32,
        )
        for block in range(blocks):
            for col_step in range(3):
                di_send_ref[block, row_step * 3 + col_step] = product[
                    block * size : (block + 1) * size, col_step * mid : (col_step + 1) * mid
                ].astype(low)
    di_recv_ref[blk] = di_send_ref[blk]
    wait_halo()
    fill_taps(im_ref, 0, grad_ref[...], mask_ref[1], pixels, half, 2)
    product = jnp.dot(
        im_ref[0], wd_ref[layer].reshape(9 * mid, narrow), preferred_element_type=jnp.float32
    )
    for part in range(parts):
        send1_ref[part] = product[:, part * mid : (part + 1) * mid].astype(low)
    recv1_ref[ch] = send1_ref[ch]
    wait_parts = send_slots(
        lambda peer: send1_ref.at[peer], recv1_ref, part_send.at[1], part_recv.at[1], CH, parts
    )
    wait_dilated = send_slots(
        lambda peer: di_send_ref.at[peer], di_recv_ref, sum_send.at[1], sum_recv.at[1], BLK, blocks
    )
    for job in jobs:
        job[0]()
    chunks.run(plan[3])
    wait_parts()
    grad = narrow_norm(
        recv1_ref, normed1_ref, inverse1_ref, 0, stat1_ref, 2, first_ref
    )
    gath_ref[ch] = grad.astype(low)
    wait_parts = send_slots(
        lambda _: gath_ref.at[ch], gath_ref, part_send.at[2], part_recv.at[2], CH, parts
    )
    product = lax.dot_general(
        cur_ref[...], gath_ref[ch], (((0,), (0,)), ((), ())), preferred_element_type=jnp.float32
    )
    size = feat // blocks
    for block in range(blocks):
        re_send_ref[block] = product[block * size : (block + 1) * size].astype(low)
    re_recv_ref[blk] = re_send_ref[blk]
    wait_reduce = send_slots(
        lambda peer: re_send_ref.at[peer], re_recv_ref, sum_send.at[2], sum_recv.at[2], BLK, blocks
    )
    chunks.run(plan[5])
    wait_parts()
    for part in range(parts):
        low_ref[:, part * mid : (part + 1) * mid] = gath_ref[part]
    out_ref[...] += jnp.dot(low_ref[...], wr_ref[:, own_wide], preferred_element_type=jnp.float32)
    chunks.run(2 * blocks - chunks.done)
    messages_store(messages_out, accs[:2])
    heads_store(heads_out, accs[2])
    for part in (1, 2, 3):
        for job in jobs:
            job[part]()
    wait_gates()
    gate_out[...] = sum_slots(gates_ref, blocks)
    wait_expand()
    expand_ref[...] = sum_slots(ex_recv_ref, blocks)
    wait_dilated()
    dilated_ref[...] = sum_slots(di_recv_ref, blocks)
    wait_reduce()
    reduce_ref[...] = sum_slots(re_recv_ref, blocks)


def trunk_backward(blocks, parts, layer, jobs, operands, norms, sources, gates):
    pixels, wide = operands[0].shape
    feat = wide * parts
    mid = operands[7].shape[1]
    narrow = mid * parts
    rows = operands[11].shape[0]
    f32, low = jnp.float32, jnp.bfloat16
    shape = jax.ShapeDtypeStruct
    small, large = narrow // blocks, feat // blocks
    inside = pl.BlockSpec(memory_space=pltpu.VMEM)
    anywhere = pl.BlockSpec(memory_space=pl.ANY)
    rows_two = pixels + 2 * lanes
    return job_call(
        functools.partial(trunk_backward_kernel, blocks, parts, layer),
        jobs,
        blocks,
        in_specs=[inside] * (len(operands) + len(norms)) + [anywhere] * len(sources) + [inside] * len(gates),
        out_specs=[inside] * 10,
        out_shape=[
            shape((pixels, wide), f32),
            shape((small, wide), f32),
            shape((9, small, mid), f32),
            shape((large, mid), f32),
            shape((2, wide), f32),
            shape((2, mid), f32),
            shape((2, mid), f32),
            shape(operands[-1].shape, f32),
            shape((6, 9, small, mid), f32),
            shape((4, 9, large, mid), f32),
        ],
        scratch_shapes=[
            pltpu.VMEM((pixels, wide), low),
            pltpu.VMEM((rows, mid), low),
            pltpu.VMEM((1, pixels, 9 * mid), low),
            pltpu.VMEM((parts, pixels, mid), low),
            pltpu.VMEM((parts, pixels, mid), low),
            pltpu.VMEM((parts, pixels, mid), low),
            pltpu.VMEM((parts, pixels, mid), low),
            pltpu.VMEM((parts, pixels, mid), low),
            pltpu.VMEM((pixels, narrow), low),
            pltpu.VMEM((blocks, small, wide), low),
            pltpu.VMEM((blocks, small, wide), low),
            pltpu.VMEM((blocks, 9, small, mid), low),
            pltpu.VMEM((blocks, 9, small, mid), low),
            pltpu.VMEM((blocks, large, mid), low),
            pltpu.VMEM((blocks, large, mid), low),
            pltpu.VMEM((blocks, 2, wide), f32),
            pltpu.VMEM((blocks, 2, mid), f32),
            pltpu.VMEM((blocks, 2, mid), f32),
            pltpu.VMEM((blocks,) + operands[-1].shape, f32),
            pltpu.SemaphoreType.DMA((4, blocks)),
            pltpu.SemaphoreType.DMA((4, blocks)),
            pltpu.SemaphoreType.DMA((2,)),
            pltpu.SemaphoreType.DMA((2,)),
            pltpu.SemaphoreType.DMA((3, parts)),
            pltpu.SemaphoreType.DMA((3, parts)),
            pltpu.SemaphoreType.DMA((3, blocks)),
            pltpu.SemaphoreType.DMA((3, blocks)),
            pltpu.VMEM((2, 2, rows_two, 2 * small), low),
            pltpu.VMEM((2, 2, pixels, mid), low),
            pltpu.VMEM((2, 2, pixels, mid), low),
            pltpu.VMEM((2, rows_two, large), low),
            pltpu.VMEM((2, 4, pixels, mid), low),
            pltpu.VMEM((2, pixels, lanes), jnp.int32),
            pltpu.VMEM((18 * small, len(group_pairs[0]) * mid), f32),
            pltpu.VMEM((18 * small, len(group_pairs[1]) * mid), f32),
            pltpu.VMEM((9 * large, 4 * mid), f32),
            pltpu.VMEM((pixels, 9 * max(large, 2 * small)), low),
            pltpu.SemaphoreType.DMA((2, 6)),
        ],
        compiler_params=comm_params(60 + layer),
        cost_estimate=pl.CostEstimate(
            flops=4 * pixels * (2 * narrow * wide + 9 * mid * narrow) + 2 * 10**10,
            bytes_accessed=200 * 2**20,
            transcendentals=0,
        ),
    )(*operands, *norms, *sources, *gates)


def gather_parts(values):
    return lax.all_gather(values, CH, axis=0, tiled=False)


def reduce_parts(values):
    return lax.psum_scatter(values, CH, scatter_dimension=0, tiled=False)


def own_slice(values, size, axis):
    return lax.dynamic_slice_in_dim(values, lax.axis_index(CH) * size, size, axis)


def shards(
    features_in,
    w_reduce,
    w_dilated,
    w_expand,
    w_heads,
    w_messages,
    norm_gain,
    norm_bias,
    wide_gain,
    wide_bias,
    gate_gain,
    gate_bias,
    canvas_ids,
    output_cotangent,
    task_cotangents,
):
    rows, cols, wide = features_in.shape
    pixels = rows * cols
    blocks = lax.axis_size(BLK)
    parts = lax.axis_size(CH)
    layers = w_reduce.shape[0]
    mid = w_reduce.shape[1]
    feat = wide * parts
    narrow = mid * parts
    low = jnp.bfloat16
    dilated_t = w_dilated.transpose(0, 2, 1, 3)
    heads_t = w_heads.transpose(0, 1, 3, 2, 4)
    messages_t = w_messages.transpose(0, 1, 3, 2, 4)
    current, *rest = prologue(
        blocks,
        parts,
        features_in.reshape(pixels, wide),
        w_reduce,
        w_expand,
        (norm_gain, norm_bias, wide_gain, wide_bias),
        canvas_ids,
    )
    reduce_full, expand_full = [rest[2]], [rest[3]]
    norms_all, bits, all_bits = rest[4:8], rest[8], rest[9]
    cotangents = task_cotangents.reshape(layers, 2, pixels, mid)
    kept = []
    for layer in range(layers):
        keep = types.SimpleNamespace(input=current)
        results, (keep.cotangents,) = trunk_forward(
            blocks,
            parts,
            cols,
            layer,
            [(gather_kind, cotangents, layer)],
            current,
            reduce_full[layer],
            dilated_t,
            expand_full[layer],
            bits,
            norms_all,
            (w_reduce, w_expand) if layer + 1 < layers else (),
        )
        (
            current,
            keep.first_ext,
            keep.second_full,
            keep.normed1,
            keep.inverse1,
            keep.normed2,
            keep.inverse2,
            keep.normed3,
            keep.inverse3,
            *mine,
        ) = results
        if layer:
            current, kept[-1].features = lax.optimization_barrier((current, kept[-1].features))
        keep.output = current
        (keep.heads_pre, features, keep.ends, *fetched), _ = heads_forward(
            blocks,
            layer,
            [],
            cols,
            current,
            heads_t,
            bits,
            mine,
        )
        if fetched:
            reduce_full.append(fetched[0])
            expand_full.append(fetched[1])
        current, features = lax.optimization_barrier((current, features))
        keep.features = gather_parts(features)
        kept.append(keep)
    output = own_slice(current, wide, 1).reshape(rows, cols, wide)

    for layer in range(layers):
        keep = kept[layer]
        (keep.maps, keep.local, keep.gate_sums, partial, keep.message_values), moved = messages_both(
            blocks,
            layer,
            [(gather_kind, keep.ends)] + ([] if layer else [(swap_kind, kept[1].output)]),
            0,
            bool(layer),
            cols,
            keep.features,
            messages_t,
            cotangents,
            gate_gain,
            gate_bias,
            bits,
        )
        keep.ends_all = moved[0]
        if layer == 0:
            kept[1].values = moved[1]
        keep.source_sums = reduce_parts(partial)

    def heads_low_of(keep):
        sums = keep.source_sums.astype(jnp.float32)
        total = jnp.stack([sums[0] + keep.local[0], sums[1], sums[2], sums[3] + keep.local[1]])
        return (total * silu_slope(keep.heads_pre)).astype(low)

    for layer in range(layers):
        keep = kept[layer]
        keep.heads_low = heads_low_of(keep)
        (partial,), moved = heads_backward(
            blocks,
            layer,
            [] if layer else [(slot_kind, keep.message_values), (swap_kind, keep.output)],
            cols,
            keep.heads_low,
            heads_t,
            bits,
            parts,
        )
        if layer == 0:
            keep.message_values, keep.values = moved
        keep.heads_partial = reduce_parts(partial)
        if layer + 1 < layers:
            kept[layer + 1].source_sums, partial = lax.optimization_barrier(
                (kept[layer + 1].source_sums, partial)
            )
    kept[0].heads_low, kept[0].heads_partial, partial = lax.optimization_barrier(
        (kept[0].heads_low, kept[0].heads_partial, partial)
    )
    kept[0].heads_all, kept[1].heads_all = exchange(
        blocks, [(gather_kind, keep.heads_low) for keep in kept]
    )

    upstream = output_cotangent.reshape(pixels, wide).astype(jnp.float32)
    for layer in reversed(range(layers)):
        keep = kept[layer]
        (
            upstream,
            keep.expand_grad,
            keep.dilated_grad,
            keep.reduce_grad,
            keep.wide_sums,
            keep.second_sums,
            keep.first_sums,
            keep.gates,
            keep.messages_grad,
            keep.heads_grad,
        ), _ = trunk_backward(
            blocks,
            parts,
            layer,
            [],
            (
                upstream,
                keep.heads_partial,
                keep.input,
                keep.normed3,
                keep.inverse3,
                w_expand,
                keep.second_full,
                keep.normed2,
                keep.inverse2,
                dilated_t,
                bits,
                keep.first_ext,
                keep.normed1,
                keep.inverse1,
                reduce_full[layer],
                keep.gate_sums,
            ),
            (norm_gain, norm_bias, wide_gain, wide_bias),
            (
                keep.message_values,
                keep.cotangents,
                keep.ends_all,
                keep.values,
                keep.heads_all,
                all_bits,
            ),
            (gate_gain, gate_bias),
        )
    def stacked(of):
        return jnp.stack([of(keep) for keep in kept])

    narrow_sums = stacked(lambda keep: jnp.stack([keep.first_sums, keep.second_sums]))
    wide_sums = stacked(lambda keep: keep.wide_sums)
    gate_sums = stacked(lambda keep: keep.gates.reshape(2, 6, mid))
    return (
        output,
        stacked(lambda keep: keep.maps.reshape(2, rows, cols, mid)),
        upstream.reshape(rows, cols, wide),
        stacked(lambda keep: keep.reduce_grad),
        stacked(lambda keep: keep.dilated_grad),
        stacked(lambda keep: keep.expand_grad),
        stacked(lambda keep: keep.heads_grad),
        stacked(lambda keep: keep.messages_grad),
        narrow_sums[:, :, 0],
        narrow_sums[:, :, 1],
        wide_sums[:, 0],
        wide_sums[:, 1],
        gate_sums[:, 0],
        gate_sums[:, 1],
    )


def route(*args):
    mid = args[1].shape[1]
    blocks, parts = lax.axis_size(BLK), lax.axis_size(CH)
    whole_tiles = args[1].shape[0] == 2 and mid % lanes == 0 and args[0].shape[1] == lanes and parts >= 2
    if whole_tiles and blocks == 8 and 2 * mid * parts == lanes * blocks:
        return shards(*args)
    return plain_shards(*args)


def solution(mesh):
    placed = (
        P(BLK, None, CH),
        P(None, CH, None),
        P(None, CH, None, None),
        P(None, None, CH),
        P(None, None, CH, None, None),
        P(None, None, CH, None, None),
        P(None, None, CH),
        P(None, None, CH),
        P(None, CH),
        P(None, CH),
        P(None, None, CH),
        P(None, None, CH),
        P(),
        P(BLK, None, CH),
        P(None, None, BLK, None, CH),
    )
    return jax.shard_map(
        route,
        mesh=mesh,
        in_specs=placed,
        out_specs=(
            P(BLK, None, CH),
            P(None, None, BLK, None, CH),
            P(BLK, None, CH),
            P(None, BLK, CH),
            P(None, None, BLK, CH),
            P(None, BLK, CH),
            P(None, None, None, BLK, CH),
            P(None, None, None, BLK, CH),
            P(None, None, CH),
            P(None, None, CH),
            P(None, CH),
            P(None, CH),
            P(None, None, CH),
            P(None, None, CH),
        ),
        check_vma=False,
    )
```

```python
import functools
import types

import jax
import jax.numpy as jnp
from jax import lax
from jax.experimental import pallas as pl
from jax.experimental.pallas import tpu as pltpu
from jax.sharding import PartitionSpec as P

epsilon = 1e-05
BLK = "blk"
CH = "ch"
tap_offsets = tuple(((row_step, col_step) for row_step in (-1, 0, 1) for col_step in (-1, 0, 1)))
message_pairs = ((1, 0), (2, 0), (3, 0), (0, 3), (1, 3), (2, 3))


def extended_2(block, sides, width):
    for axis, dim in sides:
        count = lax.axis_size(axis)
        forward = [(i, i + 1) for i in range(count - 1)]
        backward = [(target, source) for source, target in forward]
        low = lax.ppermute(
            lax.slice_in_dim(block, block.shape[dim] - width, None, axis=dim), axis, forward
        )
        high = lax.ppermute(lax.slice_in_dim(block, 0, width, axis=dim), axis, backward)
        block = jnp.concatenate([low, block, high], axis=dim)
    return block


def silu_slope(values):
    sigmoid_value = jax.nn.sigmoid(values)
    return sigmoid_value * (1.0 + values * (1.0 - sigmoid_value))


def gather_channels(values):
    return lax.all_gather(values, CH, axis=3, tiled=True)


def reduce_channels(values):
    return lax.psum_scatter(
        values.astype(jnp.bfloat16), CH, scatter_dimension=3, tiled=True
    ).astype(jnp.float32)


def extend_rows(values, halo_width):
    return extended_2(values, ((BLK, 0),), halo_width)


def pixel_totals(first_sum, second_sum):
    return lax.psum((first_sum, second_sum), BLK)


def weight_totals(reduce_grad, dilated_grad, expand_grad, heads_grad, messages_grad):
    return (
        lax.psum_scatter(
            reduce_grad.astype(jnp.bfloat16), BLK, scatter_dimension=1, tiled=True
        ).astype(jnp.float32),
        lax.psum_scatter(
            dilated_grad.astype(jnp.bfloat16), BLK, scatter_dimension=2, tiled=True
        ).astype(jnp.float32),
        lax.psum_scatter(
            expand_grad.astype(jnp.bfloat16), BLK, scatter_dimension=1, tiled=True
        ).astype(jnp.float32),
        lax.psum_scatter(
            heads_grad.astype(jnp.bfloat16), BLK, scatter_dimension=3, tiled=True
        ).astype(jnp.float32),
        lax.psum_scatter(
            messages_grad.astype(jnp.bfloat16), BLK, scatter_dimension=3, tiled=True
        ).astype(jnp.float32),
    )


def widen(values, halo_width):
    return extend_rows(gather_channels(values), halo_width)


def local_masks(canvas_ids, row_count, dilation):
    col_count = canvas_ids.shape[1]
    padded = jnp.pad(canvas_ids, 2, constant_values=-1)
    start = lax.axis_index(BLK) * row_count
    window = lax.dynamic_slice(padded, (start, jnp.int32(0)), (row_count + 4, col_count + 4))
    centre = window[2 : 2 + row_count, 2 : 2 + col_count]
    result = []
    for row_step, col_step in tap_offsets:
        top = 2 + row_step * dilation
        left = 2 + col_step * dilation
        result.append(window[top : top + row_count, left : left + col_count] == centre)
    return jnp.stack(result)


def shifted(padded, halo_width, dilation, row_step, col_step, row_count, col_count):
    top = halo_width + row_step * dilation
    left = dilation + col_step * dilation
    return padded[top : top + row_count, left : left + col_count]


def conv_forward(extended, halo_width, dilation, weights, tap_masks):
    row_count = extended.shape[0] - 2 * halo_width
    col_count = extended.shape[1]
    padded = jnp.pad(extended, ((0, 0), (dilation, dilation), (0, 0)))
    running = jnp.zeros((row_count, col_count, weights.shape[0], weights.shape[1]), jnp.float32)
    for tap_index, (row_step, col_step) in enumerate(tap_offsets):
        window = shifted(padded, halo_width, dilation, row_step, col_step, row_count, col_count)
        product = jnp.einsum(
            "rwc,koc->rwko", window, weights[:, :, tap_index], preferred_element_type=jnp.float32
        )
        running = running + jnp.where(tap_masks[tap_index][:, :, None, None], product, 0.0)
    return running


def conv_weight_grad(extended, halo_width, dilation, gradient, tap_masks):
    row_count = extended.shape[0] - 2 * halo_width
    col_count = extended.shape[1]
    padded = jnp.pad(extended, ((0, 0), (dilation, dilation), (0, 0)))
    result = []
    for tap_index, (row_step, col_step) in enumerate(tap_offsets):
        window = shifted(padded, halo_width, dilation, row_step, col_step, row_count, col_count)
        masked = jnp.where(
            tap_masks[tap_index][:, :, None, None], gradient, jnp.zeros((), gradient.dtype)
        )
        result.append(
            jnp.einsum("rwc,rwko->kco", window, masked, preferred_element_type=jnp.float32)
        )
    return jnp.stack(result, axis=1)


def conv_input_grad(grad_extended, halo_width, dilation, weights, tap_masks):
    row_count = grad_extended.shape[0] - 2 * halo_width
    col_count = grad_extended.shape[1]
    padded = jnp.pad(grad_extended, ((0, 0), (dilation, dilation), (0, 0), (0, 0)))
    running = jnp.zeros((row_count, col_count, weights.shape[3]), jnp.float32)
    for tap_index, (row_step, col_step) in enumerate(tap_offsets):
        window = shifted(padded, halo_width, dilation, -row_step, -col_step, row_count, col_count)
        product = jnp.einsum(
            "rwko,koc->rwc", window, weights[:, :, tap_index], preferred_element_type=jnp.float32
        )
        running = running + jnp.where(tap_masks[8 - tap_index][:, :, None], product, 0.0)
    return running


def norm_forward(hidden, gain, bias, pixel_count):
    total_sum, square_sum = pixel_totals(
        jnp.sum(hidden, axis=(0, 1)), jnp.sum(hidden * hidden, axis=(0, 1))
    )
    mean_value = total_sum / pixel_count
    variance = square_sum / pixel_count - mean_value * mean_value
    inverse = lax.rsqrt(variance + epsilon)
    normed = (hidden - mean_value) * inverse
    return (gain * normed + bias, normed, inverse)


def norm_backward(upstream, normed, inverse, gain, pixel_count):
    bias_grad, gain_grad = pixel_totals(
        jnp.sum(upstream, axis=(0, 1)), jnp.sum(upstream * normed, axis=(0, 1))
    )
    hidden_grad = (
        gain * inverse * (upstream - bias_grad / pixel_count - normed * gain_grad / pixel_count)
    )
    return (hidden_grad, gain_grad, bias_grad)


def layer_forward(inputs, params, masks_one, masks_two, pixel_count):
    (
        reduce_w,
        dilated_w,
        expand_w,
        heads_w,
        messages_w,
        narrow_gain,
        narrow_bias,
        wide_g,
        wide_b,
        gate_g,
        gate_b,
    ) = params
    stored = types.SimpleNamespace()
    inputs_full = gather_channels(inputs[:, :, None, :])[:, :, 0, :]
    first_pre = jnp.einsum("rwc,oc->rwo", inputs_full, reduce_w, preferred_element_type=jnp.float32)
    first_norm, first_normed, first_inverse = norm_forward(
        first_pre, narrow_gain[0], narrow_bias[0], pixel_count
    )
    first_act = jax.nn.silu(first_norm).astype(jnp.bfloat16)
    first_ext = widen(first_act[:, :, None, :], 2)[:, :, 0, :]
    second_pre = conv_forward(first_ext, 2, 2, dilated_w[None], masks_two)[:, :, 0, :]
    second_norm, second_normed, second_inverse = norm_forward(
        second_pre, narrow_gain[1], narrow_bias[1], pixel_count
    )
    second_act = jax.nn.silu(second_norm).astype(jnp.bfloat16)
    second_full = gather_channels(second_act[:, :, None, :])[:, :, 0, :]
    third_pre = jnp.einsum("rwc,co->rwo", second_full, expand_w, preferred_element_type=jnp.float32)
    third_norm, third_normed, third_inverse = norm_forward(third_pre, wide_g, wide_b, pixel_count)
    summed = third_norm + inputs.astype(jnp.float32)
    output = jax.nn.silu(summed).astype(jnp.bfloat16)
    output_ext = widen(output[:, :, None, :], 1)[:, :, 0, :]
    heads_pre = conv_forward(output_ext, 1, 1, heads_w, masks_one)
    features = jax.nn.silu(heads_pre).astype(jnp.bfloat16)
    features_ext = widen(features, 1)
    feature_values = features.astype(jnp.float32)
    depth_map = feature_values[:, :, 0]
    segment_map = feature_values[:, :, 3]
    message_list = []
    for pair_index, (source, target) in enumerate(message_pairs):
        message = conv_forward(
            features_ext[:, :, source], 1, 1, messages_w[pair_index][None], masks_one
        )[:, :, 0]
        gate_value = jax.nn.sigmoid(
            gate_g[pair_index] * feature_values[:, :, target] + gate_b[pair_index]
        )
        message_list.append(message)
        if target == 0:
            depth_map = depth_map + gate_value * message
        else:
            segment_map = segment_map + gate_value * message
    stored.inputs_full = inputs_full
    stored.first_norm = first_norm
    stored.first_normed = first_normed
    stored.first_inverse = first_inverse
    stored.first_ext = first_ext
    stored.second_norm = second_norm
    stored.second_normed = second_normed
    stored.second_inverse = second_inverse
    stored.second_full = second_full
    stored.third_normed = third_normed
    stored.third_inverse = third_inverse
    stored.summed = summed
    stored.output_ext = output_ext
    stored.heads_pre = heads_pre
    stored.features = feature_values
    stored.features_ext = features_ext
    stored.messages = message_list
    return (output, depth_map, segment_map, stored)


def layer_backward(
    stored, upstream, depth_grad, segment_grad, params, masks_one, masks_two, pixel_count
):
    (
        reduce_w,
        dilated_w,
        expand_w,
        heads_w,
        messages_w,
        narrow_gain,
        narrow_bias,
        wide_g,
        wide_b,
        gate_g,
        gate_b,
    ) = params
    feature_values = stored.features
    zero_map = jnp.zeros_like(depth_grad)
    feature_grads = [depth_grad, zero_map, zero_map, segment_grad]
    message_grads = []
    gain_terms = []
    bias_terms = []
    for pair_index, (source, target) in enumerate(message_pairs):
        target_grad = depth_grad if target == 0 else segment_grad
        gate_value = jax.nn.sigmoid(
            gate_g[pair_index] * feature_values[:, :, target] + gate_b[pair_index]
        )
        message_grads.append(target_grad * gate_value)
        slope = target_grad * stored.messages[pair_index] * gate_value * (1.0 - gate_value)
        gain_terms.append(jnp.sum(slope * feature_values[:, :, target], axis=(0, 1)))
        bias_terms.append(jnp.sum(slope, axis=(0, 1)))
        feature_grads[target] = feature_grads[target] + slope * gate_g[pair_index]
    gate_gain_grad, gate_bias_grad = pixel_totals(jnp.stack(gain_terms), jnp.stack(bias_terms))
    message_stack = jnp.stack(message_grads, axis=2).astype(jnp.bfloat16)
    message_ext = extend_rows(message_stack, 1)
    weight_parts = []
    source_partials = [None, None, None, None]
    for pair_index, (source, target) in enumerate(message_pairs):
        weight_parts.append(
            conv_weight_grad(
                stored.features_ext[:, :, source],
                1,
                1,
                message_stack[:, :, pair_index : pair_index + 1],
                masks_one,
            )
        )
        partial_grad = conv_input_grad(
            message_ext[:, :, pair_index : pair_index + 1],
            1,
            1,
            messages_w[pair_index][None],
            masks_one,
        )
        if source_partials[source] is None:
            source_partials[source] = partial_grad
        else:
            source_partials[source] = source_partials[source] + partial_grad
    messages_w_grad = jnp.concatenate(weight_parts, axis=0)
    source_sums = reduce_channels(jnp.stack(source_partials, axis=2))
    features_total = jnp.stack(feature_grads, axis=2) + source_sums
    heads_grad = (features_total * silu_slope(stored.heads_pre)).astype(jnp.bfloat16)
    heads_w_grad = conv_weight_grad(stored.output_ext, 1, 1, heads_grad, masks_one)
    heads_ext = extend_rows(heads_grad, 1)
    output_partial = conv_input_grad(heads_ext, 1, 1, heads_w, masks_one)
    output_total = upstream + reduce_channels(output_partial[:, :, None, :])[:, :, 0, :]
    summed_grad = output_total * silu_slope(stored.summed)
    third_grad, wide_gain_grad, wide_bias_grad = norm_backward(
        summed_grad, stored.third_normed, stored.third_inverse, wide_g, pixel_count
    )
    third_low = third_grad.astype(jnp.bfloat16)
    expand_w_grad = jnp.einsum(
        "rwc,rwo->co", stored.second_full, third_low, preferred_element_type=jnp.float32
    )
    second_partial = jnp.einsum(
        "rwo,co->rwc", third_low, expand_w, preferred_element_type=jnp.float32
    )
    second_act_grad = reduce_channels(second_partial[:, :, None, :])[:, :, 0, :]
    second_grad, second_gain_grad, second_bias_grad = norm_backward(
        second_act_grad * silu_slope(stored.second_norm),
        stored.second_normed,
        stored.second_inverse,
        narrow_gain[1],
        pixel_count,
    )
    second_low = second_grad.astype(jnp.bfloat16)[:, :, None, :]
    dilated_w_grad = conv_weight_grad(stored.first_ext, 2, 2, second_low, masks_two)[0]
    second_ext = extend_rows(second_low, 2)
    first_partial = conv_input_grad(second_ext, 2, 2, dilated_w[None], masks_two)
    first_act_grad = reduce_channels(first_partial[:, :, None, :])[:, :, 0, :]
    first_grad, first_gain_grad, first_bias_grad = norm_backward(
        first_act_grad * silu_slope(stored.first_norm),
        stored.first_normed,
        stored.first_inverse,
        narrow_gain[0],
        pixel_count,
    )
    first_low = first_grad.astype(jnp.bfloat16)
    reduce_w_grad = jnp.einsum(
        "rwc,rwo->co", stored.inputs_full, first_low, preferred_element_type=jnp.float32
    )
    inputs_partial = jnp.einsum(
        "rwo,oc->rwc", first_low, reduce_w, preferred_element_type=jnp.float32
    )
    inputs_grad = reduce_channels(inputs_partial[:, :, None, :])[:, :, 0, :] + summed_grad
    weight_grads = (reduce_w_grad, dilated_w_grad, expand_w_grad, heads_w_grad, messages_w_grad)
    small_grads = (
        jnp.stack([first_gain_grad, second_gain_grad]),
        jnp.stack([first_bias_grad, second_bias_grad]),
        wide_gain_grad,
        wide_bias_grad,
        gate_gain_grad,
        gate_bias_grad,
    )
    return (inputs_grad, weight_grads, small_grads)


def plain_shards(
    features_in,
    w_reduce,
    w_dilated,
    w_expand,
    w_heads,
    w_messages,
    norm_gain,
    norm_bias,
    wide_gain,
    wide_bias,
    gate_gain,
    gate_bias,
    canvas_ids,
    output_cotangent,
    task_cotangents,
):
    row_count = features_in.shape[0]
    col_count = features_in.shape[1]
    pixel_count = float(row_count * col_count * lax.axis_size(BLK))
    masks_one = local_masks(canvas_ids, row_count, 1)
    masks_two = local_masks(canvas_ids, row_count, 2)
    layer_count = w_reduce.shape[0]
    layer_params = []
    for layer_index in range(layer_count):
        layer_params.append(
            (
                w_reduce[layer_index],
                w_dilated[layer_index],
                w_expand[layer_index],
                w_heads[layer_index],
                w_messages[layer_index],
                norm_gain[layer_index],
                norm_bias[layer_index],
                wide_gain[layer_index],
                wide_bias[layer_index],
                gate_gain[layer_index],
                gate_bias[layer_index],
            )
        )
    current = features_in
    stored_list = []
    task_list = []
    for layer_index in range(layer_count):
        current, depth_map, segment_map, stored = layer_forward(
            current, layer_params[layer_index], masks_one, masks_two, pixel_count
        )
        stored_list.append(stored)
        task_list.append(jnp.stack([depth_map, segment_map]).astype(jnp.bfloat16))
    upstream = output_cotangent.astype(jnp.float32)
    weight_list = [None] * layer_count
    small_list = [None] * layer_count
    for layer_index in reversed(range(layer_count)):
        upstream, weight_grads, small_grads = layer_backward(
            stored_list[layer_index],
            upstream,
            task_cotangents[layer_index, 0].astype(jnp.float32),
            task_cotangents[layer_index, 1].astype(jnp.float32),
            layer_params[layer_index],
            masks_one,
            masks_two,
            pixel_count,
        )
        weight_list[layer_index] = weight_grads
        small_list[layer_index] = small_grads
    stacked = [
        jnp.stack([weight_list[layer_index][member] for layer_index in range(layer_count)])
        for member in range(5)
    ]
    weight_sums = weight_totals(stacked[0], stacked[1], stacked[2], stacked[3], stacked[4])
    small_sums = [
        jnp.stack([small_list[layer_index][member] for layer_index in range(layer_count)])
        for member in range(6)
    ]
    return (
        current,
        jnp.stack(task_list),
        upstream,
        weight_sums[0],
        weight_sums[1],
        weight_sums[2],
        weight_sums[3],
        weight_sums[4],
        small_sums[0],
        small_sums[1],
        small_sums[2],
        small_sums[3],
        small_sums[4],
        small_sums[5],
    )


lanes = 128
source_order = ((1, 0, 4), (2, 1, 5), (0, 3), (3, 2))


def whole(shape):
    return pl.BlockSpec(shape, lambda *_: (0,) * len(shape))


def contract_last(left, right):
    return lax.dot_general(
        left, right, (((1,), (1,)), ((), ())), preferred_element_type=jnp.float32
    )


def sigmoid(values):
    return 1.0 / (1.0 + jnp.exp(-values))


def masked(values, bits, place):
    taken = (bits & (1 << place)) != 0
    width = values.shape[1]
    parts = [
        jnp.where(taken, values[:, start : start + lanes], 0.0) for start in range(0, width, lanes)
    ]
    return parts[0] if len(parts) == 1 else jnp.concatenate(parts, axis=1)


MESH = pl.DeviceIdType.MESH
groups = ((1, 2), (0, 3))
targets = (0, 3)
group_pairs = ((0, 4, 1, 5), (3, 2))


def remote(source, target, send_sem, recv_sem, axis, peer):
    return pltpu.make_async_remote_copy(
        src_ref=source,
        dst_ref=target,
        send_sem=send_sem,
        recv_sem=recv_sem,
        device_id={axis: peer},
        device_id_type=MESH,
    )


def comm_params(key):
    return pltpu.CompilerParams(
        vmem_limit_bytes=60 * 2**20, collective_id=key, has_side_effects=True
    )


def announce(targets):
    barrier = pltpu.get_barrier_semaphore()
    for axis, peer in targets:
        pl.semaphore_signal(barrier, inc=1, device_id={axis: peer}, device_id_type=MESH)
    pl.semaphore_wait(barrier, len(targets))


def near_blocks():
    me = lax.axis_index(BLK)

    def turned(bit):
        return me + bit - 2 * bit * lax.rem(me // bit, 2)

    return turned(1), turned(2), turned(4)


def others(axis, count):
    me = lax.axis_index(axis)
    return [lax.rem(me + step, count) for step in range(1, count)]


def round_trip(own_source, target_of, half_of, sems):
    near_send, slot_recv, pass_send, local_sem = sems
    me = lax.axis_index(BLK)
    sibling, *peers = near_blocks()
    far = me + peers[0] - me + peers[1] - me
    own = pltpu.make_async_copy(own_source, target_of(me), local_sem.at[0])

    def near(step, peer):
        return remote(
            own_source, target_of(me), near_send.at[step], slot_recv.at[me], BLK, peer
        )

    def half(side, block, recv_sem, peer):
        part = half_of(block, side)
        return remote(part, part, near_send.at[3 + side], recv_sem, BLK, peer)

    def passing(step, block):
        part = target_of(block)
        return remote(part, part, pass_send.at[step], slot_recv.at[block], BLK, sibling)

    def start():
        own.start()
        for step, peer in enumerate(peers + [sibling]):
            near(step, peer).start()

    def sent_half(side):
        recv_sem = slot_recv.at[peers[0]] if side == 0 else local_sem.at[1]
        return half(side, peers[side], recv_sem, peers[1 - side])

    def middle():
        for side in range(2):
            copy = passing(side, peers[side])
            copy.wait_recv()
            sent_half(side).start()
            copy.start()

    def forward():
        half(0, far, slot_recv.at[far], sibling).wait_recv()
        half(1, far, local_sem.at[1], sibling).wait_recv()
        passing(2, far).start()

    def finish():
        for block in (sibling, sibling + peers[0] - me, sibling + peers[1] - me, sibling + far - me):
            passing(0, block).wait_recv()
        for step, peer in enumerate(peers + [sibling]):
            near(step, peer).wait_send()
        for side in range(2):
            sent_half(side).wait_send()
            passing(side, peers[side]).wait_send()
        passing(2, far).wait_send()
        own.wait()

    return start, middle, forward, finish


def gather_job(source, target, sems, blocks):
    count = source.shape[0] // 2
    return round_trip(
        source,
        lambda block: target.at[block],
        lambda block, side: target.at[block, pl.ds(side * count, count)],
        sems,
    )


def swap_job(source, target, sems, blocks):
    slot_send, slot_recv, _, local_sem = sems
    me = lax.axis_index(BLK)
    width = source.shape[1] // blocks

    def part_of(block):
        return source.at[:, pl.ds(pl.multiple_of(block * width, width), width)]

    own = pltpu.make_async_copy(part_of(me), target.at[me], local_sem.at[0])

    def copy(step, peer, slot):
        return remote(
            part_of(peer), target.at[slot], slot_send.at[step], slot_recv.at[slot], BLK, peer
        )

    def start():
        for step, peer in enumerate(others(BLK, blocks)):
            copy(step, peer, me).start()
        own.start()

    def finish():
        for step, peer in enumerate(others(BLK, blocks)):
            copy(step, peer, peer).wait_recv()
            copy(step, peer, me).wait_send()
        own.wait()

    return start, lambda: None, lambda: None, finish


def half_swap_job(half):
    def job(source, target, sems, blocks):
        count = source.shape[0] // 2
        return swap_job(source.at[pl.ds(half * count, count)], target, sems, blocks)

    return job


def slot_job(source, target, sems, blocks):
    slot_send, slot_recv, _, local_sem = sems
    me = lax.axis_index(BLK)
    own = pltpu.make_async_copy(source.at[me], target.at[me], local_sem.at[0])

    def copy(step, peer, slot):
        return remote(
            source.at[peer], target.at[slot], slot_send.at[step], slot_recv.at[slot], BLK, peer
        )

    def start():
        for step, peer in enumerate(others(BLK, blocks)):
            copy(step, peer, me).start()
        own.start()

    def finish():
        for step, peer in enumerate(others(BLK, blocks)):
            copy(step, peer, peer).wait_recv()
            copy(step, peer, me).wait_send()
        own.wait()

    return start, lambda: None, lambda: None, finish


def line_job(source, target, sems, blocks):
    line_send, line_recv, _, local_sem = sems
    parts = target.shape[0]
    ch = lax.axis_index(CH)
    right, left = lax.rem(ch + 1, parts), lax.rem(ch + parts - 1, parts)
    own = pltpu.make_async_copy(source, target.at[ch], local_sem.at[0])

    def sides(hop):
        return (
            (0, lax.rem(ch + parts - hop, parts), right, ch - hop >= 0, ch < parts - 1),
            (1, lax.rem(ch + hop, parts), left, ch + hop < parts, ch > 0),
        )

    def copy(block, side, hop, peer):
        return remote(
            source if hop == 0 else target.at[block],
            target.at[block],
            line_send.at[side * (parts - 1) + hop],
            line_recv.at[block],
            CH,
            peer,
        )

    def move(hop):
        for side, block, peer, valid, goes in sides(hop):
            if hop > 0:

                @pl.when(valid)
                def _():
                    copy(block, side, hop, peer).wait_recv()

            if hop < parts - 1:

                @pl.when(valid & goes)
                def _():
                    copy(block, side, hop, peer).start()

    def start():
        own.start()
        move(0)

    def middle():
        move(1)

    def forward():
        for hop in range(2, parts - 1):
            move(hop)

    def finish():
        if parts > 2:
            move(parts - 1)
        for hop in range(parts - 1):
            for side, block, peer, valid, goes in sides(hop):

                @pl.when(valid & goes)
                def _():
                    copy(block, side, hop, peer).wait_send()

        own.wait()

    return start, middle, forward, finish


job_kinds = (gather_job, half_swap_job(0), slot_job, line_job, half_swap_job(1))
gather_kind, upper_kind, slot_kind, line_kind, lower_kind = 0, 1, 2, 3, 4


def job_target(kind, shape, dtype, blocks):
    if kind == gather_kind:
        shape = (blocks,) + shape
    elif kind == line_kind:
        shape = (lax.axis_size(CH),) + shape
    elif kind in (upper_kind, lower_kind):
        shape = (blocks, shape[0] // 2, shape[1] // blocks)
    return jax.ShapeDtypeStruct(shape, dtype)


def job_sems(blocks):
    dma = pltpu.SemaphoreType.DMA
    return [dma((blocks,)), dma((blocks,)), dma((blocks,)), dma((2,))]


def job_call(kernel, jobs, blocks, in_specs, out_specs, out_shape, scratch_shapes, **options):
    anywhere = pl.BlockSpec(memory_space=pl.ANY)
    n_in, n_out, n_scratch = len(in_specs), len(out_specs), len(scratch_shapes)
    count = len(jobs)

    def wrapped(*refs):
        ins, refs = refs[:n_in], refs[n_in:]
        sources, refs = refs[:count], refs[count:]
        outs, refs = refs[:n_out], refs[n_out:]
        targets, refs = refs[:count], refs[count:]
        scratch, sems = refs[:n_scratch], refs[n_scratch:]
        running = [
            job_kinds[kind](
                sources[place].at[index[0]] if index else sources[place],
                targets[place],
                sems[4 * place : 4 * place + 4],
                blocks,
            )
            for place, (kind, _, *index) in enumerate(jobs)
        ]
        kernel(running, *ins, *outs, *scratch)

    def call(*operands):
        result = pl.pallas_call(
            wrapped,
            in_specs=list(in_specs) + [anywhere] * count,
            out_specs=list(out_specs) + [anywhere] * count,
            out_shape=list(out_shape) + [
                job_target(kind, source.shape[len(index) :], source.dtype, blocks)
                for kind, source, *index in jobs
            ],
            scratch_shapes=list(scratch_shapes) + job_sems(blocks) * count,
            **options,
        )(*operands, *[job[1] for job in jobs])
        return result[:n_out], result[n_out:]

    return call


def stripe_job(wr_ref, we_ref, layer, mine, sems, blocks, parts):
    part_send, part_recv, local_sem = sems
    _, mid, feat = wr_ref.shape
    _, narrow, wide = we_ref.shape
    blk, ch = lax.axis_index(BLK), lax.axis_index(CH)

    def cut(index, size):
        return pl.ds(pl.multiple_of(index * size, size), size)

    def source(array):
        if array == 0:
            return wr_ref.at[layer, :, cut(blk, feat // blocks)]
        return we_ref.at[layer, cut(blk, narrow // blocks), :]

    def share(array, part):
        if array == 0:
            return mine[0].at[cut(part, mid), :]
        return mine[1].at[:, cut(part, wide)]

    def own(array):
        return pltpu.make_async_copy(source(array), share(array, ch), local_sem.at[array])

    def copy(array, step, peer, slot):
        return remote(
            source(array),
            share(array, slot),
            part_send.at[array, step],
            part_recv.at[array, slot],
            CH,
            peer,
        )

    def start():
        for array in range(2):
            own(array).start()
            for step, peer in enumerate(others(CH, parts)):
                copy(array, step, peer, ch).start()

    def finish():
        for array in range(2):
            for step, peer in enumerate(others(CH, parts)):
                copy(array, step, peer, peer).wait_recv()
            own(array).wait()
            for step, peer in enumerate(others(CH, parts)):
                copy(array, step, peer, ch).wait_send()

    return start, finish


def stripe_sems(parts):
    dma = pltpu.SemaphoreType.DMA
    return [dma((2, parts)), dma((2, parts)), dma((2,))]


def stripe_shapes(parts, blocks, reduce_w, expand_w):
    _, mid, feat = reduce_w.shape
    narrow = mid * parts
    return [
        jax.ShapeDtypeStruct((narrow, feat // blocks), reduce_w.dtype),
        jax.ShapeDtypeStruct((narrow // blocks, feat), expand_w.dtype),
    ]


def spread_jobs(mine, fulls, sems, blocks):
    half_rows = mine[0].shape[0] // 2
    width, height = mine[0].shape[1], mine[1].shape[0]
    half_cols = mine[1].shape[1] // 2

    def cut(index, size):
        return pl.ds(pl.multiple_of(index * size, size), size)

    return [
        round_trip(
            mine[0],
            lambda block: fulls[0].at[:, cut(block, width)],
            lambda block, side: fulls[0].at[pl.ds(side * half_rows, half_rows), cut(block, width)],
            sems[:4],
        ),
        round_trip(
            mine[1],
            lambda block: fulls[1].at[cut(block, height), :],
            lambda block, side: fulls[1].at[cut(block, height), pl.ds(side * half_cols, half_cols)],
            sems[4:],
        ),
    ]


def prologue_kernel(
    blocks,
    parts,
    feat_ref,
    wr_ref,
    we_ref,
    *refs,
):
    small_refs, ids_ref, cur_ref, mine_r, mine_e = refs[:4], *refs[4:8]
    full_r, full_e, small_outs, own_ref, all_ref = *refs[8:10], refs[10:14], *refs[14:16]
    line_send, line_recv, small_send, small_recv, local_sem, *sems = refs[16:]
    pixels, wide = feat_ref.shape
    blk, ch = lax.axis_index(BLK), lax.axis_index(CH)
    smalls = tuple(zip(small_refs, small_outs))

    def lane_part(index):
        return cur_ref.at[:, pl.ds(pl.multiple_of(index * wide, wide), wide)]

    start, gathered = stripe_job(wr_ref, we_ref, 0, (mine_r, mine_e), sems[:3], blocks, parts)
    jobs = spread_jobs((mine_r, mine_e), (full_r, full_e), sems[3:], blocks)
    own = pltpu.make_async_copy(feat_ref, lane_part(ch), local_sem.at[0])
    own.start()
    announce(
        [(CH, peer) for peer in others(CH, parts)] + [(BLK, peer) for peer in near_blocks()]
    )
    start()

    right, left = lax.rem(ch + 1, parts), lax.rem(ch + parts - 1, parts)

    def sides(hop):
        return (
            (0, lax.rem(ch + parts - hop, parts), right, ch - hop >= 0, ch < parts - 1),
            (1, lax.rem(ch + hop, parts), left, ch + hop < parts, ch > 0),
        )

    def line_copy(block, side, hop, peer):
        return remote(
            feat_ref if hop == 0 else lane_part(block),
            lane_part(block),
            line_send.at[side, hop],
            line_recv.at[block],
            CH,
            peer,
        )

    def line_hop(hop):
        for side, block, peer, valid, goes in sides(hop):
            if hop > 0:

                @pl.when(valid)
                def _():
                    line_copy(block, side, hop, peer).wait_recv()

            if hop < parts - 1:

                @pl.when(valid & goes)
                def _():
                    line_copy(block, side, hop, peer).start()

    def small_copy(place, step, peer, slot):
        source, target = smalls[place]
        return remote(
            source,
            target.at[slot],
            small_send.at[place, step],
            small_recv.at[place, slot],
            CH,
            peer,
        )

    def small_own(place):
        source, target = smalls[place]
        return pltpu.make_async_copy(source, target.at[ch], local_sem.at[1 + place])

    line_hop(0)
    for place in range(4):
        small_own(place).start()
        for step, peer in enumerate(others(CH, parts)):
            small_copy(place, step, peer, ch).start()
    gathered()
    for job in jobs:
        job[0]()

    rows = own_ref.shape[1] // lanes
    lane = lax.broadcasted_iota(jnp.int32, (1, lanes), 1)

    def moved(values, step):
        turned = values if step == 0 else pltpu.roll(values, (lanes - step) % lanes, 1)
        return jnp.where((lane + step >= 0) & (lane + step < lanes), turned, -2)

    def spread(target, row, bits):
        block = jnp.broadcast_to(bits.astype(jnp.float32), (lanes, lanes)).T
        target[pl.ds(pl.multiple_of(row * lanes, lanes), lanes), :] = block.astype(jnp.int32)

    def own_row(row, state):
        place = 2 + blk * rows + row
        for word, reach in enumerate((1, 2)):
            bits = jnp.zeros((1, lanes), jnp.int32)
            for tap, (row_step, col_step) in enumerate(tap_offsets):
                a, b = row_step * reach, col_step * reach
                taken = moved(ids_ref[place], -b) == ids_ref[place + a]
                bits = bits | jnp.where(taken, 1 << tap, 0)
                taken = moved(ids_ref[place - a], -b) == ids_ref[place]
                bits = bits | jnp.where(taken, 1 << (9 + tap), 0)
            spread(own_ref.at[word], row, bits)
        return state

    lax.fori_loop(0, rows, own_row, 0)

    def any_row(row, state):
        bits = jnp.zeros((1, lanes), jnp.int32)
        for tap, (row_step, col_step) in enumerate(tap_offsets):
            taken = moved(ids_ref[2 + row + row_step], col_step) == ids_ref[2 + row]
            bits = bits | jnp.where(taken, 1 << tap, 0)
        spread(all_ref, row, bits)
        return state

    lax.fori_loop(0, ids_ref.shape[0] - 4, any_row, 0)
    for hop in range(1, parts):
        line_hop(hop)
        if hop <= 2:
            for job in jobs:
                job[hop]()
    if parts == 2:
        for job in jobs:
            job[2]()
    for job in jobs:
        job[3]()
    for hop in range(parts - 1):
        for side, block, peer, valid, goes in sides(hop):

            @pl.when(valid & goes)
            def _():
                line_copy(block, side, hop, peer).wait_send()

    for place in range(4):
        for step, peer in enumerate(others(CH, parts)):
            small_copy(place, step, peer, peer).wait_recv()
            small_copy(place, step, peer, ch).wait_send()
        small_own(place).wait()
    own.wait()


def prologue(blocks, parts, features, reduce_w, expand_w, terms, canvas_ids):
    layers, mid, feat = reduce_w.shape
    pixels, wide = features.shape
    narrow = mid * parts
    f32, low = jnp.float32, jnp.bfloat16
    shape = jax.ShapeDtypeStruct
    ids = jnp.pad(canvas_ids, ((2, 2), (0, 0)), constant_values=-1)[:, None]
    anywhere = pl.BlockSpec(memory_space=pl.ANY)
    inside = pl.BlockSpec(memory_space=pltpu.VMEM)
    dma = pltpu.SemaphoreType.DMA
    return pl.pallas_call(
        functools.partial(prologue_kernel, blocks, parts),
        in_specs=[anywhere] * 7 + [inside],
        out_specs=[anywhere] * 9 + [inside] * 2,
        out_shape=[
            shape((pixels, feat), low),
            *stripe_shapes(parts, blocks, reduce_w, expand_w),
            shape((narrow, feat), low),
            shape((narrow, feat), low),
            *[shape((parts,) + term.shape, f32) for term in terms],
            shape((2, pixels, lanes), jnp.int32),
            shape((pixels * blocks, lanes), jnp.int32),
        ],
        scratch_shapes=[
            dma((2, parts)),
            dma((parts,)),
            dma((4, parts)),
            dma((4, parts)),
            dma((5,)),
        ]
        + stripe_sems(parts)
        + job_sems(blocks) * 2,
        compiler_params=comm_params(5),
        cost_estimate=pl.CostEstimate(flops=10**6, bytes_accessed=10**8, transcendentals=0),
    )(features, reduce_w, expand_w, *terms, ids)


def greet_line(blocks):
    barrier = pltpu.get_barrier_semaphore()
    me = lax.axis_index(BLK)
    for peer in (lax.rem(me + 1, blocks), lax.rem(me + blocks - 1, blocks)):
        pl.semaphore_signal(barrier, inc=1, device_id={BLK: peer}, device_id_type=MESH)
    pl.semaphore_wait(barrier, 2)


def greet_blocks(blocks):
    announce([(BLK, peer) for peer in others(BLK, blocks)])


def edge_copies(main_ref, low_ref, high_ref, edge, send_sem, recv_sem, blocks):
    me = lax.axis_index(BLK)
    lead = (slice(None),) * (len(main_ref.shape) - 2)
    pixels = main_ref.shape[-2]
    up = remote(
        main_ref.at[lead + (pl.ds(pixels - edge, edge),)],
        low_ref,
        send_sem.at[0],
        recv_sem.at[0],
        BLK,
        lax.rem(me + 1, blocks),
    )
    down = remote(
        main_ref.at[lead + (pl.ds(0, edge),)],
        high_ref,
        send_sem.at[1],
        recv_sem.at[1],
        BLK,
        lax.rem(me + blocks - 1, blocks),
    )

    def start():
        @pl.when(me < blocks - 1)
        def _():
            up.start()

        @pl.when(me > 0)
        def _():
            down.start()

    def finish(zero=True):
        @pl.when(me > 0)
        def _():
            up.wait_recv()
            down.wait_send()

        @pl.when(me < blocks - 1)
        def _():
            down.wait_recv()
            up.wait_send()

        if zero:

            @pl.when(me == 0)
            def _():
                low_ref[...] = jnp.zeros(low_ref.shape, low_ref.dtype)

            @pl.when(me == blocks - 1)
            def _():
                high_ref[...] = jnp.zeros(high_ref.shape, high_ref.dtype)

    return start, finish


def heads_forward_kernel(blocks, fetch, jobs, main_ref, w_ref, mask_ref, *refs):
    if fetch:
        mine_r, mine_e, *refs = refs
    pre_ref, act_ref, ends_ref, *refs = refs
    if fetch:
        full_r, full_e, *refs = refs
    ext_ref, z_ref, local_sem, halo_send, halo_recv, *sems = refs
    step = pl.program_id(0)
    head_count, pixels, mid = pre_ref.shape
    cols = (ext_ref.shape[0] - pixels) // 2
    feat = ext_ref.shape[1]
    start, finish = edge_copies(
        main_ref,
        ext_ref.at[pl.ds(0, cols)],
        ext_ref.at[pl.ds(cols + pixels, cols)],
        cols,
        halo_send,
        halo_recv,
        blocks,
    )
    own = pltpu.make_async_copy(main_ref, ext_ref.at[pl.ds(cols, pixels)], local_sem.at[0])
    if fetch:
        jobs = jobs + spread_jobs((mine_r, mine_e), (full_r, full_e), sems, blocks)

    @pl.when(step == 0)
    def _():
        own.start()
        if jobs:
            greet_blocks(blocks)
        else:
            greet_line(blocks)
        start()
        for job in jobs:
            job[0]()
        own.wait()

    @pl.when(step == 3)
    def _():
        finish()

    if jobs:

        @pl.when(step == 7)
        def _():
            for job in jobs:
                job[1]()

    row_step = jnp.where(step < 3, 1, jnp.where(step < 6, 0, 2))
    col_step = lax.rem(step, 3)
    window = ext_ref[pl.ds(pl.multiple_of(row_step * cols, cols), pixels), :]
    product = contract_last(window, w_ref[0].reshape(head_count * mid, feat))
    product = masked(product, mask_ref[0], tap_at(step))

    @pl.when(step < 3)
    def _():
        z_ref[col_step] = product

    @pl.when(step >= 3)
    def _():
        z_ref[col_step] += product

    @pl.when(step == 8)
    def _():
        for head in range(head_count):
            part = slice(head * mid, (head + 1) * mid)
            total = (
                z_ref[1, :, part]
                + pltpu.roll(z_ref[0, :, part], 1, 0)
                + pltpu.roll(z_ref[2, :, part], pixels - 1, 0)
            )
            pre_ref[head] = total
            value = (total * sigmoid(total)).astype(jnp.bfloat16)
            act_ref[head] = value
            if head in targets:
                ends_ref[targets.index(head)] = value
        for job in jobs:
            job[2]()
        for job in jobs:
            job[3]()


def tap_at(step):
    return jnp.where(step < 3, step + 3, jnp.where(step < 6, step - 3, step))


def heads_forward(blocks, layer, jobs, cols, main, weights, mask, mine):
    _, head_count, _, mid, feat = weights.shape
    pixels = main.shape[0]
    f32, low = jnp.float32, jnp.bfloat16
    shape = jax.ShapeDtypeStruct
    anywhere = pl.BlockSpec(memory_space=pl.ANY)
    dma = pltpu.SemaphoreType.DMA
    return job_call(
        functools.partial(heads_forward_kernel, blocks, bool(mine)),
        jobs,
        blocks,
        grid=(9,),
        in_specs=[
            anywhere,
            pl.BlockSpec((1, head_count, 1, mid, feat), lambda t: (layer, 0, tap_at(t), 0, 0)),
            pl.BlockSpec((1, pixels, lanes), lambda t: (0, 0, 0)),
        ]
        + [anywhere] * len(mine),
        out_specs=[whole((head_count, pixels, mid))] * 2
        + [whole((2, pixels, mid))]
        + [anywhere] * len(mine),
        out_shape=[
            shape((head_count, pixels, mid), f32),
            shape((head_count, pixels, mid), low),
            shape((2, pixels, mid), low),
        ]
        + [shape((mine[0].shape[0], feat), low) for _ in mine],
        scratch_shapes=[
            pltpu.VMEM((pixels + 2 * cols, feat), low),
            pltpu.VMEM((3, pixels, head_count * mid), f32),
            dma((1,)),
            dma((2,)),
            dma((2,)),
        ]
        + (job_sems(blocks) * 2 if mine else []),
        compiler_params=comm_params(6 + layer),
        cost_estimate=pl.CostEstimate(
            flops=18 * pixels * head_count * mid * feat,
            bytes_accessed=18 * head_count * mid * feat,
            transcendentals=0,
        ),
    )(main, weights, mask, *mine)


def fill_taps(im_ref, slot, grad, bits, pixels, cols, dilation):
    rows, mid = grad.shape
    wide = grad.astype(jnp.float32)
    shifted_by = (pltpu.roll(wide, rows - dilation, 0), wide, pltpu.roll(wide, dilation, 0))
    for tap, (row_step, col_step) in enumerate(tap_offsets):
        start = (1 - row_step) * dilation * cols
        part = shifted_by[col_step + 1][start : start + pixels]
        im_ref[slot, :, tap * mid : (tap + 1) * mid] = masked(part, bits, 9 + tap).astype(
            jnp.bfloat16
        )


def messages_kernel(
    blocks,
    layer,
    ahead,
    jobs,
    feat_ref,
    w_hbm,
    cots_ref,
    gain_ref,
    bias_ref,
    mask_ref,
    maps_ref,
    local_ref,
    sums_ref,
    part_ref,
    values_ref,
    pack_ref,
    main_ref,
    low_ref,
    high_ref,
    cot_low,
    cot_high,
    w_ref,
    lhs_ref,
    z_ref,
    im_ref,
    grad_ref,
    *sems,
):
    w_sem, local_sem, halo_send, halo_recv, cot_send, cot_recv, *sems = sems
    parts, heads, pixels, mid = feat_ref.shape
    cot_ref = cots_ref.at[layer]
    cols = low_ref.shape[2]
    pairs = w_ref.shape[0]
    me, ch = lax.axis_index(BLK), lax.axis_index(CH)
    low = jnp.bfloat16
    loads = [
        pltpu.make_async_copy(w_hbm.at[layer, pair], w_ref.at[pair], w_sem.at[pair])
        for pair in range(pairs)
    ]
    main_copy = pltpu.make_async_copy(feat_ref, main_ref, local_sem.at[0])
    main_copy.start()
    for pair in (0, 4, 1, 5, 3, 2):
        loads[pair].start()
    greet(blocks, parts)
    early, jobs = jobs[:ahead], jobs[ahead:]
    for job in early:
        job[0]()
    start, finish = edge_copies(feat_ref, low_ref, high_ref, cols, halo_send, halo_recv, blocks)
    start()
    cot_start, cot_finish = edge_copies(
        cot_ref, cot_low, cot_high, cols, cot_send, cot_recv, blocks
    )
    cot_start()
    for job in jobs:
        job[0]()
    main_copy.wait()
    size = parts * mid // blocks
    for block in range(blocks):
        part, first = block * size // mid, block * size % mid
        for index, (one, two) in enumerate(groups):
            (pack_ref if sems else values_ref)[block, index] = jnp.concatenate(
                [main_ref[part, one][:, first : first + size], main_ref[part, two][:, first : first + size]],
                axis=1,
            )
    if sems:
        jobs = jobs + [slot_job(pack_ref, values_ref, sems, blocks)]
        jobs[-1][0]()
    for source in range(heads):
        for part in range(parts):
            lhs_ref[source, cols : cols + pixels, part * mid : (part + 1) * mid] = main_ref[part, source]
    order = (0, 4, 1, 5, 3, 2)
    bits = mask_ref[0]

    def taps(pair, row_step):
        source = message_pairs[pair][0]
        product = contract_last(
            lhs_ref[source, row_step * cols : row_step * cols + pixels, :],
            w_ref[pair, 3 * row_step : 3 * row_step + 3].reshape(3 * mid, parts * mid),
        )
        for col_step in range(3):
            value = masked(
                product[:, col_step * mid : (col_step + 1) * mid], bits, row_step * 3 + col_step
            )
            if row_step == 1:
                z_ref[pair, col_step] = value
            else:
                z_ref[pair, col_step] += value

    for pair in order:
        loads[pair].wait()
        taps(pair, 1)
    finish()
    cot_finish()
    for source in range(heads):
        for part in range(parts):
            chan = slice(part * mid, (part + 1) * mid)
            lhs_ref[source, 0:cols, chan] = low_ref[part, source]
            lhs_ref[source, cols + pixels :, chan] = high_ref[part, source]
    for pair in order:
        taps(pair, 0)
        taps(pair, 2)
    for job in early:
        job[1]()
    values = {}
    cots = {}
    for place, target in enumerate((0, 3)):
        values[target] = main_ref[ch, target].astype(jnp.float32)
        cots[target] = cot_ref[place].astype(jnp.float32)
    for place, target in enumerate((0, 3)):
        value, cot = values[target], cots[target]
        total, slopes = value, cot
        for pair in range(pairs):
            if message_pairs[pair][1] != target:
                continue
            message = (
                z_ref[pair, 1]
                + pltpu.roll(z_ref[pair, 0], 1, 0)
                + pltpu.roll(z_ref[pair, 2], pixels - 1, 0)
            )
            gain, bias = gain_ref[layer, pair : pair + 1], bias_ref[layer, pair : pair + 1]
            gate = sigmoid(gain * value + bias)
            total = total + gate * message
            grad_ref[pair] = (cot * gate).astype(low)
            slope = cot * message * gate * (1.0 - gate)
            sums_ref[pair : pair + 1] = jnp.sum(slope * value, axis=0, keepdims=True)
            sums_ref[pairs + pair : pairs + pair + 1] = jnp.sum(slope, axis=0, keepdims=True)
            slopes = slopes + slope * gain
        maps_ref[place] = total.astype(low)
        local_ref[place] = slopes

    for job in jobs:
        job[1]()

    def product_of(pair, slot):
        source, target = message_pairs[pair]
        place = 0 if target == 0 else 1
        gain, bias = gain_ref[layer, pair : pair + 1], bias_ref[layer, pair : pair + 1]

        def border(cot, feat):
            return (
                cot[place].astype(jnp.float32)
                * sigmoid(gain * feat[ch, target].astype(jnp.float32) + bias)
            ).astype(low)

        grad = jnp.concatenate(
            [border(cot_low, low_ref), grad_ref[pair], border(cot_high, high_ref)], axis=0
        )
        fill_taps(im_ref, slot, grad, bits, pixels, cols, 1)
        return jnp.dot(
            im_ref[slot],
            w_ref[pair].reshape(9 * mid, parts * mid),
            preferred_element_type=jnp.float32,
        )

    for count, (source, *members) in enumerate(source_order):
        if count == 2:
            for job in early:
                job[2]()
        total = product_of(members[0], 0)
        for pair in members[1:]:
            total = total + product_of(pair, 1)
        for part in range(parts):
            part_ref[part, source] = total[:, part * mid : (part + 1) * mid].astype(low)
    for job in jobs:
        job[2]()
    for job in early + jobs:
        job[3]()


def messages_both(blocks, layer, jobs, ahead, send, cols, features, weights, cotangents, gains, biases, mask):
    parts, heads, pixels, mid = features.shape
    pairs = weights.shape[1]
    narrow = parts * mid
    f32, low = jnp.float32, jnp.bfloat16
    shape = jax.ShapeDtypeStruct
    anywhere = pl.BlockSpec(memory_space=pl.ANY)
    inside = pl.BlockSpec(memory_space=pltpu.VMEM)
    dma = pltpu.SemaphoreType.DMA
    wide = 2 * narrow // blocks
    values = shape((blocks, 2, pixels, wide), low)
    return job_call(
        functools.partial(messages_kernel, blocks, layer, ahead),
        jobs,
        blocks,
        in_specs=[anywhere, anywhere] + [inside] * 4,
        out_specs=[inside] * 4 + [anywhere if send else inside],
        out_shape=[
            shape((2, pixels, mid), low),
            shape((2, pixels, mid), f32),
            shape((2 * pairs, mid), f32),
            shape((parts, heads, pixels, mid), low),
            values,
        ],
        scratch_shapes=[
            pltpu.VMEM(values.shape if send else (8, lanes), low),
            pltpu.VMEM((parts, heads, pixels, mid), low),
            pltpu.VMEM((parts, heads, cols, mid), low),
            pltpu.VMEM((parts, heads, cols, mid), low),
            pltpu.VMEM((2, cols, mid), low),
            pltpu.VMEM((2, cols, mid), low),
            pltpu.VMEM((pairs, 9, mid, narrow), low),
            pltpu.VMEM((heads, pixels + 2 * cols, narrow), low),
            pltpu.VMEM((pairs, 3, pixels, mid), f32),
            pltpu.VMEM((2, pixels, 9 * mid), low),
            pltpu.VMEM((pairs, pixels, mid), low),
            dma((pairs,)),
            dma((1,)),
            dma((2,)),
            dma((2,)),
            dma((2,)),
            dma((2,)),
        ]
        + (job_sems(blocks) if send else []),
        compiler_params=comm_params(10 + layer),
        cost_estimate=pl.CostEstimate(
            flops=36 * pixels * pairs * mid * narrow,
            bytes_accessed=18 * pairs * mid * narrow,
            transcendentals=0,
        ),
    )(features, weights, cotangents, gains, biases, mask)


def heads_backward_kernel(
    blocks,
    jobs,
    main_ref,
    w_ref,
    mask_ref,
    out_ref,
    low_ref,
    high_ref,
    im_ref,
    halo_send,
    halo_recv,
):
    step = pl.program_id(0)
    head_count, pixels, mid = main_ref.shape
    cols = low_ref.shape[1]

    @pl.when(step == 0)
    def _():
        start, finish = edge_copies(main_ref, low_ref, high_ref, cols, halo_send, halo_recv, blocks)
        if jobs:
            greet_blocks(blocks)
        else:
            greet_line(blocks)
        start()
        for job in jobs:
            job[0]()
        finish()
        for head in range(head_count):
            grad = jnp.concatenate([low_ref[head], main_ref[head], high_ref[head]], axis=0)
            fill_taps(im_ref, head, grad, mask_ref[0], pixels, cols, 1)

    total = None
    for head in range(head_count):
        product = jnp.dot(
            im_ref[head],
            w_ref[0, head].reshape(9 * mid, w_ref.shape[4]),
            preferred_element_type=jnp.float32,
        )
        total = product if total is None else total + product
    out_ref[0] = total.astype(jnp.bfloat16)

    if jobs:

        @pl.when(step == pl.num_programs(0) - 1)
        def _():
            for part in (1, 2, 3):
                for job in jobs:
                    job[part]()


def heads_backward(blocks, layer, jobs, cols, main, weights, mask, parts):
    _, head_count, taps, mid, feat = weights.shape
    pixels = main.shape[1]
    width = feat // parts
    dma = pltpu.SemaphoreType.DMA
    return job_call(
        functools.partial(heads_backward_kernel, blocks),
        jobs,
        blocks,
        grid=(parts,),
        in_specs=[
            whole(main.shape),
            pl.BlockSpec((1, head_count, taps, mid, width), lambda j: (layer, 0, 0, 0, j)),
            pl.BlockSpec((1, pixels, lanes), lambda j: (0, 0, 0)),
        ],
        out_specs=[pl.BlockSpec((1, pixels, width), lambda j: (j, 0, 0))],
        out_shape=[jax.ShapeDtypeStruct((parts, pixels, width), jnp.bfloat16)],
        scratch_shapes=[
            pltpu.VMEM((head_count, cols, mid), jnp.bfloat16),
            pltpu.VMEM((head_count, cols, mid), jnp.bfloat16),
            pltpu.VMEM((head_count, pixels, taps * mid), jnp.bfloat16),
            dma((2,)),
            dma((2,)),
        ],
        compiler_params=comm_params(20 + layer),
        cost_estimate=pl.CostEstimate(
            flops=18 * pixels * head_count * mid * feat,
            bytes_accessed=18 * head_count * mid * feat,
            transcendentals=0,
        ),
    )(main, weights, mask)


class WeightChunks:
    def __init__(self, blocks, layer, sources, gates, buffers, accs, lhs, sems):
        self.blocks, self.layer = blocks, layer
        (self.mv, self.cot, self.ends, self.hv_up, self.hv_low, self.hg, self.bits) = sources
        self.gain, self.bias = gates
        (self.mv_buf, self.cot_buf, self.ends_buf, self.hv_buf, self.hg_buf, self.bits_buf) = buffers
        self.accs, self.lhs, self.sems = accs, lhs, sems
        self.done = 0
        self.pixels = 2 * self.hv_up.shape[1]

    def copies(self, heads, index):
        pixels, last = self.pixels, self.blocks - 1
        before, after = jnp.maximum(index - 1, 0), jnp.minimum(index + 1, last)
        slot = lax.rem(index, 2)
        buffer = self.hv_buf if heads else self.mv_buf
        if heads:
            half = pixels // 2
            pairs = [
                (
                    self.hv_low.at[before, pl.ds(half - lanes, lanes)],
                    buffer.at[slot, pl.ds(0, lanes)],
                ),
                (self.hv_up.at[index], buffer.at[slot, pl.ds(lanes, half)]),
                (self.hv_low.at[index], buffer.at[slot, pl.ds(lanes + half, half)]),
                (
                    self.hv_up.at[after, pl.ds(0, lanes)],
                    buffer.at[slot, pl.ds(lanes + pixels, lanes)],
                ),
            ]
        else:
            every = slice(None)
            pairs = [
                (
                    self.mv.at[before, every, pl.ds(pixels - lanes, lanes)],
                    buffer.at[slot, every, pl.ds(0, lanes)],
                ),
                (self.mv.at[index], buffer.at[slot, every, pl.ds(lanes, pixels)]),
                (
                    self.mv.at[after, every, pl.ds(0, lanes)],
                    buffer.at[slot, every, pl.ds(lanes + pixels, lanes)],
                ),
            ]
        pairs.append(
            (
                self.bits.at[pl.ds(pl.multiple_of(index * pixels, pixels), pixels)],
                self.bits_buf.at[slot],
            )
        )
        if heads:
            pairs.append((self.hg.at[index], self.hg_buf.at[slot]))
        else:
            pairs.append((self.cot.at[index], self.cot_buf.at[slot]))
            pairs.append((self.ends.at[index], self.ends_buf.at[slot]))
        return [
            pltpu.make_async_copy(source, target, self.sems.at[slot, place])
            for place, (source, target) in enumerate(pairs)
        ]

    def fetch(self, heads, index):
        for copy in self.copies(heads, index):
            copy.start()

    def begin(self):
        for acc in self.accs:
            acc[...] = jnp.zeros(acc.shape, acc.dtype)
        self.fetch(False, 0)

    def add(self, heads, index):
        slot = lax.rem(index, 2)
        pixels = self.pixels
        for copy in self.copies(heads, index):
            copy.wait()

        @pl.when(index + 1 < self.blocks)
        def _():
            self.fetch(heads, index + 1)

        if not heads:

            @pl.when(index + 1 == self.blocks)
            def _():
                self.fetch(True, 0)

        bits = self.bits_buf[slot]
        for place, members in enumerate((tuple(range(4)),) if heads else group_pairs):
            window = (self.hv_buf[slot] if heads else self.mv_buf[slot, place]).astype(jnp.float32)
            size, chans = window.shape
            shifted_by = (pltpu.roll(window, 1, 0), window, pltpu.roll(window, size - 1, 0))
            for tap, (row_step, col_step) in enumerate(tap_offsets):
                top = (1 + row_step) * lanes
                part = shifted_by[col_step + 1][top : top + pixels]
                self.lhs[:, tap * chans : (tap + 1) * chans] = masked(part, bits, tap).astype(
                    jnp.bfloat16
                )
            if heads:
                grads = [self.hg_buf[slot, member] for member in members]
            else:
                grads = [self.message_grad(slot, pair) for pair in members]
            acc = self.accs[2] if heads else self.accs[place]
            acc[...] += lax.dot_general(
                self.lhs[:, : 9 * chans],
                jnp.concatenate(grads, axis=1),
                (((0,), (0,)), ((), ())),
                preferred_element_type=jnp.float32,
            )

    def message_grad(self, slot, pair):
        place = targets.index(message_pairs[pair][1])
        gain = self.gain[self.layer, pair : pair + 1]
        bias = self.bias[self.layer, pair : pair + 1]
        gate = sigmoid(gain * self.ends_buf[slot, place].astype(jnp.float32) + bias)
        return (self.cot_buf[slot, place].astype(jnp.float32) * gate).astype(jnp.bfloat16)

    def run(self, count):
        while count:
            heads = self.done >= self.blocks
            start = self.done % self.blocks
            size = min(count, self.blocks - start)

            def step(index, state):
                self.add(heads, index)
                return state

            lax.fori_loop(start, start + size, step, 0)
            self.done += size
            count -= size


def exchange_kernel(blocks, jobs, done_ref):
    greet_blocks(blocks)
    for part in range(4):
        for job in jobs:
            job[part]()
    done_ref[...] = jnp.zeros(done_ref.shape, done_ref.dtype)


def exchange(blocks, jobs):
    _, moved = job_call(
        functools.partial(exchange_kernel, blocks),
        jobs,
        blocks,
        in_specs=[],
        out_specs=[pl.BlockSpec(memory_space=pltpu.VMEM)],
        out_shape=[jax.ShapeDtypeStruct((8, lanes), jnp.float32)],
        scratch_shapes=[],
        compiler_params=comm_params(30),
        cost_estimate=pl.CostEstimate(flops=10**6, bytes_accessed=10**8, transcendentals=0),
    )()
    return moved


def heads_store(out_ref, acc_ref):
    head_count, taps, chans, mid = out_ref.shape
    for head in range(head_count):
        for tap in range(taps):
            out_ref[head, tap] = acc_ref[
                tap * chans : (tap + 1) * chans, head * mid : (head + 1) * mid
            ]


def messages_store(out_ref, acc_refs):
    _, taps, size, mid = out_ref.shape
    for index, members in enumerate(group_pairs):
        for place, pair in enumerate(members):
            side = groups[index].index(message_pairs[pair][0])
            for tap in range(taps):
                start = (2 * tap + side) * size
                out_ref[pair, tap] = acc_refs[index][
                    start : start + size, place * mid : (place + 1) * mid
                ]


def greet(blocks, parts):
    barrier = pltpu.get_barrier_semaphore()
    blk, ch = lax.axis_index(BLK), lax.axis_index(CH)
    for step in range(1, blocks):
        pl.semaphore_signal(
            barrier, inc=1, device_id={BLK: lax.rem(blk + step, blocks)}, device_id_type=MESH
        )
    for step in range(1, parts):
        pl.semaphore_signal(
            barrier, inc=1, device_id={CH: lax.rem(ch + step, parts)}, device_id_type=MESH
        )
    pl.semaphore_wait(barrier, blocks + parts - 2)


def send_slots(source_of, target_ref, send_sem, recv_sem, axis, count):
    me = lax.axis_index(axis)
    copies = []
    for step in range(1, count):
        peer = lax.rem(me + step, count)
        copy = pltpu.make_async_remote_copy(
            src_ref=source_of(peer),
            dst_ref=target_ref.at[me],
            send_sem=send_sem.at[step],
            recv_sem=recv_sem.at[me],
            device_id={axis: peer},
            device_id_type=MESH,
        )
        copy.start()
        copies.append(copy)

    def finish():
        for step in range(1, count):
            peer = lax.rem(me + step, count)
            pltpu.make_async_remote_copy(
                src_ref=target_ref.at[peer],
                dst_ref=target_ref.at[peer],
                send_sem=send_sem.at[step],
                recv_sem=recv_sem.at[peer],
                device_id={axis: peer},
                device_id_type=MESH,
            ).wait_recv()
        for copy in copies:
            copy.wait_send()

    return finish


def block_totals(first, second, stat_ref, send_sem, recv_sem, blocks, meanwhile=None):
    me = lax.axis_index(BLK)
    stat_ref[me, 0:1] = first
    stat_ref[me, 1:2] = second
    finish = send_slots(lambda _: stat_ref.at[me], stat_ref, send_sem, recv_sem, BLK, blocks)
    if meanwhile is not None:
        meanwhile()
    finish()
    total = stat_ref[0]
    for block in range(1, blocks):
        total = total + stat_ref[block]
    return total[0:1], total[1:2]


def fold(values):
    rows, width = values.shape
    return values.reshape(rows // 8, 8, width).sum(axis=0)


def row_loop(rows, block, body, carry):
    def step(index, state):
        return body(pl.ds(pl.multiple_of(index * block, block), block), state)

    return lax.fori_loop(0, rows // block, step, carry)


def moments(ref, block):
    rows, width = ref.shape

    def body(part, state):
        values = ref[part, :]
        return state[0] + fold(values), state[1] + fold(values * values)

    zero = jnp.zeros((8, width), jnp.float32)
    total, square = row_loop(rows, block, body, (zero, zero))
    return total.sum(axis=0, keepdims=True), square.sum(axis=0, keepdims=True)


def halo_copies(ref, edge, pixels, send_sem, recv_sem, blocks):
    me = lax.axis_index(BLK)

    def copy(source, target, side, peer):
        return pltpu.make_async_remote_copy(
            src_ref=ref.at[pl.ds(source, edge)],
            dst_ref=ref.at[pl.ds(target, edge)],
            send_sem=send_sem.at[side],
            recv_sem=recv_sem.at[side],
            device_id={BLK: peer},
            device_id_type=MESH,
        )

    up = copy(pixels, 0, 0, lax.rem(me + 1, blocks))
    down = copy(edge, edge + pixels, 1, lax.rem(me + blocks - 1, blocks))

    @pl.when(me < blocks - 1)
    def _():
        up.start()

    @pl.when(me > 0)
    def _():
        down.start()

    @pl.when(me == 0)
    def _():
        ref[0:edge, :] = jnp.zeros((edge, ref.shape[1]), ref.dtype)

    @pl.when(me == blocks - 1)
    def _():
        ref[edge + pixels :, :] = jnp.zeros((edge, ref.shape[1]), ref.dtype)

    def finish():
        @pl.when(me > 0)
        def _():
            up.wait_recv()
            down.wait_send()

        @pl.when(me < blocks - 1)
        def _():
            down.wait_recv()
            up.wait_send()

    return finish


def trunk_forward_kernel(
    blocks,
    parts,
    layer,
    fetch,
    jobs,
    cur_ref,
    wr_ref,
    wd_ref,
    we_ref,
    mask_ref,
    gains_ref,
    biases_ref,
    wide_gains_ref,
    wide_biases_ref,
    *refs,
):
    if fetch:
        raw_r, raw_e, *refs = refs
    out_ref, ext_out_ref, full_ref, normed1_ref, inverse1_ref, normed2_ref, inverse2_ref = refs[:7]
    normed3_ref, inverse3_ref = refs[7:9]
    refs = refs[9:]
    if fetch:
        full_r, full_e, *refs = refs
    pre1_ref, pre3_ref, ext_ref, z_ref, gath_ref, stat1_ref, stat2_ref, stat3_ref = refs[:8]
    term1_ref, term3_ref, stat_send, stat_recv, halo_send, halo_recv, part_send, part_recv = refs[8:16]
    pixels, feat = cur_ref.shape
    mid = normed1_ref.shape[1]
    wide = normed3_ref.shape[1]
    edge = (ext_ref.shape[0] - pixels) // 2
    ch = lax.axis_index(CH)
    pixel_count = float(pixels * blocks)
    greet(blocks, parts)

    def whole_row(row_of):
        return jnp.concatenate([row_of(part) for part in range(parts)], axis=1)

    gain1 = whole_row(lambda part: gains_ref[part, layer, 0:1])
    bias1 = whole_row(lambda part: biases_ref[part, layer, 0:1])
    gain3 = whole_row(lambda part: wide_gains_ref[part, layer : layer + 1])
    bias3 = whole_row(lambda part: wide_biases_ref[part, layer : layer + 1])
    if fetch:
        start, finish = stripe_job(
            raw_r, raw_e, fetch, (full_r, full_e), refs[16:], blocks, parts
        )

    def terms(total, square):
        mean_value = total / pixel_count
        variance = square / pixel_count - mean_value * mean_value
        return mean_value, lax.rsqrt(variance + epsilon)

    pre1_ref[...] = contract_last(cur_ref[...], wr_ref[...])
    total, square = moments(pre1_ref, 64)
    mean_value, inverse = terms(
        *block_totals(total, square, stat1_ref, stat_send.at[0], stat_recv.at[0], blocks)
    )
    term1_ref[0:1] = mean_value
    term1_ref[1:2] = inverse

    def first(part, state):
        value = gain1 * ((pre1_ref[part, :] - mean_value) * inverse) + bias1
        pre1_ref[part, :] = value * sigmoid(value)
        return state

    own_mid = pl.ds(pl.multiple_of(ch * mid, mid), mid)
    normed1_ref[...] = (pre1_ref[:, own_mid] - term1_ref[0:1, own_mid]) * term1_ref[1:2, own_mid]
    inverse1_ref[...] = term1_ref[1:2, own_mid]
    row_loop(pixels, 64, first, 0)
    ext_ref[edge : edge + pixels, :] = pre1_ref[...].astype(jnp.bfloat16)
    wait_halo = halo_copies(ext_ref, edge, pixels, halo_send, halo_recv, blocks)

    half = edge // 2
    for row_step in (1, 0, 2):
        if row_step == 0:
            wait_halo()
        top = 2 * row_step * half
        product = contract_last(
            ext_ref[top : top + pixels, :],
            wd_ref[layer, 3 * row_step : 3 * row_step + 3].reshape(3 * mid, parts * mid),
        )
        for col_step in range(3):
            part = masked(
                product[:, col_step * mid : (col_step + 1) * mid],
                mask_ref[1],
                row_step * 3 + col_step,
            )
            if row_step == 1:
                z_ref[col_step] = part
            else:
                z_ref[col_step] += part
    second_pre = (
        z_ref[1] + pltpu.roll(z_ref[0], 2, 0) + pltpu.roll(z_ref[2], pixels - 2, 0)
    )
    mean_value, inverse = terms(
        *block_totals(
            jnp.sum(second_pre, axis=0, keepdims=True),
            jnp.sum(second_pre * second_pre, axis=0, keepdims=True),
            stat2_ref,
            stat_send.at[1],
            stat_recv.at[1],
            blocks,
        )
    )
    normed = (second_pre - mean_value) * inverse
    normed2_ref[...] = normed
    inverse2_ref[...] = inverse
    value = gains_ref[ch, layer, 1:2] * normed + biases_ref[ch, layer, 1:2]
    gath_ref[ch] = (value * sigmoid(value)).astype(jnp.bfloat16)
    wait_parts = send_slots(
        lambda _: gath_ref.at[ch], gath_ref, part_send, part_recv, CH, parts
    )
    for job in jobs:
        job[0]()
    ext_out_ref[...] = ext_ref[...]
    wait_parts()
    if fetch:
        start()
    for part in range(parts):
        full_ref[:, part * mid : (part + 1) * mid] = gath_ref[part]
    for part in range(parts):
        lane = slice(part * wide, (part + 1) * wide)
        pre3_ref[:, lane] = jnp.dot(
            full_ref[...], we_ref[:, lane], preferred_element_type=jnp.float32
        )
    for job in jobs:
        job[1]()
    total, square = moments(pre3_ref, 16)
    mean_value, inverse = terms(
        *block_totals(total, square, stat3_ref, stat_send.at[2], stat_recv.at[2], blocks)
    )
    term3_ref[0:1] = mean_value
    term3_ref[1:2] = inverse

    def last(part, state):
        value = (
            gain3 * ((pre3_ref[part, :] - mean_value) * inverse)
            + bias3
            + cur_ref[part, :].astype(jnp.float32)
        )
        out_ref[part, :] = (value * sigmoid(value)).astype(jnp.bfloat16)
        return state

    row_loop(pixels, 16, last, 0)
    own_wide = pl.ds(pl.multiple_of(ch * wide, wide), wide)
    for job in jobs:
        job[2]()
    normed3_ref[...] = (pre3_ref[:, own_wide] - term3_ref[0:1, own_wide]) * term3_ref[1:2, own_wide]
    inverse3_ref[...] = term3_ref[1:2, own_wide]
    if fetch:
        finish()
    for job in jobs:
        job[3]()


def trunk_forward(
    blocks, parts, cols, layer, jobs, current, reduce_w, dilated_w, expand_w, mask, norms, raw
):
    pixels, feat = current.shape
    narrow = reduce_w.shape[0]
    mid, wide = narrow // parts, feat // parts
    edge = 2 * cols
    f32, low = jnp.float32, jnp.bfloat16
    shape = jax.ShapeDtypeStruct
    rows = edge * 2 + pixels
    inside = pl.BlockSpec(memory_space=pltpu.VMEM)
    anywhere = pl.BlockSpec(memory_space=pl.ANY)
    fetch = layer + 1 if raw else 0
    return job_call(
        functools.partial(trunk_forward_kernel, blocks, parts, layer, fetch),
        jobs,
        blocks,
        in_specs=[inside] * 9 + [anywhere] * len(raw),
        out_specs=[inside] * 9 + [anywhere] * len(raw),
        out_shape=[
            shape((pixels, feat), low),
            shape((rows, narrow), low),
            shape((pixels, narrow), low),
            shape((pixels, mid), f32),
            shape((1, mid), f32),
            shape((pixels, mid), f32),
            shape((1, mid), f32),
            shape((pixels, wide), f32),
            shape((1, wide), f32),
        ]
        + (stripe_shapes(parts, blocks, *raw) if raw else []),
        scratch_shapes=[
            pltpu.VMEM((pixels, narrow), f32),
            pltpu.VMEM((pixels, feat), f32),
            pltpu.VMEM((rows, narrow), low),
            pltpu.VMEM((3, pixels, mid), f32),
            pltpu.VMEM((parts, pixels, mid), low),
            pltpu.VMEM((blocks, 2, narrow), f32),
            pltpu.VMEM((blocks, 2, mid), f32),
            pltpu.VMEM((blocks, 2, feat), f32),
            pltpu.VMEM((2, narrow), f32),
            pltpu.VMEM((2, feat), f32),
            pltpu.SemaphoreType.DMA((3, blocks)),
            pltpu.SemaphoreType.DMA((3, blocks)),
            pltpu.SemaphoreType.DMA((2,)),
            pltpu.SemaphoreType.DMA((2,)),
            pltpu.SemaphoreType.DMA((parts,)),
            pltpu.SemaphoreType.DMA((parts,)),
        ]
        + (stripe_sems(parts) if raw else []),
        compiler_params=comm_params(50 + layer),
        cost_estimate=pl.CostEstimate(
            flops=2 * pixels * (2 * narrow * feat + 9 * mid * narrow),
            bytes_accessed=150 * 2**20,
            transcendentals=0,
        ),
    )(current, reduce_w, dilated_w, expand_w, mask, *norms, *raw)


def slope_of(values):
    gate = sigmoid(values)
    return gate * (1.0 + values * (1.0 - gate))


def sum_slots(ref, count):
    total = ref[0].astype(jnp.float32)
    for slot in range(1, count):
        total = total + ref[slot].astype(jnp.float32)
    return total


plan = (2, 4, 2, 4, 1, 3)


def trunk_backward_kernel(
    blocks,
    parts,
    layer,
    jobs,
    *refs,
):
    up_ref, heads_ref, cur_ref, normed3_ref, inverse3_ref = refs[:5]
    refs = refs[5:]
    we_ref, full_ref, normed2_ref, inverse2_ref, wd_ref = refs[:5]
    refs = refs[5:]
    mask_ref, ext_ref, normed1_ref, inverse1_ref, wr_ref = refs[:5]
    refs = refs[5:]
    gate_ref, gains_ref, biases_ref, wide_gains_ref, wide_biases_ref = refs[:5]
    refs = refs[5:]
    sources, gates, refs = refs[:7], refs[7:9], refs[9:]
    out_ref, expand_ref, dilated_ref, reduce_ref, wide_ref = refs[:5]
    refs = refs[5:]
    second_ref, first_ref, gate_out = refs[:3]
    refs = refs[3:]
    messages_out, heads_out, *refs = refs
    third_ref, grad_ref, im_ref, send2_ref, recv2_ref = refs[:5]
    refs = refs[5:]
    send1_ref, recv1_ref, gath_ref, low_ref, ex_send_ref = refs[:5]
    refs = refs[5:]
    ex_recv_ref, di_send_ref, di_recv_ref, re_send_ref, re_recv_ref = refs[:5]
    refs = refs[5:]
    stat3_ref, stat2_ref, stat1_ref, gates_ref, stat_send = refs[:5]
    refs = refs[5:]
    stat_recv, halo_send, halo_recv, part_send, part_recv = refs[:5]
    refs = refs[5:]
    sum_send, sum_recv = refs[:2]
    refs = refs[2:]
    buffers, accs, (lhs_ref, chunk_sem) = refs[:6], refs[6:9], refs[9:]
    chunks = WeightChunks(blocks, layer, sources, gates, buffers, accs, lhs_ref, chunk_sem)
    pixels, wide = up_ref.shape
    mid = normed1_ref.shape[1]
    narrow = mid * parts
    feat = cur_ref.shape[1]
    edge = (grad_ref.shape[0] - pixels) // 2
    half = edge // 2
    blk = lax.axis_index(BLK)
    ch = lax.axis_index(CH)
    pixel_count = float(pixels * blocks)
    low = jnp.bfloat16
    gain3 = wide_gains_ref[layer : layer + 1]
    bias3 = wide_biases_ref[layer : layer + 1]
    greet(blocks, parts)
    chunks.begin()
    own_wide = pl.ds(pl.multiple_of(ch * wide, wide), wide)
    gates_ref[blk] = gate_ref[...]
    wait_gates = send_slots(
        lambda _: gates_ref.at[blk], gates_ref, stat_send.at[3], stat_recv.at[3], BLK, blocks
    )

    def start(part, state):
        normed = normed3_ref[part, :]
        summed = (
            gain3 * normed + bias3 + cur_ref[part, own_wide].astype(jnp.float32)
        )
        value = (up_ref[part, :] + heads_ref[part, :].astype(jnp.float32)) * slope_of(summed)
        out_ref[part, :] = value
        return state[0] + fold(value), state[1] + fold(value * normed)

    zero = jnp.zeros((8, wide), jnp.float32)
    bias_sum, gain_sum = row_loop(pixels, 32, start, (zero, zero))
    bias_grad, gain_grad = block_totals(
        bias_sum.sum(axis=0, keepdims=True),
        gain_sum.sum(axis=0, keepdims=True),
        stat3_ref,
        stat_send.at[0],
        stat_recv.at[0],
        blocks,
        lambda: chunks.run(plan[0]),
    )
    wide_ref[0:1] = gain_grad
    wide_ref[1:2] = bias_grad
    scale = gain3 * inverse3_ref[...]
    bias_part = bias_grad / pixel_count
    gain_part = gain_grad / pixel_count

    def third(part, state):
        third_ref[part, :] = (
            scale * (out_ref[part, :] - bias_part - normed3_ref[part, :] * gain_part)
        ).astype(low)
        return state

    row_loop(pixels, 32, third, 0)
    product = contract_last(third_ref[...], we_ref[layer])
    for part in range(parts):
        send2_ref[part] = product[:, part * mid : (part + 1) * mid].astype(low)
    recv2_ref[ch] = send2_ref[ch]
    wait_parts = send_slots(
        lambda peer: send2_ref.at[peer], recv2_ref, part_send.at[0], part_recv.at[0], CH, parts
    )
    size = narrow // blocks
    product = lax.dot_general(
        full_ref[...], third_ref[...], (((0,), (0,)), ((), ())), preferred_element_type=jnp.float32
    )
    for block in range(blocks):
        ex_send_ref[block] = product[block * size : (block + 1) * size].astype(low)
    ex_recv_ref[blk] = ex_send_ref[blk]
    wait_expand = send_slots(
        lambda peer: ex_send_ref.at[peer], ex_recv_ref, sum_send.at[0], sum_recv.at[0], BLK, blocks
    )
    chunks.run(plan[1])
    wait_parts()

    def narrow_norm(recv_ref, normed_ref, inverse_ref, norm, stat_ref, phase, sums_ref):
        gain = gains_ref[layer, norm : norm + 1]
        bias = biases_ref[layer, norm : norm + 1]
        normed = normed_ref[...]
        value = sum_slots(recv_ref, parts) * slope_of(gain * normed + bias)
        bias_grad, gain_grad = block_totals(
            jnp.sum(value, axis=0, keepdims=True),
            jnp.sum(value * normed, axis=0, keepdims=True),
            stat_ref,
            stat_send.at[phase],
            stat_recv.at[phase],
            blocks,
            lambda: chunks.run(plan[2 * phase]),
        )
        sums_ref[0:1] = gain_grad
        sums_ref[1:2] = bias_grad
        return (
            gain
            * inverse_ref[...]
            * (value - bias_grad / pixel_count - normed * (gain_grad / pixel_count))
        )

    grad = narrow_norm(
        recv2_ref, normed2_ref, inverse2_ref, 1, stat2_ref, 1, second_ref
    )
    grad_ref[edge : edge + pixels, :] = grad.astype(low)
    wait_halo = halo_copies(grad_ref, edge, pixels, halo_send, halo_recv, blocks)
    own = grad_ref[edge : edge + pixels, :].astype(jnp.float32)
    turned = (pltpu.roll(own, pixels - 2, 0), own, pltpu.roll(own, 2, 0))
    for row_step in range(3):
        side = jnp.concatenate(
            [
                masked(turned[col_step], mask_ref[1], row_step * 3 + col_step).astype(low)
                for col_step in range(3)
            ],
            axis=1,
        )
        top = 2 * row_step * half
        product = lax.dot_general(
            ext_ref[top : top + pixels, :],
            side,
            (((0,), (0,)), ((), ())),
            preferred_element_type=jnp.float32,
        )
        for block in range(blocks):
            for col_step in range(3):
                di_send_ref[block, row_step * 3 + col_step] = product[
                    block * size : (block + 1) * size, col_step * mid : (col_step + 1) * mid
                ].astype(low)
    di_recv_ref[blk] = di_send_ref[blk]
    wait_halo()
    fill_taps(im_ref, 0, grad_ref[...], mask_ref[1], pixels, half, 2)
    product = jnp.dot(
        im_ref[0], wd_ref[layer].reshape(9 * mid, narrow), preferred_element_type=jnp.float32
    )
    for part in range(parts):
        send1_ref[part] = product[:, part * mid : (part + 1) * mid].astype(low)
    recv1_ref[ch] = send1_ref[ch]
    wait_parts = send_slots(
        lambda peer: send1_ref.at[peer], recv1_ref, part_send.at[1], part_recv.at[1], CH, parts
    )
    wait_dilated = send_slots(
        lambda peer: di_send_ref.at[peer], di_recv_ref, sum_send.at[1], sum_recv.at[1], BLK, blocks
    )
    for job in jobs:
        job[0]()
    chunks.run(plan[3])
    wait_parts()
    grad = narrow_norm(
        recv1_ref, normed1_ref, inverse1_ref, 0, stat1_ref, 2, first_ref
    )
    gath_ref[ch] = grad.astype(low)
    wait_parts = send_slots(
        lambda _: gath_ref.at[ch], gath_ref, part_send.at[2], part_recv.at[2], CH, parts
    )
    product = lax.dot_general(
        cur_ref[...], gath_ref[ch], (((0,), (0,)), ((), ())), preferred_element_type=jnp.float32
    )
    size = feat // blocks
    for block in range(blocks):
        re_send_ref[block] = product[block * size : (block + 1) * size].astype(low)
    re_recv_ref[blk] = re_send_ref[blk]
    wait_reduce = send_slots(
        lambda peer: re_send_ref.at[peer], re_recv_ref, sum_send.at[2], sum_recv.at[2], BLK, blocks
    )
    chunks.run(plan[5])
    wait_parts()
    for part in range(parts):
        low_ref[:, part * mid : (part + 1) * mid] = gath_ref[part]
    out_ref[...] += jnp.dot(low_ref[...], wr_ref[:, own_wide], preferred_element_type=jnp.float32)
    chunks.run(2 * blocks - chunks.done)
    messages_store(messages_out, accs[:2])
    heads_store(heads_out, accs[2])
    for part in (1, 2, 3):
        for job in jobs:
            job[part]()
    wait_gates()
    gate_out[...] = sum_slots(gates_ref, blocks)
    wait_expand()
    expand_ref[...] = sum_slots(ex_recv_ref, blocks)
    wait_dilated()
    dilated_ref[...] = sum_slots(di_recv_ref, blocks)
    wait_reduce()
    reduce_ref[...] = sum_slots(re_recv_ref, blocks)


def trunk_backward(blocks, parts, layer, jobs, operands, norms, sources, gates):
    pixels, wide = operands[0].shape
    feat = wide * parts
    mid = operands[7].shape[1]
    narrow = mid * parts
    rows = operands[11].shape[0]
    f32, low = jnp.float32, jnp.bfloat16
    shape = jax.ShapeDtypeStruct
    small, large = narrow // blocks, feat // blocks
    inside = pl.BlockSpec(memory_space=pltpu.VMEM)
    anywhere = pl.BlockSpec(memory_space=pl.ANY)
    rows_two = pixels + 2 * lanes
    return job_call(
        functools.partial(trunk_backward_kernel, blocks, parts, layer),
        jobs,
        blocks,
        in_specs=[inside] * (len(operands) + len(norms)) + [anywhere] * len(sources) + [inside] * len(gates),
        out_specs=[inside] * 10,
        out_shape=[
            shape((pixels, wide), f32),
            shape((small, wide), f32),
            shape((9, small, mid), f32),
            shape((large, mid), f32),
            shape((2, wide), f32),
            shape((2, mid), f32),
            shape((2, mid), f32),
            shape(operands[-1].shape, f32),
            shape((6, 9, small, mid), f32),
            shape((4, 9, large, mid), f32),
        ],
        scratch_shapes=[
            pltpu.VMEM((pixels, wide), low),
            pltpu.VMEM((rows, mid), low),
            pltpu.VMEM((1, pixels, 9 * mid), low),
            pltpu.VMEM((parts, pixels, mid), low),
            pltpu.VMEM((parts, pixels, mid), low),
            pltpu.VMEM((parts, pixels, mid), low),
            pltpu.VMEM((parts, pixels, mid), low),
            pltpu.VMEM((parts, pixels, mid), low),
            pltpu.VMEM((pixels, narrow), low),
            pltpu.VMEM((blocks, small, wide), low),
            pltpu.VMEM((blocks, small, wide), low),
            pltpu.VMEM((blocks, 9, small, mid), low),
            pltpu.VMEM((blocks, 9, small, mid), low),
            pltpu.VMEM((blocks, large, mid), low),
            pltpu.VMEM((blocks, large, mid), low),
            pltpu.VMEM((blocks, 2, wide), f32),
            pltpu.VMEM((blocks, 2, mid), f32),
            pltpu.VMEM((blocks, 2, mid), f32),
            pltpu.VMEM((blocks,) + operands[-1].shape, f32),
            pltpu.SemaphoreType.DMA((4, blocks)),
            pltpu.SemaphoreType.DMA((4, blocks)),
            pltpu.SemaphoreType.DMA((2,)),
            pltpu.SemaphoreType.DMA((2,)),
            pltpu.SemaphoreType.DMA((3, parts)),
            pltpu.SemaphoreType.DMA((3, parts)),
            pltpu.SemaphoreType.DMA((3, blocks)),
            pltpu.SemaphoreType.DMA((3, blocks)),
            pltpu.VMEM((2, 2, rows_two, 2 * small), low),
            pltpu.VMEM((2, 2, pixels, mid), low),
            pltpu.VMEM((2, 2, pixels, mid), low),
            pltpu.VMEM((2, rows_two, large), low),
            pltpu.VMEM((2, 4, pixels, mid), low),
            pltpu.VMEM((2, pixels, lanes), jnp.int32),
            pltpu.VMEM((18 * small, len(group_pairs[0]) * mid), f32),
            pltpu.VMEM((18 * small, len(group_pairs[1]) * mid), f32),
            pltpu.VMEM((9 * large, 4 * mid), f32),
            pltpu.VMEM((pixels, 9 * max(large, 2 * small)), low),
            pltpu.SemaphoreType.DMA((2, 6)),
        ],
        compiler_params=comm_params(60 + layer),
        cost_estimate=pl.CostEstimate(
            flops=4 * pixels * (2 * narrow * wide + 9 * mid * narrow) + 2 * 10**10,
            bytes_accessed=200 * 2**20,
            transcendentals=0,
        ),
    )(*operands, *norms, *sources, *gates)


def gather_parts(values):
    return lax.all_gather(values, CH, axis=0, tiled=False)


def reduce_parts(values):
    return lax.psum_scatter(values, CH, scatter_dimension=0, tiled=False)


def own_slice(values, size, axis):
    return lax.dynamic_slice_in_dim(values, lax.axis_index(CH) * size, size, axis)


def shards(
    features_in,
    w_reduce,
    w_dilated,
    w_expand,
    w_heads,
    w_messages,
    norm_gain,
    norm_bias,
    wide_gain,
    wide_bias,
    gate_gain,
    gate_bias,
    canvas_ids,
    output_cotangent,
    task_cotangents,
):
    rows, cols, wide = features_in.shape
    pixels = rows * cols
    blocks = lax.axis_size(BLK)
    parts = lax.axis_size(CH)
    layers = w_reduce.shape[0]
    mid = w_reduce.shape[1]
    feat = wide * parts
    narrow = mid * parts
    low = jnp.bfloat16
    dilated_t = w_dilated.transpose(0, 2, 1, 3)
    heads_t = w_heads.transpose(0, 1, 3, 2, 4)
    messages_t = w_messages.transpose(0, 1, 3, 2, 4)
    current, *rest = prologue(
        blocks,
        parts,
        features_in.reshape(pixels, wide),
        w_reduce,
        w_expand,
        (norm_gain, norm_bias, wide_gain, wide_bias),
        canvas_ids,
    )
    reduce_full, expand_full = [rest[2]], [rest[3]]
    norms_all, bits, all_bits = rest[4:8], rest[8], rest[9]
    cotangents = task_cotangents.reshape(layers, 2, pixels, mid)
    kept = []
    for layer in range(layers):
        keep = types.SimpleNamespace(input=current)
        results, (keep.cotangents,) = trunk_forward(
            blocks,
            parts,
            cols,
            layer,
            [(gather_kind, cotangents, layer)],
            current,
            reduce_full[layer],
            dilated_t,
            expand_full[layer],
            bits,
            norms_all,
            (w_reduce, w_expand) if layer + 1 < layers else (),
        )
        (
            current,
            keep.first_ext,
            keep.second_full,
            keep.normed1,
            keep.inverse1,
            keep.normed2,
            keep.inverse2,
            keep.normed3,
            keep.inverse3,
            *mine,
        ) = results
        if layer:
            current, kept[-1].features = lax.optimization_barrier((current, kept[-1].features))
        keep.output = current
        (keep.heads_pre, features, keep.ends, *fetched), _ = heads_forward(
            blocks,
            layer,
            [],
            cols,
            current,
            heads_t,
            bits,
            mine,
        )
        if fetched:
            reduce_full.append(fetched[0])
            expand_full.append(fetched[1])
        current, features = lax.optimization_barrier((current, features))
        keep.features = gather_parts(features)
        kept.append(keep)
    output = own_slice(current, wide, 1).reshape(rows, cols, wide)

    for layer in range(layers):
        keep = kept[layer]
        (keep.maps, keep.local, keep.gate_sums, partial, keep.message_values), moved = messages_both(
            blocks,
            layer,
            [(gather_kind, keep.ends)] + ([] if layer else [(upper_kind, keep.output)]),
            0,
            bool(layer),
            cols,
            keep.features,
            messages_t,
            cotangents,
            gate_gain,
            gate_bias,
            bits,
        )
        keep.ends_all = moved[0]
        if layer == 0:
            keep.upper = moved[1]
        keep.source_sums = reduce_parts(partial)

    def heads_low_of(keep):
        sums = keep.source_sums.astype(jnp.float32)
        total = jnp.stack([sums[0] + keep.local[0], sums[1], sums[2], sums[3] + keep.local[1]])
        return (total * silu_slope(keep.heads_pre)).astype(low)

    for layer in range(layers):
        keep = kept[layer]
        keep.heads_low = heads_low_of(keep)
        (partial,), moved = heads_backward(
            blocks,
            layer,
            [] if layer else [(slot_kind, keep.message_values), (lower_kind, keep.output)],
            cols,
            keep.heads_low,
            heads_t,
            bits,
            parts,
        )
        if layer == 0:
            keep.message_values, keep.lower = moved
        keep.heads_partial = reduce_parts(partial)
        if layer + 1 < layers:
            kept[layer + 1].source_sums, partial = lax.optimization_barrier(
                (kept[layer + 1].source_sums, partial)
            )
    kept[0].heads_low, partial = lax.optimization_barrier((kept[0].heads_low, partial))
    kept[0].heads_all, kept[1].heads_all, kept[1].upper, kept[1].lower = exchange(
        blocks,
        [(gather_kind, keep.heads_low) for keep in kept]
        + [(upper_kind, kept[1].output), (lower_kind, kept[1].output)],
    )
    kept[1].heads_all, kept[0].heads_partial = lax.optimization_barrier(
        (kept[1].heads_all, kept[0].heads_partial)
    )

    upstream = output_cotangent.reshape(pixels, wide).astype(jnp.float32)
    for layer in reversed(range(layers)):
        keep = kept[layer]
        (
            upstream,
            keep.expand_grad,
            keep.dilated_grad,
            keep.reduce_grad,
            keep.wide_sums,
            keep.second_sums,
            keep.first_sums,
            keep.gates,
            keep.messages_grad,
            keep.heads_grad,
        ), _ = trunk_backward(
            blocks,
            parts,
            layer,
            [],
            (
                upstream,
                keep.heads_partial,
                keep.input,
                keep.normed3,
                keep.inverse3,
                w_expand,
                keep.second_full,
                keep.normed2,
                keep.inverse2,
                dilated_t,
                bits,
                keep.first_ext,
                keep.normed1,
                keep.inverse1,
                reduce_full[layer],
                keep.gate_sums,
            ),
            (norm_gain, norm_bias, wide_gain, wide_bias),
            (
                keep.message_values,
                keep.cotangents,
                keep.ends_all,
                keep.upper,
                keep.lower,
                keep.heads_all,
                all_bits,
            ),
            (gate_gain, gate_bias),
        )
    def stacked(of):
        return jnp.stack([of(keep) for keep in kept])

    narrow_sums = stacked(lambda keep: jnp.stack([keep.first_sums, keep.second_sums]))
    wide_sums = stacked(lambda keep: keep.wide_sums)
    gate_sums = stacked(lambda keep: keep.gates.reshape(2, 6, mid))
    return (
        output,
        stacked(lambda keep: keep.maps.reshape(2, rows, cols, mid)),
        upstream.reshape(rows, cols, wide),
        stacked(lambda keep: keep.reduce_grad),
        stacked(lambda keep: keep.dilated_grad),
        stacked(lambda keep: keep.expand_grad),
        stacked(lambda keep: keep.heads_grad),
        stacked(lambda keep: keep.messages_grad),
        narrow_sums[:, :, 0],
        narrow_sums[:, :, 1],
        wide_sums[:, 0],
        wide_sums[:, 1],
        gate_sums[:, 0],
        gate_sums[:, 1],
    )


def route(*args):
    mid = args[1].shape[1]
    blocks, parts = lax.axis_size(BLK), lax.axis_size(CH)
    whole_tiles = args[1].shape[0] == 2 and mid % lanes == 0 and args[0].shape[1] == lanes and parts >= 2
    if whole_tiles and blocks == 8 and 2 * mid * parts == lanes * blocks:
        return shards(*args)
    return plain_shards(*args)


def solution(mesh):
    placed = (
        P(BLK, None, CH),
        P(None, CH, None),
        P(None, CH, None, None),
        P(None, None, CH),
        P(None, None, CH, None, None),
        P(None, None, CH, None, None),
        P(None, None, CH),
        P(None, None, CH),
        P(None, CH),
        P(None, CH),
        P(None, None, CH),
        P(None, None, CH),
        P(),
        P(BLK, None, CH),
        P(None, None, BLK, None, CH),
    )
    return jax.shard_map(
        route,
        mesh=mesh,
        in_specs=placed,
        out_specs=(
            P(BLK, None, CH),
            P(None, None, BLK, None, CH),
            P(BLK, None, CH),
            P(None, BLK, CH),
            P(None, None, BLK, CH),
            P(None, BLK, CH),
            P(None, None, None, BLK, CH),
            P(None, None, None, BLK, CH),
            P(None, None, CH),
            P(None, None, CH),
            P(None, CH),
            P(None, CH),
            P(None, None, CH),
            P(None, None, CH),
        ),
        check_vma=False,
    )
```

```python
import functools
import types

import jax
import jax.numpy as jnp
from jax import lax
from jax.experimental import pallas as pl
from jax.experimental.pallas import tpu as pltpu
from jax.sharding import PartitionSpec as P

epsilon = 1e-05
BLK = "blk"
CH = "ch"
tap_offsets = tuple(((row_step, col_step) for row_step in (-1, 0, 1) for col_step in (-1, 0, 1)))
message_pairs = ((1, 0), (2, 0), (3, 0), (0, 3), (1, 3), (2, 3))


def extended_2(block, sides, width):
    for axis, dim in sides:
        count = lax.axis_size(axis)
        forward = [(i, i + 1) for i in range(count - 1)]
        backward = [(target, source) for source, target in forward]
        low = lax.ppermute(
            lax.slice_in_dim(block, block.shape[dim] - width, None, axis=dim), axis, forward
        )
        high = lax.ppermute(lax.slice_in_dim(block, 0, width, axis=dim), axis, backward)
        block = jnp.concatenate([low, block, high], axis=dim)
    return block


def silu_slope(values):
    sigmoid_value = jax.nn.sigmoid(values)
    return sigmoid_value * (1.0 + values * (1.0 - sigmoid_value))


def gather_channels(values):
    return lax.all_gather(values, CH, axis=3, tiled=True)


def reduce_channels(values):
    return lax.psum_scatter(
        values.astype(jnp.bfloat16), CH, scatter_dimension=3, tiled=True
    ).astype(jnp.float32)


def extend_rows(values, halo_width):
    return extended_2(values, ((BLK, 0),), halo_width)


def pixel_totals(first_sum, second_sum):
    return lax.psum((first_sum, second_sum), BLK)


def weight_totals(reduce_grad, dilated_grad, expand_grad, heads_grad, messages_grad):
    return (
        lax.psum_scatter(
            reduce_grad.astype(jnp.bfloat16), BLK, scatter_dimension=1, tiled=True
        ).astype(jnp.float32),
        lax.psum_scatter(
            dilated_grad.astype(jnp.bfloat16), BLK, scatter_dimension=2, tiled=True
        ).astype(jnp.float32),
        lax.psum_scatter(
            expand_grad.astype(jnp.bfloat16), BLK, scatter_dimension=1, tiled=True
        ).astype(jnp.float32),
        lax.psum_scatter(
            heads_grad.astype(jnp.bfloat16), BLK, scatter_dimension=3, tiled=True
        ).astype(jnp.float32),
        lax.psum_scatter(
            messages_grad.astype(jnp.bfloat16), BLK, scatter_dimension=3, tiled=True
        ).astype(jnp.float32),
    )


def widen(values, halo_width):
    return extend_rows(gather_channels(values), halo_width)


def local_masks(canvas_ids, row_count, dilation):
    col_count = canvas_ids.shape[1]
    padded = jnp.pad(canvas_ids, 2, constant_values=-1)
    start = lax.axis_index(BLK) * row_count
    window = lax.dynamic_slice(padded, (start, jnp.int32(0)), (row_count + 4, col_count + 4))
    centre = window[2 : 2 + row_count, 2 : 2 + col_count]
    result = []
    for row_step, col_step in tap_offsets:
        top = 2 + row_step * dilation
        left = 2 + col_step * dilation
        result.append(window[top : top + row_count, left : left + col_count] == centre)
    return jnp.stack(result)


def shifted(padded, halo_width, dilation, row_step, col_step, row_count, col_count):
    top = halo_width + row_step * dilation
    left = dilation + col_step * dilation
    return padded[top : top + row_count, left : left + col_count]


def conv_forward(extended, halo_width, dilation, weights, tap_masks):
    row_count = extended.shape[0] - 2 * halo_width
    col_count = extended.shape[1]
    padded = jnp.pad(extended, ((0, 0), (dilation, dilation), (0, 0)))
    running = jnp.zeros((row_count, col_count, weights.shape[0], weights.shape[1]), jnp.float32)
    for tap_index, (row_step, col_step) in enumerate(tap_offsets):
        window = shifted(padded, halo_width, dilation, row_step, col_step, row_count, col_count)
        product = jnp.einsum(
            "rwc,koc->rwko", window, weights[:, :, tap_index], preferred_element_type=jnp.float32
        )
        running = running + jnp.where(tap_masks[tap_index][:, :, None, None], product, 0.0)
    return running


def conv_weight_grad(extended, halo_width, dilation, gradient, tap_masks):
    row_count = extended.shape[0] - 2 * halo_width
    col_count = extended.shape[1]
    padded = jnp.pad(extended, ((0, 0), (dilation, dilation), (0, 0)))
    result = []
    for tap_index, (row_step, col_step) in enumerate(tap_offsets):
        window = shifted(padded, halo_width, dilation, row_step, col_step, row_count, col_count)
        masked = jnp.where(
            tap_masks[tap_index][:, :, None, None], gradient, jnp.zeros((), gradient.dtype)
        )
        result.append(
            jnp.einsum("rwc,rwko->kco", window, masked, preferred_element_type=jnp.float32)
        )
    return jnp.stack(result, axis=1)


def conv_input_grad(grad_extended, halo_width, dilation, weights, tap_masks):
    row_count = grad_extended.shape[0] - 2 * halo_width
    col_count = grad_extended.shape[1]
    padded = jnp.pad(grad_extended, ((0, 0), (dilation, dilation), (0, 0), (0, 0)))
    running = jnp.zeros((row_count, col_count, weights.shape[3]), jnp.float32)
    for tap_index, (row_step, col_step) in enumerate(tap_offsets):
        window = shifted(padded, halo_width, dilation, -row_step, -col_step, row_count, col_count)
        product = jnp.einsum(
            "rwko,koc->rwc", window, weights[:, :, tap_index], preferred_element_type=jnp.float32
        )
        running = running + jnp.where(tap_masks[8 - tap_index][:, :, None], product, 0.0)
    return running


def norm_forward(hidden, gain, bias, pixel_count):
    total_sum, square_sum = pixel_totals(
        jnp.sum(hidden, axis=(0, 1)), jnp.sum(hidden * hidden, axis=(0, 1))
    )
    mean_value = total_sum / pixel_count
    variance = square_sum / pixel_count - mean_value * mean_value
    inverse = lax.rsqrt(variance + epsilon)
    normed = (hidden - mean_value) * inverse
    return (gain * normed + bias, normed, inverse)


def norm_backward(upstream, normed, inverse, gain, pixel_count):
    bias_grad, gain_grad = pixel_totals(
        jnp.sum(upstream, axis=(0, 1)), jnp.sum(upstream * normed, axis=(0, 1))
    )
    hidden_grad = (
        gain * inverse * (upstream - bias_grad / pixel_count - normed * gain_grad / pixel_count)
    )
    return (hidden_grad, gain_grad, bias_grad)


def layer_forward(inputs, params, masks_one, masks_two, pixel_count):
    (
        reduce_w,
        dilated_w,
        expand_w,
        heads_w,
        messages_w,
        narrow_gain,
        narrow_bias,
        wide_g,
        wide_b,
        gate_g,
        gate_b,
    ) = params
    stored = types.SimpleNamespace()
    inputs_full = gather_channels(inputs[:, :, None, :])[:, :, 0, :]
    first_pre = jnp.einsum("rwc,oc->rwo", inputs_full, reduce_w, preferred_element_type=jnp.float32)
    first_norm, first_normed, first_inverse = norm_forward(
        first_pre, narrow_gain[0], narrow_bias[0], pixel_count
    )
    first_act = jax.nn.silu(first_norm).astype(jnp.bfloat16)
    first_ext = widen(first_act[:, :, None, :], 2)[:, :, 0, :]
    second_pre = conv_forward(first_ext, 2, 2, dilated_w[None], masks_two)[:, :, 0, :]
    second_norm, second_normed, second_inverse = norm_forward(
        second_pre, narrow_gain[1], narrow_bias[1], pixel_count
    )
    second_act = jax.nn.silu(second_norm).astype(jnp.bfloat16)
    second_full = gather_channels(second_act[:, :, None, :])[:, :, 0, :]
    third_pre = jnp.einsum("rwc,co->rwo", second_full, expand_w, preferred_element_type=jnp.float32)
    third_norm, third_normed, third_inverse = norm_forward(third_pre, wide_g, wide_b, pixel_count)
    summed = third_norm + inputs.astype(jnp.float32)
    output = jax.nn.silu(summed).astype(jnp.bfloat16)
    output_ext = widen(output[:, :, None, :], 1)[:, :, 0, :]
    heads_pre = conv_forward(output_ext, 1, 1, heads_w, masks_one)
    features = jax.nn.silu(heads_pre).astype(jnp.bfloat16)
    features_ext = widen(features, 1)
    feature_values = features.astype(jnp.float32)
    depth_map = feature_values[:, :, 0]
    segment_map = feature_values[:, :, 3]
    message_list = []
    for pair_index, (source, target) in enumerate(message_pairs):
        message = conv_forward(
            features_ext[:, :, source], 1, 1, messages_w[pair_index][None], masks_one
        )[:, :, 0]
        gate_value = jax.nn.sigmoid(
            gate_g[pair_index] * feature_values[:, :, target] + gate_b[pair_index]
        )
        message_list.append(message)
        if target == 0:
            depth_map = depth_map + gate_value * message
        else:
            segment_map = segment_map + gate_value * message
    stored.inputs_full = inputs_full
    stored.first_norm = first_norm
    stored.first_normed = first_normed
    stored.first_inverse = first_inverse
    stored.first_ext = first_ext
    stored.second_norm = second_norm
    stored.second_normed = second_normed
    stored.second_inverse = second_inverse
    stored.second_full = second_full
    stored.third_normed = third_normed
    stored.third_inverse = third_inverse
    stored.summed = summed
    stored.output_ext = output_ext
    stored.heads_pre = heads_pre
    stored.features = feature_values
    stored.features_ext = features_ext
    stored.messages = message_list
    return (output, depth_map, segment_map, stored)


def layer_backward(
    stored, upstream, depth_grad, segment_grad, params, masks_one, masks_two, pixel_count
):
    (
        reduce_w,
        dilated_w,
        expand_w,
        heads_w,
        messages_w,
        narrow_gain,
        narrow_bias,
        wide_g,
        wide_b,
        gate_g,
        gate_b,
    ) = params
    feature_values = stored.features
    zero_map = jnp.zeros_like(depth_grad)
    feature_grads = [depth_grad, zero_map, zero_map, segment_grad]
    message_grads = []
    gain_terms = []
    bias_terms = []
    for pair_index, (source, target) in enumerate(message_pairs):
        target_grad = depth_grad if target == 0 else segment_grad
        gate_value = jax.nn.sigmoid(
            gate_g[pair_index] * feature_values[:, :, target] + gate_b[pair_index]
        )
        message_grads.append(target_grad * gate_value)
        slope = target_grad * stored.messages[pair_index] * gate_value * (1.0 - gate_value)
        gain_terms.append(jnp.sum(slope * feature_values[:, :, target], axis=(0, 1)))
        bias_terms.append(jnp.sum(slope, axis=(0, 1)))
        feature_grads[target] = feature_grads[target] + slope * gate_g[pair_index]
    gate_gain_grad, gate_bias_grad = pixel_totals(jnp.stack(gain_terms), jnp.stack(bias_terms))
    message_stack = jnp.stack(message_grads, axis=2).astype(jnp.bfloat16)
    message_ext = extend_rows(message_stack, 1)
    weight_parts = []
    source_partials = [None, None, None, None]
    for pair_index, (source, target) in enumerate(message_pairs):
        weight_parts.append(
            conv_weight_grad(
                stored.features_ext[:, :, source],
                1,
                1,
                message_stack[:, :, pair_index : pair_index + 1],
                masks_one,
            )
        )
        partial_grad = conv_input_grad(
            message_ext[:, :, pair_index : pair_index + 1],
            1,
            1,
            messages_w[pair_index][None],
            masks_one,
        )
        if source_partials[source] is None:
            source_partials[source] = partial_grad
        else:
            source_partials[source] = source_partials[source] + partial_grad
    messages_w_grad = jnp.concatenate(weight_parts, axis=0)
    source_sums = reduce_channels(jnp.stack(source_partials, axis=2))
    features_total = jnp.stack(feature_grads, axis=2) + source_sums
    heads_grad = (features_total * silu_slope(stored.heads_pre)).astype(jnp.bfloat16)
    heads_w_grad = conv_weight_grad(stored.output_ext, 1, 1, heads_grad, masks_one)
    heads_ext = extend_rows(heads_grad, 1)
    output_partial = conv_input_grad(heads_ext, 1, 1, heads_w, masks_one)
    output_total = upstream + reduce_channels(output_partial[:, :, None, :])[:, :, 0, :]
    summed_grad = output_total * silu_slope(stored.summed)
    third_grad, wide_gain_grad, wide_bias_grad = norm_backward(
        summed_grad, stored.third_normed, stored.third_inverse, wide_g, pixel_count
    )
    third_low = third_grad.astype(jnp.bfloat16)
    expand_w_grad = jnp.einsum(
        "rwc,rwo->co", stored.second_full, third_low, preferred_element_type=jnp.float32
    )
    second_partial = jnp.einsum(
        "rwo,co->rwc", third_low, expand_w, preferred_element_type=jnp.float32
    )
    second_act_grad = reduce_channels(second_partial[:, :, None, :])[:, :, 0, :]
    second_grad, second_gain_grad, second_bias_grad = norm_backward(
        second_act_grad * silu_slope(stored.second_norm),
        stored.second_normed,
        stored.second_inverse,
        narrow_gain[1],
        pixel_count,
    )
    second_low = second_grad.astype(jnp.bfloat16)[:, :, None, :]
    dilated_w_grad = conv_weight_grad(stored.first_ext, 2, 2, second_low, masks_two)[0]
    second_ext = extend_rows(second_low, 2)
    first_partial = conv_input_grad(second_ext, 2, 2, dilated_w[None], masks_two)
    first_act_grad = reduce_channels(first_partial[:, :, None, :])[:, :, 0, :]
    first_grad, first_gain_grad, first_bias_grad = norm_backward(
        first_act_grad * silu_slope(stored.first_norm),
        stored.first_normed,
        stored.first_inverse,
        narrow_gain[0],
        pixel_count,
    )
    first_low = first_grad.astype(jnp.bfloat16)
    reduce_w_grad = jnp.einsum(
        "rwc,rwo->co", stored.inputs_full, first_low, preferred_element_type=jnp.float32
    )
    inputs_partial = jnp.einsum(
        "rwo,oc->rwc", first_low, reduce_w, preferred_element_type=jnp.float32
    )
    inputs_grad = reduce_channels(inputs_partial[:, :, None, :])[:, :, 0, :] + summed_grad
    weight_grads = (reduce_w_grad, dilated_w_grad, expand_w_grad, heads_w_grad, messages_w_grad)
    small_grads = (
        jnp.stack([first_gain_grad, second_gain_grad]),
        jnp.stack([first_bias_grad, second_bias_grad]),
        wide_gain_grad,
        wide_bias_grad,
        gate_gain_grad,
        gate_bias_grad,
    )
    return (inputs_grad, weight_grads, small_grads)


def plain_shards(
    features_in,
    w_reduce,
    w_dilated,
    w_expand,
    w_heads,
    w_messages,
    norm_gain,
    norm_bias,
    wide_gain,
    wide_bias,
    gate_gain,
    gate_bias,
    canvas_ids,
    output_cotangent,
    task_cotangents,
):
    row_count = features_in.shape[0]
    col_count = features_in.shape[1]
    pixel_count = float(row_count * col_count * lax.axis_size(BLK))
    masks_one = local_masks(canvas_ids, row_count, 1)
    masks_two = local_masks(canvas_ids, row_count, 2)
    layer_count = w_reduce.shape[0]
    layer_params = []
    for layer_index in range(layer_count):
        layer_params.append(
            (
                w_reduce[layer_index],
                w_dilated[layer_index],
                w_expand[layer_index],
                w_heads[layer_index],
                w_messages[layer_index],
                norm_gain[layer_index],
                norm_bias[layer_index],
                wide_gain[layer_index],
                wide_bias[layer_index],
                gate_gain[layer_index],
                gate_bias[layer_index],
            )
        )
    current = features_in
    stored_list = []
    task_list = []
    for layer_index in range(layer_count):
        current, depth_map, segment_map, stored = layer_forward(
            current, layer_params[layer_index], masks_one, masks_two, pixel_count
        )
        stored_list.append(stored)
        task_list.append(jnp.stack([depth_map, segment_map]).astype(jnp.bfloat16))
    upstream = output_cotangent.astype(jnp.float32)
    weight_list = [None] * layer_count
    small_list = [None] * layer_count
    for layer_index in reversed(range(layer_count)):
        upstream, weight_grads, small_grads = layer_backward(
            stored_list[layer_index],
            upstream,
            task_cotangents[layer_index, 0].astype(jnp.float32),
            task_cotangents[layer_index, 1].astype(jnp.float32),
            layer_params[layer_index],
            masks_one,
            masks_two,
            pixel_count,
        )
        weight_list[layer_index] = weight_grads
        small_list[layer_index] = small_grads
    stacked = [
        jnp.stack([weight_list[layer_index][member] for layer_index in range(layer_count)])
        for member in range(5)
    ]
    weight_sums = weight_totals(stacked[0], stacked[1], stacked[2], stacked[3], stacked[4])
    small_sums = [
        jnp.stack([small_list[layer_index][member] for layer_index in range(layer_count)])
        for member in range(6)
    ]
    return (
        current,
        jnp.stack(task_list),
        upstream,
        weight_sums[0],
        weight_sums[1],
        weight_sums[2],
        weight_sums[3],
        weight_sums[4],
        small_sums[0],
        small_sums[1],
        small_sums[2],
        small_sums[3],
        small_sums[4],
        small_sums[5],
    )


lanes = 128
source_order = ((1, 0, 4), (2, 1, 5), (0, 3), (3, 2))


def whole(shape):
    return pl.BlockSpec(shape, lambda *_: (0,) * len(shape))


def contract_last(left, right):
    return lax.dot_general(
        left, right, (((1,), (1,)), ((), ())), preferred_element_type=jnp.float32
    )


def sigmoid(values):
    return 1.0 / (1.0 + jnp.exp(-values))


def masked(values, bits, place):
    taken = (bits & (1 << place)) != 0
    width = values.shape[1]
    parts = [
        jnp.where(taken, values[:, start : start + lanes], 0.0) for start in range(0, width, lanes)
    ]
    return parts[0] if len(parts) == 1 else jnp.concatenate(parts, axis=1)


MESH = pl.DeviceIdType.MESH
groups = ((1, 2), (0, 3))
targets = (0, 3)
group_pairs = ((0, 4, 1, 5), (3, 2))


def remote(source, target, send_sem, recv_sem, axis, peer):
    return pltpu.make_async_remote_copy(
        src_ref=source,
        dst_ref=target,
        send_sem=send_sem,
        recv_sem=recv_sem,
        device_id={axis: peer},
        device_id_type=MESH,
    )


def comm_params(key):
    return pltpu.CompilerParams(
        vmem_limit_bytes=60 * 2**20, collective_id=key, has_side_effects=True
    )


def announce(targets):
    barrier = pltpu.get_barrier_semaphore()
    for axis, peer in targets:
        pl.semaphore_signal(barrier, inc=1, device_id={axis: peer}, device_id_type=MESH)
    pl.semaphore_wait(barrier, len(targets))


def near_blocks():
    me = lax.axis_index(BLK)

    def turned(bit):
        return me + bit - 2 * bit * lax.rem(me // bit, 2)

    return turned(1), turned(2), turned(4)


def others(axis, count):
    me = lax.axis_index(axis)
    return [lax.rem(me + step, count) for step in range(1, count)]


def round_trip(own_source, target_of, half_of, sems):
    near_send, slot_recv, pass_send, local_sem = sems
    me = lax.axis_index(BLK)
    sibling, *peers = near_blocks()
    far = me + peers[0] - me + peers[1] - me
    own = pltpu.make_async_copy(own_source, target_of(me), local_sem.at[0])

    def near(step, peer):
        return remote(
            own_source, target_of(me), near_send.at[step], slot_recv.at[me], BLK, peer
        )

    def half(side, block, recv_sem, peer):
        part = half_of(block, side)
        return remote(part, part, near_send.at[3 + side], recv_sem, BLK, peer)

    def passing(step, block):
        part = target_of(block)
        return remote(part, part, pass_send.at[step], slot_recv.at[block], BLK, sibling)

    def start():
        own.start()
        for step, peer in enumerate(peers + [sibling]):
            near(step, peer).start()

    def sent_half(side):
        recv_sem = slot_recv.at[peers[0]] if side == 0 else local_sem.at[1]
        return half(side, peers[side], recv_sem, peers[1 - side])

    def middle():
        for side in range(2):
            copy = passing(side, peers[side])
            copy.wait_recv()
            sent_half(side).start()
            copy.start()

    def forward():
        half(0, far, slot_recv.at[far], sibling).wait_recv()
        half(1, far, local_sem.at[1], sibling).wait_recv()
        passing(2, far).start()

    def finish():
        for block in (sibling, sibling + peers[0] - me, sibling + peers[1] - me, sibling + far - me):
            passing(0, block).wait_recv()
        for step, peer in enumerate(peers + [sibling]):
            near(step, peer).wait_send()
        for side in range(2):
            sent_half(side).wait_send()
            passing(side, peers[side]).wait_send()
        passing(2, far).wait_send()
        own.wait()

    return start, middle, forward, finish


def gather_job(source, target, sems, blocks):
    count = source.shape[0] // 2
    return round_trip(
        source,
        lambda block: target.at[block],
        lambda block, side: target.at[block, pl.ds(side * count, count)],
        sems,
    )


def swap_job(source, target, sems, blocks):
    slot_send, slot_recv, _, local_sem = sems
    me = lax.axis_index(BLK)
    width = source.shape[1] // blocks

    def part_of(block):
        return source.at[:, pl.ds(pl.multiple_of(block * width, width), width)]

    own = pltpu.make_async_copy(part_of(me), target.at[me], local_sem.at[0])

    def copy(step, peer, slot):
        return remote(
            part_of(peer), target.at[slot], slot_send.at[step], slot_recv.at[slot], BLK, peer
        )

    def start():
        for step, peer in enumerate(others(BLK, blocks)):
            copy(step, peer, me).start()
        own.start()

    def finish():
        for step, peer in enumerate(others(BLK, blocks)):
            copy(step, peer, peer).wait_recv()
            copy(step, peer, me).wait_send()
        own.wait()

    return start, lambda: None, lambda: None, finish


def half_swap_job(half):
    def job(source, target, sems, blocks):
        count = source.shape[0] // 2
        return swap_job(source.at[pl.ds(half * count, count)], target, sems, blocks)

    return job


def slot_job(source, target, sems, blocks):
    slot_send, slot_recv, _, local_sem = sems
    me = lax.axis_index(BLK)
    own = pltpu.make_async_copy(source.at[me], target.at[me], local_sem.at[0])

    def copy(step, peer, slot):
        return remote(
            source.at[peer], target.at[slot], slot_send.at[step], slot_recv.at[slot], BLK, peer
        )

    def start():
        for step, peer in enumerate(others(BLK, blocks)):
            copy(step, peer, me).start()
        own.start()

    def finish():
        for step, peer in enumerate(others(BLK, blocks)):
            copy(step, peer, peer).wait_recv()
            copy(step, peer, me).wait_send()
        own.wait()

    return start, lambda: None, lambda: None, finish


def line_job(source, target, sems, blocks):
    line_send, line_recv, _, local_sem = sems
    parts = target.shape[0]
    ch = lax.axis_index(CH)
    right, left = lax.rem(ch + 1, parts), lax.rem(ch + parts - 1, parts)
    own = pltpu.make_async_copy(source, target.at[ch], local_sem.at[0])

    def sides(hop):
        return (
            (0, lax.rem(ch + parts - hop, parts), right, ch - hop >= 0, ch < parts - 1),
            (1, lax.rem(ch + hop, parts), left, ch + hop < parts, ch > 0),
        )

    def copy(block, side, hop, peer):
        return remote(
            source if hop == 0 else target.at[block],
            target.at[block],
            line_send.at[side * (parts - 1) + hop],
            line_recv.at[block],
            CH,
            peer,
        )

    def move(hop):
        for side, block, peer, valid, goes in sides(hop):
            if hop > 0:

                @pl.when(valid)
                def _():
                    copy(block, side, hop, peer).wait_recv()

            if hop < parts - 1:

                @pl.when(valid & goes)
                def _():
                    copy(block, side, hop, peer).start()

    def start():
        own.start()
        move(0)

    def middle():
        move(1)

    def forward():
        for hop in range(2, parts - 1):
            move(hop)

    def finish():
        if parts > 2:
            move(parts - 1)
        for hop in range(parts - 1):
            for side, block, peer, valid, goes in sides(hop):

                @pl.when(valid & goes)
                def _():
                    copy(block, side, hop, peer).wait_send()

        own.wait()

    return start, middle, forward, finish


job_kinds = (gather_job, half_swap_job(0), slot_job, line_job, half_swap_job(1))
gather_kind, upper_kind, slot_kind, line_kind, lower_kind = 0, 1, 2, 3, 4


def job_target(kind, shape, dtype, blocks):
    if kind == gather_kind:
        shape = (blocks,) + shape
    elif kind == line_kind:
        shape = (lax.axis_size(CH),) + shape
    elif kind in (upper_kind, lower_kind):
        shape = (blocks, shape[0] // 2, shape[1] // blocks)
    return jax.ShapeDtypeStruct(shape, dtype)


def job_sems(blocks):
    dma = pltpu.SemaphoreType.DMA
    return [dma((blocks,)), dma((blocks,)), dma((blocks,)), dma((2,))]


def job_call(kernel, jobs, blocks, in_specs, out_specs, out_shape, scratch_shapes, **options):
    anywhere = pl.BlockSpec(memory_space=pl.ANY)
    n_in, n_out, n_scratch = len(in_specs), len(out_specs), len(scratch_shapes)
    count = len(jobs)

    def wrapped(*refs):
        ins, refs = refs[:n_in], refs[n_in:]
        sources, refs = refs[:count], refs[count:]
        outs, refs = refs[:n_out], refs[n_out:]
        targets, refs = refs[:count], refs[count:]
        scratch, sems = refs[:n_scratch], refs[n_scratch:]
        running = [
            job_kinds[kind](
                sources[place].at[index[0]] if index else sources[place],
                targets[place],
                sems[4 * place : 4 * place + 4],
                blocks,
            )
            for place, (kind, _, *index) in enumerate(jobs)
        ]
        kernel(running, *ins, *outs, *scratch)

    def call(*operands):
        result = pl.pallas_call(
            wrapped,
            in_specs=list(in_specs) + [anywhere] * count,
            out_specs=list(out_specs) + [anywhere] * count,
            out_shape=list(out_shape) + [
                job_target(kind, source.shape[len(index) :], source.dtype, blocks)
                for kind, source, *index in jobs
            ],
            scratch_shapes=list(scratch_shapes) + job_sems(blocks) * count,
            **options,
        )(*operands, *[job[1] for job in jobs])
        return result[:n_out], result[n_out:]

    return call


def stripe_job(wr_ref, we_ref, layer, mine, sems, blocks, parts):
    part_send, part_recv, local_sem = sems
    _, mid, feat = wr_ref.shape
    _, narrow, wide = we_ref.shape
    blk, ch = lax.axis_index(BLK), lax.axis_index(CH)

    def cut(index, size):
        return pl.ds(pl.multiple_of(index * size, size), size)

    def source(array):
        if array == 0:
            return wr_ref.at[layer, :, cut(blk, feat // blocks)]
        return we_ref.at[layer, cut(blk, narrow // blocks), :]

    def share(array, part):
        if array == 0:
            return mine[0].at[cut(part, mid), :]
        return mine[1].at[:, cut(part, wide)]

    def own(array):
        return pltpu.make_async_copy(source(array), share(array, ch), local_sem.at[array])

    def copy(array, step, peer, slot):
        return remote(
            source(array),
            share(array, slot),
            part_send.at[array, step],
            part_recv.at[array, slot],
            CH,
            peer,
        )

    def start():
        for array in range(2):
            own(array).start()
            for step, peer in enumerate(others(CH, parts)):
                copy(array, step, peer, ch).start()

    def finish():
        for array in range(2):
            for step, peer in enumerate(others(CH, parts)):
                copy(array, step, peer, peer).wait_recv()
            own(array).wait()
            for step, peer in enumerate(others(CH, parts)):
                copy(array, step, peer, ch).wait_send()

    return start, finish


def stripe_sems(parts):
    dma = pltpu.SemaphoreType.DMA
    return [dma((2, parts)), dma((2, parts)), dma((2,))]


def stripe_shapes(parts, blocks, reduce_w, expand_w):
    _, mid, feat = reduce_w.shape
    narrow = mid * parts
    return [
        jax.ShapeDtypeStruct((narrow, feat // blocks), reduce_w.dtype),
        jax.ShapeDtypeStruct((narrow // blocks, feat), expand_w.dtype),
    ]


def spread_jobs(mine, fulls, sems, blocks):
    half_rows = mine[0].shape[0] // 2
    width, height = mine[0].shape[1], mine[1].shape[0]
    half_cols = mine[1].shape[1] // 2

    def cut(index, size):
        return pl.ds(pl.multiple_of(index * size, size), size)

    return [
        round_trip(
            mine[0],
            lambda block: fulls[0].at[:, cut(block, width)],
            lambda block, side: fulls[0].at[pl.ds(side * half_rows, half_rows), cut(block, width)],
            sems[:4],
        ),
        round_trip(
            mine[1],
            lambda block: fulls[1].at[cut(block, height), :],
            lambda block, side: fulls[1].at[cut(block, height), pl.ds(side * half_cols, half_cols)],
            sems[4:],
        ),
    ]


def prologue_kernel(
    blocks,
    parts,
    feat_ref,
    wr_ref,
    we_ref,
    *refs,
):
    small_refs, ids_ref, cur_ref, mine_r, mine_e = refs[:4], *refs[4:8]
    full_r, full_e, small_outs, own_ref, all_ref = *refs[8:10], refs[10:14], *refs[14:16]
    line_send, line_recv, small_send, small_recv, local_sem, *sems = refs[16:]
    pixels, wide = feat_ref.shape
    blk, ch = lax.axis_index(BLK), lax.axis_index(CH)
    smalls = tuple(zip(small_refs, small_outs))

    def lane_part(index):
        return cur_ref.at[:, pl.ds(pl.multiple_of(index * wide, wide), wide)]

    start, gathered = stripe_job(wr_ref, we_ref, 0, (mine_r, mine_e), sems[:3], blocks, parts)
    jobs = spread_jobs((mine_r, mine_e), (full_r, full_e), sems[3:], blocks)
    own = pltpu.make_async_copy(feat_ref, lane_part(ch), local_sem.at[0])
    own.start()
    announce(
        [(CH, peer) for peer in others(CH, parts)] + [(BLK, peer) for peer in near_blocks()]
    )
    start()

    right, left = lax.rem(ch + 1, parts), lax.rem(ch + parts - 1, parts)

    def sides(hop):
        return (
            (0, lax.rem(ch + parts - hop, parts), right, ch - hop >= 0, ch < parts - 1),
            (1, lax.rem(ch + hop, parts), left, ch + hop < parts, ch > 0),
        )

    def line_copy(block, side, hop, peer):
        return remote(
            feat_ref if hop == 0 else lane_part(block),
            lane_part(block),
            line_send.at[side, hop],
            line_recv.at[block],
            CH,
            peer,
        )

    def line_hop(hop):
        for side, block, peer, valid, goes in sides(hop):
            if hop > 0:

                @pl.when(valid)
                def _():
                    line_copy(block, side, hop, peer).wait_recv()

            if hop < parts - 1:

                @pl.when(valid & goes)
                def _():
                    line_copy(block, side, hop, peer).start()

    def small_copy(place, step, peer, slot):
        source, target = smalls[place]
        return remote(
            source,
            target.at[slot],
            small_send.at[place, step],
            small_recv.at[place, slot],
            CH,
            peer,
        )

    def small_own(place):
        source, target = smalls[place]
        return pltpu.make_async_copy(source, target.at[ch], local_sem.at[1 + place])

    line_hop(0)
    for place in range(4):
        small_own(place).start()
        for step, peer in enumerate(others(CH, parts)):
            small_copy(place, step, peer, ch).start()
    gathered()
    for job in jobs:
        job[0]()

    rows = own_ref.shape[1] // lanes
    lane = lax.broadcasted_iota(jnp.int32, (1, lanes), 1)

    def moved(values, step):
        turned = values if step == 0 else pltpu.roll(values, (lanes - step) % lanes, 1)
        return jnp.where((lane + step >= 0) & (lane + step < lanes), turned, -2)

    def spread(target, row, bits):
        block = jnp.broadcast_to(bits.astype(jnp.float32), (lanes, lanes)).T
        target[pl.ds(pl.multiple_of(row * lanes, lanes), lanes), :] = block.astype(jnp.int32)

    def own_row(row, state):
        place = 2 + blk * rows + row
        for word, reach in enumerate((1, 2)):
            bits = jnp.zeros((1, lanes), jnp.int32)
            for tap, (row_step, col_step) in enumerate(tap_offsets):
                a, b = row_step * reach, col_step * reach
                taken = moved(ids_ref[place], -b) == ids_ref[place + a]
                bits = bits | jnp.where(taken, 1 << tap, 0)
                taken = moved(ids_ref[place - a], -b) == ids_ref[place]
                bits = bits | jnp.where(taken, 1 << (9 + tap), 0)
            spread(own_ref.at[word], row, bits)
        return state

    lax.fori_loop(0, rows, own_row, 0)

    def any_row(row, state):
        bits = jnp.zeros((1, lanes), jnp.int32)
        for tap, (row_step, col_step) in enumerate(tap_offsets):
            taken = moved(ids_ref[2 + row + row_step], col_step) == ids_ref[2 + row]
            bits = bits | jnp.where(taken, 1 << tap, 0)
        spread(all_ref, row, bits)
        return state

    lax.fori_loop(0, ids_ref.shape[0] - 4, any_row, 0)
    for hop in range(1, parts):
        line_hop(hop)
        if hop <= 2:
            for job in jobs:
                job[hop]()
    if parts == 2:
        for job in jobs:
            job[2]()
    for job in jobs:
        job[3]()
    for hop in range(parts - 1):
        for side, block, peer, valid, goes in sides(hop):

            @pl.when(valid & goes)
            def _():
                line_copy(block, side, hop, peer).wait_send()

    for place in range(4):
        for step, peer in enumerate(others(CH, parts)):
            small_copy(place, step, peer, peer).wait_recv()
            small_copy(place, step, peer, ch).wait_send()
        small_own(place).wait()
    own.wait()


def prologue(blocks, parts, features, reduce_w, expand_w, terms, canvas_ids):
    layers, mid, feat = reduce_w.shape
    pixels, wide = features.shape
    narrow = mid * parts
    f32, low = jnp.float32, jnp.bfloat16
    shape = jax.ShapeDtypeStruct
    ids = jnp.pad(canvas_ids, ((2, 2), (0, 0)), constant_values=-1)[:, None]
    anywhere = pl.BlockSpec(memory_space=pl.ANY)
    inside = pl.BlockSpec(memory_space=pltpu.VMEM)
    dma = pltpu.SemaphoreType.DMA
    return pl.pallas_call(
        functools.partial(prologue_kernel, blocks, parts),
        in_specs=[anywhere] * 7 + [inside],
        out_specs=[anywhere] * 9 + [inside] * 2,
        out_shape=[
            shape((pixels, feat), low),
            *stripe_shapes(parts, blocks, reduce_w, expand_w),
            shape((narrow, feat), low),
            shape((narrow, feat), low),
            *[shape((parts,) + term.shape, f32) for term in terms],
            shape((2, pixels, lanes), jnp.int32),
            shape((pixels * blocks, lanes), jnp.int32),
        ],
        scratch_shapes=[
            dma((2, parts)),
            dma((parts,)),
            dma((4, parts)),
            dma((4, parts)),
            dma((5,)),
        ]
        + stripe_sems(parts)
        + job_sems(blocks) * 2,
        compiler_params=comm_params(5),
        cost_estimate=pl.CostEstimate(flops=10**6, bytes_accessed=10**8, transcendentals=0),
    )(features, reduce_w, expand_w, *terms, ids)


def greet_line(blocks):
    barrier = pltpu.get_barrier_semaphore()
    me = lax.axis_index(BLK)
    for peer in (lax.rem(me + 1, blocks), lax.rem(me + blocks - 1, blocks)):
        pl.semaphore_signal(barrier, inc=1, device_id={BLK: peer}, device_id_type=MESH)
    pl.semaphore_wait(barrier, 2)


def greet_blocks(blocks):
    announce([(BLK, peer) for peer in others(BLK, blocks)])


def edge_copies(main_ref, low_ref, high_ref, edge, send_sem, recv_sem, blocks):
    me = lax.axis_index(BLK)
    lead = (slice(None),) * (len(main_ref.shape) - 2)
    pixels = main_ref.shape[-2]
    up = remote(
        main_ref.at[lead + (pl.ds(pixels - edge, edge),)],
        low_ref,
        send_sem.at[0],
        recv_sem.at[0],
        BLK,
        lax.rem(me + 1, blocks),
    )
    down = remote(
        main_ref.at[lead + (pl.ds(0, edge),)],
        high_ref,
        send_sem.at[1],
        recv_sem.at[1],
        BLK,
        lax.rem(me + blocks - 1, blocks),
    )

    def start():
        @pl.when(me < blocks - 1)
        def _():
            up.start()

        @pl.when(me > 0)
        def _():
            down.start()

    def finish(zero=True):
        @pl.when(me > 0)
        def _():
            up.wait_recv()
            down.wait_send()

        @pl.when(me < blocks - 1)
        def _():
            down.wait_recv()
            up.wait_send()

        if zero:

            @pl.when(me == 0)
            def _():
                low_ref[...] = jnp.zeros(low_ref.shape, low_ref.dtype)

            @pl.when(me == blocks - 1)
            def _():
                high_ref[...] = jnp.zeros(high_ref.shape, high_ref.dtype)

    return start, finish


def heads_forward_kernel(blocks, fetch, jobs, main_ref, w_ref, mask_ref, *refs):
    if fetch:
        mine_r, mine_e, *refs = refs
    pre_ref, act_ref, ends_ref, *refs = refs
    if fetch:
        full_r, full_e, *refs = refs
    ext_ref, z_ref, local_sem, halo_send, halo_recv, *sems = refs
    step = pl.program_id(0)
    head_count, pixels, mid = pre_ref.shape
    cols = (ext_ref.shape[0] - pixels) // 2
    feat = ext_ref.shape[1]
    start, finish = edge_copies(
        main_ref,
        ext_ref.at[pl.ds(0, cols)],
        ext_ref.at[pl.ds(cols + pixels, cols)],
        cols,
        halo_send,
        halo_recv,
        blocks,
    )
    own = pltpu.make_async_copy(main_ref, ext_ref.at[pl.ds(cols, pixels)], local_sem.at[0])
    if fetch:
        jobs = jobs + spread_jobs((mine_r, mine_e), (full_r, full_e), sems, blocks)

    @pl.when(step == 0)
    def _():
        own.start()
        if jobs:
            greet_blocks(blocks)
        else:
            greet_line(blocks)
        start()
        for job in jobs:
            job[0]()
        own.wait()

    @pl.when(step == 3)
    def _():
        finish()

    if jobs:

        @pl.when(step == 7)
        def _():
            for job in jobs:
                job[1]()

    row_step = jnp.where(step < 3, 1, jnp.where(step < 6, 0, 2))
    col_step = lax.rem(step, 3)
    window = ext_ref[pl.ds(pl.multiple_of(row_step * cols, cols), pixels), :]
    product = contract_last(window, w_ref[0].reshape(head_count * mid, feat))
    product = masked(product, mask_ref[0], tap_at(step))

    @pl.when(step < 3)
    def _():
        z_ref[col_step] = product

    @pl.when(step >= 3)
    def _():
        z_ref[col_step] += product

    @pl.when(step == 8)
    def _():
        for head in range(head_count):
            part = slice(head * mid, (head + 1) * mid)
            total = (
                z_ref[1, :, part]
                + pltpu.roll(z_ref[0, :, part], 1, 0)
                + pltpu.roll(z_ref[2, :, part], pixels - 1, 0)
            )
            pre_ref[head] = total
            value = (total * sigmoid(total)).astype(jnp.bfloat16)
            act_ref[head] = value
            if head in targets:
                ends_ref[targets.index(head)] = value
        for job in jobs:
            job[2]()
        for job in jobs:
            job[3]()


def tap_at(step):
    return jnp.where(step < 3, step + 3, jnp.where(step < 6, step - 3, step))


def heads_forward(blocks, layer, jobs, cols, main, weights, mask, mine):
    _, head_count, _, mid, feat = weights.shape
    pixels = main.shape[0]
    f32, low = jnp.float32, jnp.bfloat16
    shape = jax.ShapeDtypeStruct
    anywhere = pl.BlockSpec(memory_space=pl.ANY)
    dma = pltpu.SemaphoreType.DMA
    return job_call(
        functools.partial(heads_forward_kernel, blocks, bool(mine)),
        jobs,
        blocks,
        grid=(9,),
        in_specs=[
            anywhere,
            pl.BlockSpec((1, head_count, 1, mid, feat), lambda t: (layer, 0, tap_at(t), 0, 0)),
            pl.BlockSpec((1, pixels, lanes), lambda t: (0, 0, 0)),
        ]
        + [anywhere] * len(mine),
        out_specs=[whole((head_count, pixels, mid))] * 2
        + [whole((2, pixels, mid))]
        + [anywhere] * len(mine),
        out_shape=[
            shape((head_count, pixels, mid), f32),
            shape((head_count, pixels, mid), low),
            shape((2, pixels, mid), low),
        ]
        + [shape((mine[0].shape[0], feat), low) for _ in mine],
        scratch_shapes=[
            pltpu.VMEM((pixels + 2 * cols, feat), low),
            pltpu.VMEM((3, pixels, head_count * mid), f32),
            dma((1,)),
            dma((2,)),
            dma((2,)),
        ]
        + (job_sems(blocks) * 2 if mine else []),
        compiler_params=comm_params(6 + layer),
        cost_estimate=pl.CostEstimate(
            flops=18 * pixels * head_count * mid * feat,
            bytes_accessed=18 * head_count * mid * feat,
            transcendentals=0,
        ),
    )(main, weights, mask, *mine)


def fill_taps(im_ref, slot, grad, bits, pixels, cols, dilation):
    rows, mid = grad.shape
    wide = grad.astype(jnp.float32)
    shifted_by = (pltpu.roll(wide, rows - dilation, 0), wide, pltpu.roll(wide, dilation, 0))
    for tap, (row_step, col_step) in enumerate(tap_offsets):
        start = (1 - row_step) * dilation * cols
        part = shifted_by[col_step + 1][start : start + pixels]
        im_ref[slot, :, tap * mid : (tap + 1) * mid] = masked(part, bits, 9 + tap).astype(
            jnp.bfloat16
        )


def messages_kernel(
    blocks,
    layer,
    ahead,
    jobs,
    feat_ref,
    w_hbm,
    cots_ref,
    gain_ref,
    bias_ref,
    mask_ref,
    maps_ref,
    local_ref,
    sums_ref,
    part_ref,
    values_ref,
    pack_ref,
    main_ref,
    low_ref,
    high_ref,
    cot_low,
    cot_high,
    w_ref,
    lhs_ref,
    z_ref,
    im_ref,
    grad_ref,
    *sems,
):
    w_sem, local_sem, halo_send, halo_recv, cot_send, cot_recv, *sems = sems
    parts, heads, pixels, mid = feat_ref.shape
    cot_ref = cots_ref.at[layer]
    cols = low_ref.shape[2]
    pairs = w_ref.shape[0]
    me, ch = lax.axis_index(BLK), lax.axis_index(CH)
    low = jnp.bfloat16
    loads = [
        pltpu.make_async_copy(w_hbm.at[layer, pair], w_ref.at[pair], w_sem.at[pair])
        for pair in range(pairs)
    ]
    main_copy = pltpu.make_async_copy(feat_ref, main_ref, local_sem.at[0])
    main_copy.start()
    for pair in (0, 4, 1, 5, 3, 2):
        loads[pair].start()
    greet(blocks, parts)
    early, jobs = jobs[:ahead], jobs[ahead:]
    for job in early:
        job[0]()
    start, finish = edge_copies(feat_ref, low_ref, high_ref, cols, halo_send, halo_recv, blocks)
    start()
    cot_start, cot_finish = edge_copies(
        cot_ref, cot_low, cot_high, cols, cot_send, cot_recv, blocks
    )
    cot_start()
    for job in jobs:
        job[0]()
    main_copy.wait()
    size = parts * mid // blocks
    for block in range(blocks):
        part, first = block * size // mid, block * size % mid
        for index, (one, two) in enumerate(groups):
            (pack_ref if sems else values_ref)[block, index] = jnp.concatenate(
                [main_ref[part, one][:, first : first + size], main_ref[part, two][:, first : first + size]],
                axis=1,
            )
    if sems:
        jobs = jobs + [slot_job(pack_ref, values_ref, sems, blocks)]
        jobs[-1][0]()
    for source in range(heads):
        for part in range(parts):
            lhs_ref[source, cols : cols + pixels, part * mid : (part + 1) * mid] = main_ref[part, source]
    order = (0, 4, 1, 5, 3, 2)
    bits = mask_ref[0]

    def taps(pair, row_step):
        source = message_pairs[pair][0]
        product = contract_last(
            lhs_ref[source, row_step * cols : row_step * cols + pixels, :],
            w_ref[pair, 3 * row_step : 3 * row_step + 3].reshape(3 * mid, parts * mid),
        )
        for col_step in range(3):
            value = masked(
                product[:, col_step * mid : (col_step + 1) * mid], bits, row_step * 3 + col_step
            )
            if row_step == 1:
                z_ref[pair, col_step] = value
            else:
                z_ref[pair, col_step] += value

    for pair in order:
        loads[pair].wait()
        taps(pair, 1)
    finish()
    cot_finish()
    for source in range(heads):
        for part in range(parts):
            chan = slice(part * mid, (part + 1) * mid)
            lhs_ref[source, 0:cols, chan] = low_ref[part, source]
            lhs_ref[source, cols + pixels :, chan] = high_ref[part, source]
    for pair in order:
        taps(pair, 0)
        taps(pair, 2)
    for job in early:
        job[1]()
    values = {}
    cots = {}
    for place, target in enumerate((0, 3)):
        values[target] = main_ref[ch, target].astype(jnp.float32)
        cots[target] = cot_ref[place].astype(jnp.float32)
    for place, target in enumerate((0, 3)):
        value, cot = values[target], cots[target]
        total, slopes = value, cot
        for pair in range(pairs):
            if message_pairs[pair][1] != target:
                continue
            message = (
                z_ref[pair, 1]
                + pltpu.roll(z_ref[pair, 0], 1, 0)
                + pltpu.roll(z_ref[pair, 2], pixels - 1, 0)
            )
            gain, bias = gain_ref[layer, pair : pair + 1], bias_ref[layer, pair : pair + 1]
            gate = sigmoid(gain * value + bias)
            total = total + gate * message
            grad_ref[pair] = (cot * gate).astype(low)
            slope = cot * message * gate * (1.0 - gate)
            sums_ref[pair : pair + 1] = jnp.sum(slope * value, axis=0, keepdims=True)
            sums_ref[pairs + pair : pairs + pair + 1] = jnp.sum(slope, axis=0, keepdims=True)
            slopes = slopes + slope * gain
        maps_ref[place] = total.astype(low)
        local_ref[place] = slopes

    for job in jobs:
        job[1]()

    def product_of(pair, slot):
        source, target = message_pairs[pair]
        place = 0 if target == 0 else 1
        gain, bias = gain_ref[layer, pair : pair + 1], bias_ref[layer, pair : pair + 1]

        def border(cot, feat):
            return (
                cot[place].astype(jnp.float32)
                * sigmoid(gain * feat[ch, target].astype(jnp.float32) + bias)
            ).astype(low)

        grad = jnp.concatenate(
            [border(cot_low, low_ref), grad_ref[pair], border(cot_high, high_ref)], axis=0
        )
        fill_taps(im_ref, slot, grad, bits, pixels, cols, 1)
        return jnp.dot(
            im_ref[slot],
            w_ref[pair].reshape(9 * mid, parts * mid),
            preferred_element_type=jnp.float32,
        )

    for count, (source, *members) in enumerate(source_order):
        if count == 2:
            for job in early:
                job[2]()
        total = product_of(members[0], 0)
        for pair in members[1:]:
            total = total + product_of(pair, 1)
        for part in range(parts):
            part_ref[part, source] = total[:, part * mid : (part + 1) * mid].astype(low)
    for job in jobs:
        job[2]()
    for job in early + jobs:
        job[3]()


def messages_both(blocks, layer, jobs, ahead, send, cols, features, weights, cotangents, gains, biases, mask):
    parts, heads, pixels, mid = features.shape
    pairs = weights.shape[1]
    narrow = parts * mid
    f32, low = jnp.float32, jnp.bfloat16
    shape = jax.ShapeDtypeStruct
    anywhere = pl.BlockSpec(memory_space=pl.ANY)
    inside = pl.BlockSpec(memory_space=pltpu.VMEM)
    dma = pltpu.SemaphoreType.DMA
    wide = 2 * narrow // blocks
    values = shape((blocks, 2, pixels, wide), low)
    return job_call(
        functools.partial(messages_kernel, blocks, layer, ahead),
        jobs,
        blocks,
        in_specs=[anywhere, anywhere] + [inside] * 4,
        out_specs=[inside] * 4 + [anywhere if send else inside],
        out_shape=[
            shape((2, pixels, mid), low),
            shape((2, pixels, mid), f32),
            shape((2 * pairs, mid), f32),
            shape((parts, heads, pixels, mid), low),
            values,
        ],
        scratch_shapes=[
            pltpu.VMEM(values.shape if send else (8, lanes), low),
            pltpu.VMEM((parts, heads, pixels, mid), low),
            pltpu.VMEM((parts, heads, cols, mid), low),
            pltpu.VMEM((parts, heads, cols, mid), low),
            pltpu.VMEM((2, cols, mid), low),
            pltpu.VMEM((2, cols, mid), low),
            pltpu.VMEM((pairs, 9, mid, narrow), low),
            pltpu.VMEM((heads, pixels + 2 * cols, narrow), low),
            pltpu.VMEM((pairs, 3, pixels, mid), f32),
            pltpu.VMEM((2, pixels, 9 * mid), low),
            pltpu.VMEM((pairs, pixels, mid), low),
            dma((pairs,)),
            dma((1,)),
            dma((2,)),
            dma((2,)),
            dma((2,)),
            dma((2,)),
        ]
        + (job_sems(blocks) if send else []),
        compiler_params=comm_params(10 + layer),
        cost_estimate=pl.CostEstimate(
            flops=36 * pixels * pairs * mid * narrow,
            bytes_accessed=18 * pairs * mid * narrow,
            transcendentals=0,
        ),
    )(features, weights, cotangents, gains, biases, mask)


def heads_backward_kernel(
    blocks,
    jobs,
    main_ref,
    w_ref,
    mask_ref,
    out_ref,
    low_ref,
    high_ref,
    im_ref,
    halo_send,
    halo_recv,
):
    step = pl.program_id(0)
    head_count, pixels, mid = main_ref.shape
    cols = low_ref.shape[1]

    @pl.when(step == 0)
    def _():
        start, finish = edge_copies(main_ref, low_ref, high_ref, cols, halo_send, halo_recv, blocks)
        if jobs:
            greet_blocks(blocks)
        else:
            greet_line(blocks)
        start()
        for job in jobs:
            job[0]()
        finish()
        for head in range(head_count):
            grad = jnp.concatenate([low_ref[head], main_ref[head], high_ref[head]], axis=0)
            fill_taps(im_ref, head, grad, mask_ref[0], pixels, cols, 1)

    total = None
    for head in range(head_count):
        product = jnp.dot(
            im_ref[head],
            w_ref[0, head].reshape(9 * mid, w_ref.shape[4]),
            preferred_element_type=jnp.float32,
        )
        total = product if total is None else total + product
    out_ref[0] = total.astype(jnp.bfloat16)

    if jobs:

        @pl.when(step == pl.num_programs(0) - 1)
        def _():
            for part in (1, 2, 3):
                for job in jobs:
                    job[part]()


def heads_backward(blocks, layer, jobs, cols, main, weights, mask, parts):
    _, head_count, taps, mid, feat = weights.shape
    pixels = main.shape[1]
    width = feat // parts
    dma = pltpu.SemaphoreType.DMA
    return job_call(
        functools.partial(heads_backward_kernel, blocks),
        jobs,
        blocks,
        grid=(parts,),
        in_specs=[
            whole(main.shape),
            pl.BlockSpec((1, head_count, taps, mid, width), lambda j: (layer, 0, 0, 0, j)),
            pl.BlockSpec((1, pixels, lanes), lambda j: (0, 0, 0)),
        ],
        out_specs=[pl.BlockSpec((1, pixels, width), lambda j: (j, 0, 0))],
        out_shape=[jax.ShapeDtypeStruct((parts, pixels, width), jnp.bfloat16)],
        scratch_shapes=[
            pltpu.VMEM((head_count, cols, mid), jnp.bfloat16),
            pltpu.VMEM((head_count, cols, mid), jnp.bfloat16),
            pltpu.VMEM((head_count, pixels, taps * mid), jnp.bfloat16),
            dma((2,)),
            dma((2,)),
        ],
        compiler_params=comm_params(20 + layer),
        cost_estimate=pl.CostEstimate(
            flops=18 * pixels * head_count * mid * feat,
            bytes_accessed=18 * head_count * mid * feat,
            transcendentals=0,
        ),
    )(main, weights, mask)


class WeightChunks:
    def __init__(self, blocks, layer, sources, gates, buffers, accs, lhs, sems):
        self.blocks, self.layer = blocks, layer
        (self.mv, self.cot, self.ends, self.hv_up, self.hv_low, self.hg, self.bits) = sources
        self.gain, self.bias = gates
        (self.mv_buf, self.cot_buf, self.ends_buf, self.hv_buf, self.hg_buf, self.bits_buf) = buffers
        self.accs, self.lhs, self.sems = accs, lhs, sems
        self.done = 0
        self.pixels = 2 * self.hv_up.shape[1]

    def copies(self, heads, index):
        pixels, last = self.pixels, self.blocks - 1
        before, after = jnp.maximum(index - 1, 0), jnp.minimum(index + 1, last)
        slot = lax.rem(index, 2)
        buffer = self.hv_buf if heads else self.mv_buf
        if heads:
            half = pixels // 2
            pairs = [
                (
                    self.hv_low.at[before, pl.ds(half - lanes, lanes)],
                    buffer.at[slot, pl.ds(0, lanes)],
                ),
                (self.hv_up.at[index], buffer.at[slot, pl.ds(lanes, half)]),
                (self.hv_low.at[index], buffer.at[slot, pl.ds(lanes + half, half)]),
                (
                    self.hv_up.at[after, pl.ds(0, lanes)],
                    buffer.at[slot, pl.ds(lanes + pixels, lanes)],
                ),
            ]
        else:
            every = slice(None)
            pairs = [
                (
                    self.mv.at[before, every, pl.ds(pixels - lanes, lanes)],
                    buffer.at[slot, every, pl.ds(0, lanes)],
                ),
                (self.mv.at[index], buffer.at[slot, every, pl.ds(lanes, pixels)]),
                (
                    self.mv.at[after, every, pl.ds(0, lanes)],
                    buffer.at[slot, every, pl.ds(lanes + pixels, lanes)],
                ),
            ]
        pairs.append(
            (
                self.bits.at[pl.ds(pl.multiple_of(index * pixels, pixels), pixels)],
                self.bits_buf.at[slot],
            )
        )
        if heads:
            pairs.append((self.hg.at[index], self.hg_buf.at[slot]))
        else:
            pairs.append((self.cot.at[index], self.cot_buf.at[slot]))
            pairs.append((self.ends.at[index], self.ends_buf.at[slot]))
        return [
            pltpu.make_async_copy(source, target, self.sems.at[slot, place])
            for place, (source, target) in enumerate(pairs)
        ]

    def fetch(self, heads, index):
        for copy in self.copies(heads, index):
            copy.start()

    def begin(self):
        for acc in self.accs:
            acc[...] = jnp.zeros(acc.shape, acc.dtype)
        self.fetch(False, 0)

    def add(self, heads, index):
        slot = lax.rem(index, 2)
        pixels = self.pixels
        for copy in self.copies(heads, index):
            copy.wait()

        @pl.when(index + 1 < self.blocks)
        def _():
            self.fetch(heads, index + 1)

        if not heads:

            @pl.when(index + 1 == self.blocks)
            def _():
                self.fetch(True, 0)

        bits = self.bits_buf[slot]
        for place, members in enumerate((tuple(range(4)),) if heads else group_pairs):
            window = (self.hv_buf[slot] if heads else self.mv_buf[slot, place]).astype(jnp.float32)
            size, chans = window.shape
            shifted_by = (pltpu.roll(window, 1, 0), window, pltpu.roll(window, size - 1, 0))
            for tap, (row_step, col_step) in enumerate(tap_offsets):
                top = (1 + row_step) * lanes
                part = shifted_by[col_step + 1][top : top + pixels]
                self.lhs[:, tap * chans : (tap + 1) * chans] = masked(part, bits, tap).astype(
                    jnp.bfloat16
                )
            if heads:
                grads = [self.hg_buf[slot, member] for member in members]
            else:
                grads = [self.message_grad(slot, pair) for pair in members]
            acc = self.accs[2] if heads else self.accs[place]
            acc[...] += lax.dot_general(
                self.lhs[:, : 9 * chans],
                jnp.concatenate(grads, axis=1),
                (((0,), (0,)), ((), ())),
                preferred_element_type=jnp.float32,
            )

    def message_grad(self, slot, pair):
        place = targets.index(message_pairs[pair][1])
        gain = self.gain[self.layer, pair : pair + 1]
        bias = self.bias[self.layer, pair : pair + 1]
        gate = sigmoid(gain * self.ends_buf[slot, place].astype(jnp.float32) + bias)
        return (self.cot_buf[slot, place].astype(jnp.float32) * gate).astype(jnp.bfloat16)

    def run(self, count):
        while count:
            heads = self.done >= self.blocks
            start = self.done % self.blocks
            size = min(count, self.blocks - start)

            def step(index, state):
                self.add(heads, index)
                return state

            lax.fori_loop(start, start + size, step, 0)
            self.done += size
            count -= size


def exchange_kernel(blocks, jobs, done_ref):
    greet_blocks(blocks)
    for part in range(4):
        for job in jobs:
            job[part]()
    done_ref[...] = jnp.zeros(done_ref.shape, done_ref.dtype)


def exchange(blocks, jobs):
    _, moved = job_call(
        functools.partial(exchange_kernel, blocks),
        jobs,
        blocks,
        in_specs=[],
        out_specs=[pl.BlockSpec(memory_space=pltpu.VMEM)],
        out_shape=[jax.ShapeDtypeStruct((8, lanes), jnp.float32)],
        scratch_shapes=[],
        compiler_params=comm_params(30),
        cost_estimate=pl.CostEstimate(flops=10**6, bytes_accessed=10**8, transcendentals=0),
    )()
    return moved


def heads_store(out_ref, acc_ref):
    head_count, taps, chans, mid = out_ref.shape
    for head in range(head_count):
        for tap in range(taps):
            out_ref[head, tap] = acc_ref[
                tap * chans : (tap + 1) * chans, head * mid : (head + 1) * mid
            ]


def messages_store(out_ref, acc_refs):
    _, taps, size, mid = out_ref.shape
    for index, members in enumerate(group_pairs):
        for place, pair in enumerate(members):
            side = groups[index].index(message_pairs[pair][0])
            for tap in range(taps):
                start = (2 * tap + side) * size
                out_ref[pair, tap] = acc_refs[index][
                    start : start + size, place * mid : (place + 1) * mid
                ]


def greet(blocks, parts):
    barrier = pltpu.get_barrier_semaphore()
    blk, ch = lax.axis_index(BLK), lax.axis_index(CH)
    for step in range(1, blocks):
        pl.semaphore_signal(
            barrier, inc=1, device_id={BLK: lax.rem(blk + step, blocks)}, device_id_type=MESH
        )
    for step in range(1, parts):
        pl.semaphore_signal(
            barrier, inc=1, device_id={CH: lax.rem(ch + step, parts)}, device_id_type=MESH
        )
    pl.semaphore_wait(barrier, blocks + parts - 2)


def send_slots(source_of, target_ref, send_sem, recv_sem, axis, count):
    me = lax.axis_index(axis)
    copies = []
    for step in range(1, count):
        peer = lax.rem(me + step, count)
        copy = pltpu.make_async_remote_copy(
            src_ref=source_of(peer),
            dst_ref=target_ref.at[me],
            send_sem=send_sem.at[step],
            recv_sem=recv_sem.at[me],
            device_id={axis: peer},
            device_id_type=MESH,
        )
        copy.start()
        copies.append(copy)

    def finish():
        for step in range(1, count):
            peer = lax.rem(me + step, count)
            pltpu.make_async_remote_copy(
                src_ref=target_ref.at[peer],
                dst_ref=target_ref.at[peer],
                send_sem=send_sem.at[step],
                recv_sem=recv_sem.at[peer],
                device_id={axis: peer},
                device_id_type=MESH,
            ).wait_recv()
        for copy in copies:
            copy.wait_send()

    return finish


def block_totals(first, second, stat_ref, send_sem, recv_sem, blocks, meanwhile=None):
    me = lax.axis_index(BLK)
    stat_ref[me, 0:1] = first
    stat_ref[me, 1:2] = second
    finish = send_slots(lambda _: stat_ref.at[me], stat_ref, send_sem, recv_sem, BLK, blocks)
    if meanwhile is not None:
        meanwhile()
    finish()
    total = stat_ref[0]
    for block in range(1, blocks):
        total = total + stat_ref[block]
    return total[0:1], total[1:2]


def fold(values):
    rows, width = values.shape
    return values.reshape(rows // 8, 8, width).sum(axis=0)


def row_loop(rows, block, body, carry):
    def step(index, state):
        return body(pl.ds(pl.multiple_of(index * block, block), block), state)

    return lax.fori_loop(0, rows // block, step, carry)


def moments(ref, block):
    rows, width = ref.shape

    def body(part, state):
        values = ref[part, :]
        return state[0] + fold(values), state[1] + fold(values * values)

    zero = jnp.zeros((8, width), jnp.float32)
    total, square = row_loop(rows, block, body, (zero, zero))
    return total.sum(axis=0, keepdims=True), square.sum(axis=0, keepdims=True)


def halo_copies(ref, edge, pixels, send_sem, recv_sem, blocks):
    me = lax.axis_index(BLK)

    def copy(source, target, side, peer):
        return pltpu.make_async_remote_copy(
            src_ref=ref.at[pl.ds(source, edge)],
            dst_ref=ref.at[pl.ds(target, edge)],
            send_sem=send_sem.at[side],
            recv_sem=recv_sem.at[side],
            device_id={BLK: peer},
            device_id_type=MESH,
        )

    up = copy(pixels, 0, 0, lax.rem(me + 1, blocks))
    down = copy(edge, edge + pixels, 1, lax.rem(me + blocks - 1, blocks))

    @pl.when(me < blocks - 1)
    def _():
        up.start()

    @pl.when(me > 0)
    def _():
        down.start()

    @pl.when(me == 0)
    def _():
        ref[0:edge, :] = jnp.zeros((edge, ref.shape[1]), ref.dtype)

    @pl.when(me == blocks - 1)
    def _():
        ref[edge + pixels :, :] = jnp.zeros((edge, ref.shape[1]), ref.dtype)

    def finish():
        @pl.when(me > 0)
        def _():
            up.wait_recv()
            down.wait_send()

        @pl.when(me < blocks - 1)
        def _():
            down.wait_recv()
            up.wait_send()

    return finish


def trunk_forward_kernel(
    blocks,
    parts,
    layer,
    fetch,
    jobs,
    cur_ref,
    wr_ref,
    wd_ref,
    we_ref,
    mask_ref,
    gains_ref,
    biases_ref,
    wide_gains_ref,
    wide_biases_ref,
    *refs,
):
    if fetch:
        raw_r, raw_e, *refs = refs
    out_ref, ext_out_ref, full_ref, normed1_ref, inverse1_ref, normed2_ref, inverse2_ref = refs[:7]
    normed3_ref, inverse3_ref = refs[7:9]
    refs = refs[9:]
    if fetch:
        full_r, full_e, *refs = refs
    pre1_ref, pre3_ref, ext_ref, z_ref, gath_ref, stat1_ref, stat2_ref, stat3_ref = refs[:8]
    term1_ref, term3_ref, stat_send, stat_recv, halo_send, halo_recv, part_send, part_recv = refs[8:16]
    pixels, feat = cur_ref.shape
    mid = normed1_ref.shape[1]
    wide = normed3_ref.shape[1]
    edge = (ext_ref.shape[0] - pixels) // 2
    ch = lax.axis_index(CH)
    pixel_count = float(pixels * blocks)
    greet(blocks, parts)

    def whole_row(row_of):
        return jnp.concatenate([row_of(part) for part in range(parts)], axis=1)

    gain1 = whole_row(lambda part: gains_ref[part, layer, 0:1])
    bias1 = whole_row(lambda part: biases_ref[part, layer, 0:1])
    gain3 = whole_row(lambda part: wide_gains_ref[part, layer : layer + 1])
    bias3 = whole_row(lambda part: wide_biases_ref[part, layer : layer + 1])
    if fetch:
        start, finish = stripe_job(
            raw_r, raw_e, fetch, (full_r, full_e), refs[16:], blocks, parts
        )

    def terms(total, square):
        mean_value = total / pixel_count
        variance = square / pixel_count - mean_value * mean_value
        return mean_value, lax.rsqrt(variance + epsilon)

    pre1_ref[...] = contract_last(cur_ref[...], wr_ref[...])
    total, square = moments(pre1_ref, 64)
    mean_value, inverse = terms(
        *block_totals(total, square, stat1_ref, stat_send.at[0], stat_recv.at[0], blocks)
    )
    term1_ref[0:1] = mean_value
    term1_ref[1:2] = inverse

    def first(part, state):
        value = gain1 * ((pre1_ref[part, :] - mean_value) * inverse) + bias1
        pre1_ref[part, :] = value * sigmoid(value)
        return state

    own_mid = pl.ds(pl.multiple_of(ch * mid, mid), mid)
    normed1_ref[...] = (pre1_ref[:, own_mid] - term1_ref[0:1, own_mid]) * term1_ref[1:2, own_mid]
    inverse1_ref[...] = term1_ref[1:2, own_mid]
    row_loop(pixels, 64, first, 0)
    ext_ref[edge : edge + pixels, :] = pre1_ref[...].astype(jnp.bfloat16)
    wait_halo = halo_copies(ext_ref, edge, pixels, halo_send, halo_recv, blocks)

    half = edge // 2
    for row_step in (1, 0, 2):
        if row_step == 0:
            wait_halo()
        top = 2 * row_step * half
        product = contract_last(
            ext_ref[top : top + pixels, :],
            wd_ref[layer, 3 * row_step : 3 * row_step + 3].reshape(3 * mid, parts * mid),
        )
        for col_step in range(3):
            part = masked(
                product[:, col_step * mid : (col_step + 1) * mid],
                mask_ref[1],
                row_step * 3 + col_step,
            )
            if row_step == 1:
                z_ref[col_step] = part
            else:
                z_ref[col_step] += part
    second_pre = (
        z_ref[1] + pltpu.roll(z_ref[0], 2, 0) + pltpu.roll(z_ref[2], pixels - 2, 0)
    )
    mean_value, inverse = terms(
        *block_totals(
            jnp.sum(second_pre, axis=0, keepdims=True),
            jnp.sum(second_pre * second_pre, axis=0, keepdims=True),
            stat2_ref,
            stat_send.at[1],
            stat_recv.at[1],
            blocks,
        )
    )
    normed = (second_pre - mean_value) * inverse
    normed2_ref[...] = normed
    inverse2_ref[...] = inverse
    value = gains_ref[ch, layer, 1:2] * normed + biases_ref[ch, layer, 1:2]
    gath_ref[ch] = (value * sigmoid(value)).astype(jnp.bfloat16)
    wait_parts = send_slots(
        lambda _: gath_ref.at[ch], gath_ref, part_send, part_recv, CH, parts
    )
    for job in jobs:
        job[0]()
    ext_out_ref[...] = ext_ref[...]
    wait_parts()
    if fetch:
        start()
    for part in range(parts):
        full_ref[:, part * mid : (part + 1) * mid] = gath_ref[part]
    for part in range(parts):
        lane = slice(part * wide, (part + 1) * wide)
        pre3_ref[:, lane] = jnp.dot(
            full_ref[...], we_ref[:, lane], preferred_element_type=jnp.float32
        )
    for job in jobs:
        job[1]()
    total, square = moments(pre3_ref, 16)
    mean_value, inverse = terms(
        *block_totals(total, square, stat3_ref, stat_send.at[2], stat_recv.at[2], blocks)
    )
    term3_ref[0:1] = mean_value
    term3_ref[1:2] = inverse

    def last(part, state):
        value = (
            gain3 * ((pre3_ref[part, :] - mean_value) * inverse)
            + bias3
            + cur_ref[part, :].astype(jnp.float32)
        )
        out_ref[part, :] = (value * sigmoid(value)).astype(jnp.bfloat16)
        return state

    row_loop(pixels, 16, last, 0)
    own_wide = pl.ds(pl.multiple_of(ch * wide, wide), wide)
    for job in jobs:
        job[2]()
    normed3_ref[...] = (pre3_ref[:, own_wide] - term3_ref[0:1, own_wide]) * term3_ref[1:2, own_wide]
    inverse3_ref[...] = term3_ref[1:2, own_wide]
    if fetch:
        finish()
    for job in jobs:
        job[3]()


def trunk_forward(
    blocks, parts, cols, layer, jobs, current, reduce_w, dilated_w, expand_w, mask, norms, raw
):
    pixels, feat = current.shape
    narrow = reduce_w.shape[0]
    mid, wide = narrow // parts, feat // parts
    edge = 2 * cols
    f32, low = jnp.float32, jnp.bfloat16
    shape = jax.ShapeDtypeStruct
    rows = edge * 2 + pixels
    inside = pl.BlockSpec(memory_space=pltpu.VMEM)
    anywhere = pl.BlockSpec(memory_space=pl.ANY)
    fetch = layer + 1 if raw else 0
    return job_call(
        functools.partial(trunk_forward_kernel, blocks, parts, layer, fetch),
        jobs,
        blocks,
        in_specs=[inside] * 9 + [anywhere] * len(raw),
        out_specs=[inside] * 9 + [anywhere] * len(raw),
        out_shape=[
            shape((pixels, feat), low),
            shape((rows, narrow), low),
            shape((pixels, narrow), low),
            shape((pixels, mid), f32),
            shape((1, mid), f32),
            shape((pixels, mid), f32),
            shape((1, mid), f32),
            shape((pixels, wide), f32),
            shape((1, wide), f32),
        ]
        + (stripe_shapes(parts, blocks, *raw) if raw else []),
        scratch_shapes=[
            pltpu.VMEM((pixels, narrow), f32),
            pltpu.VMEM((pixels, feat), f32),
            pltpu.VMEM((rows, narrow), low),
            pltpu.VMEM((3, pixels, mid), f32),
            pltpu.VMEM((parts, pixels, mid), low),
            pltpu.VMEM((blocks, 2, narrow), f32),
            pltpu.VMEM((blocks, 2, mid), f32),
            pltpu.VMEM((blocks, 2, feat), f32),
            pltpu.VMEM((2, narrow), f32),
            pltpu.VMEM((2, feat), f32),
            pltpu.SemaphoreType.DMA((3, blocks)),
            pltpu.SemaphoreType.DMA((3, blocks)),
            pltpu.SemaphoreType.DMA((2,)),
            pltpu.SemaphoreType.DMA((2,)),
            pltpu.SemaphoreType.DMA((parts,)),
            pltpu.SemaphoreType.DMA((parts,)),
        ]
        + (stripe_sems(parts) if raw else []),
        compiler_params=comm_params(50 + layer),
        cost_estimate=pl.CostEstimate(
            flops=2 * pixels * (2 * narrow * feat + 9 * mid * narrow),
            bytes_accessed=150 * 2**20,
            transcendentals=0,
        ),
    )(current, reduce_w, dilated_w, expand_w, mask, *norms, *raw)


def slope_of(values):
    gate = sigmoid(values)
    return gate * (1.0 + values * (1.0 - gate))


def sum_slots(ref, count):
    total = ref[0].astype(jnp.float32)
    for slot in range(1, count):
        total = total + ref[slot].astype(jnp.float32)
    return total


plan = (2, 4, 2, 4, 1, 3)


def trunk_backward_kernel(
    blocks,
    parts,
    layer,
    jobs,
    *refs,
):
    up_ref, heads_ref, cur_ref, normed3_ref, inverse3_ref = refs[:5]
    refs = refs[5:]
    we_ref, full_ref, normed2_ref, inverse2_ref, wd_ref = refs[:5]
    refs = refs[5:]
    mask_ref, ext_ref, normed1_ref, inverse1_ref, wr_ref = refs[:5]
    refs = refs[5:]
    gate_ref, gains_ref, biases_ref, wide_gains_ref, wide_biases_ref = refs[:5]
    refs = refs[5:]
    sources, gates, refs = refs[:7], refs[7:9], refs[9:]
    out_ref, expand_ref, dilated_ref, reduce_ref, wide_ref = refs[:5]
    refs = refs[5:]
    second_ref, first_ref, gate_out = refs[:3]
    refs = refs[3:]
    messages_out, heads_out, *refs = refs
    third_ref, grad_ref, im_ref, send2_ref, recv2_ref = refs[:5]
    refs = refs[5:]
    send1_ref, recv1_ref, gath_ref, low_ref, ex_send_ref = refs[:5]
    refs = refs[5:]
    ex_recv_ref, di_send_ref, di_recv_ref, re_send_ref, re_recv_ref = refs[:5]
    refs = refs[5:]
    stat3_ref, stat2_ref, stat1_ref, gates_ref, stat_send = refs[:5]
    refs = refs[5:]
    stat_recv, halo_send, halo_recv, part_send, part_recv = refs[:5]
    refs = refs[5:]
    sum_send, sum_recv = refs[:2]
    refs = refs[2:]
    buffers, accs, (lhs_ref, chunk_sem) = refs[:6], refs[6:9], refs[9:]
    chunks = WeightChunks(blocks, layer, sources, gates, buffers, accs, lhs_ref, chunk_sem)
    pixels, wide = up_ref.shape
    mid = normed1_ref.shape[1]
    narrow = mid * parts
    feat = cur_ref.shape[1]
    edge = (grad_ref.shape[0] - pixels) // 2
    half = edge // 2
    blk = lax.axis_index(BLK)
    ch = lax.axis_index(CH)
    pixel_count = float(pixels * blocks)
    low = jnp.bfloat16
    gain3 = wide_gains_ref[layer : layer + 1]
    bias3 = wide_biases_ref[layer : layer + 1]
    greet(blocks, parts)
    chunks.begin()
    own_wide = pl.ds(pl.multiple_of(ch * wide, wide), wide)
    gates_ref[blk] = gate_ref[...]
    wait_gates = send_slots(
        lambda _: gates_ref.at[blk], gates_ref, stat_send.at[3], stat_recv.at[3], BLK, blocks
    )

    def start(part, state):
        normed = normed3_ref[part, :]
        summed = (
            gain3 * normed + bias3 + cur_ref[part, own_wide].astype(jnp.float32)
        )
        value = (up_ref[part, :] + heads_ref[part, :].astype(jnp.float32)) * slope_of(summed)
        out_ref[part, :] = value
        return state[0] + fold(value), state[1] + fold(value * normed)

    zero = jnp.zeros((8, wide), jnp.float32)
    bias_sum, gain_sum = row_loop(pixels, 32, start, (zero, zero))
    bias_grad, gain_grad = block_totals(
        bias_sum.sum(axis=0, keepdims=True),
        gain_sum.sum(axis=0, keepdims=True),
        stat3_ref,
        stat_send.at[0],
        stat_recv.at[0],
        blocks,
        lambda: chunks.run(plan[0]),
    )
    wide_ref[0:1] = gain_grad
    wide_ref[1:2] = bias_grad
    scale = gain3 * inverse3_ref[...]
    bias_part = bias_grad / pixel_count
    gain_part = gain_grad / pixel_count

    def third(part, state):
        third_ref[part, :] = (
            scale * (out_ref[part, :] - bias_part - normed3_ref[part, :] * gain_part)
        ).astype(low)
        return state

    row_loop(pixels, 32, third, 0)
    product = contract_last(third_ref[...], we_ref[layer])
    for part in range(parts):
        send2_ref[part] = product[:, part * mid : (part + 1) * mid].astype(low)
    recv2_ref[ch] = send2_ref[ch]
    wait_parts = send_slots(
        lambda peer: send2_ref.at[peer], recv2_ref, part_send.at[0], part_recv.at[0], CH, parts
    )
    size = narrow // blocks
    product = lax.dot_general(
        full_ref[...], third_ref[...], (((0,), (0,)), ((), ())), preferred_element_type=jnp.float32
    )
    for block in range(blocks):
        ex_send_ref[block] = product[block * size : (block + 1) * size].astype(low)
    ex_recv_ref[blk] = ex_send_ref[blk]
    wait_expand = send_slots(
        lambda peer: ex_send_ref.at[peer], ex_recv_ref, sum_send.at[0], sum_recv.at[0], BLK, blocks
    )
    chunks.run(plan[1])
    wait_parts()

    def narrow_norm(recv_ref, normed_ref, inverse_ref, norm, stat_ref, phase, sums_ref):
        gain = gains_ref[layer, norm : norm + 1]
        bias = biases_ref[layer, norm : norm + 1]
        normed = normed_ref[...]
        value = sum_slots(recv_ref, parts) * slope_of(gain * normed + bias)
        bias_grad, gain_grad = block_totals(
            jnp.sum(value, axis=0, keepdims=True),
            jnp.sum(value * normed, axis=0, keepdims=True),
            stat_ref,
            stat_send.at[phase],
            stat_recv.at[phase],
            blocks,
            lambda: chunks.run(plan[2 * phase]),
        )
        sums_ref[0:1] = gain_grad
        sums_ref[1:2] = bias_grad
        return (
            gain
            * inverse_ref[...]
            * (value - bias_grad / pixel_count - normed * (gain_grad / pixel_count))
        )

    grad = narrow_norm(
        recv2_ref, normed2_ref, inverse2_ref, 1, stat2_ref, 1, second_ref
    )
    grad_ref[edge : edge + pixels, :] = grad.astype(low)
    wait_halo = halo_copies(grad_ref, edge, pixels, halo_send, halo_recv, blocks)
    own = grad_ref[edge : edge + pixels, :].astype(jnp.float32)
    turned = (pltpu.roll(own, pixels - 2, 0), own, pltpu.roll(own, 2, 0))
    for row_step in range(3):
        side = jnp.concatenate(
            [
                masked(turned[col_step], mask_ref[1], row_step * 3 + col_step).astype(low)
                for col_step in range(3)
            ],
            axis=1,
        )
        top = 2 * row_step * half
        product = lax.dot_general(
            ext_ref[top : top + pixels, :],
            side,
            (((0,), (0,)), ((), ())),
            preferred_element_type=jnp.float32,
        )
        for block in range(blocks):
            for col_step in range(3):
                di_send_ref[block, row_step * 3 + col_step] = product[
                    block * size : (block + 1) * size, col_step * mid : (col_step + 1) * mid
                ].astype(low)
    di_recv_ref[blk] = di_send_ref[blk]
    wait_halo()
    fill_taps(im_ref, 0, grad_ref[...], mask_ref[1], pixels, half, 2)
    product = jnp.dot(
        im_ref[0], wd_ref[layer].reshape(9 * mid, narrow), preferred_element_type=jnp.float32
    )
    for part in range(parts):
        send1_ref[part] = product[:, part * mid : (part + 1) * mid].astype(low)
    recv1_ref[ch] = send1_ref[ch]
    wait_parts = send_slots(
        lambda peer: send1_ref.at[peer], recv1_ref, part_send.at[1], part_recv.at[1], CH, parts
    )
    wait_dilated = send_slots(
        lambda peer: di_send_ref.at[peer], di_recv_ref, sum_send.at[1], sum_recv.at[1], BLK, blocks
    )
    for job in jobs:
        job[0]()
    chunks.run(plan[3])
    wait_parts()
    grad = narrow_norm(
        recv1_ref, normed1_ref, inverse1_ref, 0, stat1_ref, 2, first_ref
    )
    gath_ref[ch] = grad.astype(low)
    wait_parts = send_slots(
        lambda _: gath_ref.at[ch], gath_ref, part_send.at[2], part_recv.at[2], CH, parts
    )
    product = lax.dot_general(
        cur_ref[...], gath_ref[ch], (((0,), (0,)), ((), ())), preferred_element_type=jnp.float32
    )
    size = feat // blocks
    for block in range(blocks):
        re_send_ref[block] = product[block * size : (block + 1) * size].astype(low)
    re_recv_ref[blk] = re_send_ref[blk]
    wait_reduce = send_slots(
        lambda peer: re_send_ref.at[peer], re_recv_ref, sum_send.at[2], sum_recv.at[2], BLK, blocks
    )
    chunks.run(plan[5])
    wait_parts()
    for part in range(parts):
        low_ref[:, part * mid : (part + 1) * mid] = gath_ref[part]
    out_ref[...] += jnp.dot(low_ref[...], wr_ref[:, own_wide], preferred_element_type=jnp.float32)
    chunks.run(2 * blocks - chunks.done)
    messages_store(messages_out, accs[:2])
    heads_store(heads_out, accs[2])
    for part in (1, 2, 3):
        for job in jobs:
            job[part]()
    wait_gates()
    gate_out[...] = sum_slots(gates_ref, blocks)
    wait_expand()
    expand_ref[...] = sum_slots(ex_recv_ref, blocks)
    wait_dilated()
    dilated_ref[...] = sum_slots(di_recv_ref, blocks)
    wait_reduce()
    reduce_ref[...] = sum_slots(re_recv_ref, blocks)


def trunk_backward(blocks, parts, layer, jobs, operands, norms, sources, gates):
    pixels, wide = operands[0].shape
    feat = wide * parts
    mid = operands[7].shape[1]
    narrow = mid * parts
    rows = operands[11].shape[0]
    f32, low = jnp.float32, jnp.bfloat16
    shape = jax.ShapeDtypeStruct
    small, large = narrow // blocks, feat // blocks
    inside = pl.BlockSpec(memory_space=pltpu.VMEM)
    anywhere = pl.BlockSpec(memory_space=pl.ANY)
    rows_two = pixels + 2 * lanes
    return job_call(
        functools.partial(trunk_backward_kernel, blocks, parts, layer),
        jobs,
        blocks,
        in_specs=[inside] * (len(operands) + len(norms)) + [anywhere] * len(sources) + [inside] * len(gates),
        out_specs=[inside] * 10,
        out_shape=[
            shape((pixels, wide), f32),
            shape((small, wide), f32),
            shape((9, small, mid), f32),
            shape((large, mid), f32),
            shape((2, wide), f32),
            shape((2, mid), f32),
            shape((2, mid), f32),
            shape(operands[-1].shape, f32),
            shape((6, 9, small, mid), f32),
            shape((4, 9, large, mid), f32),
        ],
        scratch_shapes=[
            pltpu.VMEM((pixels, wide), low),
            pltpu.VMEM((rows, mid), low),
            pltpu.VMEM((1, pixels, 9 * mid), low),
            pltpu.VMEM((parts, pixels, mid), low),
            pltpu.VMEM((parts, pixels, mid), low),
            pltpu.VMEM((parts, pixels, mid), low),
            pltpu.VMEM((parts, pixels, mid), low),
            pltpu.VMEM((parts, pixels, mid), low),
            pltpu.VMEM((pixels, narrow), low),
            pltpu.VMEM((blocks, small, wide), low),
            pltpu.VMEM((blocks, small, wide), low),
            pltpu.VMEM((blocks, 9, small, mid), low),
            pltpu.VMEM((blocks, 9, small, mid), low),
            pltpu.VMEM((blocks, large, mid), low),
            pltpu.VMEM((blocks, large, mid), low),
            pltpu.VMEM((blocks, 2, wide), f32),
            pltpu.VMEM((blocks, 2, mid), f32),
            pltpu.VMEM((blocks, 2, mid), f32),
            pltpu.VMEM((blocks,) + operands[-1].shape, f32),
            pltpu.SemaphoreType.DMA((4, blocks)),
            pltpu.SemaphoreType.DMA((4, blocks)),
            pltpu.SemaphoreType.DMA((2,)),
            pltpu.SemaphoreType.DMA((2,)),
            pltpu.SemaphoreType.DMA((3, parts)),
            pltpu.SemaphoreType.DMA((3, parts)),
            pltpu.SemaphoreType.DMA((3, blocks)),
            pltpu.SemaphoreType.DMA((3, blocks)),
            pltpu.VMEM((2, 2, rows_two, 2 * small), low),
            pltpu.VMEM((2, 2, pixels, mid), low),
            pltpu.VMEM((2, 2, pixels, mid), low),
            pltpu.VMEM((2, rows_two, large), low),
            pltpu.VMEM((2, 4, pixels, mid), low),
            pltpu.VMEM((2, pixels, lanes), jnp.int32),
            pltpu.VMEM((18 * small, len(group_pairs[0]) * mid), f32),
            pltpu.VMEM((18 * small, len(group_pairs[1]) * mid), f32),
            pltpu.VMEM((9 * large, 4 * mid), f32),
            pltpu.VMEM((pixels, 9 * max(large, 2 * small)), low),
            pltpu.SemaphoreType.DMA((2, 6)),
        ],
        compiler_params=comm_params(60 + layer),
        cost_estimate=pl.CostEstimate(
            flops=4 * pixels * (2 * narrow * wide + 9 * mid * narrow) + 2 * 10**10,
            bytes_accessed=200 * 2**20,
            transcendentals=0,
        ),
    )(*operands, *norms, *sources, *gates)


def gather_parts(values):
    return lax.all_gather(values, CH, axis=0, tiled=False)


def reduce_parts(values):
    return lax.psum_scatter(values, CH, scatter_dimension=0, tiled=False)


def own_slice(values, size, axis):
    return lax.dynamic_slice_in_dim(values, lax.axis_index(CH) * size, size, axis)


def shards(
    features_in,
    w_reduce,
    w_dilated,
    w_expand,
    w_heads,
    w_messages,
    norm_gain,
    norm_bias,
    wide_gain,
    wide_bias,
    gate_gain,
    gate_bias,
    canvas_ids,
    output_cotangent,
    task_cotangents,
):
    rows, cols, wide = features_in.shape
    pixels = rows * cols
    blocks = lax.axis_size(BLK)
    parts = lax.axis_size(CH)
    layers = w_reduce.shape[0]
    mid = w_reduce.shape[1]
    feat = wide * parts
    narrow = mid * parts
    low = jnp.bfloat16
    dilated_t = w_dilated.transpose(0, 2, 1, 3)
    heads_t = w_heads.transpose(0, 1, 3, 2, 4)
    messages_t = w_messages.transpose(0, 1, 3, 2, 4)
    current, *rest = prologue(
        blocks,
        parts,
        features_in.reshape(pixels, wide),
        w_reduce,
        w_expand,
        (norm_gain, norm_bias, wide_gain, wide_bias),
        canvas_ids,
    )
    reduce_full, expand_full = [rest[2]], [rest[3]]
    norms_all, bits, all_bits = rest[4:8], rest[8], rest[9]
    cotangents = task_cotangents.reshape(layers, 2, pixels, mid)
    kept = []
    for layer in range(layers):
        keep = types.SimpleNamespace(input=current)
        results, (keep.cotangents,) = trunk_forward(
            blocks,
            parts,
            cols,
            layer,
            [(gather_kind, cotangents, layer)],
            current,
            reduce_full[layer],
            dilated_t,
            expand_full[layer],
            bits,
            norms_all,
            (w_reduce, w_expand) if layer + 1 < layers else (),
        )
        (
            current,
            keep.first_ext,
            keep.second_full,
            keep.normed1,
            keep.inverse1,
            keep.normed2,
            keep.inverse2,
            keep.normed3,
            keep.inverse3,
            *mine,
        ) = results
        if layer:
            current, kept[-1].features = lax.optimization_barrier((current, kept[-1].features))
        keep.output = current
        (keep.heads_pre, features, keep.ends, *fetched), _ = heads_forward(
            blocks,
            layer,
            [],
            cols,
            current,
            heads_t,
            bits,
            mine,
        )
        if fetched:
            reduce_full.append(fetched[0])
            expand_full.append(fetched[1])
        current, features = lax.optimization_barrier((current, features))
        keep.features = gather_parts(features)
        kept.append(keep)
    output = own_slice(current, wide, 1).reshape(rows, cols, wide)

    for layer in range(layers):
        keep = kept[layer]
        (keep.maps, keep.local, keep.gate_sums, partial, keep.message_values), moved = messages_both(
            blocks,
            layer,
            [(gather_kind, keep.ends)] + ([] if layer else [(upper_kind, keep.output)]),
            0,
            bool(layer),
            cols,
            keep.features,
            messages_t,
            cotangents,
            gate_gain,
            gate_bias,
            bits,
        )
        keep.ends_all = moved[0]
        if layer == 0:
            keep.upper = moved[1]
        keep.source_sums = reduce_parts(partial)

    def heads_low_of(keep):
        sums = keep.source_sums.astype(jnp.float32)
        total = jnp.stack([sums[0] + keep.local[0], sums[1], sums[2], sums[3] + keep.local[1]])
        return (total * silu_slope(keep.heads_pre)).astype(low)

    for layer in range(layers):
        keep = kept[layer]
        keep.heads_low = heads_low_of(keep)
        (partial,), moved = heads_backward(
            blocks,
            layer,
            [(upper_kind, keep.output), (lower_kind, keep.output)]
            if layer
            else [(slot_kind, keep.message_values), (lower_kind, keep.output)],
            cols,
            keep.heads_low,
            heads_t,
            bits,
            parts,
        )
        if layer == 0:
            keep.message_values, keep.lower = moved
        else:
            keep.upper, keep.lower = moved
        keep.heads_partial = reduce_parts(partial)
        if layer + 1 < layers:
            kept[layer + 1].source_sums, partial = lax.optimization_barrier(
                (kept[layer + 1].source_sums, partial)
            )
    kept[0].heads_low, partial = lax.optimization_barrier((kept[0].heads_low, partial))
    kept[0].heads_all, kept[1].heads_all = exchange(
        blocks, [(gather_kind, keep.heads_low) for keep in kept]
    )
    kept[1].heads_all, kept[0].heads_partial = lax.optimization_barrier(
        (kept[1].heads_all, kept[0].heads_partial)
    )

    upstream = output_cotangent.reshape(pixels, wide).astype(jnp.float32)
    for layer in reversed(range(layers)):
        keep = kept[layer]
        (
            upstream,
            keep.expand_grad,
            keep.dilated_grad,
            keep.reduce_grad,
            keep.wide_sums,
            keep.second_sums,
            keep.first_sums,
            keep.gates,
            keep.messages_grad,
            keep.heads_grad,
        ), _ = trunk_backward(
            blocks,
            parts,
            layer,
            [],
            (
                upstream,
                keep.heads_partial,
                keep.input,
                keep.normed3,
                keep.inverse3,
                w_expand,
                keep.second_full,
                keep.normed2,
                keep.inverse2,
                dilated_t,
                bits,
                keep.first_ext,
                keep.normed1,
                keep.inverse1,
                reduce_full[layer],
                keep.gate_sums,
            ),
            (norm_gain, norm_bias, wide_gain, wide_bias),
            (
                keep.message_values,
                keep.cotangents,
                keep.ends_all,
                keep.upper,
                keep.lower,
                keep.heads_all,
                all_bits,
            ),
            (gate_gain, gate_bias),
        )
    def stacked(of):
        return jnp.stack([of(keep) for keep in kept])

    narrow_sums = stacked(lambda keep: jnp.stack([keep.first_sums, keep.second_sums]))
    wide_sums = stacked(lambda keep: keep.wide_sums)
    gate_sums = stacked(lambda keep: keep.gates.reshape(2, 6, mid))
    return (
        output,
        stacked(lambda keep: keep.maps.reshape(2, rows, cols, mid)),
        upstream.reshape(rows, cols, wide),
        stacked(lambda keep: keep.reduce_grad),
        stacked(lambda keep: keep.dilated_grad),
        stacked(lambda keep: keep.expand_grad),
        stacked(lambda keep: keep.heads_grad),
        stacked(lambda keep: keep.messages_grad),
        narrow_sums[:, :, 0],
        narrow_sums[:, :, 1],
        wide_sums[:, 0],
        wide_sums[:, 1],
        gate_sums[:, 0],
        gate_sums[:, 1],
    )


def route(*args):
    mid = args[1].shape[1]
    blocks, parts = lax.axis_size(BLK), lax.axis_size(CH)
    whole_tiles = args[1].shape[0] == 2 and mid % lanes == 0 and args[0].shape[1] == lanes and parts >= 2
    if whole_tiles and blocks == 8 and 2 * mid * parts == lanes * blocks:
        return shards(*args)
    return plain_shards(*args)


def solution(mesh):
    placed = (
        P(BLK, None, CH),
        P(None, CH, None),
        P(None, CH, None, None),
        P(None, None, CH),
        P(None, None, CH, None, None),
        P(None, None, CH, None, None),
        P(None, None, CH),
        P(None, None, CH),
        P(None, CH),
        P(None, CH),
        P(None, None, CH),
        P(None, None, CH),
        P(),
        P(BLK, None, CH),
        P(None, None, BLK, None, CH),
    )
    return jax.shard_map(
        route,
        mesh=mesh,
        in_specs=placed,
        out_specs=(
            P(BLK, None, CH),
            P(None, None, BLK, None, CH),
            P(BLK, None, CH),
            P(None, BLK, CH),
            P(None, None, BLK, CH),
            P(None, BLK, CH),
            P(None, None, None, BLK, CH),
            P(None, None, None, BLK, CH),
            P(None, None, CH),
            P(None, None, CH),
            P(None, CH),
            P(None, CH),
            P(None, None, CH),
            P(None, None, CH),
        ),
        check_vma=False,
    )
```

```python
import functools
import types

import jax
import jax.numpy as jnp
from jax import lax
from jax.experimental import pallas as pl
from jax.experimental.pallas import tpu as pltpu
from jax.sharding import PartitionSpec as P

epsilon = 1e-05
BLK = "blk"
CH = "ch"
tap_offsets = tuple(((row_step, col_step) for row_step in (-1, 0, 1) for col_step in (-1, 0, 1)))
message_pairs = ((1, 0), (2, 0), (3, 0), (0, 3), (1, 3), (2, 3))


def extended_2(block, sides, width):
    for axis, dim in sides:
        count = lax.axis_size(axis)
        forward = [(i, i + 1) for i in range(count - 1)]
        backward = [(target, source) for source, target in forward]
        low = lax.ppermute(
            lax.slice_in_dim(block, block.shape[dim] - width, None, axis=dim), axis, forward
        )
        high = lax.ppermute(lax.slice_in_dim(block, 0, width, axis=dim), axis, backward)
        block = jnp.concatenate([low, block, high], axis=dim)
    return block


def silu_slope(values):
    sigmoid_value = jax.nn.sigmoid(values)
    return sigmoid_value * (1.0 + values * (1.0 - sigmoid_value))


def gather_channels(values):
    return lax.all_gather(values, CH, axis=3, tiled=True)


def reduce_channels(values):
    return lax.psum_scatter(
        values.astype(jnp.bfloat16), CH, scatter_dimension=3, tiled=True
    ).astype(jnp.float32)


def extend_rows(values, halo_width):
    return extended_2(values, ((BLK, 0),), halo_width)


def pixel_totals(first_sum, second_sum):
    return lax.psum((first_sum, second_sum), BLK)


def weight_totals(reduce_grad, dilated_grad, expand_grad, heads_grad, messages_grad):
    return (
        lax.psum_scatter(
            reduce_grad.astype(jnp.bfloat16), BLK, scatter_dimension=1, tiled=True
        ).astype(jnp.float32),
        lax.psum_scatter(
            dilated_grad.astype(jnp.bfloat16), BLK, scatter_dimension=2, tiled=True
        ).astype(jnp.float32),
        lax.psum_scatter(
            expand_grad.astype(jnp.bfloat16), BLK, scatter_dimension=1, tiled=True
        ).astype(jnp.float32),
        lax.psum_scatter(
            heads_grad.astype(jnp.bfloat16), BLK, scatter_dimension=3, tiled=True
        ).astype(jnp.float32),
        lax.psum_scatter(
            messages_grad.astype(jnp.bfloat16), BLK, scatter_dimension=3, tiled=True
        ).astype(jnp.float32),
    )


def widen(values, halo_width):
    return extend_rows(gather_channels(values), halo_width)


def local_masks(canvas_ids, row_count, dilation):
    col_count = canvas_ids.shape[1]
    padded = jnp.pad(canvas_ids, 2, constant_values=-1)
    start = lax.axis_index(BLK) * row_count
    window = lax.dynamic_slice(padded, (start, jnp.int32(0)), (row_count + 4, col_count + 4))
    centre = window[2 : 2 + row_count, 2 : 2 + col_count]
    result = []
    for row_step, col_step in tap_offsets:
        top = 2 + row_step * dilation
        left = 2 + col_step * dilation
        result.append(window[top : top + row_count, left : left + col_count] == centre)
    return jnp.stack(result)


def shifted(padded, halo_width, dilation, row_step, col_step, row_count, col_count):
    top = halo_width + row_step * dilation
    left = dilation + col_step * dilation
    return padded[top : top + row_count, left : left + col_count]


def conv_forward(extended, halo_width, dilation, weights, tap_masks):
    row_count = extended.shape[0] - 2 * halo_width
    col_count = extended.shape[1]
    padded = jnp.pad(extended, ((0, 0), (dilation, dilation), (0, 0)))
    running = jnp.zeros((row_count, col_count, weights.shape[0], weights.shape[1]), jnp.float32)
    for tap_index, (row_step, col_step) in enumerate(tap_offsets):
        window = shifted(padded, halo_width, dilation, row_step, col_step, row_count, col_count)
        product = jnp.einsum(
            "rwc,koc->rwko", window, weights[:, :, tap_index], preferred_element_type=jnp.float32
        )
        running = running + jnp.where(tap_masks[tap_index][:, :, None, None], product, 0.0)
    return running


def conv_weight_grad(extended, halo_width, dilation, gradient, tap_masks):
    row_count = extended.shape[0] - 2 * halo_width
    col_count = extended.shape[1]
    padded = jnp.pad(extended, ((0, 0), (dilation, dilation), (0, 0)))
    result = []
    for tap_index, (row_step, col_step) in enumerate(tap_offsets):
        window = shifted(padded, halo_width, dilation, row_step, col_step, row_count, col_count)
        masked = jnp.where(
            tap_masks[tap_index][:, :, None, None], gradient, jnp.zeros((), gradient.dtype)
        )
        result.append(
            jnp.einsum("rwc,rwko->kco", window, masked, preferred_element_type=jnp.float32)
        )
    return jnp.stack(result, axis=1)


def conv_input_grad(grad_extended, halo_width, dilation, weights, tap_masks):
    row_count = grad_extended.shape[0] - 2 * halo_width
    col_count = grad_extended.shape[1]
    padded = jnp.pad(grad_extended, ((0, 0), (dilation, dilation), (0, 0), (0, 0)))
    running = jnp.zeros((row_count, col_count, weights.shape[3]), jnp.float32)
    for tap_index, (row_step, col_step) in enumerate(tap_offsets):
        window = shifted(padded, halo_width, dilation, -row_step, -col_step, row_count, col_count)
        product = jnp.einsum(
            "rwko,koc->rwc", window, weights[:, :, tap_index], preferred_element_type=jnp.float32
        )
        running = running + jnp.where(tap_masks[8 - tap_index][:, :, None], product, 0.0)
    return running


def norm_forward(hidden, gain, bias, pixel_count):
    total_sum, square_sum = pixel_totals(
        jnp.sum(hidden, axis=(0, 1)), jnp.sum(hidden * hidden, axis=(0, 1))
    )
    mean_value = total_sum / pixel_count
    variance = square_sum / pixel_count - mean_value * mean_value
    inverse = lax.rsqrt(variance + epsilon)
    normed = (hidden - mean_value) * inverse
    return (gain * normed + bias, normed, inverse)


def norm_backward(upstream, normed, inverse, gain, pixel_count):
    bias_grad, gain_grad = pixel_totals(
        jnp.sum(upstream, axis=(0, 1)), jnp.sum(upstream * normed, axis=(0, 1))
    )
    hidden_grad = (
        gain * inverse * (upstream - bias_grad / pixel_count - normed * gain_grad / pixel_count)
    )
    return (hidden_grad, gain_grad, bias_grad)


def layer_forward(inputs, params, masks_one, masks_two, pixel_count):
    (
        reduce_w,
        dilated_w,
        expand_w,
        heads_w,
        messages_w,
        narrow_gain,
        narrow_bias,
        wide_g,
        wide_b,
        gate_g,
        gate_b,
    ) = params
    stored = types.SimpleNamespace()
    inputs_full = gather_channels(inputs[:, :, None, :])[:, :, 0, :]
    first_pre = jnp.einsum("rwc,oc->rwo", inputs_full, reduce_w, preferred_element_type=jnp.float32)
    first_norm, first_normed, first_inverse = norm_forward(
        first_pre, narrow_gain[0], narrow_bias[0], pixel_count
    )
    first_act = jax.nn.silu(first_norm).astype(jnp.bfloat16)
    first_ext = widen(first_act[:, :, None, :], 2)[:, :, 0, :]
    second_pre = conv_forward(first_ext, 2, 2, dilated_w[None], masks_two)[:, :, 0, :]
    second_norm, second_normed, second_inverse = norm_forward(
        second_pre, narrow_gain[1], narrow_bias[1], pixel_count
    )
    second_act = jax.nn.silu(second_norm).astype(jnp.bfloat16)
    second_full = gather_channels(second_act[:, :, None, :])[:, :, 0, :]
    third_pre = jnp.einsum("rwc,co->rwo", second_full, expand_w, preferred_element_type=jnp.float32)
    third_norm, third_normed, third_inverse = norm_forward(third_pre, wide_g, wide_b, pixel_count)
    summed = third_norm + inputs.astype(jnp.float32)
    output = jax.nn.silu(summed).astype(jnp.bfloat16)
    output_ext = widen(output[:, :, None, :], 1)[:, :, 0, :]
    heads_pre = conv_forward(output_ext, 1, 1, heads_w, masks_one)
    features = jax.nn.silu(heads_pre).astype(jnp.bfloat16)
    features_ext = widen(features, 1)
    feature_values = features.astype(jnp.float32)
    depth_map = feature_values[:, :, 0]
    segment_map = feature_values[:, :, 3]
    message_list = []
    for pair_index, (source, target) in enumerate(message_pairs):
        message = conv_forward(
            features_ext[:, :, source], 1, 1, messages_w[pair_index][None], masks_one
        )[:, :, 0]
        gate_value = jax.nn.sigmoid(
            gate_g[pair_index] * feature_values[:, :, target] + gate_b[pair_index]
        )
        message_list.append(message)
        if target == 0:
            depth_map = depth_map + gate_value * message
        else:
            segment_map = segment_map + gate_value * message
    stored.inputs_full = inputs_full
    stored.first_norm = first_norm
    stored.first_normed = first_normed
    stored.first_inverse = first_inverse
    stored.first_ext = first_ext
    stored.second_norm = second_norm
    stored.second_normed = second_normed
    stored.second_inverse = second_inverse
    stored.second_full = second_full
    stored.third_normed = third_normed
    stored.third_inverse = third_inverse
    stored.summed = summed
    stored.output_ext = output_ext
    stored.heads_pre = heads_pre
    stored.features = feature_values
    stored.features_ext = features_ext
    stored.messages = message_list
    return (output, depth_map, segment_map, stored)


def layer_backward(
    stored, upstream, depth_grad, segment_grad, params, masks_one, masks_two, pixel_count
):
    (
        reduce_w,
        dilated_w,
        expand_w,
        heads_w,
        messages_w,
        narrow_gain,
        narrow_bias,
        wide_g,
        wide_b,
        gate_g,
        gate_b,
    ) = params
    feature_values = stored.features
    zero_map = jnp.zeros_like(depth_grad)
    feature_grads = [depth_grad, zero_map, zero_map, segment_grad]
    message_grads = []
    gain_terms = []
    bias_terms = []
    for pair_index, (source, target) in enumerate(message_pairs):
        target_grad = depth_grad if target == 0 else segment_grad
        gate_value = jax.nn.sigmoid(
            gate_g[pair_index] * feature_values[:, :, target] + gate_b[pair_index]
        )
        message_grads.append(target_grad * gate_value)
        slope = target_grad * stored.messages[pair_index] * gate_value * (1.0 - gate_value)
        gain_terms.append(jnp.sum(slope * feature_values[:, :, target], axis=(0, 1)))
        bias_terms.append(jnp.sum(slope, axis=(0, 1)))
        feature_grads[target] = feature_grads[target] + slope * gate_g[pair_index]
    gate_gain_grad, gate_bias_grad = pixel_totals(jnp.stack(gain_terms), jnp.stack(bias_terms))
    message_stack = jnp.stack(message_grads, axis=2).astype(jnp.bfloat16)
    message_ext = extend_rows(message_stack, 1)
    weight_parts = []
    source_partials = [None, None, None, None]
    for pair_index, (source, target) in enumerate(message_pairs):
        weight_parts.append(
            conv_weight_grad(
                stored.features_ext[:, :, source],
                1,
                1,
                message_stack[:, :, pair_index : pair_index + 1],
                masks_one,
            )
        )
        partial_grad = conv_input_grad(
            message_ext[:, :, pair_index : pair_index + 1],
            1,
            1,
            messages_w[pair_index][None],
            masks_one,
        )
        if source_partials[source] is None:
            source_partials[source] = partial_grad
        else:
            source_partials[source] = source_partials[source] + partial_grad
    messages_w_grad = jnp.concatenate(weight_parts, axis=0)
    source_sums = reduce_channels(jnp.stack(source_partials, axis=2))
    features_total = jnp.stack(feature_grads, axis=2) + source_sums
    heads_grad = (features_total * silu_slope(stored.heads_pre)).astype(jnp.bfloat16)
    heads_w_grad = conv_weight_grad(stored.output_ext, 1, 1, heads_grad, masks_one)
    heads_ext = extend_rows(heads_grad, 1)
    output_partial = conv_input_grad(heads_ext, 1, 1, heads_w, masks_one)
    output_total = upstream + reduce_channels(output_partial[:, :, None, :])[:, :, 0, :]
    summed_grad = output_total * silu_slope(stored.summed)
    third_grad, wide_gain_grad, wide_bias_grad = norm_backward(
        summed_grad, stored.third_normed, stored.third_inverse, wide_g, pixel_count
    )
    third_low = third_grad.astype(jnp.bfloat16)
    expand_w_grad = jnp.einsum(
        "rwc,rwo->co", stored.second_full, third_low, preferred_element_type=jnp.float32
    )
    second_partial = jnp.einsum(
        "rwo,co->rwc", third_low, expand_w, preferred_element_type=jnp.float32
    )
    second_act_grad = reduce_channels(second_partial[:, :, None, :])[:, :, 0, :]
    second_grad, second_gain_grad, second_bias_grad = norm_backward(
        second_act_grad * silu_slope(stored.second_norm),
        stored.second_normed,
        stored.second_inverse,
        narrow_gain[1],
        pixel_count,
    )
    second_low = second_grad.astype(jnp.bfloat16)[:, :, None, :]
    dilated_w_grad = conv_weight_grad(stored.first_ext, 2, 2, second_low, masks_two)[0]
    second_ext = extend_rows(second_low, 2)
    first_partial = conv_input_grad(second_ext, 2, 2, dilated_w[None], masks_two)
    first_act_grad = reduce_channels(first_partial[:, :, None, :])[:, :, 0, :]
    first_grad, first_gain_grad, first_bias_grad = norm_backward(
        first_act_grad * silu_slope(stored.first_norm),
        stored.first_normed,
        stored.first_inverse,
        narrow_gain[0],
        pixel_count,
    )
    first_low = first_grad.astype(jnp.bfloat16)
    reduce_w_grad = jnp.einsum(
        "rwc,rwo->co", stored.inputs_full, first_low, preferred_element_type=jnp.float32
    )
    inputs_partial = jnp.einsum(
        "rwo,oc->rwc", first_low, reduce_w, preferred_element_type=jnp.float32
    )
    inputs_grad = reduce_channels(inputs_partial[:, :, None, :])[:, :, 0, :] + summed_grad
    weight_grads = (reduce_w_grad, dilated_w_grad, expand_w_grad, heads_w_grad, messages_w_grad)
    small_grads = (
        jnp.stack([first_gain_grad, second_gain_grad]),
        jnp.stack([first_bias_grad, second_bias_grad]),
        wide_gain_grad,
        wide_bias_grad,
        gate_gain_grad,
        gate_bias_grad,
    )
    return (inputs_grad, weight_grads, small_grads)


def plain_shards(
    features_in,
    w_reduce,
    w_dilated,
    w_expand,
    w_heads,
    w_messages,
    norm_gain,
    norm_bias,
    wide_gain,
    wide_bias,
    gate_gain,
    gate_bias,
    canvas_ids,
    output_cotangent,
    task_cotangents,
):
    row_count = features_in.shape[0]
    col_count = features_in.shape[1]
    pixel_count = float(row_count * col_count * lax.axis_size(BLK))
    masks_one = local_masks(canvas_ids, row_count, 1)
    masks_two = local_masks(canvas_ids, row_count, 2)
    layer_count = w_reduce.shape[0]
    layer_params = []
    for layer_index in range(layer_count):
        layer_params.append(
            (
                w_reduce[layer_index],
                w_dilated[layer_index],
                w_expand[layer_index],
                w_heads[layer_index],
                w_messages[layer_index],
                norm_gain[layer_index],
                norm_bias[layer_index],
                wide_gain[layer_index],
                wide_bias[layer_index],
                gate_gain[layer_index],
                gate_bias[layer_index],
            )
        )
    current = features_in
    stored_list = []
    task_list = []
    for layer_index in range(layer_count):
        current, depth_map, segment_map, stored = layer_forward(
            current, layer_params[layer_index], masks_one, masks_two, pixel_count
        )
        stored_list.append(stored)
        task_list.append(jnp.stack([depth_map, segment_map]).astype(jnp.bfloat16))
    upstream = output_cotangent.astype(jnp.float32)
    weight_list = [None] * layer_count
    small_list = [None] * layer_count
    for layer_index in reversed(range(layer_count)):
        upstream, weight_grads, small_grads = layer_backward(
            stored_list[layer_index],
            upstream,
            task_cotangents[layer_index, 0].astype(jnp.float32),
            task_cotangents[layer_index, 1].astype(jnp.float32),
            layer_params[layer_index],
            masks_one,
            masks_two,
            pixel_count,
        )
        weight_list[layer_index] = weight_grads
        small_list[layer_index] = small_grads
    stacked = [
        jnp.stack([weight_list[layer_index][member] for layer_index in range(layer_count)])
        for member in range(5)
    ]
    weight_sums = weight_totals(stacked[0], stacked[1], stacked[2], stacked[3], stacked[4])
    small_sums = [
        jnp.stack([small_list[layer_index][member] for layer_index in range(layer_count)])
        for member in range(6)
    ]
    return (
        current,
        jnp.stack(task_list),
        upstream,
        weight_sums[0],
        weight_sums[1],
        weight_sums[2],
        weight_sums[3],
        weight_sums[4],
        small_sums[0],
        small_sums[1],
        small_sums[2],
        small_sums[3],
        small_sums[4],
        small_sums[5],
    )


lanes = 128
source_order = ((1, 0, 4), (2, 1, 5), (0, 3), (3, 2))


def whole(shape):
    return pl.BlockSpec(shape, lambda *_: (0,) * len(shape))


def contract_last(left, right):
    return lax.dot_general(
        left, right, (((1,), (1,)), ((), ())), preferred_element_type=jnp.float32
    )


def sigmoid(values):
    return 1.0 / (1.0 + jnp.exp(-values))


def masked(values, bits, place):
    taken = (bits & (1 << place)) != 0
    width = values.shape[1]
    parts = [
        jnp.where(taken, values[:, start : start + lanes], 0.0) for start in range(0, width, lanes)
    ]
    return parts[0] if len(parts) == 1 else jnp.concatenate(parts, axis=1)


MESH = pl.DeviceIdType.MESH
groups = ((1, 2), (0, 3))
targets = (0, 3)
group_pairs = ((0, 4, 1, 5), (3, 2))


def remote(source, target, send_sem, recv_sem, axis, peer):
    return pltpu.make_async_remote_copy(
        src_ref=source,
        dst_ref=target,
        send_sem=send_sem,
        recv_sem=recv_sem,
        device_id={axis: peer},
        device_id_type=MESH,
    )


def comm_params(key):
    return pltpu.CompilerParams(
        vmem_limit_bytes=60 * 2**20, collective_id=key, has_side_effects=True
    )


def announce(targets):
    barrier = pltpu.get_barrier_semaphore()
    for axis, peer in targets:
        pl.semaphore_signal(barrier, inc=1, device_id={axis: peer}, device_id_type=MESH)
    pl.semaphore_wait(barrier, len(targets))


def near_blocks():
    me = lax.axis_index(BLK)

    def turned(bit):
        return me + bit - 2 * bit * lax.rem(me // bit, 2)

    return turned(1), turned(2), turned(4)


def others(axis, count):
    me = lax.axis_index(axis)
    return [lax.rem(me + step, count) for step in range(1, count)]


def round_trip(own_source, target_of, half_of, sems):
    near_send, slot_recv, pass_send, local_sem = sems
    me = lax.axis_index(BLK)
    sibling, *peers = near_blocks()
    far = me + peers[0] - me + peers[1] - me
    own = pltpu.make_async_copy(own_source, target_of(me), local_sem.at[0])

    def near(step, peer):
        return remote(
            own_source, target_of(me), near_send.at[step], slot_recv.at[me], BLK, peer
        )

    def half(side, block, recv_sem, peer):
        part = half_of(block, side)
        return remote(part, part, near_send.at[3 + side], recv_sem, BLK, peer)

    def passing(step, block):
        part = target_of(block)
        return remote(part, part, pass_send.at[step], slot_recv.at[block], BLK, sibling)

    def start():
        own.start()
        for step, peer in enumerate(peers + [sibling]):
            near(step, peer).start()

    def sent_half(side):
        recv_sem = slot_recv.at[peers[0]] if side == 0 else local_sem.at[1]
        return half(side, peers[side], recv_sem, peers[1 - side])

    def middle():
        for side in range(2):
            copy = passing(side, peers[side])
            copy.wait_recv()
            sent_half(side).start()
            copy.start()

    def forward():
        half(0, far, slot_recv.at[far], sibling).wait_recv()
        half(1, far, local_sem.at[1], sibling).wait_recv()
        passing(2, far).start()

    def finish():
        for block in (sibling, sibling + peers[0] - me, sibling + peers[1] - me, sibling + far - me):
            passing(0, block).wait_recv()
        for step, peer in enumerate(peers + [sibling]):
            near(step, peer).wait_send()
        for side in range(2):
            sent_half(side).wait_send()
            passing(side, peers[side]).wait_send()
        passing(2, far).wait_send()
        own.wait()

    return start, middle, forward, finish


def gather_job(source, target, sems, blocks):
    count = source.shape[0] // 2
    return round_trip(
        source,
        lambda block: target.at[block],
        lambda block, side: target.at[block, pl.ds(side * count, count)],
        sems,
    )


def swap_job(source, target, sems, blocks):
    slot_send, slot_recv, _, local_sem = sems
    me = lax.axis_index(BLK)
    width = source.shape[1] // blocks

    def part_of(block):
        return source.at[:, pl.ds(pl.multiple_of(block * width, width), width)]

    own = pltpu.make_async_copy(part_of(me), target.at[me], local_sem.at[0])

    def copy(step, peer, slot):
        return remote(
            part_of(peer), target.at[slot], slot_send.at[step], slot_recv.at[slot], BLK, peer
        )

    def start():
        for step, peer in enumerate(others(BLK, blocks)):
            copy(step, peer, me).start()
        own.start()

    def finish():
        for step, peer in enumerate(others(BLK, blocks)):
            copy(step, peer, peer).wait_recv()
            copy(step, peer, me).wait_send()
        own.wait()

    return start, lambda: None, lambda: None, finish


def half_swap_job(half):
    def job(source, target, sems, blocks):
        count = source.shape[0] // 2
        return swap_job(source.at[pl.ds(half * count, count)], target, sems, blocks)

    return job


def slot_job(source, target, sems, blocks):
    slot_send, slot_recv, _, local_sem = sems
    me = lax.axis_index(BLK)
    own = pltpu.make_async_copy(source.at[me], target.at[me], local_sem.at[0])

    def copy(step, peer, slot):
        return remote(
            source.at[peer], target.at[slot], slot_send.at[step], slot_recv.at[slot], BLK, peer
        )

    def start():
        for step, peer in enumerate(others(BLK, blocks)):
            copy(step, peer, me).start()
        own.start()

    def finish():
        for step, peer in enumerate(others(BLK, blocks)):
            copy(step, peer, peer).wait_recv()
            copy(step, peer, me).wait_send()
        own.wait()

    return start, lambda: None, lambda: None, finish


def line_job(source, target, sems, blocks):
    line_send, line_recv, _, local_sem = sems
    parts = target.shape[0]
    ch = lax.axis_index(CH)
    right, left = lax.rem(ch + 1, parts), lax.rem(ch + parts - 1, parts)
    own = pltpu.make_async_copy(source, target.at[ch], local_sem.at[0])

    def sides(hop):
        return (
            (0, lax.rem(ch + parts - hop, parts), right, ch - hop >= 0, ch < parts - 1),
            (1, lax.rem(ch + hop, parts), left, ch + hop < parts, ch > 0),
        )

    def copy(block, side, hop, peer):
        return remote(
            source if hop == 0 else target.at[block],
            target.at[block],
            line_send.at[side * (parts - 1) + hop],
            line_recv.at[block],
            CH,
            peer,
        )

    def move(hop):
        for side, block, peer, valid, goes in sides(hop):
            if hop > 0:

                @pl.when(valid)
                def _():
                    copy(block, side, hop, peer).wait_recv()

            if hop < parts - 1:

                @pl.when(valid & goes)
                def _():
                    copy(block, side, hop, peer).start()

    def start():
        own.start()
        move(0)

    def middle():
        move(1)

    def forward():
        for hop in range(2, parts - 1):
            move(hop)

    def finish():
        if parts > 2:
            move(parts - 1)
        for hop in range(parts - 1):
            for side, block, peer, valid, goes in sides(hop):

                @pl.when(valid & goes)
                def _():
                    copy(block, side, hop, peer).wait_send()

        own.wait()

    return start, middle, forward, finish


job_kinds = (gather_job, half_swap_job(0), slot_job, line_job, half_swap_job(1))
gather_kind, upper_kind, slot_kind, line_kind, lower_kind = 0, 1, 2, 3, 4


def job_target(kind, shape, dtype, blocks):
    if kind == gather_kind:
        shape = (blocks,) + shape
    elif kind == line_kind:
        shape = (lax.axis_size(CH),) + shape
    elif kind in (upper_kind, lower_kind):
        shape = (blocks, shape[0] // 2, shape[1] // blocks)
    return jax.ShapeDtypeStruct(shape, dtype)


def job_sems(blocks):
    dma = pltpu.SemaphoreType.DMA
    return [dma((blocks,)), dma((blocks,)), dma((blocks,)), dma((2,))]


def job_call(kernel, jobs, blocks, in_specs, out_specs, out_shape, scratch_shapes, **options):
    anywhere = pl.BlockSpec(memory_space=pl.ANY)
    n_in, n_out, n_scratch = len(in_specs), len(out_specs), len(scratch_shapes)
    count = len(jobs)

    def wrapped(*refs):
        ins, refs = refs[:n_in], refs[n_in:]
        sources, refs = refs[:count], refs[count:]
        outs, refs = refs[:n_out], refs[n_out:]
        targets, refs = refs[:count], refs[count:]
        scratch, sems = refs[:n_scratch], refs[n_scratch:]
        running = [
            job_kinds[kind](
                sources[place].at[index[0]] if index else sources[place],
                targets[place],
                sems[4 * place : 4 * place + 4],
                blocks,
            )
            for place, (kind, _, *index) in enumerate(jobs)
        ]
        kernel(running, *ins, *outs, *scratch)

    def call(*operands):
        result = pl.pallas_call(
            wrapped,
            in_specs=list(in_specs) + [anywhere] * count,
            out_specs=list(out_specs) + [anywhere] * count,
            out_shape=list(out_shape) + [
                job_target(kind, source.shape[len(index) :], source.dtype, blocks)
                for kind, source, *index in jobs
            ],
            scratch_shapes=list(scratch_shapes) + job_sems(blocks) * count,
            **options,
        )(*operands, *[job[1] for job in jobs])
        return result[:n_out], result[n_out:]

    return call


def stripe_job(wr_ref, we_ref, layer, mine, sems, blocks, parts):
    part_send, part_recv, local_sem = sems
    _, mid, feat = wr_ref.shape
    _, narrow, wide = we_ref.shape
    blk, ch = lax.axis_index(BLK), lax.axis_index(CH)

    def cut(index, size):
        return pl.ds(pl.multiple_of(index * size, size), size)

    def source(array):
        if array == 0:
            return wr_ref.at[layer, :, cut(blk, feat // blocks)]
        return we_ref.at[layer, cut(blk, narrow // blocks), :]

    def share(array, part):
        if array == 0:
            return mine[0].at[cut(part, mid), :]
        return mine[1].at[:, cut(part, wide)]

    def own(array):
        return pltpu.make_async_copy(source(array), share(array, ch), local_sem.at[array])

    def copy(array, step, peer, slot):
        return remote(
            source(array),
            share(array, slot),
            part_send.at[array, step],
            part_recv.at[array, slot],
            CH,
            peer,
        )

    def start():
        for array in range(2):
            own(array).start()
            for step, peer in enumerate(others(CH, parts)):
                copy(array, step, peer, ch).start()

    def finish():
        for array in range(2):
            for step, peer in enumerate(others(CH, parts)):
                copy(array, step, peer, peer).wait_recv()
            own(array).wait()
            for step, peer in enumerate(others(CH, parts)):
                copy(array, step, peer, ch).wait_send()

    return start, finish


def stripe_sems(parts):
    dma = pltpu.SemaphoreType.DMA
    return [dma((2, parts)), dma((2, parts)), dma((2,))]


def stripe_shapes(parts, blocks, reduce_w, expand_w):
    _, mid, feat = reduce_w.shape
    narrow = mid * parts
    return [
        jax.ShapeDtypeStruct((narrow, feat // blocks), reduce_w.dtype),
        jax.ShapeDtypeStruct((narrow // blocks, feat), expand_w.dtype),
    ]


def spread_jobs(mine, fulls, sems, blocks):
    half_rows = mine[0].shape[0] // 2
    width, height = mine[0].shape[1], mine[1].shape[0]
    half_cols = mine[1].shape[1] // 2

    def cut(index, size):
        return pl.ds(pl.multiple_of(index * size, size), size)

    return [
        round_trip(
            mine[0],
            lambda block: fulls[0].at[:, cut(block, width)],
            lambda block, side: fulls[0].at[pl.ds(side * half_rows, half_rows), cut(block, width)],
            sems[:4],
        ),
        round_trip(
            mine[1],
            lambda block: fulls[1].at[cut(block, height), :],
            lambda block, side: fulls[1].at[cut(block, height), pl.ds(side * half_cols, half_cols)],
            sems[4:],
        ),
    ]


def prologue_kernel(
    blocks,
    parts,
    feat_ref,
    wr_ref,
    we_ref,
    *refs,
):
    small_refs, ids_ref, cur_ref, mine_r, mine_e = refs[:4], *refs[4:8]
    full_r, full_e, small_outs, own_ref, all_ref = *refs[8:10], refs[10:14], *refs[14:16]
    line_send, line_recv, small_send, small_recv, local_sem, *sems = refs[16:]
    pixels, wide = feat_ref.shape
    blk, ch = lax.axis_index(BLK), lax.axis_index(CH)
    smalls = tuple(zip(small_refs, small_outs))

    def lane_part(index):
        return cur_ref.at[:, pl.ds(pl.multiple_of(index * wide, wide), wide)]

    start, gathered = stripe_job(wr_ref, we_ref, 0, (mine_r, mine_e), sems[:3], blocks, parts)
    jobs = spread_jobs((mine_r, mine_e), (full_r, full_e), sems[3:], blocks)
    own = pltpu.make_async_copy(feat_ref, lane_part(ch), local_sem.at[0])
    own.start()
    announce(
        [(CH, peer) for peer in others(CH, parts)] + [(BLK, peer) for peer in near_blocks()]
    )
    start()

    right, left = lax.rem(ch + 1, parts), lax.rem(ch + parts - 1, parts)

    def sides(hop):
        return (
            (0, lax.rem(ch + parts - hop, parts), right, ch - hop >= 0, ch < parts - 1),
            (1, lax.rem(ch + hop, parts), left, ch + hop < parts, ch > 0),
        )

    def line_copy(block, side, hop, peer):
        return remote(
            feat_ref if hop == 0 else lane_part(block),
            lane_part(block),
            line_send.at[side, hop],
            line_recv.at[block],
            CH,
            peer,
        )

    def line_hop(hop):
        for side, block, peer, valid, goes in sides(hop):
            if hop > 0:

                @pl.when(valid)
                def _():
                    line_copy(block, side, hop, peer).wait_recv()

            if hop < parts - 1:

                @pl.when(valid & goes)
                def _():
                    line_copy(block, side, hop, peer).start()

    def small_copy(place, step, peer, slot):
        source, target = smalls[place]
        return remote(
            source,
            target.at[slot],
            small_send.at[place, step],
            small_recv.at[place, slot],
            CH,
            peer,
        )

    def small_own(place):
        source, target = smalls[place]
        return pltpu.make_async_copy(source, target.at[ch], local_sem.at[1 + place])

    line_hop(0)
    for place in range(4):
        small_own(place).start()
        for step, peer in enumerate(others(CH, parts)):
            small_copy(place, step, peer, ch).start()
    gathered()
    for job in jobs:
        job[0]()

    rows = own_ref.shape[1] // lanes
    lane = lax.broadcasted_iota(jnp.int32, (1, lanes), 1)

    def moved(values, step):
        turned = values if step == 0 else pltpu.roll(values, (lanes - step) % lanes, 1)
        return jnp.where((lane + step >= 0) & (lane + step < lanes), turned, -2)

    def spread(target, row, bits):
        block = jnp.broadcast_to(bits.astype(jnp.float32), (lanes, lanes)).T
        target[pl.ds(pl.multiple_of(row * lanes, lanes), lanes), :] = block.astype(jnp.int32)

    def own_row(row, state):
        place = 2 + blk * rows + row
        for word, reach in enumerate((1, 2)):
            bits = jnp.zeros((1, lanes), jnp.int32)
            for tap, (row_step, col_step) in enumerate(tap_offsets):
                a, b = row_step * reach, col_step * reach
                taken = moved(ids_ref[place], -b) == ids_ref[place + a]
                bits = bits | jnp.where(taken, 1 << tap, 0)
                taken = moved(ids_ref[place - a], -b) == ids_ref[place]
                bits = bits | jnp.where(taken, 1 << (9 + tap), 0)
            spread(own_ref.at[word], row, bits)
        return state

    lax.fori_loop(0, rows, own_row, 0)

    def any_row(row, state):
        bits = jnp.zeros((1, lanes), jnp.int32)
        for tap, (row_step, col_step) in enumerate(tap_offsets):
            taken = moved(ids_ref[2 + row + row_step], col_step) == ids_ref[2 + row]
            bits = bits | jnp.where(taken, 1 << tap, 0)
        spread(all_ref, row, bits)
        return state

    lax.fori_loop(0, ids_ref.shape[0] - 4, any_row, 0)
    for hop in range(1, parts):
        line_hop(hop)
        if hop <= 2:
            for job in jobs:
                job[hop]()
    if parts == 2:
        for job in jobs:
            job[2]()
    for job in jobs:
        job[3]()
    for hop in range(parts - 1):
        for side, block, peer, valid, goes in sides(hop):

            @pl.when(valid & goes)
            def _():
                line_copy(block, side, hop, peer).wait_send()

    for place in range(4):
        for step, peer in enumerate(others(CH, parts)):
            small_copy(place, step, peer, peer).wait_recv()
            small_copy(place, step, peer, ch).wait_send()
        small_own(place).wait()
    own.wait()


def prologue(blocks, parts, features, reduce_w, expand_w, terms, canvas_ids):
    layers, mid, feat = reduce_w.shape
    pixels, wide = features.shape
    narrow = mid * parts
    f32, low = jnp.float32, jnp.bfloat16
    shape = jax.ShapeDtypeStruct
    ids = jnp.pad(canvas_ids, ((2, 2), (0, 0)), constant_values=-1)[:, None]
    anywhere = pl.BlockSpec(memory_space=pl.ANY)
    inside = pl.BlockSpec(memory_space=pltpu.VMEM)
    dma = pltpu.SemaphoreType.DMA
    return pl.pallas_call(
        functools.partial(prologue_kernel, blocks, parts),
        in_specs=[anywhere] * 7 + [inside],
        out_specs=[anywhere] * 9 + [inside] * 2,
        out_shape=[
            shape((pixels, feat), low),
            *stripe_shapes(parts, blocks, reduce_w, expand_w),
            shape((narrow, feat), low),
            shape((narrow, feat), low),
            *[shape((parts,) + term.shape, f32) for term in terms],
            shape((2, pixels, lanes), jnp.int32),
            shape((pixels * blocks, lanes), jnp.int32),
        ],
        scratch_shapes=[
            dma((2, parts)),
            dma((parts,)),
            dma((4, parts)),
            dma((4, parts)),
            dma((5,)),
        ]
        + stripe_sems(parts)
        + job_sems(blocks) * 2,
        compiler_params=comm_params(5),
        cost_estimate=pl.CostEstimate(flops=10**6, bytes_accessed=10**8, transcendentals=0),
    )(features, reduce_w, expand_w, *terms, ids)


def greet_line(blocks):
    barrier = pltpu.get_barrier_semaphore()
    me = lax.axis_index(BLK)
    for peer in (lax.rem(me + 1, blocks), lax.rem(me + blocks - 1, blocks)):
        pl.semaphore_signal(barrier, inc=1, device_id={BLK: peer}, device_id_type=MESH)
    pl.semaphore_wait(barrier, 2)


def greet_blocks(blocks):
    announce([(BLK, peer) for peer in others(BLK, blocks)])


def edge_copies(main_ref, low_ref, high_ref, edge, send_sem, recv_sem, blocks):
    me = lax.axis_index(BLK)
    lead = (slice(None),) * (len(main_ref.shape) - 2)
    pixels = main_ref.shape[-2]
    up = remote(
        main_ref.at[lead + (pl.ds(pixels - edge, edge),)],
        low_ref,
        send_sem.at[0],
        recv_sem.at[0],
        BLK,
        lax.rem(me + 1, blocks),
    )
    down = remote(
        main_ref.at[lead + (pl.ds(0, edge),)],
        high_ref,
        send_sem.at[1],
        recv_sem.at[1],
        BLK,
        lax.rem(me + blocks - 1, blocks),
    )

    def start():
        @pl.when(me < blocks - 1)
        def _():
            up.start()

        @pl.when(me > 0)
        def _():
            down.start()

    def finish(zero=True):
        @pl.when(me > 0)
        def _():
            up.wait_recv()
            down.wait_send()

        @pl.when(me < blocks - 1)
        def _():
            down.wait_recv()
            up.wait_send()

        if zero:

            @pl.when(me == 0)
            def _():
                low_ref[...] = jnp.zeros(low_ref.shape, low_ref.dtype)

            @pl.when(me == blocks - 1)
            def _():
                high_ref[...] = jnp.zeros(high_ref.shape, high_ref.dtype)

    return start, finish


def heads_forward_kernel(blocks, fetch, jobs, main_ref, w_ref, mask_ref, *refs):
    if fetch:
        mine_r, mine_e, *refs = refs
    pre_ref, act_ref, ends_ref, *refs = refs
    if fetch:
        full_r, full_e, *refs = refs
    ext_ref, z_ref, local_sem, halo_send, halo_recv, *sems = refs
    step = pl.program_id(0)
    head_count, pixels, mid = pre_ref.shape
    cols = (ext_ref.shape[0] - pixels) // 2
    feat = ext_ref.shape[1]
    start, finish = edge_copies(
        main_ref,
        ext_ref.at[pl.ds(0, cols)],
        ext_ref.at[pl.ds(cols + pixels, cols)],
        cols,
        halo_send,
        halo_recv,
        blocks,
    )
    own = pltpu.make_async_copy(main_ref, ext_ref.at[pl.ds(cols, pixels)], local_sem.at[0])
    if fetch:
        jobs = jobs + spread_jobs((mine_r, mine_e), (full_r, full_e), sems, blocks)

    @pl.when(step == 0)
    def _():
        own.start()
        if jobs:
            greet_blocks(blocks)
        else:
            greet_line(blocks)
        start()
        for job in jobs:
            job[0]()
        own.wait()

    @pl.when(step == 3)
    def _():
        finish()

    if jobs:

        @pl.when(step == 7)
        def _():
            for job in jobs:
                job[1]()

    row_step = jnp.where(step < 3, 1, jnp.where(step < 6, 0, 2))
    col_step = lax.rem(step, 3)
    window = ext_ref[pl.ds(pl.multiple_of(row_step * cols, cols), pixels), :]
    product = contract_last(window, w_ref[0].reshape(head_count * mid, feat))
    product = masked(product, mask_ref[0], tap_at(step))

    @pl.when(step < 3)
    def _():
        z_ref[col_step] = product

    @pl.when(step >= 3)
    def _():
        z_ref[col_step] += product

    @pl.when(step == 8)
    def _():
        for head in range(head_count):
            part = slice(head * mid, (head + 1) * mid)
            total = (
                z_ref[1, :, part]
                + pltpu.roll(z_ref[0, :, part], 1, 0)
                + pltpu.roll(z_ref[2, :, part], pixels - 1, 0)
            )
            pre_ref[head] = total
            value = (total * sigmoid(total)).astype(jnp.bfloat16)
            act_ref[head] = value
            if head in targets:
                ends_ref[targets.index(head)] = value
        for job in jobs:
            job[2]()
        for job in jobs:
            job[3]()


def tap_at(step):
    return jnp.where(step < 3, step + 3, jnp.where(step < 6, step - 3, step))


def heads_forward(blocks, layer, jobs, cols, main, weights, mask, mine):
    _, head_count, _, mid, feat = weights.shape
    pixels = main.shape[0]
    f32, low = jnp.float32, jnp.bfloat16
    shape = jax.ShapeDtypeStruct
    anywhere = pl.BlockSpec(memory_space=pl.ANY)
    dma = pltpu.SemaphoreType.DMA
    return job_call(
        functools.partial(heads_forward_kernel, blocks, bool(mine)),
        jobs,
        blocks,
        grid=(9,),
        in_specs=[
            anywhere,
            pl.BlockSpec((1, head_count, 1, mid, feat), lambda t: (layer, 0, tap_at(t), 0, 0)),
            pl.BlockSpec((1, pixels, lanes), lambda t: (0, 0, 0)),
        ]
        + [anywhere] * len(mine),
        out_specs=[whole((head_count, pixels, mid))] * 2
        + [whole((2, pixels, mid))]
        + [anywhere] * len(mine),
        out_shape=[
            shape((head_count, pixels, mid), f32),
            shape((head_count, pixels, mid), low),
            shape((2, pixels, mid), low),
        ]
        + [shape((mine[0].shape[0], feat), low) for _ in mine],
        scratch_shapes=[
            pltpu.VMEM((pixels + 2 * cols, feat), low),
            pltpu.VMEM((3, pixels, head_count * mid), f32),
            dma((1,)),
            dma((2,)),
            dma((2,)),
        ]
        + (job_sems(blocks) * 2 if mine else []),
        compiler_params=comm_params(6 + layer),
        cost_estimate=pl.CostEstimate(
            flops=18 * pixels * head_count * mid * feat,
            bytes_accessed=18 * head_count * mid * feat,
            transcendentals=0,
        ),
    )(main, weights, mask, *mine)


def fill_taps(im_ref, slot, grad, bits, pixels, cols, dilation):
    rows, mid = grad.shape
    wide = grad.astype(jnp.float32)
    shifted_by = (pltpu.roll(wide, rows - dilation, 0), wide, pltpu.roll(wide, dilation, 0))
    for tap, (row_step, col_step) in enumerate(tap_offsets):
        start = (1 - row_step) * dilation * cols
        part = shifted_by[col_step + 1][start : start + pixels]
        im_ref[slot, :, tap * mid : (tap + 1) * mid] = masked(part, bits, 9 + tap).astype(
            jnp.bfloat16
        )


def messages_kernel(
    blocks,
    layer,
    ahead,
    jobs,
    feat_ref,
    w_hbm,
    cots_ref,
    gain_ref,
    bias_ref,
    mask_ref,
    maps_ref,
    local_ref,
    sums_ref,
    part_ref,
    values_ref,
    pack_ref,
    main_ref,
    low_ref,
    high_ref,
    cot_low,
    cot_high,
    w_ref,
    lhs_ref,
    z_ref,
    im_ref,
    grad_ref,
    *sems,
):
    w_sem, local_sem, halo_send, halo_recv, cot_send, cot_recv, *sems = sems
    parts, heads, pixels, mid = feat_ref.shape
    cot_ref = cots_ref.at[layer]
    cols = low_ref.shape[2]
    pairs = w_ref.shape[0]
    me, ch = lax.axis_index(BLK), lax.axis_index(CH)
    low = jnp.bfloat16
    loads = [
        pltpu.make_async_copy(w_hbm.at[layer, pair], w_ref.at[pair], w_sem.at[pair])
        for pair in range(pairs)
    ]
    main_copy = pltpu.make_async_copy(feat_ref, main_ref, local_sem.at[0])
    main_copy.start()
    for pair in (0, 4, 1, 5, 3, 2):
        loads[pair].start()
    greet(blocks, parts)
    early, jobs = jobs[:ahead], jobs[ahead:]
    for job in early:
        job[0]()
    start, finish = edge_copies(feat_ref, low_ref, high_ref, cols, halo_send, halo_recv, blocks)
    start()
    cot_start, cot_finish = edge_copies(
        cot_ref, cot_low, cot_high, cols, cot_send, cot_recv, blocks
    )
    cot_start()
    for job in jobs:
        job[0]()
    main_copy.wait()
    size = parts * mid // blocks
    for block in range(blocks):
        part, first = block * size // mid, block * size % mid
        for index, (one, two) in enumerate(groups):
            (pack_ref if sems else values_ref)[block, index] = jnp.concatenate(
                [main_ref[part, one][:, first : first + size], main_ref[part, two][:, first : first + size]],
                axis=1,
            )
    if sems:
        jobs = jobs + [slot_job(pack_ref, values_ref, sems, blocks)]
        jobs[-1][0]()
    for source in range(heads):
        for part in range(parts):
            lhs_ref[source, cols : cols + pixels, part * mid : (part + 1) * mid] = main_ref[part, source]
    order = (0, 4, 1, 5, 3, 2)
    bits = mask_ref[0]

    def taps(pair, row_step):
        source = message_pairs[pair][0]
        product = contract_last(
            lhs_ref[source, row_step * cols : row_step * cols + pixels, :],
            w_ref[pair, 3 * row_step : 3 * row_step + 3].reshape(3 * mid, parts * mid),
        )
        for col_step in range(3):
            value = masked(
                product[:, col_step * mid : (col_step + 1) * mid], bits, row_step * 3 + col_step
            )
            if row_step == 1:
                z_ref[pair, col_step] = value
            else:
                z_ref[pair, col_step] += value

    for pair in order:
        loads[pair].wait()
        taps(pair, 1)
    finish()
    cot_finish()
    for source in range(heads):
        for part in range(parts):
            chan = slice(part * mid, (part + 1) * mid)
            lhs_ref[source, 0:cols, chan] = low_ref[part, source]
            lhs_ref[source, cols + pixels :, chan] = high_ref[part, source]
    for pair in order:
        taps(pair, 0)
        taps(pair, 2)
    for job in early:
        job[1]()
    values = {}
    cots = {}
    for place, target in enumerate((0, 3)):
        values[target] = main_ref[ch, target].astype(jnp.float32)
        cots[target] = cot_ref[place].astype(jnp.float32)
    for place, target in enumerate((0, 3)):
        value, cot = values[target], cots[target]
        total, slopes = value, cot
        for pair in range(pairs):
            if message_pairs[pair][1] != target:
                continue
            message = (
                z_ref[pair, 1]
                + pltpu.roll(z_ref[pair, 0], 1, 0)
                + pltpu.roll(z_ref[pair, 2], pixels - 1, 0)
            )
            gain, bias = gain_ref[layer, pair : pair + 1], bias_ref[layer, pair : pair + 1]
            gate = sigmoid(gain * value + bias)
            total = total + gate * message
            grad_ref[pair] = (cot * gate).astype(low)
            slope = cot * message * gate * (1.0 - gate)
            sums_ref[pair : pair + 1] = jnp.sum(slope * value, axis=0, keepdims=True)
            sums_ref[pairs + pair : pairs + pair + 1] = jnp.sum(slope, axis=0, keepdims=True)
            slopes = slopes + slope * gain
        maps_ref[place] = total.astype(low)
        local_ref[place] = slopes

    for job in jobs:
        job[1]()

    def product_of(pair, slot):
        source, target = message_pairs[pair]
        place = 0 if target == 0 else 1
        gain, bias = gain_ref[layer, pair : pair + 1], bias_ref[layer, pair : pair + 1]

        def border(cot, feat):
            return (
                cot[place].astype(jnp.float32)
                * sigmoid(gain * feat[ch, target].astype(jnp.float32) + bias)
            ).astype(low)

        grad = jnp.concatenate(
            [border(cot_low, low_ref), grad_ref[pair], border(cot_high, high_ref)], axis=0
        )
        fill_taps(im_ref, slot, grad, bits, pixels, cols, 1)
        return jnp.dot(
            im_ref[slot],
            w_ref[pair].reshape(9 * mid, parts * mid),
            preferred_element_type=jnp.float32,
        )

    for count, (source, *members) in enumerate(source_order):
        if count == 2:
            for job in early:
                job[2]()
        total = product_of(members[0], 0)
        for pair in members[1:]:
            total = total + product_of(pair, 1)
        for part in range(parts):
            part_ref[part, source] = total[:, part * mid : (part + 1) * mid].astype(low)
    for job in jobs:
        job[2]()
    for job in early + jobs:
        job[3]()


def messages_both(blocks, layer, jobs, ahead, send, cols, features, weights, cotangents, gains, biases, mask):
    parts, heads, pixels, mid = features.shape
    pairs = weights.shape[1]
    narrow = parts * mid
    f32, low = jnp.float32, jnp.bfloat16
    shape = jax.ShapeDtypeStruct
    anywhere = pl.BlockSpec(memory_space=pl.ANY)
    inside = pl.BlockSpec(memory_space=pltpu.VMEM)
    dma = pltpu.SemaphoreType.DMA
    wide = 2 * narrow // blocks
    values = shape((blocks, 2, pixels, wide), low)
    return job_call(
        functools.partial(messages_kernel, blocks, layer, ahead),
        jobs,
        blocks,
        in_specs=[anywhere, anywhere] + [inside] * 4,
        out_specs=[inside] * 4 + [anywhere if send else inside],
        out_shape=[
            shape((2, pixels, mid), low),
            shape((2, pixels, mid), f32),
            shape((2 * pairs, mid), f32),
            shape((parts, heads, pixels, mid), low),
            values,
        ],
        scratch_shapes=[
            pltpu.VMEM(values.shape if send else (8, lanes), low),
            pltpu.VMEM((parts, heads, pixels, mid), low),
            pltpu.VMEM((parts, heads, cols, mid), low),
            pltpu.VMEM((parts, heads, cols, mid), low),
            pltpu.VMEM((2, cols, mid), low),
            pltpu.VMEM((2, cols, mid), low),
            pltpu.VMEM((pairs, 9, mid, narrow), low),
            pltpu.VMEM((heads, pixels + 2 * cols, narrow), low),
            pltpu.VMEM((pairs, 3, pixels, mid), f32),
            pltpu.VMEM((2, pixels, 9 * mid), low),
            pltpu.VMEM((pairs, pixels, mid), low),
            dma((pairs,)),
            dma((1,)),
            dma((2,)),
            dma((2,)),
            dma((2,)),
            dma((2,)),
        ]
        + (job_sems(blocks) if send else []),
        compiler_params=comm_params(10 + layer),
        cost_estimate=pl.CostEstimate(
            flops=36 * pixels * pairs * mid * narrow,
            bytes_accessed=18 * pairs * mid * narrow,
            transcendentals=0,
        ),
    )(features, weights, cotangents, gains, biases, mask)


def heads_backward_kernel(
    blocks,
    jobs,
    main_ref,
    w_ref,
    mask_ref,
    out_ref,
    low_ref,
    high_ref,
    im_ref,
    halo_send,
    halo_recv,
):
    step = pl.program_id(0)
    head_count, pixels, mid = main_ref.shape
    cols = low_ref.shape[1]

    @pl.when(step == 0)
    def _():
        start, finish = edge_copies(main_ref, low_ref, high_ref, cols, halo_send, halo_recv, blocks)
        if jobs:
            greet_blocks(blocks)
        else:
            greet_line(blocks)
        start()
        for job in jobs:
            job[0]()
        finish()
        for head in range(head_count):
            grad = jnp.concatenate([low_ref[head], main_ref[head], high_ref[head]], axis=0)
            fill_taps(im_ref, head, grad, mask_ref[0], pixels, cols, 1)

    total = None
    for head in range(head_count):
        product = jnp.dot(
            im_ref[head],
            w_ref[0, head].reshape(9 * mid, w_ref.shape[4]),
            preferred_element_type=jnp.float32,
        )
        total = product if total is None else total + product
    out_ref[0] = total.astype(jnp.bfloat16)

    if jobs:

        @pl.when(step == pl.num_programs(0) - 1)
        def _():
            for part in (1, 2, 3):
                for job in jobs:
                    job[part]()


def heads_backward(blocks, layer, jobs, cols, main, weights, mask, parts):
    _, head_count, taps, mid, feat = weights.shape
    pixels = main.shape[1]
    width = feat // parts
    dma = pltpu.SemaphoreType.DMA
    return job_call(
        functools.partial(heads_backward_kernel, blocks),
        jobs,
        blocks,
        grid=(parts,),
        in_specs=[
            whole(main.shape),
            pl.BlockSpec((1, head_count, taps, mid, width), lambda j: (layer, 0, 0, 0, j)),
            pl.BlockSpec((1, pixels, lanes), lambda j: (0, 0, 0)),
        ],
        out_specs=[pl.BlockSpec((1, pixels, width), lambda j: (j, 0, 0))],
        out_shape=[jax.ShapeDtypeStruct((parts, pixels, width), jnp.bfloat16)],
        scratch_shapes=[
            pltpu.VMEM((head_count, cols, mid), jnp.bfloat16),
            pltpu.VMEM((head_count, cols, mid), jnp.bfloat16),
            pltpu.VMEM((head_count, pixels, taps * mid), jnp.bfloat16),
            dma((2,)),
            dma((2,)),
        ],
        compiler_params=comm_params(20 + layer),
        cost_estimate=pl.CostEstimate(
            flops=18 * pixels * head_count * mid * feat,
            bytes_accessed=18 * head_count * mid * feat,
            transcendentals=0,
        ),
    )(main, weights, mask)


class WeightChunks:
    def __init__(self, blocks, layer, sources, gates, buffers, accs, lhs, sems):
        self.blocks, self.layer = blocks, layer
        (self.mv, self.cot, self.ends, self.hv_up, self.hv_low, self.hg, self.bits) = sources
        self.gain, self.bias = gates
        (self.mv_buf, self.cot_buf, self.ends_buf, self.hv_buf, self.hg_buf, self.bits_buf) = buffers
        self.accs, self.lhs, self.sems = accs, lhs, sems
        self.done = 0
        self.pixels = 2 * self.hv_up.shape[1]

    def copies(self, heads, index):
        pixels, last = self.pixels, self.blocks - 1
        before, after = jnp.maximum(index - 1, 0), jnp.minimum(index + 1, last)
        slot = lax.rem(index, 2)
        buffer = self.hv_buf if heads else self.mv_buf
        if heads:
            half = pixels // 2
            pairs = [
                (
                    self.hv_low.at[before, pl.ds(half - lanes, lanes)],
                    buffer.at[slot, pl.ds(0, lanes)],
                ),
                (self.hv_up.at[index], buffer.at[slot, pl.ds(lanes, half)]),
                (self.hv_low.at[index], buffer.at[slot, pl.ds(lanes + half, half)]),
                (
                    self.hv_up.at[after, pl.ds(0, lanes)],
                    buffer.at[slot, pl.ds(lanes + pixels, lanes)],
                ),
            ]
        else:
            every = slice(None)
            pairs = [
                (
                    self.mv.at[before, every, pl.ds(pixels - lanes, lanes)],
                    buffer.at[slot, every, pl.ds(0, lanes)],
                ),
                (self.mv.at[index], buffer.at[slot, every, pl.ds(lanes, pixels)]),
                (
                    self.mv.at[after, every, pl.ds(0, lanes)],
                    buffer.at[slot, every, pl.ds(lanes + pixels, lanes)],
                ),
            ]
        pairs.append(
            (
                self.bits.at[pl.ds(pl.multiple_of(index * pixels, pixels), pixels)],
                self.bits_buf.at[slot],
            )
        )
        if heads:
            pairs.append((self.hg.at[index], self.hg_buf.at[slot]))
        else:
            pairs.append((self.cot.at[index], self.cot_buf.at[slot]))
            pairs.append((self.ends.at[index], self.ends_buf.at[slot]))
        return [
            pltpu.make_async_copy(source, target, self.sems.at[slot, place])
            for place, (source, target) in enumerate(pairs)
        ]

    def fetch(self, heads, index):
        for copy in self.copies(heads, index):
            copy.start()

    def begin(self):
        for acc in self.accs:
            acc[...] = jnp.zeros(acc.shape, acc.dtype)
        self.fetch(False, 0)

    def add(self, heads, index):
        slot = lax.rem(index, 2)
        pixels = self.pixels
        for copy in self.copies(heads, index):
            copy.wait()

        @pl.when(index + 1 < self.blocks)
        def _():
            self.fetch(heads, index + 1)

        if not heads:

            @pl.when(index + 1 == self.blocks)
            def _():
                self.fetch(True, 0)

        bits = self.bits_buf[slot]
        for place, members in enumerate((tuple(range(4)),) if heads else group_pairs):
            window = (self.hv_buf[slot] if heads else self.mv_buf[slot, place]).astype(jnp.float32)
            size, chans = window.shape
            shifted_by = (pltpu.roll(window, 1, 0), window, pltpu.roll(window, size - 1, 0))
            for tap, (row_step, col_step) in enumerate(tap_offsets):
                top = (1 + row_step) * lanes
                part = shifted_by[col_step + 1][top : top + pixels]
                self.lhs[:, tap * chans : (tap + 1) * chans] = masked(part, bits, tap).astype(
                    jnp.bfloat16
                )
            if heads:
                grads = [self.hg_buf[slot, member] for member in members]
            else:
                grads = [self.message_grad(slot, pair) for pair in members]
            acc = self.accs[2] if heads else self.accs[place]
            acc[...] += lax.dot_general(
                self.lhs[:, : 9 * chans],
                jnp.concatenate(grads, axis=1),
                (((0,), (0,)), ((), ())),
                preferred_element_type=jnp.float32,
            )

    def message_grad(self, slot, pair):
        place = targets.index(message_pairs[pair][1])
        gain = self.gain[self.layer, pair : pair + 1]
        bias = self.bias[self.layer, pair : pair + 1]
        gate = sigmoid(gain * self.ends_buf[slot, place].astype(jnp.float32) + bias)
        return (self.cot_buf[slot, place].astype(jnp.float32) * gate).astype(jnp.bfloat16)

    def run(self, count):
        while count:
            heads = self.done >= self.blocks
            start = self.done % self.blocks
            size = min(count, self.blocks - start)

            def step(index, state):
                self.add(heads, index)
                return state

            lax.fori_loop(start, start + size, step, 0)
            self.done += size
            count -= size


def exchange_kernel(blocks, jobs, done_ref):
    greet_blocks(blocks)
    for part in range(4):
        for job in jobs:
            job[part]()
    done_ref[...] = jnp.zeros(done_ref.shape, done_ref.dtype)


def exchange(blocks, jobs):
    _, moved = job_call(
        functools.partial(exchange_kernel, blocks),
        jobs,
        blocks,
        in_specs=[],
        out_specs=[pl.BlockSpec(memory_space=pltpu.VMEM)],
        out_shape=[jax.ShapeDtypeStruct((8, lanes), jnp.float32)],
        scratch_shapes=[],
        compiler_params=comm_params(30),
        cost_estimate=pl.CostEstimate(flops=10**6, bytes_accessed=10**8, transcendentals=0),
    )()
    return moved


def heads_store(out_ref, acc_ref):
    head_count, taps, chans, mid = out_ref.shape
    for head in range(head_count):
        for tap in range(taps):
            out_ref[head, tap] = acc_ref[
                tap * chans : (tap + 1) * chans, head * mid : (head + 1) * mid
            ]


def messages_store(out_ref, acc_refs):
    _, taps, size, mid = out_ref.shape
    for index, members in enumerate(group_pairs):
        for place, pair in enumerate(members):
            side = groups[index].index(message_pairs[pair][0])
            for tap in range(taps):
                start = (2 * tap + side) * size
                out_ref[pair, tap] = acc_refs[index][
                    start : start + size, place * mid : (place + 1) * mid
                ]


def greet(blocks, parts):
    barrier = pltpu.get_barrier_semaphore()
    blk, ch = lax.axis_index(BLK), lax.axis_index(CH)
    for step in range(1, blocks):
        pl.semaphore_signal(
            barrier, inc=1, device_id={BLK: lax.rem(blk + step, blocks)}, device_id_type=MESH
        )
    for step in range(1, parts):
        pl.semaphore_signal(
            barrier, inc=1, device_id={CH: lax.rem(ch + step, parts)}, device_id_type=MESH
        )
    pl.semaphore_wait(barrier, blocks + parts - 2)


def send_slots(source_of, target_ref, send_sem, recv_sem, axis, count):
    me = lax.axis_index(axis)
    copies = []
    for step in range(1, count):
        peer = lax.rem(me + step, count)
        copy = pltpu.make_async_remote_copy(
            src_ref=source_of(peer),
            dst_ref=target_ref.at[me],
            send_sem=send_sem.at[step],
            recv_sem=recv_sem.at[me],
            device_id={axis: peer},
            device_id_type=MESH,
        )
        copy.start()
        copies.append(copy)

    def finish():
        for step in range(1, count):
            peer = lax.rem(me + step, count)
            pltpu.make_async_remote_copy(
                src_ref=target_ref.at[peer],
                dst_ref=target_ref.at[peer],
                send_sem=send_sem.at[step],
                recv_sem=recv_sem.at[peer],
                device_id={axis: peer},
                device_id_type=MESH,
            ).wait_recv()
        for copy in copies:
            copy.wait_send()

    return finish


def block_totals(first, second, stat_ref, send_sem, recv_sem, blocks, meanwhile=None):
    me = lax.axis_index(BLK)
    stat_ref[me, 0:1] = first
    stat_ref[me, 1:2] = second
    finish = send_slots(lambda _: stat_ref.at[me], stat_ref, send_sem, recv_sem, BLK, blocks)
    if meanwhile is not None:
        meanwhile()
    finish()
    total = stat_ref[0]
    for block in range(1, blocks):
        total = total + stat_ref[block]
    return total[0:1], total[1:2]


def fold(values):
    rows, width = values.shape
    return values.reshape(rows // 8, 8, width).sum(axis=0)


def row_loop(rows, block, body, carry):
    def step(index, state):
        return body(pl.ds(pl.multiple_of(index * block, block), block), state)

    return lax.fori_loop(0, rows // block, step, carry)


def moments(ref, block):
    rows, width = ref.shape

    def body(part, state):
        values = ref[part, :]
        return state[0] + fold(values), state[1] + fold(values * values)

    zero = jnp.zeros((8, width), jnp.float32)
    total, square = row_loop(rows, block, body, (zero, zero))
    return total.sum(axis=0, keepdims=True), square.sum(axis=0, keepdims=True)


def halo_copies(ref, edge, pixels, send_sem, recv_sem, blocks):
    me = lax.axis_index(BLK)

    def copy(source, target, side, peer):
        return pltpu.make_async_remote_copy(
            src_ref=ref.at[pl.ds(source, edge)],
            dst_ref=ref.at[pl.ds(target, edge)],
            send_sem=send_sem.at[side],
            recv_sem=recv_sem.at[side],
            device_id={BLK: peer},
            device_id_type=MESH,
        )

    up = copy(pixels, 0, 0, lax.rem(me + 1, blocks))
    down = copy(edge, edge + pixels, 1, lax.rem(me + blocks - 1, blocks))

    @pl.when(me < blocks - 1)
    def _():
        up.start()

    @pl.when(me > 0)
    def _():
        down.start()

    @pl.when(me == 0)
    def _():
        ref[0:edge, :] = jnp.zeros((edge, ref.shape[1]), ref.dtype)

    @pl.when(me == blocks - 1)
    def _():
        ref[edge + pixels :, :] = jnp.zeros((edge, ref.shape[1]), ref.dtype)

    def finish():
        @pl.when(me > 0)
        def _():
            up.wait_recv()
            down.wait_send()

        @pl.when(me < blocks - 1)
        def _():
            down.wait_recv()
            up.wait_send()

    return finish


def trunk_forward_kernel(
    blocks,
    parts,
    layer,
    fetch,
    jobs,
    cur_ref,
    wr_ref,
    wd_ref,
    we_ref,
    mask_ref,
    gains_ref,
    biases_ref,
    wide_gains_ref,
    wide_biases_ref,
    *refs,
):
    if fetch:
        raw_r, raw_e, *refs = refs
    out_ref, ext_out_ref, full_ref, normed1_ref, inverse1_ref, normed2_ref, inverse2_ref = refs[:7]
    normed3_ref, inverse3_ref = refs[7:9]
    refs = refs[9:]
    if fetch:
        full_r, full_e, *refs = refs
    pre1_ref, pre3_ref, ext_ref, z_ref, gath_ref, stat1_ref, stat2_ref, stat3_ref = refs[:8]
    term1_ref, term3_ref, stat_send, stat_recv, halo_send, halo_recv, part_send, part_recv = refs[8:16]
    pixels, feat = cur_ref.shape
    mid = normed1_ref.shape[1]
    wide = normed3_ref.shape[1]
    edge = (ext_ref.shape[0] - pixels) // 2
    ch = lax.axis_index(CH)
    pixel_count = float(pixels * blocks)
    greet(blocks, parts)

    def whole_row(row_of):
        return jnp.concatenate([row_of(part) for part in range(parts)], axis=1)

    gain1 = whole_row(lambda part: gains_ref[part, layer, 0:1])
    bias1 = whole_row(lambda part: biases_ref[part, layer, 0:1])
    gain3 = whole_row(lambda part: wide_gains_ref[part, layer : layer + 1])
    bias3 = whole_row(lambda part: wide_biases_ref[part, layer : layer + 1])
    if fetch:
        start, finish = stripe_job(
            raw_r, raw_e, fetch, (full_r, full_e), refs[16:], blocks, parts
        )

    def terms(total, square):
        mean_value = total / pixel_count
        variance = square / pixel_count - mean_value * mean_value
        return mean_value, lax.rsqrt(variance + epsilon)

    pre1_ref[...] = contract_last(cur_ref[...], wr_ref[...])
    total, square = moments(pre1_ref, 64)
    mean_value, inverse = terms(
        *block_totals(total, square, stat1_ref, stat_send.at[0], stat_recv.at[0], blocks)
    )
    term1_ref[0:1] = mean_value
    term1_ref[1:2] = inverse

    def first(part, state):
        value = gain1 * ((pre1_ref[part, :] - mean_value) * inverse) + bias1
        pre1_ref[part, :] = value * sigmoid(value)
        return state

    own_mid = pl.ds(pl.multiple_of(ch * mid, mid), mid)
    normed1_ref[...] = (pre1_ref[:, own_mid] - term1_ref[0:1, own_mid]) * term1_ref[1:2, own_mid]
    inverse1_ref[...] = term1_ref[1:2, own_mid]
    row_loop(pixels, 64, first, 0)
    ext_ref[edge : edge + pixels, :] = pre1_ref[...].astype(jnp.bfloat16)
    wait_halo = halo_copies(ext_ref, edge, pixels, halo_send, halo_recv, blocks)

    half = edge // 2
    for row_step in (1, 0, 2):
        if row_step == 0:
            wait_halo()
        top = 2 * row_step * half
        product = contract_last(
            ext_ref[top : top + pixels, :],
            wd_ref[layer, 3 * row_step : 3 * row_step + 3].reshape(3 * mid, parts * mid),
        )
        for col_step in range(3):
            part = masked(
                product[:, col_step * mid : (col_step + 1) * mid],
                mask_ref[1],
                row_step * 3 + col_step,
            )
            if row_step == 1:
                z_ref[col_step] = part
            else:
                z_ref[col_step] += part
    second_pre = (
        z_ref[1] + pltpu.roll(z_ref[0], 2, 0) + pltpu.roll(z_ref[2], pixels - 2, 0)
    )
    mean_value, inverse = terms(
        *block_totals(
            jnp.sum(second_pre, axis=0, keepdims=True),
            jnp.sum(second_pre * second_pre, axis=0, keepdims=True),
            stat2_ref,
            stat_send.at[1],
            stat_recv.at[1],
            blocks,
        )
    )
    normed = (second_pre - mean_value) * inverse
    normed2_ref[...] = normed
    inverse2_ref[...] = inverse
    value = gains_ref[ch, layer, 1:2] * normed + biases_ref[ch, layer, 1:2]
    gath_ref[ch] = (value * sigmoid(value)).astype(jnp.bfloat16)
    wait_parts = send_slots(
        lambda _: gath_ref.at[ch], gath_ref, part_send, part_recv, CH, parts
    )
    for job in jobs:
        job[0]()
    ext_out_ref[...] = ext_ref[...]
    wait_parts()
    if fetch:
        start()
    for part in range(parts):
        full_ref[:, part * mid : (part + 1) * mid] = gath_ref[part]
    for part in range(parts):
        lane = slice(part * wide, (part + 1) * wide)
        pre3_ref[:, lane] = jnp.dot(
            full_ref[...], we_ref[:, lane], preferred_element_type=jnp.float32
        )
    for job in jobs:
        job[1]()
    total, square = moments(pre3_ref, 16)
    mean_value, inverse = terms(
        *block_totals(total, square, stat3_ref, stat_send.at[2], stat_recv.at[2], blocks)
    )
    term3_ref[0:1] = mean_value
    term3_ref[1:2] = inverse

    def last(part, state):
        value = (
            gain3 * ((pre3_ref[part, :] - mean_value) * inverse)
            + bias3
            + cur_ref[part, :].astype(jnp.float32)
        )
        out_ref[part, :] = (value * sigmoid(value)).astype(jnp.bfloat16)
        return state

    row_loop(pixels, 16, last, 0)
    own_wide = pl.ds(pl.multiple_of(ch * wide, wide), wide)
    for job in jobs:
        job[2]()
    normed3_ref[...] = (pre3_ref[:, own_wide] - term3_ref[0:1, own_wide]) * term3_ref[1:2, own_wide]
    inverse3_ref[...] = term3_ref[1:2, own_wide]
    if fetch:
        finish()
    for job in jobs:
        job[3]()


def trunk_forward(
    blocks, parts, cols, layer, jobs, current, reduce_w, dilated_w, expand_w, mask, norms, raw
):
    pixels, feat = current.shape
    narrow = reduce_w.shape[0]
    mid, wide = narrow // parts, feat // parts
    edge = 2 * cols
    f32, low = jnp.float32, jnp.bfloat16
    shape = jax.ShapeDtypeStruct
    rows = edge * 2 + pixels
    inside = pl.BlockSpec(memory_space=pltpu.VMEM)
    anywhere = pl.BlockSpec(memory_space=pl.ANY)
    fetch = layer + 1 if raw else 0
    return job_call(
        functools.partial(trunk_forward_kernel, blocks, parts, layer, fetch),
        jobs,
        blocks,
        in_specs=[inside] * 9 + [anywhere] * len(raw),
        out_specs=[inside] * 9 + [anywhere] * len(raw),
        out_shape=[
            shape((pixels, feat), low),
            shape((rows, narrow), low),
            shape((pixels, narrow), low),
            shape((pixels, mid), f32),
            shape((1, mid), f32),
            shape((pixels, mid), f32),
            shape((1, mid), f32),
            shape((pixels, wide), f32),
            shape((1, wide), f32),
        ]
        + (stripe_shapes(parts, blocks, *raw) if raw else []),
        scratch_shapes=[
            pltpu.VMEM((pixels, narrow), f32),
            pltpu.VMEM((pixels, feat), f32),
            pltpu.VMEM((rows, narrow), low),
            pltpu.VMEM((3, pixels, mid), f32),
            pltpu.VMEM((parts, pixels, mid), low),
            pltpu.VMEM((blocks, 2, narrow), f32),
            pltpu.VMEM((blocks, 2, mid), f32),
            pltpu.VMEM((blocks, 2, feat), f32),
            pltpu.VMEM((2, narrow), f32),
            pltpu.VMEM((2, feat), f32),
            pltpu.SemaphoreType.DMA((3, blocks)),
            pltpu.SemaphoreType.DMA((3, blocks)),
            pltpu.SemaphoreType.DMA((2,)),
            pltpu.SemaphoreType.DMA((2,)),
            pltpu.SemaphoreType.DMA((parts,)),
            pltpu.SemaphoreType.DMA((parts,)),
        ]
        + (stripe_sems(parts) if raw else []),
        compiler_params=comm_params(50 + layer),
        cost_estimate=pl.CostEstimate(
            flops=2 * pixels * (2 * narrow * feat + 9 * mid * narrow),
            bytes_accessed=150 * 2**20,
            transcendentals=0,
        ),
    )(current, reduce_w, dilated_w, expand_w, mask, *norms, *raw)


def slope_of(values):
    gate = sigmoid(values)
    return gate * (1.0 + values * (1.0 - gate))


def sum_slots(ref, count):
    total = ref[0].astype(jnp.float32)
    for slot in range(1, count):
        total = total + ref[slot].astype(jnp.float32)
    return total


plan = (1, 5, 1, 5, 1, 3)


def trunk_backward_kernel(
    blocks,
    parts,
    layer,
    jobs,
    *refs,
):
    up_ref, heads_ref, cur_ref, normed3_ref, inverse3_ref = refs[:5]
    refs = refs[5:]
    we_ref, full_ref, normed2_ref, inverse2_ref, wd_ref = refs[:5]
    refs = refs[5:]
    mask_ref, ext_ref, normed1_ref, inverse1_ref, wr_ref = refs[:5]
    refs = refs[5:]
    gate_ref, gains_ref, biases_ref, wide_gains_ref, wide_biases_ref = refs[:5]
    refs = refs[5:]
    sources, gates, refs = refs[:7], refs[7:9], refs[9:]
    out_ref, expand_ref, dilated_ref, reduce_ref, wide_ref = refs[:5]
    refs = refs[5:]
    second_ref, first_ref, gate_out = refs[:3]
    refs = refs[3:]
    messages_out, heads_out, *refs = refs
    third_ref, grad_ref, im_ref, send2_ref, recv2_ref = refs[:5]
    refs = refs[5:]
    send1_ref, recv1_ref, gath_ref, low_ref, ex_send_ref = refs[:5]
    refs = refs[5:]
    ex_recv_ref, di_send_ref, di_recv_ref, re_send_ref, re_recv_ref = refs[:5]
    refs = refs[5:]
    stat3_ref, stat2_ref, stat1_ref, gates_ref, stat_send = refs[:5]
    refs = refs[5:]
    stat_recv, halo_send, halo_recv, part_send, part_recv = refs[:5]
    refs = refs[5:]
    sum_send, sum_recv = refs[:2]
    refs = refs[2:]
    buffers, accs, (lhs_ref, chunk_sem) = refs[:6], refs[6:9], refs[9:]
    chunks = WeightChunks(blocks, layer, sources, gates, buffers, accs, lhs_ref, chunk_sem)
    pixels, wide = up_ref.shape
    mid = normed1_ref.shape[1]
    narrow = mid * parts
    feat = cur_ref.shape[1]
    edge = (grad_ref.shape[0] - pixels) // 2
    half = edge // 2
    blk = lax.axis_index(BLK)
    ch = lax.axis_index(CH)
    pixel_count = float(pixels * blocks)
    low = jnp.bfloat16
    gain3 = wide_gains_ref[layer : layer + 1]
    bias3 = wide_biases_ref[layer : layer + 1]
    greet(blocks, parts)
    chunks.begin()
    own_wide = pl.ds(pl.multiple_of(ch * wide, wide), wide)
    gates_ref[blk] = gate_ref[...]
    wait_gates = send_slots(
        lambda _: gates_ref.at[blk], gates_ref, stat_send.at[3], stat_recv.at[3], BLK, blocks
    )

    def start(part, state):
        normed = normed3_ref[part, :]
        summed = (
            gain3 * normed + bias3 + cur_ref[part, own_wide].astype(jnp.float32)
        )
        value = (up_ref[part, :] + heads_ref[part, :].astype(jnp.float32)) * slope_of(summed)
        out_ref[part, :] = value
        return state[0] + fold(value), state[1] + fold(value * normed)

    zero = jnp.zeros((8, wide), jnp.float32)
    bias_sum, gain_sum = row_loop(pixels, 32, start, (zero, zero))
    bias_grad, gain_grad = block_totals(
        bias_sum.sum(axis=0, keepdims=True),
        gain_sum.sum(axis=0, keepdims=True),
        stat3_ref,
        stat_send.at[0],
        stat_recv.at[0],
        blocks,
        lambda: chunks.run(plan[0]),
    )
    wide_ref[0:1] = gain_grad
    wide_ref[1:2] = bias_grad
    scale = gain3 * inverse3_ref[...]
    bias_part = bias_grad / pixel_count
    gain_part = gain_grad / pixel_count

    def third(part, state):
        third_ref[part, :] = (
            scale * (out_ref[part, :] - bias_part - normed3_ref[part, :] * gain_part)
        ).astype(low)
        return state

    row_loop(pixels, 32, third, 0)
    product = contract_last(third_ref[...], we_ref[layer])
    for part in range(parts):
        send2_ref[part] = product[:, part * mid : (part + 1) * mid].astype(low)
    recv2_ref[ch] = send2_ref[ch]
    wait_parts = send_slots(
        lambda peer: send2_ref.at[peer], recv2_ref, part_send.at[0], part_recv.at[0], CH, parts
    )
    size = narrow // blocks
    product = lax.dot_general(
        full_ref[...], third_ref[...], (((0,), (0,)), ((), ())), preferred_element_type=jnp.float32
    )
    for block in range(blocks):
        ex_send_ref[block] = product[block * size : (block + 1) * size].astype(low)
    ex_recv_ref[blk] = ex_send_ref[blk]
    wait_expand = send_slots(
        lambda peer: ex_send_ref.at[peer], ex_recv_ref, sum_send.at[0], sum_recv.at[0], BLK, blocks
    )
    chunks.run(plan[1])
    wait_parts()

    def narrow_norm(recv_ref, normed_ref, inverse_ref, norm, stat_ref, phase, sums_ref):
        gain = gains_ref[layer, norm : norm + 1]
        bias = biases_ref[layer, norm : norm + 1]
        normed = normed_ref[...]
        value = sum_slots(recv_ref, parts) * slope_of(gain * normed + bias)
        bias_grad, gain_grad = block_totals(
            jnp.sum(value, axis=0, keepdims=True),
            jnp.sum(value * normed, axis=0, keepdims=True),
            stat_ref,
            stat_send.at[phase],
            stat_recv.at[phase],
            blocks,
            lambda: chunks.run(plan[2 * phase]),
        )
        sums_ref[0:1] = gain_grad
        sums_ref[1:2] = bias_grad
        return (
            gain
            * inverse_ref[...]
            * (value - bias_grad / pixel_count - normed * (gain_grad / pixel_count))
        )

    grad = narrow_norm(
        recv2_ref, normed2_ref, inverse2_ref, 1, stat2_ref, 1, second_ref
    )
    grad_ref[edge : edge + pixels, :] = grad.astype(low)
    wait_halo = halo_copies(grad_ref, edge, pixels, halo_send, halo_recv, blocks)
    own = grad_ref[edge : edge + pixels, :].astype(jnp.float32)
    turned = (pltpu.roll(own, pixels - 2, 0), own, pltpu.roll(own, 2, 0))
    for row_step in range(3):
        side = jnp.concatenate(
            [
                masked(turned[col_step], mask_ref[1], row_step * 3 + col_step).astype(low)
                for col_step in range(3)
            ],
            axis=1,
        )
        top = 2 * row_step * half
        product = lax.dot_general(
            ext_ref[top : top + pixels, :],
            side,
            (((0,), (0,)), ((), ())),
            preferred_element_type=jnp.float32,
        )
        for block in range(blocks):
            for col_step in range(3):
                di_send_ref[block, row_step * 3 + col_step] = product[
                    block * size : (block + 1) * size, col_step * mid : (col_step + 1) * mid
                ].astype(low)
    di_recv_ref[blk] = di_send_ref[blk]
    wait_halo()
    fill_taps(im_ref, 0, grad_ref[...], mask_ref[1], pixels, half, 2)
    product = jnp.dot(
        im_ref[0], wd_ref[layer].reshape(9 * mid, narrow), preferred_element_type=jnp.float32
    )
    for part in range(parts):
        send1_ref[part] = product[:, part * mid : (part + 1) * mid].astype(low)
    recv1_ref[ch] = send1_ref[ch]
    wait_parts = send_slots(
        lambda peer: send1_ref.at[peer], recv1_ref, part_send.at[1], part_recv.at[1], CH, parts
    )
    wait_dilated = send_slots(
        lambda peer: di_send_ref.at[peer], di_recv_ref, sum_send.at[1], sum_recv.at[1], BLK, blocks
    )
    for job in jobs:
        job[0]()
    chunks.run(plan[3])
    wait_parts()
    grad = narrow_norm(
        recv1_ref, normed1_ref, inverse1_ref, 0, stat1_ref, 2, first_ref
    )
    gath_ref[ch] = grad.astype(low)
    wait_parts = send_slots(
        lambda _: gath_ref.at[ch], gath_ref, part_send.at[2], part_recv.at[2], CH, parts
    )
    product = lax.dot_general(
        cur_ref[...], gath_ref[ch], (((0,), (0,)), ((), ())), preferred_element_type=jnp.float32
    )
    size = feat // blocks
    for block in range(blocks):
        re_send_ref[block] = product[block * size : (block + 1) * size].astype(low)
    re_recv_ref[blk] = re_send_ref[blk]
    wait_reduce = send_slots(
        lambda peer: re_send_ref.at[peer], re_recv_ref, sum_send.at[2], sum_recv.at[2], BLK, blocks
    )
    chunks.run(plan[5])
    wait_parts()
    for part in range(parts):
        low_ref[:, part * mid : (part + 1) * mid] = gath_ref[part]
    out_ref[...] += jnp.dot(low_ref[...], wr_ref[:, own_wide], preferred_element_type=jnp.float32)
    chunks.run(2 * blocks - chunks.done)
    messages_store(messages_out, accs[:2])
    heads_store(heads_out, accs[2])
    for part in (1, 2, 3):
        for job in jobs:
            job[part]()
    wait_gates()
    gate_out[...] = sum_slots(gates_ref, blocks)
    wait_expand()
    expand_ref[...] = sum_slots(ex_recv_ref, blocks)
    wait_dilated()
    dilated_ref[...] = sum_slots(di_recv_ref, blocks)
    wait_reduce()
    reduce_ref[...] = sum_slots(re_recv_ref, blocks)


def trunk_backward(blocks, parts, layer, jobs, operands, norms, sources, gates):
    pixels, wide = operands[0].shape
    feat = wide * parts
    mid = operands[7].shape[1]
    narrow = mid * parts
    rows = operands[11].shape[0]
    f32, low = jnp.float32, jnp.bfloat16
    shape = jax.ShapeDtypeStruct
    small, large = narrow // blocks, feat // blocks
    inside = pl.BlockSpec(memory_space=pltpu.VMEM)
    anywhere = pl.BlockSpec(memory_space=pl.ANY)
    rows_two = pixels + 2 * lanes
    return job_call(
        functools.partial(trunk_backward_kernel, blocks, parts, layer),
        jobs,
        blocks,
        in_specs=[inside] * (len(operands) + len(norms)) + [anywhere] * len(sources) + [inside] * len(gates),
        out_specs=[inside] * 10,
        out_shape=[
            shape((pixels, wide), f32),
            shape((small, wide), f32),
            shape((9, small, mid), f32),
            shape((large, mid), f32),
            shape((2, wide), f32),
            shape((2, mid), f32),
            shape((2, mid), f32),
            shape(operands[-1].shape, f32),
            shape((6, 9, small, mid), f32),
            shape((4, 9, large, mid), f32),
        ],
        scratch_shapes=[
            pltpu.VMEM((pixels, wide), low),
            pltpu.VMEM((rows, mid), low),
            pltpu.VMEM((1, pixels, 9 * mid), low),
            pltpu.VMEM((parts, pixels, mid), low),
            pltpu.VMEM((parts, pixels, mid), low),
            pltpu.VMEM((parts, pixels, mid), low),
            pltpu.VMEM((parts, pixels, mid), low),
            pltpu.VMEM((parts, pixels, mid), low),
            pltpu.VMEM((pixels, narrow), low),
            pltpu.VMEM((blocks, small, wide), low),
            pltpu.VMEM((blocks, small, wide), low),
            pltpu.VMEM((blocks, 9, small, mid), low),
            pltpu.VMEM((blocks, 9, small, mid), low),
            pltpu.VMEM((blocks, large, mid), low),
            pltpu.VMEM((blocks, large, mid), low),
            pltpu.VMEM((blocks, 2, wide), f32),
            pltpu.VMEM((blocks, 2, mid), f32),
            pltpu.VMEM((blocks, 2, mid), f32),
            pltpu.VMEM((blocks,) + operands[-1].shape, f32),
            pltpu.SemaphoreType.DMA((4, blocks)),
            pltpu.SemaphoreType.DMA((4, blocks)),
            pltpu.SemaphoreType.DMA((2,)),
            pltpu.SemaphoreType.DMA((2,)),
            pltpu.SemaphoreType.DMA((3, parts)),
            pltpu.SemaphoreType.DMA((3, parts)),
            pltpu.SemaphoreType.DMA((3, blocks)),
            pltpu.SemaphoreType.DMA((3, blocks)),
            pltpu.VMEM((2, 2, rows_two, 2 * small), low),
            pltpu.VMEM((2, 2, pixels, mid), low),
            pltpu.VMEM((2, 2, pixels, mid), low),
            pltpu.VMEM((2, rows_two, large), low),
            pltpu.VMEM((2, 4, pixels, mid), low),
            pltpu.VMEM((2, pixels, lanes), jnp.int32),
            pltpu.VMEM((18 * small, len(group_pairs[0]) * mid), f32),
            pltpu.VMEM((18 * small, len(group_pairs[1]) * mid), f32),
            pltpu.VMEM((9 * large, 4 * mid), f32),
            pltpu.VMEM((pixels, 9 * max(large, 2 * small)), low),
            pltpu.SemaphoreType.DMA((2, 6)),
        ],
        compiler_params=comm_params(60 + layer),
        cost_estimate=pl.CostEstimate(
            flops=4 * pixels * (2 * narrow * wide + 9 * mid * narrow) + 2 * 10**10,
            bytes_accessed=200 * 2**20,
            transcendentals=0,
        ),
    )(*operands, *norms, *sources, *gates)


def gather_parts(values):
    return lax.all_gather(values, CH, axis=0, tiled=False)


def reduce_parts(values):
    return lax.psum_scatter(values, CH, scatter_dimension=0, tiled=False)


def own_slice(values, size, axis):
    return lax.dynamic_slice_in_dim(values, lax.axis_index(CH) * size, size, axis)


def shards(
    features_in,
    w_reduce,
    w_dilated,
    w_expand,
    w_heads,
    w_messages,
    norm_gain,
    norm_bias,
    wide_gain,
    wide_bias,
    gate_gain,
    gate_bias,
    canvas_ids,
    output_cotangent,
    task_cotangents,
):
    rows, cols, wide = features_in.shape
    pixels = rows * cols
    blocks = lax.axis_size(BLK)
    parts = lax.axis_size(CH)
    layers = w_reduce.shape[0]
    mid = w_reduce.shape[1]
    feat = wide * parts
    narrow = mid * parts
    low = jnp.bfloat16
    dilated_t = w_dilated.transpose(0, 2, 1, 3)
    heads_t = w_heads.transpose(0, 1, 3, 2, 4)
    messages_t = w_messages.transpose(0, 1, 3, 2, 4)
    current, *rest = prologue(
        blocks,
        parts,
        features_in.reshape(pixels, wide),
        w_reduce,
        w_expand,
        (norm_gain, norm_bias, wide_gain, wide_bias),
        canvas_ids,
    )
    reduce_full, expand_full = [rest[2]], [rest[3]]
    norms_all, bits, all_bits = rest[4:8], rest[8], rest[9]
    cotangents = task_cotangents.reshape(layers, 2, pixels, mid)
    kept = []
    for layer in range(layers):
        keep = types.SimpleNamespace(input=current)
        results, (keep.cotangents,) = trunk_forward(
            blocks,
            parts,
            cols,
            layer,
            [(gather_kind, cotangents, layer)],
            current,
            reduce_full[layer],
            dilated_t,
            expand_full[layer],
            bits,
            norms_all,
            (w_reduce, w_expand) if layer + 1 < layers else (),
        )
        (
            current,
            keep.first_ext,
            keep.second_full,
            keep.normed1,
            keep.inverse1,
            keep.normed2,
            keep.inverse2,
            keep.normed3,
            keep.inverse3,
            *mine,
        ) = results
        if layer:
            current, kept[-1].features = lax.optimization_barrier((current, kept[-1].features))
        keep.output = current
        (keep.heads_pre, features, keep.ends, *fetched), _ = heads_forward(
            blocks,
            layer,
            [],
            cols,
            current,
            heads_t,
            bits,
            mine,
        )
        if fetched:
            reduce_full.append(fetched[0])
            expand_full.append(fetched[1])
        current, features = lax.optimization_barrier((current, features))
        keep.features = gather_parts(features)
        kept.append(keep)
    output = own_slice(current, wide, 1).reshape(rows, cols, wide)

    for layer in range(layers):
        keep = kept[layer]
        (keep.maps, keep.local, keep.gate_sums, partial, keep.message_values), moved = messages_both(
            blocks,
            layer,
            [(gather_kind, keep.ends)] + ([] if layer else [(upper_kind, keep.output)]),
            0,
            bool(layer),
            cols,
            keep.features,
            messages_t,
            cotangents,
            gate_gain,
            gate_bias,
            bits,
        )
        keep.ends_all = moved[0]
        if layer == 0:
            keep.upper = moved[1]
        keep.source_sums = reduce_parts(partial)

    def heads_low_of(keep):
        sums = keep.source_sums.astype(jnp.float32)
        total = jnp.stack([sums[0] + keep.local[0], sums[1], sums[2], sums[3] + keep.local[1]])
        return (total * silu_slope(keep.heads_pre)).astype(low)

    for layer in range(layers):
        keep = kept[layer]
        keep.heads_low = heads_low_of(keep)
        (partial,), moved = heads_backward(
            blocks,
            layer,
            [(upper_kind, keep.output), (lower_kind, keep.output)]
            if layer
            else [(slot_kind, keep.message_values), (lower_kind, keep.output)],
            cols,
            keep.heads_low,
            heads_t,
            bits,
            parts,
        )
        if layer == 0:
            keep.message_values, keep.lower = moved
        else:
            keep.upper, keep.lower = moved
        keep.heads_partial = reduce_parts(partial)
        if layer + 1 < layers:
            kept[layer + 1].source_sums, partial = lax.optimization_barrier(
                (kept[layer + 1].source_sums, partial)
            )
    kept[0].heads_low, partial = lax.optimization_barrier((kept[0].heads_low, partial))
    kept[0].heads_all, kept[1].heads_all = exchange(
        blocks, [(gather_kind, keep.heads_low) for keep in kept]
    )
    kept[1].heads_all, kept[0].heads_partial = lax.optimization_barrier(
        (kept[1].heads_all, kept[0].heads_partial)
    )

    upstream = output_cotangent.reshape(pixels, wide).astype(jnp.float32)
    for layer in reversed(range(layers)):
        keep = kept[layer]
        (
            upstream,
            keep.expand_grad,
            keep.dilated_grad,
            keep.reduce_grad,
            keep.wide_sums,
            keep.second_sums,
            keep.first_sums,
            keep.gates,
            keep.messages_grad,
            keep.heads_grad,
        ), _ = trunk_backward(
            blocks,
            parts,
            layer,
            [],
            (
                upstream,
                keep.heads_partial,
                keep.input,
                keep.normed3,
                keep.inverse3,
                w_expand,
                keep.second_full,
                keep.normed2,
                keep.inverse2,
                dilated_t,
                bits,
                keep.first_ext,
                keep.normed1,
                keep.inverse1,
                reduce_full[layer],
                keep.gate_sums,
            ),
            (norm_gain, norm_bias, wide_gain, wide_bias),
            (
                keep.message_values,
                keep.cotangents,
                keep.ends_all,
                keep.upper,
                keep.lower,
                keep.heads_all,
                all_bits,
            ),
            (gate_gain, gate_bias),
        )
    def stacked(of):
        return jnp.stack([of(keep) for keep in kept])

    narrow_sums = stacked(lambda keep: jnp.stack([keep.first_sums, keep.second_sums]))
    wide_sums = stacked(lambda keep: keep.wide_sums)
    gate_sums = stacked(lambda keep: keep.gates.reshape(2, 6, mid))
    return (
        output,
        stacked(lambda keep: keep.maps.reshape(2, rows, cols, mid)),
        upstream.reshape(rows, cols, wide),
        stacked(lambda keep: keep.reduce_grad),
        stacked(lambda keep: keep.dilated_grad),
        stacked(lambda keep: keep.expand_grad),
        stacked(lambda keep: keep.heads_grad),
        stacked(lambda keep: keep.messages_grad),
        narrow_sums[:, :, 0],
        narrow_sums[:, :, 1],
        wide_sums[:, 0],
        wide_sums[:, 1],
        gate_sums[:, 0],
        gate_sums[:, 1],
    )


def route(*args):
    mid = args[1].shape[1]
    blocks, parts = lax.axis_size(BLK), lax.axis_size(CH)
    whole_tiles = args[1].shape[0] == 2 and mid % lanes == 0 and args[0].shape[1] == lanes and parts >= 2
    if whole_tiles and blocks == 8 and 2 * mid * parts == lanes * blocks:
        return shards(*args)
    return plain_shards(*args)


def solution(mesh):
    placed = (
        P(BLK, None, CH),
        P(None, CH, None),
        P(None, CH, None, None),
        P(None, None, CH),
        P(None, None, CH, None, None),
        P(None, None, CH, None, None),
        P(None, None, CH),
        P(None, None, CH),
        P(None, CH),
        P(None, CH),
        P(None, None, CH),
        P(None, None, CH),
        P(),
        P(BLK, None, CH),
        P(None, None, BLK, None, CH),
    )
    return jax.shard_map(
        route,
        mesh=mesh,
        in_specs=placed,
        out_specs=(
            P(BLK, None, CH),
            P(None, None, BLK, None, CH),
            P(BLK, None, CH),
            P(None, BLK, CH),
            P(None, None, BLK, CH),
            P(None, BLK, CH),
            P(None, None, None, BLK, CH),
            P(None, None, None, BLK, CH),
            P(None, None, CH),
            P(None, None, CH),
            P(None, CH),
            P(None, CH),
            P(None, None, CH),
            P(None, None, CH),
        ),
        check_vma=False,
    )
```
